32 devices in a mesh: ch: 8 (over z, x), tok: 4 (over y, core).
Axes of the slice: x: 2, y: 2, z: 4, core: 2. Of those that a mesh axis runs over, the one named last changes fastest.
Arguments:
- inputs: bfloat16 [4, 768, 4096], P(None, 'ch', 'tok'), may hold values from -6 to 6
- out_grad: bfloat16 [4, 768, 4096], P(None, 'ch', 'tok'), may hold values from -6 to 6
- seq_lengths: int32 [4], replicated, may hold values from 2560 to 4096, as said below
- ema_alpha: float32 [768, 16], P('ch'), may hold values from -0.85 to 0.85
- ema_delta: float32 [768, 16], P('ch'), may hold values from -14 to -1.9
- ema_beta: float32 [768, 16], P('ch'), may hold values from -3 to 3
- ema_eta: float32 [768, 16], P('ch'), may hold values from -1.5 to 1.5
- ema_omega: float32 [768], P('ch'), may hold values from -2 to 2
- w_mix: bfloat16 [768, 3200], replicated, may hold values from -0.21875 to 0.21875
- b_mix: float32 [3200], replicated, may hold values from -1.5 to 1.5
- w_value: bfloat16 [768, 1536], replicated, may hold values from -0.21875 to 0.21875
- b_value: float32 [1536], replicated, may hold values from -1.5 to 1.5
- w_out: bfloat16 [1536, 768], replicated, may hold values from -0.3125 to 0.3125
- b_out: float32 [768], replicated, may hold values from -1.5 to 1.5
- qk_scale: float32 [2, 128], replicated, may hold values from 0.25 to 1.75
- qk_shift: float32 [2, 128], replicated, may hold values from -1.5 to 1.5
- ln_gain: float32 [768], replicated, may hold values from 0.5 to 1.5
- ln_bias: float32 [768], replicated, may hold values from -1.5 to 1.5
- w_up: bfloat16 [768, 1536], replicated, may hold values from -0.21875 to 0.21875
- b_up: float32 [1536], replicated, may hold values from -1.5 to 1.5
- w_down: bfloat16 [1536, 768], replicated, may hold values from -0.21875 to 0.21875
- b_down: float32 [768], replicated, may hold values from -1.5 to 1.5
Outputs:
- output: bfloat16 [4, 768, 4096], P(None, 'ch', 'tok')
- input_grad: float32 [4, 768, 4096], P(None, 'ch', 'tok')
- grad_ema_alpha: float32 [768, 16], P('ch')
- grad_ema_delta: float32 [768, 16], P('ch')
- grad_ema_beta: float32 [768, 16], P('ch')
- grad_ema_eta: float32 [768, 16], P('ch')
- grad_ema_omega: float32 [768], P('ch')
- grad_w_mix: float32 [768, 3200], P('ch')
- grad_b_mix: float32 [3200], replicated
- grad_w_value: float32 [768, 1536], P('ch')
- grad_b_value: float32 [1536], replicated
- grad_w_out: float32 [1536, 768], P('ch')
- grad_b_out: float32 [768], replicated
- grad_qk_scale: float32 [2, 128], replicated
- grad_qk_shift: float32 [2, 128], replicated
- grad_ln_gain: float32 [768], replicated
- grad_ln_bias: float32 [768], replicated
- grad_w_up: float32 [768, 1536], P('ch')
- grad_b_up: float32 [1536], replicated
- grad_w_down: float32 [1536, 768], P('ch')
- grad_b_down: float32 [768], replicated
The draws below stay inside these ranges and needn't reach their ends.
Inputs may be any that keep to these rules, and one draw needn't show every extreme that they name: `seq_lengths`: every sequence but one, chosen by the seed, has 4096 live positions; that one has 2560 or more.
All inputs are finite; a program needn't handle non-finite values.
Results may differ from the reference program's by a relative error of at most 0.025.
The reference program's roundings to bfloat16 on the way count: a program that leaves them out, or rounds other values in their place, can miss the bound.
Values may be sent and summed in bfloat16 or wider, within the bound.
No kernel may reach another device: no remote copies, remote signals or barrier semaphores. Data moves between devices by JAX's collectives and lax.ppermute only.
A program may use at most 192 MiB of HBM per device.

```python
import math
import jax
import jax.numpy as jnp
from jax import lax

D = 768
ZDIM = 128
VDIM = 1536
EMA_DIM = 16
FF = 1536
GROUP = 128
NSEQ = 4
SEQ_LEN = 4096
MIX = 3200


def decay_rates(key, fast_share):
    key_pick, key_slow, key_fast = jax.random.split(key, 3)
    fast = jax.random.bernoulli(key_pick, fast_share, (D, EMA_DIM))
    slow_rate = jnp.exp(jax.random.uniform(key_slow, (D, EMA_DIM), jnp.float32, math.log(0.5 / SEQ_LEN), math.log(4.0 / SEQ_LEN)))
    fast_rate = jnp.exp(jax.random.uniform(key_fast, (D, EMA_DIM), jnp.float32, math.log(1.0 / 64.0), math.log(1.0 / 8.0)))
    return jnp.where(fast, fast_rate, slow_rate)


def draw_ema_delta(key, part):
    share = 0.5
    damping = decay_rates(key, share)
    return jnp.log(damping) - jnp.log1p(-damping)


def draw_ema_beta(key, part):
    share = 0.5
    damping = decay_rates(key, share)
    key = jax.random.fold_in(key, 5)
    normal_part = jax.random.truncated_normal(key, -4.0, 4.0, (D, EMA_DIM), jnp.float32)
    return normal_part * jnp.sqrt(4.0 * damping)


def draw_seq_lengths(key, part):
    key = jax.random.fold_in(key, 7)
    key_pick, key_length = jax.random.split(key)
    chosen = jax.random.randint(key_pick, (), 0, NSEQ)
    shorter = jax.random.randint(key_length, (), SEQ_LEN * 5 // 8, SEQ_LEN)
    return jnp.where(jnp.arange(NSEQ) == chosen, shorter, SEQ_LEN).astype(jnp.int32)


def block_levels(rng, extent, pieces, smallest, largest):
    gain, own = 1.0, jax.random.fold_in(rng, 6)
    for axis_at, blocks in pieces:
        draws = jnp.exp(jax.random.uniform(jax.random.fold_in(own, axis_at), (blocks,), jnp.float32, smallest / len(pieces), largest / len(pieces)))
        gain = gain * jnp.repeat(draws, extent[axis_at] // blocks).reshape([-1 if axis == axis_at else 1 for axis in range(len(extent))])
    return gain


def bell_draw(own_key, dims, width, limit, cuts=(), kind=jnp.bfloat16):
    drawn = jax.random.normal(own_key, dims, jnp.float32) * width
    if len(cuts) > 0:
        drawn = block_levels(own_key, dims, cuts, -0.22, 0.18) * drawn
    return jnp.clip(drawn, min=-limit, max=limit).astype(kind)


def setup_inputs(seed: int = 0) -> dict:
    key_list = jax.random.split(jax.random.key(seed), 23)
    return {
        "inputs": bell_draw(key_list[0], (NSEQ, D, SEQ_LEN), 1.0, 6.0, ((1, 8), (2, 4))),
        "out_grad": bell_draw(key_list[1], (NSEQ, D, SEQ_LEN), 1.0, 6.0, ((1, 8), (2, 4))),
        "seq_lengths": draw_seq_lengths(jax.random.fold_in(key_list[22], 71), 0),
        "ema_alpha": jnp.clip(jax.random.uniform(key_list[3], (D, EMA_DIM), jnp.float32, -0.85, 0.85) * block_levels(key_list[3], (D, EMA_DIM), ((0, 8),), -0.4, 0.0), -0.85, 0.85),
        "ema_delta": draw_ema_delta(jax.random.fold_in(key_list[22], 71), 0),
        "ema_beta": draw_ema_beta(jax.random.fold_in(key_list[22], 71), 0),
        "ema_eta": bell_draw(key_list[6], (D, EMA_DIM), 0.25, 1.5, ((0, 8),), jnp.float32),
        "ema_omega": bell_draw(key_list[7], (D,), 0.5, 2.0, ((0, 8),), jnp.float32),
        "w_mix": bell_draw(key_list[8], (D, MIX), D ** -0.5, 0.21875),
        "b_mix": bell_draw(key_list[9], (MIX,), 0.3, 1.5, (), jnp.float32),
        "w_value": bell_draw(key_list[10], (D, VDIM), D ** -0.5, 0.21875),
        "b_value": bell_draw(key_list[11], (VDIM,), 0.3, 1.5, (), jnp.float32),
        "w_out": bell_draw(key_list[12], (VDIM, D), (VDIM // 4) ** -0.5, 0.3125),
        "b_out": bell_draw(key_list[13], (D,), 0.3, 1.5, (), jnp.float32),
        "qk_scale": jnp.clip(1.0 + 0.15 * jax.random.normal(key_list[14], (2, ZDIM), jnp.float32), 0.25, 1.75),
        "qk_shift": bell_draw(key_list[15], (2, ZDIM), 0.3, 1.5, (), jnp.float32),
        "ln_gain": jnp.clip(1.0 + 0.1 * jax.random.normal(key_list[16], (D,), jnp.float32), 0.5, 1.5),
        "ln_bias": bell_draw(key_list[17], (D,), 0.3, 1.5, (), jnp.float32),
        "w_up": bell_draw(key_list[18], (D, FF), D ** -0.5, 0.21875),
        "b_up": bell_draw(key_list[19], (FF,), 0.3, 1.5, (), jnp.float32),
        "w_down": bell_draw(key_list[20], (FF, D), (FF // 2) ** -0.5, 0.21875),
        "b_down": bell_draw(key_list[21], (D,), 0.3, 1.5, (), jnp.float32),
    }


highest = lax.Precision.HIGHEST

@jax.custom_vjp
def low(v):
    return lax.optimization_barrier(v.astype(jnp.bfloat16)).astype(jnp.float32)

@jax.custom_vjp
def low_back(v):
    return v

def low_keep(v):
    return (low(v), None)

def low_pass(kept, grad):
    return (grad,)

def back_keep(v):
    return (v, None)

def back_low(kept, grad):
    return (low(grad),)
low.defvjp(low_keep, low_pass)
low_back.defvjp(back_keep, back_low)

def matmul(left, right):
    return jnp.matmul(left, right, precision=highest)

def ema_apply(seq_in, alpha_logit, delta_logit, beta, eta):
    rate = jax.nn.sigmoid(alpha_logit)
    damp = jax.nn.sigmoid(delta_logit)
    log_decay = jnp.log1p(-rate * damp)
    scaled = rate * beta
    offsets = jnp.arange(GROUP, dtype=jnp.float32)
    powers = jnp.exp(offsets[None, None, :] * log_decay[:, :, None])
    kernel = lax.optimization_barrier(jnp.sum(eta[:, :, None] * scaled[:, :, None] * powers, axis=1))
    lag = jnp.arange(GROUP)[:, None] - jnp.arange(GROUP)[None, :]
    toeplitz = jnp.where(lag[None] >= 0, kernel[:, jnp.clip(lag, 0, GROUP - 1)], 0.0)
    carry_pow = eta[:, :, None] * powers * jnp.exp(log_decay)[:, :, None]
    state_pow = scaled[:, :, None] * jnp.flip(powers, axis=2)
    group_decay = jnp.exp(GROUP * log_decay)

    def advance(state, block):
        smooth = jnp.einsum('dts,ds->dt', toeplitz, block, precision=highest)
        smooth = smooth + jnp.einsum('djt,dj->dt', carry_pow, state, precision=highest)
        fresh = group_decay * state + jnp.einsum('djs,ds->dj', state_pow, block, precision=highest)
        return (fresh, smooth)
    blocks = seq_in.reshape(D, SEQ_LEN // GROUP, GROUP).transpose(1, 0, 2)
    start = jnp.zeros((D, EMA_DIM), jnp.float32)
    _, smooth = lax.scan(jax.checkpoint(advance), start, blocks)
    return smooth.transpose(1, 0, 2).reshape(D, SEQ_LEN)

def token_block(inputs_blk, mixed_blk, params):
    w_mix, b_mix, w_value, b_value, w_out, b_out, qk_scale, qk_shift, ln_gain, ln_bias, w_up, b_up, w_down, b_down = params
    count = inputs_blk.shape[0]
    resid = low_back(inputs_blk)
    value_pre = low_back(matmul(resid, w_value) + b_value)
    values = low(jax.nn.silu(value_pre))
    mix_pre = low_back(matmul(mixed_blk, w_mix) + b_mix)
    gate_pre = mix_pre[:, :D]
    query_pre = mix_pre[:, D:D + ZDIM]
    reset_pre = mix_pre[:, D + ZDIM:D + ZDIM + VDIM]
    hidden_mix = mix_pre[:, D + ZDIM + VDIM:]
    shared = jax.nn.silu(query_pre)
    queries = low(shared * qk_scale[0] + qk_shift[0])
    keys_all = low(shared * qk_scale[1] + qk_shift[1])
    blocks_n = count // GROUP
    query_blk = queries.reshape(blocks_n, GROUP, ZDIM)
    key_blk = keys_all.reshape(blocks_n, GROUP, ZDIM)
    value_blk = values.reshape(blocks_n, GROUP, VDIM)
    scores = low_back(jnp.einsum('cqz,ckz->cqk', query_blk, key_blk, precision=highest) * ZDIM ** (-0.5))
    position = jnp.arange(GROUP)
    causal = position[:, None] >= position[None, :]
    scores = jnp.where(causal[None], scores, -1e+30)
    probs = low(jax.nn.softmax(scores, axis=-1))
    attended = low_back(jnp.einsum('cqk,ckv->cqv', probs, value_blk, precision=highest).reshape(count, VDIM))
    reset = jax.nn.silu(reset_pre)
    gated = low(reset * attended)
    hidden_pre = low_back(hidden_mix + matmul(gated, w_out) + b_out)
    hidden = jax.nn.silu(hidden_pre)
    update = jax.nn.sigmoid(gate_pre)
    blend = update * hidden + (1.0 - update) * resid
    centered = blend - lax.optimization_barrier(jnp.mean(blend, axis=-1, keepdims=True))
    variance = lax.optimization_barrier(jnp.mean(centered * centered, axis=-1, keepdims=True))
    normed = centered * lax.rsqrt(variance + 1e-05) * ln_gain + ln_bias
    ffn_pre = low_back(matmul(low(normed), w_up) + b_up)
    ffn_hidden = low(jax.nn.silu(ffn_pre))
    return normed + matmul(ffn_hidden, w_down) + b_down

def sequence_forward(seq_in, length, ema, params):
    alpha_logit, delta_logit, beta, eta, omega = ema
    smooth = ema_apply(seq_in, alpha_logit, delta_logit, beta, eta)
    mixed = low(low_back(jax.nn.silu(smooth + omega[:, None] * seq_in)))
    block = min(4096, SEQ_LEN)
    count = SEQ_LEN // block
    rows_in = seq_in.T.reshape(count, block, D)
    rows_mix = mixed.T.reshape(count, block, D)
    block_fn = jax.checkpoint(lambda pair: token_block(pair[0], pair[1], params))
    result = lax.map(block_fn, (rows_in, rows_mix))
    result = result.reshape(SEQ_LEN, D).T
    live = jnp.arange(SEQ_LEN) < length
    return jnp.where(live[None, :], result, 0.0)

def reference(inputs, out_grad, seq_lengths, ema_alpha, ema_delta, ema_beta, ema_eta, ema_omega, w_mix, b_mix, w_value, b_value, w_out, b_out, qk_scale, qk_shift, ln_gain, ln_bias, w_up, b_up, w_down, b_down):
    ema = tuple((arr.astype(jnp.float32) for arr in (ema_alpha, ema_delta, ema_beta, ema_eta, ema_omega)))
    params = tuple((arr.astype(jnp.float32) for arr in (w_mix, b_mix, w_value, b_value, w_out, b_out, qk_scale, qk_shift, ln_gain, ln_bias, w_up, b_up, w_down, b_down)))

    def one_sequence(totals, item):
        seq_in, seq_grad, length = item

        def forward(seq_arg, ema_arg, params_arg):
            return sequence_forward(seq_arg, length, ema_arg, params_arg)
        result, pullback = jax.vjp(forward, seq_in, ema, params)
        grad_in, grad_ema, grad_params = pullback(seq_grad)
        totals = jax.tree.map(jnp.add, totals, (grad_ema, grad_params))
        return (totals, (result.astype(jnp.bfloat16), grad_in))
    zeros = jax.tree.map(jnp.zeros_like, (ema, params))
    totals, (outputs, grads_in) = lax.scan(one_sequence, zeros, (inputs.astype(jnp.float32), out_grad.astype(jnp.float32), seq_lengths))
    grad_ema, grad_params = totals
    return (outputs, grads_in, grad_ema[0], grad_ema[1], grad_ema[2], grad_ema[3], grad_ema[4], grad_params[0], grad_params[1], grad_params[2], grad_params[3], grad_params[4], grad_params[5], grad_params[6], grad_params[7], grad_params[8], grad_params[9], grad_params[10], grad_params[11], grad_params[12], grad_params[13])
```

```python
import jax
import jax.numpy as jnp
from jax import lax
from jax.sharding import PartitionSpec as P

GROUP = 128


highest = lax.Precision.HIGHEST


def prefix(shard, axis, combine, identity, reverse):
    size, position = (lax.axis_size(axis), lax.axis_index(axis))
    everything = jax.tree.map(lambda part: lax.all_gather(part, axis), shard)
    start = jax.tree.map(
        lambda part, zero: jnp.broadcast_to(jnp.asarray(zero, part.dtype), part.shape),
        shard,
        identity,
    )

    def lap(k, before):
        at = size - 1 - k if reverse else k
        reached = at > position if reverse else at < position
        new = combine(before, jax.tree.map(lambda part: part[at], everything))
        return jax.tree.map(lambda a, b: jnp.where(reached, a, b), new, before)

    return lax.fori_loop(0, size, lap, start)


def silu_slope(preact):
    sigma = jax.nn.sigmoid(preact)
    return sigma * (1.0 + preact * (1.0 - sigma))


def decay_logs(alpha_logit, delta_logit):
    return jnp.log1p(-jax.nn.sigmoid(alpha_logit) * jax.nn.sigmoid(delta_logit))


def ema_core(seq_f, alpha_logit, delta_logit, beta, eta, omega, state_in):
    nseq_count, channels, local_len = seq_f.shape
    blocks_n = local_len // GROUP
    log_decay = decay_logs(alpha_logit, delta_logit)
    scaled = jax.nn.sigmoid(alpha_logit) * beta
    offsets = jnp.arange(GROUP, dtype=jnp.float32)
    powers = jnp.exp(offsets[None, None, :] * log_decay[:, :, None])
    kernel = jnp.einsum("dj,djt->dt", eta * scaled, powers, precision=highest)
    lag = offsets[:, None] - offsets[None, :]
    onehot = (lag[None] == offsets[:, None, None]).astype(jnp.float32)
    toeplitz = jnp.einsum("dm,mts->dts", kernel, onehot, precision=highest)
    blocks = seq_f.reshape(nseq_count, channels, blocks_n, GROUP)
    inner = jnp.einsum("dts,ndbs->ndbt", toeplitz, blocks, precision=highest)
    state_pow = scaled[:, :, None] * jnp.flip(powers, axis=2)
    running = jnp.einsum("djs,ndbs->ndbj", state_pow, blocks, precision=highest)
    span = 1
    while span < blocks_n:
        factor = jnp.exp(span * GROUP * log_decay)
        moved = jnp.pad(running, ((0, 0), (0, 0), (span, 0), (0, 0)))[:, :, :blocks_n]
        running = running + factor[None, :, None, :] * moved
        span = span * 2
    starts = jnp.pad(running, ((0, 0), (0, 0), (1, 0), (0, 0)))[:, :, :blocks_n]
    group_ids = jnp.arange(blocks_n, dtype=jnp.float32)
    entry = jnp.exp(group_ids[None, :, None] * (GROUP * log_decay)[:, None, :])
    starts = starts + entry[None] * state_in[:, :, None, :]
    carry_pow = eta[:, :, None] * powers * jnp.exp(log_decay)[:, :, None]
    smooth = inner + jnp.einsum("djt,ndbj->ndbt", carry_pow, starts, precision=highest)
    smooth = smooth.reshape(nseq_count, channels, local_len)
    return jax.nn.silu(smooth + omega[None, :, None] * seq_f)


def state_advance(seq_f, alpha_logit, delta_logit, beta, state_in):
    local_len = seq_f.shape[2]
    log_decay = decay_logs(alpha_logit, delta_logit)
    scaled = jax.nn.sigmoid(alpha_logit) * beta
    reverse_pos = jnp.arange(local_len - 1, -1, -1, dtype=jnp.float32)
    weights = scaled[:, :, None] * jnp.exp(reverse_pos[None, None, :] * log_decay[:, :, None])
    fresh = jnp.einsum("djs,nds->ndj", weights, seq_f, precision=highest)
    return jnp.exp(local_len * log_decay)[None] * state_in + fresh


def chain_combine(earlier, later):
    return (earlier[0] * later[0], later[0][None] * earlier[1] + later[1])


def to_rows(columns):
    return jnp.swapaxes(columns, 1, 2).reshape(-1, columns.shape[1])


def from_rows(table, nseq_count):
    return jnp.swapaxes(table.reshape(nseq_count, -1, table.shape[1]), 1, 2)


ORDER_A = (("tok", 1), ("ch", 0))
ORDER_B = (("ch", 0), ("tok", 1))


def bits_of(axis):
    return lax.axis_size(axis).bit_length() - 1


def exchange(part, axis, bit):
    size = lax.axis_size(axis)
    return lax.ppermute(part, axis, [(i, i ^ (1 << bit)) for i in range(size)])


def reduce_rows(grad, order):
    parts, rows, columns = grad.shape
    ch_bits, tok_bits = bits_of("ch"), bits_of("tok")
    own = rows >> (ch_bits + tok_bits)
    names = [("ch", k) for k in reversed(range(ch_bits))] + [("tok", k) for k in reversed(range(tok_bits))]
    stages = [("tok", 0)] + list(order)
    stages += [name for name in reversed(names) if name not in stages]
    kept = grad.reshape((parts,) + (2,) * len(names) + (own, columns))
    arrived = None
    for axis, bit in stages:
        at = 1 + names.index((axis, bit))
        mine = (lax.axis_index(axis) >> bit) & 1

        def pick(which):
            half = lax.dynamic_index_in_dim(kept, which, at, keepdims=False)
            if arrived is None:
                return half
            other = lax.dynamic_index_in_dim(arrived, which, at, keepdims=False)
            return (half.astype(jnp.float32) + other.astype(jnp.float32)).astype(jnp.bfloat16)

        sent, kept = pick(1 - mine), pick(mine)
        names.remove((axis, bit))
        arrived = exchange(sent, axis, bit)
    total = (kept.astype(jnp.float32) + arrived.astype(jnp.float32)).astype(jnp.bfloat16)
    whole = lax.all_gather(total, "tok", axis=1)
    return whole.reshape(parts, -1, columns).astype(jnp.float32)


def reduce_pair(wide, tall, order):
    rows, columns = tall.shape
    low = jnp.bfloat16
    merged = jnp.stack([wide.astype(low).reshape(rows, columns), tall.astype(low)])
    merged = reduce_rows(merged, order)
    return merged[0].reshape(-1, wide.shape[1]), merged[1]


def local(
    inputs,
    out_grad,
    seq_lengths,
    ema_alpha,
    ema_delta,
    ema_beta,
    ema_eta,
    ema_omega,
    w_mix,
    b_mix,
    w_value,
    b_value,
    w_out,
    b_out,
    qk_scale,
    qk_shift,
    ln_gain,
    ln_bias,
    w_up,
    b_up,
    w_down,
    b_down,
):
    nseq_count, channels, local_len = inputs.shape
    width = w_mix.shape[0]
    zwidth = qk_scale.shape[1]
    vwidth = w_value.shape[1]
    scale = zwidth ** (-0.5)
    tok_index = lax.axis_index("tok")
    seq_f = inputs.astype(jnp.float32)
    log_total = local_len * decay_logs(ema_alpha, ema_delta)
    decay_all = jnp.exp(log_total)
    zero_state = jnp.zeros((nseq_count, channels, ema_alpha.shape[1]), jnp.float32)
    state_dev = state_advance(seq_f, ema_alpha, ema_delta, ema_beta, zero_state)
    state_in = prefix(
        (decay_all, state_dev), "tok", chain_combine, (jnp.ones_like(decay_all), zero_state), False
    )[1]
    activ = ema_core(seq_f, ema_alpha, ema_delta, ema_beta, ema_eta, ema_omega, state_in)
    recv_in, recv_mix = (
        lax.all_to_all(inputs, "ch", split_axis=2, concat_axis=1, tiled=True),
        lax.all_to_all(activ.astype(jnp.bfloat16), "ch", split_axis=2, concat_axis=1, tiled=True),
    )
    tok_in = to_rows(recv_in)
    tok_mix = to_rows(recv_mix)
    row_count = tok_in.shape[0]
    blocks_n = row_count // GROUP
    value_pre = jnp.dot(tok_in, w_value, preferred_element_type=jnp.float32) + b_value
    values = jax.nn.silu(value_pre).astype(jnp.bfloat16)
    mix_pre = jnp.dot(tok_mix, w_mix, preferred_element_type=jnp.float32) + b_mix
    gate_pre = mix_pre[:, :width]
    query_pre = mix_pre[:, width : width + zwidth]
    reset_pre = mix_pre[:, width + zwidth : width + zwidth + vwidth]
    hidden_mix = mix_pre[:, width + zwidth + vwidth :]
    update = jax.nn.sigmoid(gate_pre)
    shared = jax.nn.silu(query_pre)
    queries = (shared * qk_scale[0] + qk_shift[0]).astype(jnp.bfloat16)
    keys_all = (shared * qk_scale[1] + qk_shift[1]).astype(jnp.bfloat16)
    reset = jax.nn.silu(reset_pre)
    query_blk = queries.reshape(blocks_n, GROUP, zwidth)
    key_blk = keys_all.reshape(blocks_n, GROUP, zwidth)
    value_blk = values.reshape(blocks_n, GROUP, vwidth)
    position = jnp.arange(GROUP)
    causal = position[:, None] >= position[None, :]

    def block_scores():
        raw = (
            jnp.einsum("cqz,ckz->cqk", query_blk, key_blk, preferred_element_type=jnp.float32)
            * scale
        )
        return jnp.where(causal[None], raw, -1e30)

    scores = block_scores()
    top_score = jnp.max(scores, axis=-1, keepdims=True)
    log_norm = top_score + jnp.log(jnp.sum(jnp.exp(scores - top_score), axis=-1, keepdims=True))
    probs_bf = jnp.exp(scores - log_norm).astype(jnp.bfloat16)
    attended = jnp.einsum(
        "cqk,ckv->cqv", probs_bf, value_blk, preferred_element_type=jnp.float32
    ).reshape(row_count, vwidth)
    gated = (reset * attended).astype(jnp.bfloat16)
    hidden_pre = hidden_mix + jnp.dot(gated, w_out, preferred_element_type=jnp.float32) + b_out
    hidden = jax.nn.silu(hidden_pre)
    resid = tok_in.astype(jnp.float32)
    blend = update * hidden + (1.0 - update) * resid
    centered = blend - jnp.mean(blend, axis=-1, keepdims=True)
    rstd = lax.rsqrt(jnp.mean(centered * centered, axis=-1, keepdims=True) + 1e-05)
    unit = centered * rstd
    normed = unit * ln_gain + ln_bias
    normed_bf = normed.astype(jnp.bfloat16)
    ffn_pre = jnp.dot(normed_bf, w_up, preferred_element_type=jnp.float32) + b_up
    ffn_hidden = jax.nn.silu(ffn_pre).astype(jnp.bfloat16)
    result = normed + jnp.dot(ffn_hidden, w_down, preferred_element_type=jnp.float32) + b_down
    out_local = lax.all_to_all(
        from_rows(result.astype(jnp.bfloat16), nseq_count),
        "ch",
        split_axis=1,
        concat_axis=2,
        tiled=True,
    )
    seq_pos = tok_index * local_len + jnp.arange(local_len, dtype=jnp.int32)
    live = (seq_pos[None, :] < seq_lengths[:, None])[:, None, :]
    output = jnp.where(live, out_local, jnp.zeros_like(out_local))
    grad_masked = jnp.where(live, out_grad, jnp.zeros_like(out_grad))
    grad_rows = to_rows(lax.all_to_all(grad_masked, "ch", split_axis=2, concat_axis=1, tiled=True))
    grad_f = grad_rows.astype(jnp.float32)
    g_down = jnp.dot(ffn_hidden.T, grad_rows, preferred_element_type=jnp.float32)
    g_bdown = jnp.sum(grad_f, axis=0)
    d_ffn = (
        jnp.dot(grad_rows, w_down.T, preferred_element_type=jnp.float32) * silu_slope(ffn_pre)
    ).astype(jnp.bfloat16)
    g_up = jnp.dot(normed_bf.T, d_ffn, preferred_element_type=jnp.float32)
    g_bup = jnp.sum(d_ffn.astype(jnp.float32), axis=0)
    d_normed = grad_f + jnp.dot(d_ffn, w_up.T, preferred_element_type=jnp.float32)
    g_gain = jnp.sum(d_normed * unit, axis=0)
    g_lnbias = jnp.sum(d_normed, axis=0)
    d_unit = d_normed * ln_gain
    d_blend = rstd * (
        d_unit
        - jnp.mean(d_unit, axis=-1, keepdims=True)
        - unit * jnp.mean(d_unit * unit, axis=-1, keepdims=True)
    )
    d_hidden_pre = (d_blend * update * silu_slope(hidden_pre)).astype(jnp.bfloat16)
    d_update_pre = d_blend * (hidden - resid) * update * (1.0 - update)
    d_direct = d_blend * (1.0 - update)
    g_out = jnp.dot(gated.T, d_hidden_pre, preferred_element_type=jnp.float32)
    g_bout = jnp.sum(d_hidden_pre.astype(jnp.float32), axis=0)
    d_gated = jnp.dot(d_hidden_pre, w_out.T, preferred_element_type=jnp.float32)
    d_reset_pre = d_gated * attended * silu_slope(reset_pre)
    d_attended = (d_gated * reset).astype(jnp.bfloat16).reshape(blocks_n, GROUP, vwidth)
    scores = block_scores()
    probs = jnp.exp(scores - log_norm)
    probs_bf = probs.astype(jnp.bfloat16)
    d_probs = jnp.einsum("cqv,ckv->cqk", d_attended, value_blk, preferred_element_type=jnp.float32)
    d_values = jnp.einsum(
        "cqk,cqv->ckv", probs_bf, d_attended, preferred_element_type=jnp.float32
    ).reshape(row_count, vwidth)
    d_scores = (probs * (d_probs - jnp.sum(d_probs * probs, axis=-1, keepdims=True))).astype(
        jnp.bfloat16
    )
    d_query = (
        jnp.einsum("cqk,ckz->cqz", d_scores, key_blk, preferred_element_type=jnp.float32).reshape(
            row_count, zwidth
        )
        * scale
    )
    d_key = (
        jnp.einsum("cqk,cqz->ckz", d_scores, query_blk, preferred_element_type=jnp.float32).reshape(
            row_count, zwidth
        )
        * scale
    )
    d_value_pre = (d_values * silu_slope(value_pre)).astype(jnp.bfloat16)
    g_value = jnp.dot(tok_in.T, d_value_pre, preferred_element_type=jnp.float32)
    g_bvalue = jnp.sum(d_value_pre.astype(jnp.float32), axis=0)
    d_resid = d_direct + jnp.dot(d_value_pre, w_value.T, preferred_element_type=jnp.float32)
    g_qscale = jnp.stack([jnp.sum(d_query * shared, axis=0), jnp.sum(d_key * shared, axis=0)])
    g_qshift = jnp.stack([jnp.sum(d_query, axis=0), jnp.sum(d_key, axis=0)])
    d_query_pre = (d_query * qk_scale[0] + d_key * qk_scale[1]) * silu_slope(query_pre)
    d_mix_pre = jnp.concatenate(
        [d_update_pre, d_query_pre, d_reset_pre, d_hidden_pre.astype(jnp.float32)], axis=1
    ).astype(jnp.bfloat16)
    g_mix = jnp.dot(tok_mix.T, d_mix_pre, preferred_element_type=jnp.float32)
    g_bmix = jnp.sum(d_mix_pre.astype(jnp.float32), axis=0)
    d_mix_in = jnp.dot(d_mix_pre, w_mix.T, preferred_element_type=jnp.float32)
    back_resid, back_mix = (
        lax.all_to_all(
            from_rows(d_resid.astype(jnp.bfloat16), nseq_count),
            "ch",
            split_axis=1,
            concat_axis=2,
            tiled=True,
        ),
        lax.all_to_all(
            from_rows(d_mix_in.astype(jnp.bfloat16), nseq_count),
            "ch",
            split_axis=1,
            concat_axis=2,
            tiled=True,
        ),
    )
    _, ema_pull = jax.vjp(
        ema_core, seq_f, ema_alpha, ema_delta, ema_beta, ema_eta, ema_omega, state_in
    )
    dx_ema, ga_first, gd_first, gb_first, g_eta, g_omega, state_grad = ema_pull(
        back_mix.astype(jnp.float32)
    )
    later_grad = prefix(
        (decay_all, state_grad), "tok", chain_combine, (jnp.ones_like(decay_all), zero_state), True
    )[1]
    _, state_pull = jax.vjp(state_advance, seq_f, ema_alpha, ema_delta, ema_beta, state_in)
    dx_state, ga_second, gd_second, gb_second, unused_grad = state_pull(later_grad)
    input_grad = back_resid.astype(jnp.float32) + dx_ema + dx_state
    g_up_s, g_down_s = reduce_pair(g_up, g_down, ORDER_A)
    g_value_s, g_out_s = reduce_pair(g_value, g_out, ORDER_B)
    g_mix_s = reduce_rows(g_mix.astype(jnp.bfloat16)[None], ORDER_A)[0]
    ema_grads = lax.psum(
        (ga_first + ga_second, gd_first + gd_second, gb_first + gb_second, g_eta, g_omega), "tok"
    )
    summed = (g_mix_s, g_value_s, g_out_s, g_up_s, g_down_s) + ema_grads
    smalls = lax.psum(
        (g_bmix, g_bvalue, g_bout, g_qscale, g_qshift, g_gain, g_lnbias, g_bup, g_bdown),
        ("ch", "tok"),
    )
    return (
        output,
        input_grad,
        summed[5],
        summed[6],
        summed[7],
        summed[8],
        summed[9],
        summed[0],
        smalls[0],
        summed[1],
        smalls[1],
        summed[2],
        smalls[2],
        smalls[3],
        smalls[4],
        smalls[5],
        smalls[6],
        summed[3],
        smalls[7],
        summed[4],
        smalls[8],
    )


def solution(mesh):
    placed = (
        P(None, "ch", "tok"),
        P(None, "ch", "tok"),
        P(),
        P("ch", None),
        P("ch", None),
        P("ch", None),
        P("ch", None),
        P("ch"),
        P(),
        P(),
        P(),
        P(),
        P(),
        P(),
        P(),
        P(),
        P(),
        P(),
        P(),
        P(),
        P(),
        P(),
    )
    return jax.shard_map(
        local,
        mesh=mesh,
        in_specs=placed,
        out_specs=(
            P(None, "ch", "tok"),
            P(None, "ch", "tok"),
            P("ch", None),
            P("ch", None),
            P("ch", None),
            P("ch", None),
            P("ch"),
            P("ch", None),
            P(),
            P("ch", None),
            P(),
            P("ch", None),
            P(),
            P(),
            P(),
            P(),
            P(),
            P("ch", None),
            P(),
            P("ch", None),
            P(),
        ),
        check_vma=False,
    )
```

```python
import jax
import jax.numpy as jnp
from jax import lax
from jax.experimental import pallas as pl
from jax.experimental.pallas import tpu as pltpu
from jax.sharding import PartitionSpec as P

GROUP = 128
SUB = 8
LANES = 128
f32 = jnp.float32


def by_tile(shape, dim):
    block = tuple(LANES if k == dim else size for k, size in enumerate(shape))
    return pl.BlockSpec(block, lambda i: tuple(i if k == dim else 0 for k in range(len(shape))))


def in_smem():
    return pl.BlockSpec(memory_space=pltpu.SMEM)


def roomy(mib=56):
    return pltpu.CompilerParams(vmem_limit_bytes=mib * 1024 * 1024)


def work(flops, moved, exps=0):
    return pl.CostEstimate(flops=flops, bytes_accessed=moved, transcendentals=exps)


def rates(params_ref):
    rate = jax.nn.sigmoid(params_ref[0])
    drop = rate * jax.nn.sigmoid(params_ref[1])
    weight = params_ref[3] * rate * params_ref[2]
    return 1.0 - drop, jnp.log1p(-drop), weight


def spread(ref, j):
    return jnp.broadcast_to(ref[pl.ds(j, 1), :], (SUB, LANES))


def tree_sum(parts):
    while len(parts) > 1:
        parts = [a + b for a, b in zip(parts[::2], parts[1::2])] + parts[len(parts) & ~1 :]
    return parts[0]


def block_rows(g, t):
    return pl.ds(g * GROUP + t, SUB, stride=GROUP)


def state_rows(g, j, expand):
    return pl.ds(g * expand + j, SUB, stride=expand)


def ema_ends_kernel(x_ref, params_ref, xs_ref, ends_ref, total_ref, decay_ref):
    length = x_ref.shape[1]
    expand = params_ref.shape[1]
    blocks = length // GROUP
    decay, log_decay, _ = rates(params_ref)
    decay_ref[...] = decay
    for b in range(blocks):
        rows = pl.ds(b * GROUP, GROUP)
        xs_ref[rows, :] = x_ref[:, rows].astype(f32).T
    factors = [spread(decay_ref, j) for j in range(expand)]
    for g in range(0, blocks, SUB):

        def step(t, states):
            now = xs_ref[block_rows(g, t), :]
            return tuple(f * s + now for f, s in zip(factors, states))

        states = (jnp.zeros((SUB, LANES), f32),) * expand
        states = lax.fori_loop(0, GROUP, step, states, unroll=8)
        for j in range(expand):
            ends_ref[state_rows(g, j, expand), :] = states[j]
    jump = jnp.exp(GROUP * log_decay)
    carry = jnp.zeros_like(jump)
    for b in range(blocks):
        carry = jump * carry + ends_ref[pl.ds(b * expand, expand), :]
    total_ref[...] = carry


def ema_ends(x, params):
    columns, length = x.shape
    expand = params.shape[1]
    shapes = ((length, columns), (length // GROUP * expand, columns), (expand, columns))
    return pl.pallas_call(
        ema_ends_kernel,
        grid=(columns // LANES,),
        out_shape=tuple(jax.ShapeDtypeStruct(shape, f32) for shape in shapes),
        in_specs=[by_tile(x.shape, 0), by_tile(params.shape, 2)],
        out_specs=tuple(by_tile(shape, 1) for shape in shapes),
        scratch_shapes=[pltpu.VMEM((expand, LANES), f32)],
        compiler_params=roomy(),
        cost_estimate=work(2 * expand * length * columns, 6 * length * columns),
    )(x, params)


def ema_mix_kernel(
    place_ref, xs_ref, ends_ref, params_ref, omega_ref, totals_ref,
    mixed_ref, slope_ref, entry_ref, decay_ref, weight_ref, smooth_ref,
):
    length = xs_ref.shape[0]
    expand = params_ref.shape[1]
    blocks = length // GROUP
    decay, log_decay, weight = rates(params_ref)
    decay_ref[...] = decay
    weight_ref[...] = weight
    whole = jnp.exp(length * log_decay)
    jump = jnp.exp(GROUP * log_decay)
    carry = jnp.zeros_like(jump)
    for k in range(totals_ref.shape[0]):
        carry = jnp.where(k < place_ref[0], whole * carry + totals_ref[k], carry)
    for b in range(blocks):
        rows = pl.ds(b * expand, expand)
        entry_ref[rows, :] = carry
        carry = jump * carry + ends_ref[rows, :]
    factors = [spread(decay_ref, j) for j in range(expand)]
    weights = [spread(weight_ref, j) for j in range(expand)]
    for g in range(0, blocks, SUB):

        def step(t, states):
            now = xs_ref[block_rows(g, t), :]
            states = tuple(f * s + now for f, s in zip(factors, states))
            smooth_ref[block_rows(g, t), :] = tree_sum([w * s for w, s in zip(weights, states)])
            return states

        start = tuple(entry_ref[state_rows(g, j, expand), :] for j in range(expand))
        lax.fori_loop(0, GROUP, step, start, unroll=8)
    for b in range(blocks):
        rows = pl.ds(b * GROUP, GROUP)
        pre = smooth_ref[rows, :] + omega_ref[...] * xs_ref[rows, :]
        sigma = jax.nn.sigmoid(pre)
        mixed_ref[b] = (pre * sigma).T.astype(mixed_ref.dtype)
        slope_ref[rows, :] = (sigma * (1.0 + pre * (1.0 - sigma))).astype(slope_ref.dtype)


def ema_mix(place, xs, ends, params, omega, totals):
    length, columns = xs.shape
    expand = params.shape[1]
    mixed = (length // GROUP, columns, GROUP)
    return pl.pallas_call(
        ema_mix_kernel,
        grid=(columns // LANES,),
        out_shape=(
            jax.ShapeDtypeStruct(mixed, jnp.bfloat16),
            jax.ShapeDtypeStruct(xs.shape, jnp.bfloat16),
            jax.ShapeDtypeStruct(ends.shape, f32),
        ),
        in_specs=[
            in_smem(), by_tile(xs.shape, 1), by_tile(ends.shape, 1), by_tile(params.shape, 2),
            by_tile(omega.shape, 1), by_tile(totals.shape, 2),
        ],
        out_specs=(by_tile(mixed, 1), by_tile(xs.shape, 1), by_tile(ends.shape, 1)),
        scratch_shapes=[
            pltpu.VMEM((expand, LANES), f32),
            pltpu.VMEM((expand, LANES), f32),
            pltpu.VMEM((length, LANES), f32),
        ],
        compiler_params=roomy(),
        cost_estimate=work(4 * expand * length * columns, 10 * length * columns, length * columns),
    )(place, xs, ends, params, omega, totals)


def ema_back_kernel(dmix_ref, slope_ref, params_ref, pull_ref, heads_ref, total_ref, decay_ref):
    length = slope_ref.shape[0]
    expand = params_ref.shape[1]
    blocks = length // GROUP
    decay, log_decay, _ = rates(params_ref)
    decay_ref[...] = decay
    for b in range(blocks):
        rows = pl.ds(b * GROUP, GROUP)
        pull_ref[rows, :] = dmix_ref[b].astype(f32).T * slope_ref[rows, :].astype(f32)
    factors = [spread(decay_ref, j) for j in range(expand)]
    for g in range(0, blocks, SUB):

        def step(t, states):
            now = pull_ref[block_rows(g, GROUP - 1 - t), :]
            return tuple(f * s + now for f, s in zip(factors, states))

        states = (jnp.zeros((SUB, LANES), f32),) * expand
        states = lax.fori_loop(0, GROUP, step, states, unroll=8)
        for j in range(expand):
            heads_ref[state_rows(g, j, expand), :] = states[j]
    jump = jnp.exp(GROUP * log_decay)
    carry = jnp.zeros_like(jump)
    for b in reversed(range(blocks)):
        carry = jump * carry + heads_ref[pl.ds(b * expand, expand), :]
    total_ref[...] = carry


def ema_back(dmix, slope, params):
    length, columns = slope.shape
    expand = params.shape[1]
    shapes = ((length, columns), (length // GROUP * expand, columns), (expand, columns))
    return pl.pallas_call(
        ema_back_kernel,
        grid=(columns // LANES,),
        out_shape=tuple(jax.ShapeDtypeStruct(shape, f32) for shape in shapes),
        in_specs=[by_tile(dmix.shape, 1), by_tile(slope.shape, 1), by_tile(params.shape, 2)],
        out_specs=tuple(by_tile(shape, 1) for shape in shapes),
        scratch_shapes=[pltpu.VMEM((expand, LANES), f32)],
        compiler_params=roomy(),
        cost_estimate=work(2 * expand * length * columns, 8 * length * columns),
    )(dmix, slope, params)


def ema_sums_kernel(xs_ref, pull_ref, entry_ref, params_ref, sums_ref, tails_ref, decay_ref):
    length = xs_ref.shape[0]
    expand = params_ref.shape[1]
    blocks = length // GROUP
    half = expand // 2
    decay, _, _ = rates(params_ref)
    decay_ref[...] = decay
    for low in range(0, expand, half):
        factors = [spread(decay_ref, low + j) for j in range(half)]
        zero = (jnp.zeros((SUB, LANES), f32),) * half
        plain, turned = zero, zero
        for g in range(0, blocks, SUB):

            def step(t, held):
                states, slants, plain, turned = held
                now, pull = xs_ref[block_rows(g, t), :], pull_ref[block_rows(g, t), :]
                slants = tuple(f * p + s for f, p, s in zip(factors, slants, states))
                states = tuple(f * s + now for f, s in zip(factors, states))
                plain = tuple(a + pull * s for a, s in zip(plain, states))
                turned = tuple(a + pull * p for a, p in zip(turned, slants))
                return states, slants, plain, turned

            start = tuple(entry_ref[state_rows(g, low + j, expand), :] for j in range(half))
            held = (start, zero, plain, turned)
            _, slants, plain, turned = lax.fori_loop(0, GROUP, step, held, unroll=4)
            for j in range(half):
                tails_ref[state_rows(g, low + j, expand), :] = slants[j]
        for j in range(half):
            sums_ref[pl.ds(low + j, 1), :] = jnp.sum(plain[j], axis=0, keepdims=True)
            sums_ref[pl.ds(expand + low + j, 1), :] = jnp.sum(turned[j], axis=0, keepdims=True)
    straight = jnp.zeros((SUB, LANES), f32)
    for b in range(0, length, SUB):
        straight = straight + xs_ref[pl.ds(b, SUB), :] * pull_ref[pl.ds(b, SUB), :]
    sums_ref[pl.ds(2 * expand, SUB), :] = straight


def ema_sums(xs, pull, entry, params):
    length, columns = xs.shape
    expand = params.shape[1]
    shapes = ((2 * expand + SUB, columns), entry.shape)
    return pl.pallas_call(
        ema_sums_kernel,
        grid=(columns // LANES,),
        out_shape=tuple(jax.ShapeDtypeStruct(shape, f32) for shape in shapes),
        in_specs=[by_tile(xs.shape, 1), by_tile(xs.shape, 1), by_tile(entry.shape, 1), by_tile(params.shape, 2)],
        out_specs=tuple(by_tile(shape, 1) for shape in shapes),
        scratch_shapes=[pltpu.VMEM((expand, LANES), f32)],
        compiler_params=roomy(),
        cost_estimate=work(8 * expand * length * columns, 8 * length * columns),
    )(xs, pull, entry, params)


def ema_finish_kernel(
    place_ref, pull_ref, heads_ref, params_ref, omega_ref, totals_ref, sums_ref, tails_ref, direct_ref,
    grad_ref, total_ref, decay_ref, weight_ref, enter_ref, smooth_ref,
):
    length = pull_ref.shape[0]
    expand = params_ref.shape[1]
    blocks = length // GROUP
    decay, log_decay, weight = rates(params_ref)
    decay_ref[...] = decay
    weight_ref[...] = weight
    whole = jnp.exp(length * log_decay)
    jump = jnp.exp(GROUP * log_decay)
    carry = jnp.zeros_like(jump)
    for k in reversed(range(totals_ref.shape[0])):
        carry = jnp.where(k > place_ref[0], whole * carry + totals_ref[k], carry)
    turned = sums_ref[pl.ds(expand, expand), :]
    for b in reversed(range(blocks)):
        rows = pl.ds(b * expand, expand)
        enter_ref[rows, :] = carry
        turned = turned + carry * decay * tails_ref[rows, :]
        carry = jump * carry + heads_ref[rows, :]
    total_ref[...] = sums_ref[...]
    total_ref[pl.ds(expand, expand), :] = turned
    factors = [spread(decay_ref, j) for j in range(expand)]
    weights = [spread(weight_ref, j) for j in range(expand)]
    for g in range(0, blocks, SUB):

        def step(t, states):
            now = pull_ref[block_rows(g, GROUP - 1 - t), :]
            states = tuple(f * s + now for f, s in zip(factors, states))
            back = tree_sum([w * s for w, s in zip(weights, states)])
            smooth_ref[block_rows(g, GROUP - 1 - t), :] = back
            return states

        start = tuple(enter_ref[state_rows(g, j, expand), :] for j in range(expand))
        lax.fori_loop(0, GROUP, step, start, unroll=8)
    for b in range(blocks):
        rows = pl.ds(b * GROUP, GROUP)
        back = smooth_ref[rows, :] + omega_ref[...] * pull_ref[rows, :]
        grad_ref[:, rows] = back.T + direct_ref[b].astype(f32)


def ema_finish(place, pull, heads, params, omega, totals, sums, tails, direct):
    length, columns = pull.shape
    expand = params.shape[1]
    return pl.pallas_call(
        ema_finish_kernel,
        grid=(columns // LANES,),
        out_shape=(jax.ShapeDtypeStruct((columns, length), f32), jax.ShapeDtypeStruct(sums.shape, f32)),
        in_specs=[
            in_smem(), by_tile(pull.shape, 1), by_tile(heads.shape, 1), by_tile(params.shape, 2),
            by_tile(omega.shape, 1), by_tile(totals.shape, 2), by_tile(sums.shape, 1),
            by_tile(tails.shape, 1), by_tile(direct.shape, 1),
        ],
        out_specs=(by_tile((columns, length), 0), by_tile(sums.shape, 1)),
        scratch_shapes=[
            pltpu.VMEM((expand, LANES), f32),
            pltpu.VMEM((expand, LANES), f32),
            pltpu.VMEM((heads.shape[0], LANES), f32),
            pltpu.VMEM((length, LANES), f32),
        ],
        compiler_params=roomy(),
        cost_estimate=work(4 * expand * length * columns, 14 * length * columns),
    )(place, pull, heads, params, omega, totals, sums, tails, direct)


def pad_to_lanes(part, dim):
    extra = -part.shape[dim] % LANES
    if extra == 0:
        return part
    return jnp.pad(part, [(0, extra if k == dim else 0) for k in range(part.ndim)])


def ema_params(alpha, delta, beta, eta, count):
    packed = jnp.swapaxes(jnp.stack([alpha, delta, beta, eta]), 1, 2)
    return pad_to_lanes(jnp.tile(packed, (1, 1, count)), 2)


def ema_param_grads(total, alpha, delta, beta, eta, count):
    channels, expand = alpha.shape
    summed = jnp.sum(total[:, : count * channels].reshape(-1, count, channels), axis=1)
    plain, turned = summed[:expand].T, summed[expand : 2 * expand].T
    omega = jnp.sum(summed[2 * expand :], axis=0)
    rate, damp = jax.nn.sigmoid(alpha), jax.nn.sigmoid(delta)
    g_alpha = eta * beta * rate * (1.0 - rate) * (plain - damp * rate * turned)
    g_delta = -(eta * beta * rate * rate * damp * (1.0 - damp)) * turned
    return g_alpha, g_delta, rate * eta * plain, rate * beta * plain, omega


def silu_slope(preact):
    sigma = jax.nn.sigmoid(preact)
    return sigma * (1.0 + preact * (1.0 - sigma))


def to_rows(parts):
    devices, count, channels, length = parts.shape
    return parts.transpose(1, 3, 0, 2).reshape(count * length, devices * channels)


def from_rows(table, count, devices):
    length, channels = table.shape[0] // count, table.shape[1] // devices
    return table.reshape(count, length, devices, channels).transpose(2, 0, 3, 1)


def swap(parts):
    return lax.all_to_all(parts, "ch", split_axis=0, concat_axis=0, tiled=True)


ORDER_A = (("tok", 1), ("ch", 0))
ORDER_B = (("ch", 0), ("tok", 1))


def bits_of(axis):
    return lax.axis_size(axis).bit_length() - 1


def exchange(part, axis, bit):
    size = lax.axis_size(axis)
    return lax.ppermute(part, axis, [(i, i ^ (1 << bit)) for i in range(size)])


def reduce_rows(grad, order):
    parts, rows, columns = grad.shape
    ch_bits, tok_bits = bits_of("ch"), bits_of("tok")
    own = rows >> (ch_bits + tok_bits)
    names = [("ch", k) for k in reversed(range(ch_bits))] + [("tok", k) for k in reversed(range(tok_bits))]
    stages = [("tok", 0)] + list(order)
    stages += [name for name in reversed(names) if name not in stages]
    kept = grad.reshape((parts,) + (2,) * len(names) + (own, columns))
    arrived = None
    for axis, bit in stages:
        at = 1 + names.index((axis, bit))
        mine = (lax.axis_index(axis) >> bit) & 1

        def pick(which):
            half = lax.dynamic_index_in_dim(kept, which, at, keepdims=False)
            if arrived is None:
                return half
            other = lax.dynamic_index_in_dim(arrived, which, at, keepdims=False)
            return (half.astype(jnp.float32) + other.astype(jnp.float32)).astype(jnp.bfloat16)

        sent, kept = pick(1 - mine), pick(mine)
        names.remove((axis, bit))
        arrived = exchange(sent, axis, bit)
    total = (kept.astype(jnp.float32) + arrived.astype(jnp.float32)).astype(jnp.bfloat16)
    whole = lax.all_gather(total, "tok", axis=1)
    return whole.reshape(parts, -1, columns).astype(jnp.float32)


def reduce_pair(wide, tall, order):
    rows, columns = tall.shape
    low = jnp.bfloat16
    merged = jnp.stack([wide.astype(low).reshape(rows, columns), tall.astype(low)])
    merged = reduce_rows(merged, order)
    return merged[0].reshape(-1, wide.shape[1]), merged[1]


def local(
    inputs,
    out_grad,
    seq_lengths,
    ema_alpha,
    ema_delta,
    ema_beta,
    ema_eta,
    ema_omega,
    w_mix,
    b_mix,
    w_value,
    b_value,
    w_out,
    b_out,
    qk_scale,
    qk_shift,
    ln_gain,
    ln_bias,
    w_up,
    b_up,
    w_down,
    b_down,
):
    nseq_count, channels, local_len = inputs.shape
    width = w_mix.shape[0]
    zwidth = qk_scale.shape[1]
    vwidth = w_value.shape[1]
    scale = zwidth ** (-0.5)
    tok_index = lax.axis_index("tok")
    devices = lax.axis_size("ch")
    columns = nseq_count * channels
    span = local_len // devices
    place = tok_index.astype(jnp.int32)[None]

    def by_block(part):
        return part.reshape(nseq_count, channels, devices, span).transpose(2, 0, 1, 3)

    recv_in = swap(by_block(inputs))
    params = ema_params(ema_alpha, ema_delta, ema_beta, ema_eta, nseq_count)
    omega = pad_to_lanes(jnp.tile(ema_omega, nseq_count)[None], 1)
    xs, ends, total = ema_ends(pad_to_lanes(inputs.reshape(columns, local_len), 0), params)
    totals = lax.all_gather(total, "tok")
    mixed, slope, entry = ema_mix(place, xs, ends, params, omega, totals)
    recv_mix = swap(mixed[:, :columns].reshape(devices, nseq_count, channels, span))
    tok_in = to_rows(recv_in)
    tok_mix = to_rows(recv_mix)
    row_count = tok_in.shape[0]
    blocks_n = row_count // GROUP
    value_pre = jnp.dot(tok_in, w_value, preferred_element_type=jnp.float32) + b_value
    values = jax.nn.silu(value_pre).astype(jnp.bfloat16)
    mix_pre = jnp.dot(tok_mix, w_mix, preferred_element_type=jnp.float32) + b_mix
    gate_pre = mix_pre[:, :width]
    query_pre = mix_pre[:, width : width + zwidth]
    reset_pre = mix_pre[:, width + zwidth : width + zwidth + vwidth]
    hidden_mix = mix_pre[:, width + zwidth + vwidth :]
    update = jax.nn.sigmoid(gate_pre)
    shared = jax.nn.silu(query_pre)
    queries = (shared * qk_scale[0] + qk_shift[0]).astype(jnp.bfloat16)
    keys_all = (shared * qk_scale[1] + qk_shift[1]).astype(jnp.bfloat16)
    reset = jax.nn.silu(reset_pre)
    query_blk = queries.reshape(blocks_n, GROUP, zwidth)
    key_blk = keys_all.reshape(blocks_n, GROUP, zwidth)
    value_blk = values.reshape(blocks_n, GROUP, vwidth)
    position = jnp.arange(GROUP)
    causal = position[:, None] >= position[None, :]

    def block_scores():
        raw = (
            jnp.einsum("cqz,ckz->cqk", query_blk, key_blk, preferred_element_type=jnp.float32)
            * scale
        )
        return jnp.where(causal[None], raw, -1e30)

    scores = block_scores()
    top_score = jnp.max(scores, axis=-1, keepdims=True)
    log_norm = top_score + jnp.log(jnp.sum(jnp.exp(scores - top_score), axis=-1, keepdims=True))
    probs_bf = jnp.exp(scores - log_norm).astype(jnp.bfloat16)
    attended = jnp.einsum(
        "cqk,ckv->cqv", probs_bf, value_blk, preferred_element_type=jnp.float32
    ).reshape(row_count, vwidth)
    gated = (reset * attended).astype(jnp.bfloat16)
    hidden_pre = hidden_mix + jnp.dot(gated, w_out, preferred_element_type=jnp.float32) + b_out
    hidden = jax.nn.silu(hidden_pre)
    resid = tok_in.astype(jnp.float32)
    blend = update * hidden + (1.0 - update) * resid
    centered = blend - jnp.mean(blend, axis=-1, keepdims=True)
    rstd = lax.rsqrt(jnp.mean(centered * centered, axis=-1, keepdims=True) + 1e-05)
    unit = centered * rstd
    normed = unit * ln_gain + ln_bias
    normed_bf = normed.astype(jnp.bfloat16)
    ffn_pre = jnp.dot(normed_bf, w_up, preferred_element_type=jnp.float32) + b_up
    ffn_hidden = jax.nn.silu(ffn_pre).astype(jnp.bfloat16)
    result = normed + jnp.dot(ffn_hidden, w_down, preferred_element_type=jnp.float32) + b_down
    out_local = swap(from_rows(result.astype(jnp.bfloat16), nseq_count, devices))
    seq_pos = tok_index * local_len + jnp.arange(local_len, dtype=jnp.int32)
    live = (seq_pos[None, :] < seq_lengths[:, None])[:, None, :]
    out_local = out_local.transpose(1, 2, 0, 3).reshape(inputs.shape)
    output = jnp.where(live, out_local, jnp.zeros_like(out_local))
    grad_rows = to_rows(swap(by_block(jnp.where(live, out_grad, jnp.zeros_like(out_grad)))))
    grad_f = grad_rows.astype(jnp.float32)
    g_down = jnp.dot(ffn_hidden.T, grad_rows, preferred_element_type=jnp.float32)
    g_bdown = jnp.sum(grad_f, axis=0)
    d_ffn = (
        jnp.dot(grad_rows, w_down.T, preferred_element_type=jnp.float32) * silu_slope(ffn_pre)
    ).astype(jnp.bfloat16)
    g_up = jnp.dot(normed_bf.T, d_ffn, preferred_element_type=jnp.float32)
    g_bup = jnp.sum(d_ffn.astype(jnp.float32), axis=0)
    d_normed = grad_f + jnp.dot(d_ffn, w_up.T, preferred_element_type=jnp.float32)
    g_gain = jnp.sum(d_normed * unit, axis=0)
    g_lnbias = jnp.sum(d_normed, axis=0)
    d_unit = d_normed * ln_gain
    d_blend = rstd * (
        d_unit
        - jnp.mean(d_unit, axis=-1, keepdims=True)
        - unit * jnp.mean(d_unit * unit, axis=-1, keepdims=True)
    )
    d_hidden_pre = (d_blend * update * silu_slope(hidden_pre)).astype(jnp.bfloat16)
    d_update_pre = d_blend * (hidden - resid) * update * (1.0 - update)
    d_direct = d_blend * (1.0 - update)
    g_out = jnp.dot(gated.T, d_hidden_pre, preferred_element_type=jnp.float32)
    g_bout = jnp.sum(d_hidden_pre.astype(jnp.float32), axis=0)
    d_gated = jnp.dot(d_hidden_pre, w_out.T, preferred_element_type=jnp.float32)
    d_reset_pre = d_gated * attended * silu_slope(reset_pre)
    d_attended = (d_gated * reset).astype(jnp.bfloat16).reshape(blocks_n, GROUP, vwidth)
    scores = block_scores()
    probs = jnp.exp(scores - log_norm)
    probs_bf = probs.astype(jnp.bfloat16)
    d_probs = jnp.einsum("cqv,ckv->cqk", d_attended, value_blk, preferred_element_type=jnp.float32)
    d_values = jnp.einsum(
        "cqk,cqv->ckv", probs_bf, d_attended, preferred_element_type=jnp.float32
    ).reshape(row_count, vwidth)
    d_scores = (probs * (d_probs - jnp.sum(d_probs * probs, axis=-1, keepdims=True))).astype(
        jnp.bfloat16
    )
    d_query = (
        jnp.einsum("cqk,ckz->cqz", d_scores, key_blk, preferred_element_type=jnp.float32).reshape(
            row_count, zwidth
        )
        * scale
    )
    d_key = (
        jnp.einsum("cqk,cqz->ckz", d_scores, query_blk, preferred_element_type=jnp.float32).reshape(
            row_count, zwidth
        )
        * scale
    )
    d_value_pre = (d_values * silu_slope(value_pre)).astype(jnp.bfloat16)
    g_value = jnp.dot(tok_in.T, d_value_pre, preferred_element_type=jnp.float32)
    g_bvalue = jnp.sum(d_value_pre.astype(jnp.float32), axis=0)
    d_resid = d_direct + jnp.dot(d_value_pre, w_value.T, preferred_element_type=jnp.float32)
    g_qscale = jnp.stack([jnp.sum(d_query * shared, axis=0), jnp.sum(d_key * shared, axis=0)])
    g_qshift = jnp.stack([jnp.sum(d_query, axis=0), jnp.sum(d_key, axis=0)])
    d_query_pre = (d_query * qk_scale[0] + d_key * qk_scale[1]) * silu_slope(query_pre)
    d_mix_pre = jnp.concatenate(
        [d_update_pre, d_query_pre, d_reset_pre, d_hidden_pre.astype(jnp.float32)], axis=1
    ).astype(jnp.bfloat16)
    g_mix = jnp.dot(tok_mix.T, d_mix_pre, preferred_element_type=jnp.float32)
    g_bmix = jnp.sum(d_mix_pre.astype(jnp.float32), axis=0)
    d_mix_in = jnp.dot(d_mix_pre, w_mix.T, preferred_element_type=jnp.float32)
    back_mix = swap(from_rows(d_mix_in.astype(jnp.bfloat16), nseq_count, devices))
    back_resid = swap(from_rows(d_resid.astype(jnp.bfloat16), nseq_count, devices))
    back_mix = pad_to_lanes(back_mix.reshape(devices, columns, span), 1)
    back_resid = pad_to_lanes(back_resid.reshape(devices, columns, span), 1)
    pull, heads, total = ema_back(back_mix, slope, params)
    totals = lax.all_gather(total, "tok")
    sums, tails = ema_sums(xs, pull, entry, params)
    input_grad, sums = ema_finish(place, pull, heads, params, omega, totals, sums, tails, back_resid)
    input_grad = input_grad[:columns].reshape(inputs.shape)
    g_up_s, g_down_s = reduce_pair(g_up, g_down, ORDER_A)
    g_value_s, g_out_s = reduce_pair(g_value, g_out, ORDER_B)
    g_mix_s = reduce_rows(g_mix.astype(jnp.bfloat16)[None], ORDER_A)[0]
    ema_grads = ema_param_grads(
        lax.psum(sums, "tok"), ema_alpha, ema_delta, ema_beta, ema_eta, nseq_count
    )
    summed = (g_mix_s, g_value_s, g_out_s, g_up_s, g_down_s) + ema_grads
    smalls = lax.psum(
        (g_bmix, g_bvalue, g_bout, g_qscale, g_qshift, g_gain, g_lnbias, g_bup, g_bdown),
        ("ch", "tok"),
    )
    return (
        output,
        input_grad,
        summed[5],
        summed[6],
        summed[7],
        summed[8],
        summed[9],
        summed[0],
        smalls[0],
        summed[1],
        smalls[1],
        summed[2],
        smalls[2],
        smalls[3],
        smalls[4],
        smalls[5],
        smalls[6],
        summed[3],
        smalls[7],
        summed[4],
        smalls[8],
    )


def solution(mesh):
    placed = (
        P(None, "ch", "tok"),
        P(None, "ch", "tok"),
        P(),
        P("ch", None),
        P("ch", None),
        P("ch", None),
        P("ch", None),
        P("ch"),
        P(),
        P(),
        P(),
        P(),
        P(),
        P(),
        P(),
        P(),
        P(),
        P(),
        P(),
        P(),
        P(),
        P(),
    )
    return jax.shard_map(
        local,
        mesh=mesh,
        in_specs=placed,
        out_specs=(
            P(None, "ch", "tok"),
            P(None, "ch", "tok"),
            P("ch", None),
            P("ch", None),
            P("ch", None),
            P("ch", None),
            P("ch"),
            P("ch", None),
            P(),
            P("ch", None),
            P(),
            P("ch", None),
            P(),
            P(),
            P(),
            P(),
            P(),
            P("ch", None),
            P(),
            P("ch", None),
            P(),
        ),
        check_vma=False,
    )
```

```python
import functools
import jax
import jax.numpy as jnp
from jax import lax
from jax.experimental import pallas as pl
from jax.experimental.pallas import tpu as pltpu
from jax.sharding import PartitionSpec as P

GROUP = 128
SUB = 8
LANES = 128
f32 = jnp.float32


def by_tile(shape, dim):
    block = tuple(LANES if k == dim else size for k, size in enumerate(shape))
    return pl.BlockSpec(block, lambda i: tuple(i if k == dim else 0 for k in range(len(shape))))


def in_smem():
    return pl.BlockSpec(memory_space=pltpu.SMEM)


def roomy(mib=56):
    return pltpu.CompilerParams(vmem_limit_bytes=mib * 1024 * 1024)


def work(flops, moved, exps=0):
    return pl.CostEstimate(flops=flops, bytes_accessed=moved, transcendentals=exps)


def rates(params_ref):
    rate = jax.nn.sigmoid(params_ref[0])
    drop = rate * jax.nn.sigmoid(params_ref[1])
    weight = params_ref[3] * rate * params_ref[2]
    return 1.0 - drop, jnp.log1p(-drop), weight


def spread(ref, j):
    return jnp.broadcast_to(ref[pl.ds(j, 1), :], (SUB, LANES))


def tree_sum(parts):
    while len(parts) > 1:
        parts = [a + b for a, b in zip(parts[::2], parts[1::2])] + parts[len(parts) & ~1 :]
    return parts[0]


def block_rows(g, t):
    return pl.ds(g * GROUP + t, SUB, stride=GROUP)


def state_rows(g, j, expand):
    return pl.ds(g * expand + j, SUB, stride=expand)


def ema_ends_kernel(x_ref, params_ref, xs_ref, ends_ref, total_ref, decay_ref):
    length = x_ref.shape[1]
    expand = params_ref.shape[1]
    blocks = length // GROUP
    decay, log_decay, _ = rates(params_ref)
    decay_ref[...] = decay
    for b in range(blocks):
        rows = pl.ds(b * GROUP, GROUP)
        xs_ref[rows, :] = x_ref[:, rows].astype(f32).T
    factors = [spread(decay_ref, j) for j in range(expand)]
    for g in range(0, blocks, SUB):

        def step(t, states):
            now = xs_ref[block_rows(g, t), :]
            return tuple(f * s + now for f, s in zip(factors, states))

        states = (jnp.zeros((SUB, LANES), f32),) * expand
        states = lax.fori_loop(0, GROUP, step, states, unroll=8)
        for j in range(expand):
            ends_ref[state_rows(g, j, expand), :] = states[j]
    jump = jnp.exp(GROUP * log_decay)
    carry = jnp.zeros_like(jump)
    for b in range(blocks):
        carry = jump * carry + ends_ref[pl.ds(b * expand, expand), :]
    total_ref[...] = carry


def ema_ends(x, params):
    columns, length = x.shape
    expand = params.shape[1]
    shapes = ((length, columns), (length // GROUP * expand, columns), (expand, columns))
    return pl.pallas_call(
        ema_ends_kernel,
        grid=(columns // LANES,),
        out_shape=tuple(jax.ShapeDtypeStruct(shape, f32) for shape in shapes),
        in_specs=[by_tile(x.shape, 0), by_tile(params.shape, 2)],
        out_specs=tuple(by_tile(shape, 1) for shape in shapes),
        scratch_shapes=[pltpu.VMEM((expand, LANES), f32)],
        compiler_params=roomy(),
        cost_estimate=work(2 * expand * length * columns, 6 * length * columns),
    )(x, params)


def ema_mix_kernel(
    place_ref, xs_ref, ends_ref, params_ref, omega_ref, totals_ref,
    mixed_ref, slope_ref, entry_ref, decay_ref, weight_ref, smooth_ref,
):
    length = xs_ref.shape[0]
    expand = params_ref.shape[1]
    blocks = length // GROUP
    decay, log_decay, weight = rates(params_ref)
    decay_ref[...] = decay
    weight_ref[...] = weight
    whole = jnp.exp(length * log_decay)
    jump = jnp.exp(GROUP * log_decay)
    carry = jnp.zeros_like(jump)
    for k in range(totals_ref.shape[0]):
        carry = jnp.where(k < place_ref[0], whole * carry + totals_ref[k], carry)
    for b in range(blocks):
        rows = pl.ds(b * expand, expand)
        entry_ref[rows, :] = carry
        carry = jump * carry + ends_ref[rows, :]
    factors = [spread(decay_ref, j) for j in range(expand)]
    weights = [spread(weight_ref, j) for j in range(expand)]
    for g in range(0, blocks, SUB):

        def step(t, states):
            now = xs_ref[block_rows(g, t), :]
            states = tuple(f * s + now for f, s in zip(factors, states))
            smooth_ref[block_rows(g, t), :] = tree_sum([w * s for w, s in zip(weights, states)])
            return states

        start = tuple(entry_ref[state_rows(g, j, expand), :] for j in range(expand))
        lax.fori_loop(0, GROUP, step, start, unroll=8)
    for b in range(blocks):
        rows = pl.ds(b * GROUP, GROUP)
        pre = smooth_ref[rows, :] + omega_ref[...] * xs_ref[rows, :]
        sigma = jax.nn.sigmoid(pre)
        mixed_ref[b] = (pre * sigma).T.astype(mixed_ref.dtype)
        slope_ref[rows, :] = (sigma * (1.0 + pre * (1.0 - sigma))).astype(slope_ref.dtype)


def ema_mix(place, xs, ends, params, omega, totals):
    length, columns = xs.shape
    expand = params.shape[1]
    mixed = (length // GROUP, columns, GROUP)
    return pl.pallas_call(
        ema_mix_kernel,
        grid=(columns // LANES,),
        out_shape=(
            jax.ShapeDtypeStruct(mixed, jnp.bfloat16),
            jax.ShapeDtypeStruct(xs.shape, jnp.bfloat16),
            jax.ShapeDtypeStruct(ends.shape, f32),
        ),
        in_specs=[
            in_smem(), by_tile(xs.shape, 1), by_tile(ends.shape, 1), by_tile(params.shape, 2),
            by_tile(omega.shape, 1), by_tile(totals.shape, 2),
        ],
        out_specs=(by_tile(mixed, 1), by_tile(xs.shape, 1), by_tile(ends.shape, 1)),
        scratch_shapes=[
            pltpu.VMEM((expand, LANES), f32),
            pltpu.VMEM((expand, LANES), f32),
            pltpu.VMEM((length, LANES), f32),
        ],
        compiler_params=roomy(),
        cost_estimate=work(4 * expand * length * columns, 10 * length * columns, length * columns),
    )(place, xs, ends, params, omega, totals)


def ema_back_kernel(dmix_ref, slope_ref, params_ref, pull_ref, heads_ref, total_ref, decay_ref):
    length = slope_ref.shape[0]
    expand = params_ref.shape[1]
    blocks = length // GROUP
    decay, log_decay, _ = rates(params_ref)
    decay_ref[...] = decay
    for b in range(blocks):
        rows = pl.ds(b * GROUP, GROUP)
        pull_ref[rows, :] = dmix_ref[b].astype(f32).T * slope_ref[rows, :].astype(f32)
    factors = [spread(decay_ref, j) for j in range(expand)]
    for g in range(0, blocks, SUB):

        def step(t, states):
            now = pull_ref[block_rows(g, GROUP - 1 - t), :]
            return tuple(f * s + now for f, s in zip(factors, states))

        states = (jnp.zeros((SUB, LANES), f32),) * expand
        states = lax.fori_loop(0, GROUP, step, states, unroll=8)
        for j in range(expand):
            heads_ref[state_rows(g, j, expand), :] = states[j]
    jump = jnp.exp(GROUP * log_decay)
    carry = jnp.zeros_like(jump)
    for b in reversed(range(blocks)):
        carry = jump * carry + heads_ref[pl.ds(b * expand, expand), :]
    total_ref[...] = carry


def ema_back(dmix, slope, params):
    length, columns = slope.shape
    expand = params.shape[1]
    shapes = ((length, columns), (length // GROUP * expand, columns), (expand, columns))
    return pl.pallas_call(
        ema_back_kernel,
        grid=(columns // LANES,),
        out_shape=tuple(jax.ShapeDtypeStruct(shape, f32) for shape in shapes),
        in_specs=[by_tile(dmix.shape, 1), by_tile(slope.shape, 1), by_tile(params.shape, 2)],
        out_specs=tuple(by_tile(shape, 1) for shape in shapes),
        scratch_shapes=[pltpu.VMEM((expand, LANES), f32)],
        compiler_params=roomy(),
        cost_estimate=work(2 * expand * length * columns, 8 * length * columns),
    )(dmix, slope, params)


def ema_sums_kernel(xs_ref, pull_ref, entry_ref, params_ref, sums_ref, tails_ref, decay_ref):
    length = xs_ref.shape[0]
    expand = params_ref.shape[1]
    blocks = length // GROUP
    half = expand // 2
    decay, _, _ = rates(params_ref)
    decay_ref[...] = decay
    for low in range(0, expand, half):
        factors = [spread(decay_ref, low + j) for j in range(half)]
        zero = (jnp.zeros((SUB, LANES), f32),) * half
        plain, turned = zero, zero
        for g in range(0, blocks, SUB):

            def step(t, held):
                states, slants, plain, turned = held
                now, pull = xs_ref[block_rows(g, t), :], pull_ref[block_rows(g, t), :]
                slants = tuple(f * p + s for f, p, s in zip(factors, slants, states))
                states = tuple(f * s + now for f, s in zip(factors, states))
                plain = tuple(a + pull * s for a, s in zip(plain, states))
                turned = tuple(a + pull * p for a, p in zip(turned, slants))
                return states, slants, plain, turned

            start = tuple(entry_ref[state_rows(g, low + j, expand), :] for j in range(half))
            held = (start, zero, plain, turned)
            _, slants, plain, turned = lax.fori_loop(0, GROUP, step, held, unroll=4)
            for j in range(half):
                tails_ref[state_rows(g, low + j, expand), :] = slants[j]
        for j in range(half):
            sums_ref[pl.ds(low + j, 1), :] = jnp.sum(plain[j], axis=0, keepdims=True)
            sums_ref[pl.ds(expand + low + j, 1), :] = jnp.sum(turned[j], axis=0, keepdims=True)
    straight = jnp.zeros((SUB, LANES), f32)
    for b in range(0, length, SUB):
        straight = straight + xs_ref[pl.ds(b, SUB), :] * pull_ref[pl.ds(b, SUB), :]
    sums_ref[pl.ds(2 * expand, SUB), :] = straight


def ema_sums(xs, pull, entry, params):
    length, columns = xs.shape
    expand = params.shape[1]
    shapes = ((2 * expand + SUB, columns), entry.shape)
    return pl.pallas_call(
        ema_sums_kernel,
        grid=(columns // LANES,),
        out_shape=tuple(jax.ShapeDtypeStruct(shape, f32) for shape in shapes),
        in_specs=[by_tile(xs.shape, 1), by_tile(xs.shape, 1), by_tile(entry.shape, 1), by_tile(params.shape, 2)],
        out_specs=tuple(by_tile(shape, 1) for shape in shapes),
        scratch_shapes=[pltpu.VMEM((expand, LANES), f32)],
        compiler_params=roomy(),
        cost_estimate=work(8 * expand * length * columns, 8 * length * columns),
    )(xs, pull, entry, params)


def ema_finish_kernel(
    place_ref, pull_ref, heads_ref, params_ref, omega_ref, totals_ref, sums_ref, tails_ref, direct_ref,
    grad_ref, total_ref, decay_ref, weight_ref, enter_ref, smooth_ref,
):
    length = pull_ref.shape[0]
    expand = params_ref.shape[1]
    blocks = length // GROUP
    decay, log_decay, weight = rates(params_ref)
    decay_ref[...] = decay
    weight_ref[...] = weight
    whole = jnp.exp(length * log_decay)
    jump = jnp.exp(GROUP * log_decay)
    carry = jnp.zeros_like(jump)
    for k in reversed(range(totals_ref.shape[0])):
        carry = jnp.where(k > place_ref[0], whole * carry + totals_ref[k], carry)
    turned = sums_ref[pl.ds(expand, expand), :]
    for b in reversed(range(blocks)):
        rows = pl.ds(b * expand, expand)
        enter_ref[rows, :] = carry
        turned = turned + carry * decay * tails_ref[rows, :]
        carry = jump * carry + heads_ref[rows, :]
    total_ref[...] = sums_ref[...]
    total_ref[pl.ds(expand, expand), :] = turned
    factors = [spread(decay_ref, j) for j in range(expand)]
    weights = [spread(weight_ref, j) for j in range(expand)]
    for g in range(0, blocks, SUB):

        def step(t, states):
            now = pull_ref[block_rows(g, GROUP - 1 - t), :]
            states = tuple(f * s + now for f, s in zip(factors, states))
            back = tree_sum([w * s for w, s in zip(weights, states)])
            smooth_ref[block_rows(g, GROUP - 1 - t), :] = back
            return states

        start = tuple(enter_ref[state_rows(g, j, expand), :] for j in range(expand))
        lax.fori_loop(0, GROUP, step, start, unroll=8)
    for b in range(blocks):
        rows = pl.ds(b * GROUP, GROUP)
        back = smooth_ref[rows, :] + omega_ref[...] * pull_ref[rows, :]
        grad_ref[:, rows] = back.T + direct_ref[b].astype(f32)


def ema_finish(place, pull, heads, params, omega, totals, sums, tails, direct):
    length, columns = pull.shape
    expand = params.shape[1]
    return pl.pallas_call(
        ema_finish_kernel,
        grid=(columns // LANES,),
        out_shape=(jax.ShapeDtypeStruct((columns, length), f32), jax.ShapeDtypeStruct(sums.shape, f32)),
        in_specs=[
            in_smem(), by_tile(pull.shape, 1), by_tile(heads.shape, 1), by_tile(params.shape, 2),
            by_tile(omega.shape, 1), by_tile(totals.shape, 2), by_tile(sums.shape, 1),
            by_tile(tails.shape, 1), by_tile(direct.shape, 1),
        ],
        out_specs=(by_tile((columns, length), 0), by_tile(sums.shape, 1)),
        scratch_shapes=[
            pltpu.VMEM((expand, LANES), f32),
            pltpu.VMEM((expand, LANES), f32),
            pltpu.VMEM((heads.shape[0], LANES), f32),
            pltpu.VMEM((length, LANES), f32),
        ],
        compiler_params=roomy(),
        cost_estimate=work(4 * expand * length * columns, 14 * length * columns),
    )(place, pull, heads, params, omega, totals, sums, tails, direct)


def pad_to_lanes(part, dim):
    extra = -part.shape[dim] % LANES
    if extra == 0:
        return part
    return jnp.pad(part, [(0, extra if k == dim else 0) for k in range(part.ndim)])


def ema_params(alpha, delta, beta, eta, count):
    packed = jnp.swapaxes(jnp.stack([alpha, delta, beta, eta]), 1, 2)
    return pad_to_lanes(jnp.tile(packed, (1, 1, count)), 2)


def ema_param_grads(total, alpha, delta, beta, eta, count):
    channels, expand = alpha.shape
    summed = jnp.sum(total[:, : count * channels].reshape(-1, count, channels), axis=1)
    plain, turned = summed[:expand].T, summed[expand : 2 * expand].T
    omega = jnp.sum(summed[2 * expand :], axis=0)
    rate, damp = jax.nn.sigmoid(alpha), jax.nn.sigmoid(delta)
    g_alpha = eta * beta * rate * (1.0 - rate) * (plain - damp * rate * turned)
    g_delta = -(eta * beta * rate * rate * damp * (1.0 - damp)) * turned
    return g_alpha, g_delta, rate * eta * plain, rate * beta * plain, omega


low = jnp.bfloat16
CHUNK = 256


def nn(left, right):
    return jnp.dot(left, right, preferred_element_type=f32)


def nt(left, right):
    return lax.dot_general(left, right, (((1,), (1,)), ((), ())), preferred_element_type=f32)


def silu_pair(pre):
    sigma = jax.nn.sigmoid(pre)
    return pre * sigma, sigma * (1.0 + pre * (1.0 - sigma))


def each(width, body, size=CHUNK, unroll=1):
    def lap(i, none):
        body(pl.multiple_of(i * size, size))
        return none

    lax.fori_loop(0, width // size, lap, 0, unroll=unroll)


def fetch(pairs, sems):
    copies = [pltpu.make_async_copy(src, dst, sems.at[i]) for i, (src, dst) in enumerate(pairs)]
    for copy in copies:
        copy.start()
    return copies


def wide_block(ref, n):
    part = ref[:, n]
    return part.reshape(part.shape[0] * part.shape[1], part.shape[2])


def live_lanes(place_ref, lengths_ref, n, shape):
    return place_ref[0] + lax.broadcasted_iota(jnp.int32, shape, 1) < lengths_ref[n]


def span_of(ref, n):
    return pl.ds(n * GROUP, GROUP)


def call(kernel, outs, ins, smem=0, hbm=0, scratch=(), flops=0, moved=0):
    spaces = [pltpu.SMEM] * smem + [pl.ANY] * hbm + [pltpu.VMEM] * (len(ins) - smem - hbm)
    return pl.pallas_call(
        kernel,
        out_shape=tuple(jax.ShapeDtypeStruct(shape, kind) for shape, kind in outs),
        in_specs=[pl.BlockSpec(memory_space=space) for space in spaces],
        out_specs=tuple(pl.BlockSpec(memory_space=pltpu.VMEM) for _ in outs),
        scratch_shapes=list(scratch),
        compiler_params=roomy(58),
        cost_estimate=work(flops, moved),
    )(*ins)


def vectors(width, mwidth, vwidth, ff):
    sizes = (
        ("mix", mwidth), ("value", vwidth), ("out", width), ("gain", width),
        ("shift", width), ("up", ff), ("down", width),
    )
    place, at = {}, 0
    for name, size in sizes:
        place[name] = at
        at += size
    return place


def piece(ref, base, at, size):
    return ref[:, pl.ds(pl.multiple_of(base + at, 128), size)]


def value_kernel(base, w_hbm, x_ref, vec_ref, rows_ref, values_ref, slope_ref, w_ref, sems):
    copies = fetch([(w_hbm, w_ref)], sems)
    for n in range(x_ref.shape[1]):
        rows_ref[pl.ds(n * GROUP, GROUP), :] = wide_block(x_ref, n).T
    copies[0].wait()

    def chunk(at):
        cols = pl.ds(at, CHUNK)
        act, slope = silu_pair(nn(rows_ref[...], w_ref[:, cols]) + piece(vec_ref, base, at, CHUNK))
        values_ref[:, cols] = act.astype(low)
        slope_ref[:, cols] = slope.astype(low)

    each(w_ref.shape[1], chunk)


def value_part(x, w_value, vec, where):
    width, vwidth = w_value.shape
    count = x.shape[1] * GROUP
    return call(
        functools.partial(value_kernel, where["value"]),
        [((count, width), low), ((count, vwidth), low), ((count, vwidth), low)],
        (w_value, x, vec),
        hbm=1,
        scratch=[pltpu.VMEM(w_value.shape, low), pltpu.SemaphoreType.DMA((1,))],
        flops=2 * count * width * vwidth,
        moved=8 * count * vwidth,
    )


def forward_kernel(
    where, place_ref, lengths_ref, wmix_hbm, wout_hbm, wup_hbm, wdown_hbm,
    mixed_ref, x_ref, values_ref, vec_ref, qscale_ref, qshift_ref,
    out_ref, query_ref, key_ref, shared_ref, qslope_ref, probs_ref, reset_ref, turned_ref, gated_t_ref,
    hslope_ref, uslope_ref, keep_ref, unit_ref, rstd_ref, normed_t_ref, hidden_t_ref, fslope_ref,
    wmix_ref, wout_ref, wup_ref, wdown_ref, m_ref, update_ref, gated_ref, blend_ref, normed_ref, ffn_ref, sems,
):
    width, vwidth = wout_ref.shape[1], wout_ref.shape[0]
    zwidth = qscale_ref.shape[1]
    seqs = mixed_ref.shape[1]
    copies = fetch(
        [(wmix_hbm, wmix_ref), (wout_hbm, wout_ref), (wup_hbm, wup_ref), (wdown_hbm, wdown_ref)], sems
    )
    for n in range(seqs):
        m_ref[pl.ds(n * GROUP, GROUP), :] = wide_block(mixed_ref, n).T
    copies[0].wait()

    def mix(at, size=CHUNK):
        cols = pl.ds(at, size)
        return nn(m_ref[...], wmix_ref[:, cols]) + piece(vec_ref, where["mix"], at, size)

    shared, qslope = silu_pair(mix(width, zwidth))
    shared_ref[...] = shared
    qslope_ref[...] = qslope
    query_ref[...] = (shared * qscale_ref[pl.ds(0, 1), :] + qshift_ref[pl.ds(0, 1), :]).astype(low)
    key_ref[...] = (shared * qscale_ref[pl.ds(1, 1), :] + qshift_ref[pl.ds(1, 1), :]).astype(low)
    causal = lax.broadcasted_iota(jnp.int32, (GROUP, GROUP), 0) >= lax.broadcasted_iota(
        jnp.int32, (GROUP, GROUP), 1
    )
    for n in range(seqs):
        rows = pl.ds(n * GROUP, GROUP)
        scores = jnp.where(causal, nt(query_ref[rows, :], key_ref[rows, :]) * zwidth**-0.5, -1e30)
        scores = jnp.exp(scores - jnp.max(scores, axis=-1, keepdims=True))
        probs_ref[rows, :] = scores / jnp.sum(scores, axis=-1, keepdims=True)

    def gate(at):
        update_ref[:, pl.ds(at, CHUNK)] = jax.nn.sigmoid(mix(at))

    each(width, gate)

    def attend(at):
        cols = pl.ds(at, CHUNK)
        reset, slope = silu_pair(mix(pl.multiple_of(width + zwidth + at, 128)))
        attended = jnp.concatenate(
            [
                nn(probs_ref[pl.ds(n * GROUP, GROUP), :].astype(low), values_ref[pl.ds(n * GROUP, GROUP), cols])
                for n in range(seqs)
            ],
            axis=0,
        )
        reset_ref[:, cols] = reset.astype(low)
        turned_ref[:, cols] = (attended * slope).astype(low)
        gated = (reset * attended).astype(low)
        gated_ref[:, cols] = gated
        gated_t_ref[cols, :] = gated.T

    each(vwidth, attend)
    copies[1].wait()

    def hide(at):
        cols = pl.ds(at, CHUNK)
        pre = mix(pl.multiple_of(width + zwidth + vwidth + at, 128))
        pre = pre + nn(gated_ref[...], wout_ref[:, cols]) + piece(vec_ref, where["out"], at, CHUNK)
        hidden, slope = silu_pair(pre)
        update = update_ref[:, cols]
        keep = 1.0 - update
        resid = x_ref[:, cols].astype(f32)
        hslope_ref[:, cols] = (update * slope).astype(low)
        uslope_ref[:, cols] = ((hidden - resid) * update * keep).astype(low)
        keep_ref[:, cols] = keep.astype(low)
        blend_ref[:, cols] = update * hidden + keep * resid

    each(width, hide)
    for n in range(seqs):
        rows = pl.ds(n * GROUP, GROUP)
        blend = blend_ref[rows, :]
        centered = blend - jnp.mean(blend, axis=-1, keepdims=True)
        rstd = lax.rsqrt(jnp.mean(centered * centered, axis=-1, keepdims=True) + 1e-05)
        unit = centered * rstd
        unit_ref[rows, :] = unit.astype(low)
        rstd_ref[rows, :] = jnp.broadcast_to(rstd, (GROUP, LANES))
        normed = unit * piece(vec_ref, where["gain"], 0, width) + piece(vec_ref, where["shift"], 0, width)
        blend_ref[rows, :] = normed
        normed_ref[rows, :] = normed.astype(low)
        normed_t_ref[:, rows] = normed.astype(low).T
    copies[2].wait()

    def lift(at):
        cols = pl.ds(at, CHUNK)
        act, slope = silu_pair(nn(normed_ref[...], wup_ref[:, cols]) + piece(vec_ref, where["up"], at, CHUNK))
        fslope_ref[:, cols] = slope.astype(low)
        act = act.astype(low)
        ffn_ref[:, cols] = act
        hidden_t_ref[cols, :] = act.T

    each(wup_ref.shape[1], lift)
    copies[3].wait()

    def drop(at):
        cols = pl.ds(at, CHUNK)
        blend_ref[:, cols] = blend_ref[:, cols] + nn(ffn_ref[...], wdown_ref[:, cols]) + piece(vec_ref, where["down"], at, CHUNK)

    each(width, drop)
    for n in range(seqs):
        result = blend_ref[pl.ds(n * GROUP, GROUP), :].astype(low).T
        result = jnp.where(live_lanes(place_ref, lengths_ref, n, result.shape), result, jnp.zeros_like(result))
        out_ref[:, n] = result.reshape(out_ref.shape[0], out_ref.shape[2], GROUP)


def forward_part(place, lengths, mixed, x, values, w_mix, w_out, w_up, w_down, vec, where, qk_scale, qk_shift):
    vwidth, width = w_out.shape
    zwidth = qk_scale.shape[1]
    ff = w_up.shape[1]
    count = x.shape[0]
    narrow, wide = (count, width), (count, vwidth)
    outs = [
        (mixed.shape, low), ((count, zwidth), low), ((count, zwidth), low), ((count, zwidth), f32),
        ((count, zwidth), f32), ((count, GROUP), f32), (wide, low), (wide, low), ((vwidth, count), low),
        (narrow, low), (narrow, low), (narrow, low), (narrow, low), ((count, LANES), f32),
        ((width, count), low), ((ff, count), low), ((count, ff), low),
    ]
    scratch = [pltpu.VMEM(w.shape, low) for w in (w_mix, w_out, w_up, w_down)]
    scratch += [pltpu.VMEM(narrow, low), pltpu.VMEM(narrow, f32), pltpu.VMEM(wide, low)]
    scratch += [pltpu.VMEM(narrow, f32), pltpu.VMEM(narrow, low), pltpu.VMEM((count, ff), low)]
    scratch += [pltpu.SemaphoreType.DMA((4,))]
    macs = w_mix.size + w_out.size + w_up.size + w_down.size
    return call(
        functools.partial(forward_kernel, where),
        outs,
        (place, lengths, w_mix, w_out, w_up, w_down, mixed, x, values, vec, qk_scale, qk_shift),
        smem=2,
        hbm=4,
        scratch=scratch,
        flops=2 * count * macs,
        moved=2 * macs + 30 * count * width,
    )


def column_sum(part):
    return jnp.sum(part.astype(f32), axis=0, keepdims=True)


def split_product(side, keep_ref, send_ref, left, right_ref):
    half = keep_ref.shape[1]
    total = right_ref.shape[1]
    for ref, which in ((keep_ref, side), (send_ref, 1 - side)):
        base = which * (total - half)
        for at in range(0, half, CHUNK):
            size = min(CHUNK, half - at)
            cols = pl.ds(pl.multiple_of(base + at, 128), size)
            ref[:, pl.ds(at, size)] = nn(left, right_ref[:, cols]).astype(low)


def split_narrow(side, keep_ref, send_ref, left_ref, right_ref):
    half = keep_ref.shape[1]

    def chunk(at):
        rows = pl.ds(at, CHUNK)
        both = nn(left_ref[rows, :], right_ref[...]).astype(low)
        near, far = both[:, :half], both[:, half:]
        keep_ref[rows, :] = jnp.where(side == 0, near, far)
        send_ref[rows, :] = jnp.where(side == 0, far, near)

    each(left_ref.shape[0], chunk)


def back_ffn_kernel(
    base, place_ref, lengths_ref, side_ref, wdown_hbm, wup_hbm,
    grad_ref, hidden_t_ref, fslope_ref, normed_t_ref, unit_ref, rstd_ref, vec_ref, hslope_ref, uslope_ref, kept_ref,
    down_keep_ref, down_send_ref, up_keep_ref, up_send_ref, dh_ref, du_ref, direct_ref,
    small_ref,
    wdown_ref, wup_ref, g_ref, dffn_ref, dn_ref, sems,
):
    width, ff = wup_ref.shape
    seqs = grad_ref.shape[1]
    copies = fetch([(wdown_hbm, wdown_ref), (wup_hbm, wup_ref)], sems)
    for n in range(seqs):
        part = wide_block(grad_ref, n)
        part = jnp.where(live_lanes(place_ref, lengths_ref, n, part.shape), part, jnp.zeros_like(part))
        g_ref[pl.ds(n * GROUP, GROUP), :] = part.T
    small_ref[:, pl.ds(0, width)] = column_sum(g_ref[...])
    split_narrow(side_ref[0], down_keep_ref, down_send_ref, hidden_t_ref, g_ref)
    copies[0].wait()

    def lift(at):
        part = pl.ds(at, CHUNK)
        pulled = (nt(g_ref[...], wdown_ref[part, :]) * fslope_ref[:, part].astype(f32)).astype(low)
        dffn_ref[:, part] = pulled
        small_ref[:, pl.ds(pl.multiple_of(width + at, 128), CHUNK)] = column_sum(pulled)

    each(ff, lift)
    split_product(side_ref[0], up_keep_ref, up_send_ref, normed_t_ref[...], dffn_ref)
    copies[1].wait()

    def drop(at):
        part = pl.ds(at, CHUNK)
        pulled = g_ref[:, part].astype(f32) + nt(dffn_ref[...], wup_ref[part, :])
        dn_ref[:, part] = pulled
        turned = column_sum(pulled * unit_ref[:, part].astype(f32))
        small_ref[:, pl.ds(pl.multiple_of(width + ff + at, 128), CHUNK)] = turned
        small_ref[:, pl.ds(pl.multiple_of(2 * width + ff + at, 128), CHUNK)] = column_sum(pulled)

    each(width, drop)
    for n in range(seqs):
        rows = pl.ds(n * GROUP, GROUP)
        unit = unit_ref[rows, :].astype(f32)
        pulled = dn_ref[rows, :] * piece(vec_ref, base, 0, width)
        inner = jnp.mean(pulled * unit, axis=-1, keepdims=True)
        blend = pulled - jnp.mean(pulled, axis=-1, keepdims=True) - unit * inner
        blend = blend * rstd_ref[rows, :][:, :1]
        dh_ref[rows, :] = (blend * hslope_ref[rows, :].astype(f32)).astype(low)
        du_ref[rows, :] = (blend * uslope_ref[rows, :].astype(f32)).astype(low)
        direct_ref[rows, :] = (blend * kept_ref[rows, :].astype(f32)).astype(low)


def back_ffn(place, lengths, side, grad, hidden_t, fslope, normed_t, unit, rstd, vec, where, hslope, uslope, kept, w_down, w_up):
    width, ff = w_up.shape
    count = fslope.shape[0]
    narrow = (count, width)
    outs = [((ff, width // 2), low)] * 2 + [((width, ff // 2), low)] * 2 + [(narrow, low)] * 3
    outs += [((1, 3 * width + ff), f32)]
    scratch = [pltpu.VMEM(w_down.shape, low), pltpu.VMEM(w_up.shape, low), pltpu.VMEM(narrow, low)]
    scratch += [pltpu.VMEM((count, ff), low), pltpu.VMEM(narrow, f32), pltpu.SemaphoreType.DMA((2,))]
    return call(
        functools.partial(back_ffn_kernel, where["gain"]),
        outs,
        (place, lengths, side, w_down, w_up, grad, hidden_t, fslope, normed_t, unit, rstd, vec, hslope, uslope, kept),
        smem=3,
        hbm=2,
        scratch=scratch,
        flops=8 * count * width * ff,
        moved=8 * width * ff + 20 * count * width,
    )


def back_attend_kernel(
    side_ref, wout_hbm, wmix_hbm, wvalue_hbm,
    dh_ref, du_ref, direct_ref, gated_t_ref, reset_ref, turned_ref, values_ref, vslope_ref, probs_ref,
    query_ref, key_ref, shared_ref, qslope_ref, qscale_ref,
    out_keep_ref, out_send_ref, dmix_ref, dvalue_ref, mixed_ref, resid_ref,
    small_ref,
    wout_ref, wmix_ref, wvalue_ref, datt_ref, sems,
):
    vwidth, width = wout_ref.shape
    zwidth = qscale_ref.shape[1]
    count = dh_ref.shape[0]
    seqs = count // GROUP
    copies = fetch([(wout_hbm, wout_ref), (wmix_hbm, wmix_ref), (wvalue_hbm, wvalue_ref)], sems)
    dmix_ref[:, pl.ds(0, width)] = du_ref[...]
    dmix_ref[:, pl.ds(width + zwidth + vwidth, width)] = dh_ref[...]
    small_ref[:, pl.ds(0, width)] = column_sum(dh_ref[...])
    copies[0].wait()

    def gate(at):
        part = pl.ds(at, CHUNK)
        pulled = nt(dh_ref[...], wout_ref[part, :])
        dmix_ref[:, pl.ds(pl.multiple_of(width + zwidth + at, 128), CHUNK)] = (
            pulled * turned_ref[:, part].astype(f32)
        ).astype(low)
        datt_ref[:, part] = (pulled * reset_ref[:, part].astype(f32)).astype(low)

    each(vwidth, gate)
    scale = zwidth**-0.5
    q_scale, k_scale = qscale_ref[pl.ds(0, 1), :], qscale_ref[pl.ds(1, 1), :]
    zero = jnp.zeros((1, zwidth), f32)
    sums = [zero, zero, zero, zero]
    for n in range(seqs):
        rows = pl.ds(n * GROUP, GROUP)
        probs = probs_ref[rows, :]
        pulled = nt(datt_ref[rows, :], values_ref[rows, :])
        pulled = probs * (pulled - jnp.sum(pulled * probs, axis=-1, keepdims=True))
        pulled = pulled.astype(low)
        d_query = nn(pulled, key_ref[rows, :]) * scale
        d_key = nn(pulled.T, query_ref[rows, :]) * scale
        probs_t = probs.astype(low).T
        shared = shared_ref[rows, :]
        found = (d_query * shared, d_key * shared, d_query, d_key)
        sums = [a + jnp.sum(b, axis=0, keepdims=True) for a, b in zip(sums, found)]
        dmix_ref[rows, pl.ds(width, zwidth)] = (
            (d_query * q_scale + d_key * k_scale) * qslope_ref[rows, :]
        ).astype(low)
        dvalue_ref[rows, :] = (nn(probs_t, datt_ref[rows, :]) * vslope_ref[rows, :].astype(f32)).astype(low)
    mwidth = dmix_ref.shape[1]
    for k in range(4):
        small_ref[:, pl.ds(width + mwidth + vwidth + k * zwidth, zwidth)] = sums[k]
    copies[1].wait()

    def turn(result, ref, n):
        ref[:, n] = result.astype(low).T.reshape(ref.shape[0], ref.shape[2], GROUP)

    for n in range(0, seqs, 2):
        result = nt(dmix_ref[pl.ds(n * GROUP, 2 * GROUP), :], wmix_ref[...])
        turn(result[:GROUP], mixed_ref, n)
        turn(result[GROUP:], mixed_ref, n + 1)
    copies[2].wait()
    for n in range(0, seqs, 2):
        rows = pl.ds(n * GROUP, 2 * GROUP)
        result = direct_ref[rows, :].astype(f32) + nt(dvalue_ref[rows, :], wvalue_ref[...])
        turn(result[:GROUP], resid_ref, n)
        turn(result[GROUP:], resid_ref, n + 1)
    split_narrow(side_ref[0], out_keep_ref, out_send_ref, gated_t_ref, dh_ref)
    small_ref[:, pl.ds(width, mwidth)] = column_sum(dmix_ref[...])
    small_ref[:, pl.ds(width + mwidth, vwidth)] = column_sum(dvalue_ref[...])


def back_attend(side, folded, dh, du, direct, gated_t, reset, turned, values, vslope, probs, query, key, shared, qslope, qk_scale, w_out, w_mix, w_value):
    vwidth, width = w_out.shape
    mwidth = w_mix.shape[1]
    count = dh.shape[0]
    outs = [((vwidth, width // 2), low)] * 2 + [((count, mwidth), low), ((count, vwidth), low)]
    outs += [(folded, low)] * 2 + [((1, width + mwidth + vwidth + 2 * qk_scale.size), f32)]
    scratch = [pltpu.VMEM(w.shape, low) for w in (w_out, w_mix, w_value)]
    scratch += [pltpu.VMEM((count, vwidth), low), pltpu.SemaphoreType.DMA((3,))]
    macs = 2 * w_out.size + w_mix.size + w_value.size
    return call(
        back_attend_kernel,
        outs,
        (side, w_out, w_mix, w_value, dh, du, direct, gated_t, reset, turned, values, vslope, probs, query, key, shared, qslope, qk_scale),
        smem=1,
        hbm=3,
        scratch=scratch,
        flops=2 * count * macs,
        moved=2 * macs + 20 * count * width,
    )


def back_weights_kernel(
    side_ref, mixed_ref, x_ref, dmix_ref, dvalue_ref, mix_keep_ref, mix_send_ref, value_keep_ref, value_send_ref, side_t_ref
):
    seqs = mixed_ref.shape[1]
    for n in range(seqs):
        side_t_ref[:, pl.ds(n * GROUP, GROUP)] = wide_block(mixed_ref, n)
    split_product(side_ref[0], mix_keep_ref, mix_send_ref, side_t_ref[...], dmix_ref)
    for n in range(seqs):
        side_t_ref[:, pl.ds(n * GROUP, GROUP)] = wide_block(x_ref, n)
    split_product(side_ref[0], value_keep_ref, value_send_ref, side_t_ref[...], dvalue_ref)


def back_weights(side, mixed, x, dmix, dvalue):
    count, mwidth = dmix.shape
    vwidth = dvalue.shape[1]
    width = x.shape[0] * x.shape[2]
    half = -(-mwidth // 256) * 128
    return call(
        back_weights_kernel,
        [((width, half), low)] * 2 + [((width, vwidth // 2), low)] * 2,
        (side, mixed, x, dmix, dvalue),
        smem=1,
        scratch=[pltpu.VMEM((width, count), low)],
        flops=2 * count * width * (mwidth + vwidth),
        moved=2 * width * (mwidth + vwidth),
    )


Y_FIRST = (("tok", 1), ("ch", 0))
X_FIRST = (("ch", 0), ("tok", 1))


def bits_of(axis):
    return lax.axis_size(axis).bit_length() - 1


def exchange(part, axis, bit):
    size = lax.axis_size(axis)
    return lax.ppermute(part, axis, [(i, i ^ (1 << bit)) for i in range(size)])


def side_of(axis, bit):
    return (lax.axis_index(axis) >> bit) & 1


def add(left, right):
    return (left.astype(f32) + right.astype(f32)).astype(low)


def by_owner(grad):
    dims = (2,) * (bits_of("ch") + bits_of("tok") - 1)
    return grad.reshape(dims + (-1, grad.shape[-1]))


def fold(part, columns):
    runs = [part[..., at : at + columns] for at in range(0, part.shape[-1], columns)]
    return jnp.concatenate(runs, axis=-2)


def reduce_rows(kept, sent, merge, order):
    arrived = [exchange(part, "tok", 0) for part in sent]
    names = [("ch", k) for k in reversed(range(bits_of("ch")))]
    names += [("tok", k) for k in reversed(range(1, bits_of("tok")))]
    stages = list(order) + [name for name in reversed(names) if name not in order]
    kept, arrived = [by_owner(part) for part in kept], [by_owner(part) for part in arrived]
    for axis, bit in stages:
        at = names.index((axis, bit))
        mine = side_of(axis, bit)

        def pick(which):
            def one(part):
                return lax.dynamic_index_in_dim(part, which, at, keepdims=False)

            parts = [add(one(a), one(b)) for a, b in zip(kept, arrived)]
            return merge(parts) if len(parts) > 1 else parts[0]

        sent, kept = pick(1 - mine), [pick(mine)]
        names.remove((axis, bit))
        arrived = [exchange(sent, axis, bit)]
    return add(kept[0], arrived[0])


def gather_tok(part):
    whole = part[None]
    for bit in reversed(range(bits_of("tok"))):
        other = exchange(whole, "tok", bit)
        mine = side_of("tok", bit)
        near, far = jnp.where(mine == 0, whole, other), jnp.where(mine == 0, other, whole)
        whole = jnp.stack([near, far], axis=1).reshape((-1,) + part.shape)
    return whole


def sum_tok(part):
    for bit in range(bits_of("tok")):
        part = part + exchange(part, "tok", bit)
    return part


def swap(parts):
    return lax.all_to_all(parts, "ch", split_axis=0, concat_axis=0, tiled=True)


def folded(parts):
    devices, count, channels, span = parts.shape
    if channels % 16 == 0:
        return parts
    return parts.transpose(1, 0, 2, 3).reshape(1, count, devices * channels, span)


def unfolded(parts, devices):
    if parts.shape[0] == devices:
        return parts
    _, count, channels, span = parts.shape
    return parts.reshape(count, devices, channels // devices, span).transpose(1, 0, 2, 3)


def local(
    inputs,
    out_grad,
    seq_lengths,
    ema_alpha,
    ema_delta,
    ema_beta,
    ema_eta,
    ema_omega,
    w_mix,
    b_mix,
    w_value,
    b_value,
    w_out,
    b_out,
    qk_scale,
    qk_shift,
    ln_gain,
    ln_bias,
    w_up,
    b_up,
    w_down,
    b_down,
):
    count, channels, local_len = inputs.shape
    width, mwidth = w_mix.shape
    vwidth, ff = w_value.shape[1], w_up.shape[1]
    devices = lax.axis_size("ch")
    columns = count * channels
    span = local_len // devices
    tok_index = lax.axis_index("tok").astype(jnp.int32)
    first = (tok_index * local_len + lax.axis_index("ch").astype(jnp.int32) * span)[None]
    side = (tok_index & 1)[None]
    place = tok_index[None]

    def by_block(part):
        return part.reshape(count, channels, devices, span).transpose(2, 0, 1, 3)

    def by_column(parts):
        return pad_to_lanes(unfolded(parts, devices).reshape(devices, columns, span), 1)

    recv_in = folded(swap(by_block(inputs)))
    params = ema_params(ema_alpha, ema_delta, ema_beta, ema_eta, count)
    omega = pad_to_lanes(jnp.tile(ema_omega, count)[None], 1)
    xs, ends, total = ema_ends(pad_to_lanes(inputs.reshape(columns, local_len), 0), params)
    totals = lax.all_gather(total, "tok")
    mixed, slope, entry = ema_mix(place, xs, ends, params, omega, totals)
    recv_mix = folded(swap(mixed[:, :columns].reshape(devices, count, channels, span)))
    recv_grad = folded(swap(by_block(out_grad)))

    where = vectors(width, mwidth, vwidth, ff)
    vec = jnp.concatenate([b_mix, b_value, b_out, ln_gain, ln_bias, b_up, b_down])[None]
    x, values, vslope = value_part(recv_in, w_value, vec, where)
    (
        result, query, key, shared, qslope, probs, reset, turned, gated_t,
        hslope, uslope, keep, unit, rstd, normed_t, hidden_t, fslope,
    ) = forward_part(
        first, seq_lengths, recv_mix, x, values, w_mix, w_out, w_up, w_down, vec, where, qk_scale, qk_shift
    )
    output = swap(unfolded(result, devices)).transpose(1, 2, 0, 3).reshape(inputs.shape)
    down_kept, down_sent, up_kept, up_sent, dh, du, direct, small_ffn = back_ffn(
        first, seq_lengths, side, recv_grad, hidden_t, fslope, normed_t, unit, rstd, vec, where,
        hslope, uslope, keep, w_down, w_up,
    )
    out_kept, out_sent, dmix, dvalue, back_mix, back_resid, small_attend = back_attend(
        side, recv_mix.shape, dh, du, direct, gated_t, reset, turned, values, vslope, probs,
        query, key, shared, qslope, qk_scale, w_out, w_mix, w_value,
    )
    back_mix = swap(unfolded(back_mix, devices))
    back_resid = swap(unfolded(back_resid, devices))
    mix_kept, mix_sent, value_kept, value_sent = back_weights(side, recv_mix, recv_in, dmix, dvalue)

    small = jnp.concatenate([small_ffn[0], small_attend[0]]).astype(low)
    half = mix_kept.shape[1]
    tok_size = lax.axis_size("tok")
    lines = -(-small.size // (tok_size * half))
    small_size = small.size
    small = jnp.pad(small, (0, tok_size * lines * half - small_size))
    small = small.reshape(tok_size // 2, 2, lines, half)

    def pair(parts):
        tall, wide = parts
        return jnp.concatenate([tall, fold(wide, tall.shape[-1])], axis=-2)

    def with_small(parts):
        return jnp.concatenate(parts, axis=-2)

    def spread_small(which):
        part = lax.dynamic_index_in_dim(small, which, 1, keepdims=False)
        return jnp.broadcast_to(part[None], (devices,) + part.shape).reshape(-1, half)

    owned_ffn = reduce_rows([down_kept, up_kept], [down_sent, up_sent], pair, Y_FIRST)
    owned_mid = reduce_rows([out_kept, value_kept], [out_sent, value_sent], pair, X_FIRST)
    owned_mix = reduce_rows(
        [mix_kept, spread_small(side[0])], [mix_sent, spread_small(1 - side[0])], with_small, Y_FIRST
    )

    pull, heads, total = ema_back(by_column(back_mix), slope, params)
    totals = lax.all_gather(total, "tok")
    sums, tails = ema_sums(xs, pull, entry, params)
    input_grad, sums = ema_finish(
        place, pull, heads, params, omega, totals, sums, tails, by_column(back_resid)
    )
    input_grad = input_grad[:columns].reshape(inputs.shape)
    ema_grads = ema_param_grads(sum_tok(sums), ema_alpha, ema_delta, ema_beta, ema_eta, count)

    def unpair(owned, tall_rows):
        whole = gather_tok(owned).astype(f32)
        cut = tall_rows // devices // (tok_size // 2)
        whole = whole.reshape((tok_size // 2, 2) + whole.shape[1:])
        tall, wide = whole[:, :, :cut], whole[:, :, cut:]
        tall = tall.transpose(0, 2, 1, 3).reshape(tall_rows // devices, -1)
        lone = width // devices // (tok_size // 2)
        wide = wide.reshape(tok_size // 2, 2, -1, lone, wide.shape[-1])
        wide = wide.transpose(0, 3, 1, 2, 4).reshape(width // devices, -1)
        return tall, wide

    g_down, g_up = unpair(owned_ffn, ff)
    g_out, g_value = unpair(owned_mid, vwidth)
    whole = gather_tok(owned_mix).astype(f32)
    small = whole[:, -lines:].reshape(-1)[:small_size]
    whole = whole[:, :-lines].reshape(tok_size // 2, 2, -1, half)
    g_mix = jnp.concatenate([whole[:, 0], whole[:, 1, :, 2 * half - mwidth :]], axis=-1)
    g_mix = g_mix.reshape(width // devices, mwidth)
    sizes = (width, ff, width, width, width, mwidth, vwidth, qk_scale.size, qk_scale.size)
    found, at = [], 0
    for size in sizes:
        found.append(small[at : at + size])
        at += size
    g_bdown, g_bup, g_gain, g_lnbias, g_bout, g_bmix, g_bvalue, g_qscale, g_qshift = found
    g_qscale, g_qshift = g_qscale.reshape(qk_scale.shape), g_qshift.reshape(qk_scale.shape)
    return (
        output,
        input_grad,
        *ema_grads,
        g_mix,
        g_bmix,
        g_value,
        g_bvalue,
        g_out,
        g_bout,
        g_qscale,
        g_qshift,
        g_gain,
        g_lnbias,
        g_up,
        g_bup,
        g_down,
        g_bdown,
    )


def solution(mesh):
    by_ch = P("ch", None)
    placed = P(None, "ch", "tok")
    return jax.shard_map(
        local,
        mesh=mesh,
        in_specs=(placed, placed, P()) + (by_ch,) * 4 + (P("ch"),) + (P(),) * 14,
        out_specs=(
            (placed, placed)
            + (by_ch,) * 4
            + (P("ch"), by_ch, P(), by_ch, P(), by_ch)
            + (P(),) * 5
            + (by_ch, P(), by_ch, P())
        ),
        check_vma=False,
    )
```

```python
import functools
import jax
import jax.numpy as jnp
from jax import lax
from jax.experimental import pallas as pl
from jax.experimental.pallas import tpu as pltpu
from jax.sharding import PartitionSpec as P

GROUP = 128
SUB = 8
LANES = 128
f32 = jnp.float32


def by_tile(shape, dim):
    block = tuple(LANES if k == dim else size for k, size in enumerate(shape))
    return pl.BlockSpec(block, lambda i: tuple(i if k == dim else 0 for k in range(len(shape))))


def in_smem():
    return pl.BlockSpec(memory_space=pltpu.SMEM)


def roomy(mib=8):
    return pltpu.CompilerParams(vmem_limit_bytes=mib * 1024 * 1024)


def work(flops, moved, exps=0):
    return pl.CostEstimate(flops=flops, bytes_accessed=moved, transcendentals=exps)


def launch(kernel, outs, ins, in_specs, out_specs, after=(), grid=(), scratch=(), mib=8, cost=None):
    count = len(ins)

    def run(*refs):
        kernel(*refs[:count], *refs[count + len(after) :])

    return pl.pallas_call(
        run,
        grid=grid,
        out_shape=tuple(jax.ShapeDtypeStruct(shape, kind) for shape, kind in outs),
        in_specs=list(in_specs) + [pl.BlockSpec(memory_space=pl.ANY)] * len(after),
        out_specs=tuple(out_specs),
        scratch_shapes=list(scratch),
        compiler_params=roomy(mib),
        cost_estimate=cost,
    )(*ins, *after)


def rates(params_ref):
    rate = jax.nn.sigmoid(params_ref[0])
    drop = rate * jax.nn.sigmoid(params_ref[1])
    weight = params_ref[3] * rate * params_ref[2]
    return 1.0 - drop, jnp.log1p(-drop), weight


def spread(ref, j):
    return jnp.broadcast_to(ref[pl.ds(j, 1), :], (SUB, LANES))


def tree_sum(parts):
    while len(parts) > 1:
        parts = [a + b for a, b in zip(parts[::2], parts[1::2])] + parts[len(parts) & ~1 :]
    return parts[0]


def block_rows(g, t):
    return pl.ds(g * GROUP + t, SUB, stride=GROUP)


def state_rows(g, j, expand):
    return pl.ds(g * expand + j, SUB, stride=expand)


def ema_ends_kernel(x_ref, params_ref, xs_ref, ends_ref, total_ref, decay_ref):
    length = x_ref.shape[1]
    expand = params_ref.shape[1]
    blocks = length // GROUP
    decay, log_decay, _ = rates(params_ref)
    decay_ref[...] = decay
    for b in range(blocks):
        rows = pl.ds(b * GROUP, GROUP)
        xs_ref[rows, :] = x_ref[:, rows].astype(f32).T
    factors = [spread(decay_ref, j) for j in range(expand)]
    for g in range(0, blocks, SUB):

        def step(t, states):
            now = xs_ref[block_rows(g, t), :]
            return tuple(f * s + now for f, s in zip(factors, states))

        states = (jnp.zeros((SUB, LANES), f32),) * expand
        states = lax.fori_loop(0, GROUP, step, states, unroll=8)
        for j in range(expand):
            ends_ref[state_rows(g, j, expand), :] = states[j]
    jump = jnp.exp(GROUP * log_decay)
    carry = jnp.zeros_like(jump)
    for b in range(blocks):
        carry = jump * carry + ends_ref[pl.ds(b * expand, expand), :]
    total_ref[...] = carry


def ema_ends(x, params, after=()):
    columns, length = x.shape
    expand = params.shape[1]
    shapes = ((length, columns), (length // GROUP * expand, columns), (expand, columns))
    return launch(
        ema_ends_kernel,
        [(shape, f32) for shape in shapes],
        (x, params),
        [by_tile(x.shape, 0), by_tile(params.shape, 2)],
        [by_tile(shape, 1) for shape in shapes],
        after=after,
        grid=(columns // LANES,),
        scratch=[pltpu.VMEM((expand, LANES), f32)],
        cost=work(2 * expand * length * columns, 6 * length * columns),
    )


def ema_mix_kernel(
    place_ref, xs_ref, ends_ref, params_ref, omega_ref, totals_ref,
    mixed_ref, slope_ref, entry_ref, decay_ref, weight_ref, smooth_ref,
):
    length = xs_ref.shape[0]
    expand = params_ref.shape[1]
    blocks = length // GROUP
    decay, log_decay, weight = rates(params_ref)
    decay_ref[...] = decay
    weight_ref[...] = weight
    whole = jnp.exp(length * log_decay)
    jump = jnp.exp(GROUP * log_decay)
    carry = jnp.zeros_like(jump)
    for k in range(totals_ref.shape[0]):
        carry = jnp.where(k < place_ref[0], whole * carry + totals_ref[k], carry)
    for b in range(blocks):
        rows = pl.ds(b * expand, expand)
        entry_ref[rows, :] = carry
        carry = jump * carry + ends_ref[rows, :]
    factors = [spread(decay_ref, j) for j in range(expand)]
    weights = [spread(weight_ref, j) for j in range(expand)]
    for g in range(0, blocks, SUB):

        def step(t, states):
            now = xs_ref[block_rows(g, t), :]
            states = tuple(f * s + now for f, s in zip(factors, states))
            smooth_ref[block_rows(g, t), :] = tree_sum([w * s for w, s in zip(weights, states)])
            return states

        start = tuple(entry_ref[state_rows(g, j, expand), :] for j in range(expand))
        lax.fori_loop(0, GROUP, step, start, unroll=8)
    for b in range(blocks):
        rows = pl.ds(b * GROUP, GROUP)
        pre = smooth_ref[rows, :] + omega_ref[...] * xs_ref[rows, :]
        sigma = jax.nn.sigmoid(pre)
        mixed_ref[b] = (pre * sigma).T.astype(mixed_ref.dtype)
        slope_ref[rows, :] = (sigma * (1.0 + pre * (1.0 - sigma))).astype(slope_ref.dtype)


def ema_mix(place, xs, ends, params, omega, totals, after=()):
    length, columns = xs.shape
    expand = params.shape[1]
    mixed = (length // GROUP, columns, GROUP)
    return launch(
        ema_mix_kernel,
        [(mixed, jnp.bfloat16), (xs.shape, jnp.bfloat16), (ends.shape, f32)],
        (place, xs, ends, params, omega, totals),
        [
            in_smem(), by_tile(xs.shape, 1), by_tile(ends.shape, 1), by_tile(params.shape, 2),
            by_tile(omega.shape, 1), by_tile(totals.shape, 2),
        ],
        [by_tile(mixed, 1), by_tile(xs.shape, 1), by_tile(ends.shape, 1)],
        after=after,
        grid=(columns // LANES,),
        scratch=[
            pltpu.VMEM((expand, LANES), f32),
            pltpu.VMEM((expand, LANES), f32),
            pltpu.VMEM((length, LANES), f32),
        ],
        cost=work(4 * expand * length * columns, 10 * length * columns, length * columns),
    )


def ema_back_kernel(dmix_ref, slope_ref, params_ref, pull_ref, heads_ref, total_ref, decay_ref):
    length = slope_ref.shape[0]
    expand = params_ref.shape[1]
    blocks = length // GROUP
    decay, log_decay, _ = rates(params_ref)
    decay_ref[...] = decay
    for b in range(blocks):
        rows = pl.ds(b * GROUP, GROUP)
        pull_ref[rows, :] = dmix_ref[b].astype(f32).T * slope_ref[rows, :].astype(f32)
    factors = [spread(decay_ref, j) for j in range(expand)]
    for g in range(0, blocks, SUB):

        def step(t, states):
            now = pull_ref[block_rows(g, GROUP - 1 - t), :]
            return tuple(f * s + now for f, s in zip(factors, states))

        states = (jnp.zeros((SUB, LANES), f32),) * expand
        states = lax.fori_loop(0, GROUP, step, states, unroll=8)
        for j in range(expand):
            heads_ref[state_rows(g, j, expand), :] = states[j]
    jump = jnp.exp(GROUP * log_decay)
    carry = jnp.zeros_like(jump)
    for b in reversed(range(blocks)):
        carry = jump * carry + heads_ref[pl.ds(b * expand, expand), :]
    total_ref[...] = carry


def ema_back(dmix, slope, params, after=()):
    length, columns = slope.shape
    expand = params.shape[1]
    shapes = ((length, columns), (length // GROUP * expand, columns), (expand, columns))
    return launch(
        ema_back_kernel,
        [(shape, f32) for shape in shapes],
        (dmix, slope, params),
        [by_tile(dmix.shape, 1), by_tile(slope.shape, 1), by_tile(params.shape, 2)],
        [by_tile(shape, 1) for shape in shapes],
        after=after,
        grid=(columns // LANES,),
        scratch=[pltpu.VMEM((expand, LANES), f32)],
        cost=work(2 * expand * length * columns, 8 * length * columns),
    )


def ema_finish_kernel(
    place_ref, pull_ref, heads_ref, params_ref, omega_ref, totals_ref, direct_ref,
    grad_ref, enter_ref, decay_ref, weight_ref, smooth_ref,
):
    length = pull_ref.shape[0]
    expand = params_ref.shape[1]
    blocks = length // GROUP
    decay, log_decay, weight = rates(params_ref)
    decay_ref[...] = decay
    weight_ref[...] = weight
    whole = jnp.exp(length * log_decay)
    jump = jnp.exp(GROUP * log_decay)
    carry = jnp.zeros_like(jump)
    for k in reversed(range(totals_ref.shape[0])):
        carry = jnp.where(k > place_ref[0], whole * carry + totals_ref[k], carry)
    for b in reversed(range(blocks)):
        rows = pl.ds(b * expand, expand)
        enter_ref[rows, :] = carry
        carry = jump * carry + heads_ref[rows, :]
    factors = [spread(decay_ref, j) for j in range(expand)]
    weights = [spread(weight_ref, j) for j in range(expand)]
    for g in range(0, blocks, SUB):

        def step(t, states):
            now = pull_ref[block_rows(g, GROUP - 1 - t), :]
            states = tuple(f * s + now for f, s in zip(factors, states))
            back = tree_sum([w * s for w, s in zip(weights, states)])
            smooth_ref[block_rows(g, GROUP - 1 - t), :] = back
            return states

        start = tuple(enter_ref[state_rows(g, j, expand), :] for j in range(expand))
        lax.fori_loop(0, GROUP, step, start, unroll=8)
    for b in range(blocks):
        rows = pl.ds(b * GROUP, GROUP)
        back = smooth_ref[rows, :] + omega_ref[...] * pull_ref[rows, :]
        grad_ref[:, rows] = back.T + direct_ref[b].astype(f32)


def ema_finish(place, pull, heads, params, omega, totals, direct, after=()):
    length, columns = pull.shape
    expand = params.shape[1]
    return launch(
        ema_finish_kernel,
        [((columns, length), f32), (heads.shape, f32)],
        (place, pull, heads, params, omega, totals, direct),
        [
            in_smem(), by_tile(pull.shape, 1), by_tile(heads.shape, 1), by_tile(params.shape, 2),
            by_tile(omega.shape, 1), by_tile(totals.shape, 2), by_tile(direct.shape, 1),
        ],
        [by_tile((columns, length), 0), by_tile(heads.shape, 1)],
        after=after,
        grid=(columns // LANES,),
        scratch=[
            pltpu.VMEM((expand, LANES), f32),
            pltpu.VMEM((expand, LANES), f32),
            pltpu.VMEM((length, LANES), f32),
        ],
        cost=work(4 * expand * length * columns, 14 * length * columns),
    )


def ema_sums_kernel(xs_ref, pull_ref, entry_ref, enter_ref, params_ref, sums_ref, decay_ref):
    length = xs_ref.shape[0]
    expand = params_ref.shape[1]
    blocks = length // GROUP
    half = expand // 2
    decay, _, _ = rates(params_ref)
    decay_ref[...] = decay
    for low in range(0, expand, half):
        factors = [spread(decay_ref, low + j) for j in range(half)]
        zero = (jnp.zeros((SUB, LANES), f32),) * half
        plain, turned = zero, zero
        for g in range(0, blocks, SUB):

            def step(t, held):
                states, slants, plain, turned = held
                now, pull = xs_ref[block_rows(g, t), :], pull_ref[block_rows(g, t), :]
                slants = tuple(f * p + s for f, p, s in zip(factors, slants, states))
                states = tuple(f * s + now for f, s in zip(factors, states))
                plain = tuple(a + pull * s for a, s in zip(plain, states))
                turned = tuple(a + pull * p for a, p in zip(turned, slants))
                return states, slants, plain, turned

            start = tuple(entry_ref[state_rows(g, low + j, expand), :] for j in range(half))
            held = (start, zero, plain, turned)
            _, slants, plain, turned = lax.fori_loop(0, GROUP, step, held, unroll=4)
            turned = tuple(
                a + f * p * enter_ref[state_rows(g, low + j, expand), :]
                for j, (a, f, p) in enumerate(zip(turned, factors, slants))
            )
        for j in range(half):
            sums_ref[pl.ds(low + j, 1), :] = jnp.sum(plain[j], axis=0, keepdims=True)
            sums_ref[pl.ds(expand + low + j, 1), :] = jnp.sum(turned[j], axis=0, keepdims=True)
    straight = jnp.zeros((SUB, LANES), f32)
    for b in range(0, length, SUB):
        straight = straight + xs_ref[pl.ds(b, SUB), :] * pull_ref[pl.ds(b, SUB), :]
    sums_ref[pl.ds(2 * expand, SUB), :] = straight


def ema_sums(xs, pull, entry, enter, params, after=()):
    length, columns = xs.shape
    expand = params.shape[1]
    shape = (2 * expand + SUB, columns)
    return launch(
        ema_sums_kernel,
        [(shape, f32)],
        (xs, pull, entry, enter, params),
        [by_tile(xs.shape, 1), by_tile(xs.shape, 1), by_tile(entry.shape, 1), by_tile(entry.shape, 1), by_tile(params.shape, 2)],
        [by_tile(shape, 1)],
        after=after,
        grid=(columns // LANES,),
        scratch=[pltpu.VMEM((expand, LANES), f32)],
        cost=work(8 * expand * length * columns, 8 * length * columns),
    )[0]


def pad_to_lanes(part, dim):
    extra = -part.shape[dim] % LANES
    if extra == 0:
        return part
    return jnp.pad(part, [(0, extra if k == dim else 0) for k in range(part.ndim)])


def ema_params(alpha, delta, beta, eta, count):
    packed = jnp.swapaxes(jnp.stack([alpha, delta, beta, eta]), 1, 2)
    return pad_to_lanes(jnp.tile(packed, (1, 1, count)), 2)


def ema_param_grads(total, alpha, delta, beta, eta, count):
    channels, expand = alpha.shape
    summed = jnp.sum(total[:, : count * channels].reshape(-1, count, channels), axis=1)
    plain, turned = summed[:expand].T, summed[expand : 2 * expand].T
    omega = jnp.sum(summed[2 * expand :], axis=0)
    rate, damp = jax.nn.sigmoid(alpha), jax.nn.sigmoid(delta)
    g_alpha = eta * beta * rate * (1.0 - rate) * (plain - damp * rate * turned)
    g_delta = -(eta * beta * rate * rate * damp * (1.0 - damp)) * turned
    return g_alpha, g_delta, rate * eta * plain, rate * beta * plain, omega


low = jnp.bfloat16
CHUNK = 256
MIB = (6, 14, 14, 10, 14, 12, 12, 16, 8, 8)
TABLE = 384


def nn(left, right):
    return jnp.dot(left, right, preferred_element_type=f32)


def nt(left, right):
    return lax.dot_general(left, right, (((1,), (1,)), ((), ())), preferred_element_type=f32)


def silu_pair(pre):
    sigma = jax.nn.sigmoid(pre)
    return pre * sigma, sigma * (1.0 + pre * (1.0 - sigma))


def each(width, body, size=CHUNK):
    for at in range(0, width, size):
        body(at)


def wide_block(ref, n):
    part = ref[:, n]
    return part.reshape(part.shape[0] * part.shape[1], part.shape[2])


def live_lanes(place_ref, lengths_ref, n, shape):
    return place_ref[0] + lax.broadcasted_iota(jnp.int32, shape, 1) < lengths_ref[n]


def span_of(ref, n):
    return pl.ds(n * GROUP, GROUP)


def call(kernel, outs, ins, smem=0, scratch=(), flops=0, moved=0, mib=16, after=()):
    spaces = [pltpu.SMEM] * smem + [pltpu.VMEM] * (len(ins) - smem)
    return launch(
        kernel,
        outs,
        ins,
        [pl.BlockSpec(memory_space=space) for space in spaces],
        [pl.BlockSpec(memory_space=pltpu.VMEM) for _ in outs],
        after=after,
        scratch=scratch,
        mib=mib,
        cost=work(flops, moved),
    )


def vectors(width, mwidth, vwidth, ff):
    sizes = (
        ("mix", mwidth), ("value", vwidth), ("out", width), ("gain", width),
        ("shift", width), ("up", ff), ("down", width),
    )
    place, at = {}, 0
    for name, size in sizes:
        place[name] = at
        at += size
    return place


def piece(ref, base, at, size):
    return ref[:, pl.ds(base + at, size)]


def value_kernel(base, w_ref, x_ref, vec_ref, rows_ref, values_ref, slope_ref):
    for n in range(x_ref.shape[1]):
        rows_ref[pl.ds(n * GROUP, GROUP), :] = wide_block(x_ref, n).T

    def chunk(at):
        cols = pl.ds(at, CHUNK)
        act, slope = silu_pair(nn(rows_ref[...], w_ref[:, cols]) + piece(vec_ref, base, at, CHUNK))
        values_ref[:, cols] = act.astype(low)
        slope_ref[:, cols] = slope.astype(low)

    each(w_ref.shape[1], chunk)


def value_part(x, w_value, vec, where, after=()):
    width, vwidth = w_value.shape
    count = x.shape[1] * GROUP
    return call(
        functools.partial(value_kernel, where["value"]),
        [((count, width), low), ((count, vwidth), low), ((count, vwidth), low)],
        (w_value, x, vec),
        mib=MIB[0],
        after=after,
        flops=2 * count * width * vwidth,
        moved=8 * count * vwidth,
    )


def forward_kernel(
    where, place_ref, lengths_ref, wmix_ref, wout_ref, wup_ref, wdown_ref,
    mixed_ref, x_ref, values_ref, vec_ref, qscale_ref, qshift_ref,
    out_ref, query_ref, key_ref, shared_ref, qslope_ref, probs_ref, reset_ref, turned_ref, gated_t_ref,
    hslope_ref, uslope_ref, keep_ref, unit_ref, rstd_ref, normed_t_ref, hidden_t_ref, fslope_ref,
    m_ref, update_ref, gated_ref, blend_ref, normed_ref, ffn_ref,
):
    width, vwidth = wout_ref.shape[1], wout_ref.shape[0]
    zwidth = qscale_ref.shape[1]
    seqs = mixed_ref.shape[1]
    for n in range(seqs):
        m_ref[pl.ds(n * GROUP, GROUP), :] = wide_block(mixed_ref, n).T

    def mix(at, size=CHUNK):
        cols = pl.ds(at, size)
        return nn(m_ref[...], wmix_ref[:, cols]) + piece(vec_ref, where["mix"], at, size)

    shared, qslope = silu_pair(mix(width, zwidth))
    shared_ref[...] = shared
    qslope_ref[...] = qslope
    query_ref[...] = (shared * qscale_ref[pl.ds(0, 1), :] + qshift_ref[pl.ds(0, 1), :]).astype(low)
    key_ref[...] = (shared * qscale_ref[pl.ds(1, 1), :] + qshift_ref[pl.ds(1, 1), :]).astype(low)
    causal = lax.broadcasted_iota(jnp.int32, (GROUP, GROUP), 0) >= lax.broadcasted_iota(
        jnp.int32, (GROUP, GROUP), 1
    )
    for n in range(seqs):
        rows = pl.ds(n * GROUP, GROUP)
        scores = jnp.where(causal, nt(query_ref[rows, :], key_ref[rows, :]) * zwidth**-0.5, -1e30)
        scores = jnp.exp(scores - jnp.max(scores, axis=-1, keepdims=True))
        probs_ref[rows, :] = scores / jnp.sum(scores, axis=-1, keepdims=True)

    def gate(at):
        update_ref[:, pl.ds(at, CHUNK)] = jax.nn.sigmoid(mix(at))

    each(width, gate)

    def attend(at):
        cols = pl.ds(at, CHUNK)
        reset, slope = silu_pair(mix(width + zwidth + at))
        attended = jnp.concatenate(
            [
                nn(probs_ref[pl.ds(n * GROUP, GROUP), :].astype(low), values_ref[pl.ds(n * GROUP, GROUP), cols])
                for n in range(seqs)
            ],
            axis=0,
        )
        reset_ref[:, cols] = reset.astype(low)
        turned_ref[:, cols] = (attended * slope).astype(low)
        gated = (reset * attended).astype(low)
        gated_ref[:, cols] = gated
        gated_t_ref[cols, :] = gated.T

    each(vwidth, attend)

    def hide(at):
        cols = pl.ds(at, CHUNK)
        pre = mix(width + zwidth + vwidth + at)
        pre = pre + nn(gated_ref[...], wout_ref[:, cols]) + piece(vec_ref, where["out"], at, CHUNK)
        hidden, slope = silu_pair(pre)
        update = update_ref[:, cols]
        keep = 1.0 - update
        resid = x_ref[:, cols].astype(f32)
        hslope_ref[:, cols] = (update * slope).astype(low)
        uslope_ref[:, cols] = ((hidden - resid) * update * keep).astype(low)
        keep_ref[:, cols] = keep.astype(low)
        blend_ref[:, cols] = update * hidden + keep * resid

    each(width, hide)
    for n in range(seqs):
        rows = pl.ds(n * GROUP, GROUP)
        blend = blend_ref[rows, :]
        centered = blend - jnp.mean(blend, axis=-1, keepdims=True)
        rstd = lax.rsqrt(jnp.mean(centered * centered, axis=-1, keepdims=True) + 1e-05)
        unit = centered * rstd
        unit_ref[rows, :] = unit.astype(low)
        rstd_ref[rows, :] = jnp.broadcast_to(rstd, (GROUP, LANES))
        normed = unit * piece(vec_ref, where["gain"], 0, width) + piece(vec_ref, where["shift"], 0, width)
        blend_ref[rows, :] = normed
        normed_ref[rows, :] = normed.astype(low)
        normed_t_ref[:, rows] = normed.astype(low).T

    def lift(at):
        cols = pl.ds(at, CHUNK)
        act, slope = silu_pair(nn(normed_ref[...], wup_ref[:, cols]) + piece(vec_ref, where["up"], at, CHUNK))
        fslope_ref[:, cols] = slope.astype(low)
        act = act.astype(low)
        ffn_ref[:, cols] = act
        hidden_t_ref[cols, :] = act.T

    each(wup_ref.shape[1], lift)

    def drop(at):
        cols = pl.ds(at, CHUNK)
        blend_ref[:, cols] = blend_ref[:, cols] + nn(ffn_ref[...], wdown_ref[:, cols]) + piece(vec_ref, where["down"], at, CHUNK)

    each(width, drop)
    for n in range(seqs):
        result = blend_ref[pl.ds(n * GROUP, GROUP), :].astype(low).T
        result = jnp.where(live_lanes(place_ref, lengths_ref, n, result.shape), result, jnp.zeros_like(result))
        out_ref[:, n] = result.reshape(out_ref.shape[0], out_ref.shape[2], GROUP)


def forward_part(place, lengths, mixed, x, values, w_mix, w_out, w_up, w_down, vec, where, qk_scale, qk_shift, after=()):
    vwidth, width = w_out.shape
    zwidth = qk_scale.shape[1]
    ff = w_up.shape[1]
    count = x.shape[0]
    narrow, wide = (count, width), (count, vwidth)
    outs = [
        (mixed.shape, low), ((count, zwidth), low), ((count, zwidth), low), ((count, zwidth), f32),
        ((count, zwidth), f32), ((count, GROUP), f32), (wide, low), (wide, low), ((vwidth, count), low),
        (narrow, low), (narrow, low), (narrow, low), (narrow, low), ((count, LANES), f32),
        ((width, count), low), ((ff, count), low), ((count, ff), low),
    ]
    scratch = [pltpu.VMEM(narrow, low), pltpu.VMEM(narrow, f32), pltpu.VMEM(wide, low)]
    scratch += [pltpu.VMEM(narrow, f32), pltpu.VMEM(narrow, low), pltpu.VMEM((count, ff), low)]
    macs = w_mix.size + w_out.size + w_up.size + w_down.size
    return call(
        functools.partial(forward_kernel, where),
        outs,
        (place, lengths, w_mix, w_out, w_up, w_down, mixed, x, values, vec, qk_scale, qk_shift),
        smem=2,
        mib=MIB[1],
        after=after,
        scratch=scratch,
        flops=2 * count * macs,
        moved=2 * macs + 30 * count * width,
    )


def column_sum(part):
    return jnp.sum(part.astype(f32), axis=0, keepdims=True)


def split_product(side, keep_ref, send_ref, left, right_ref):
    half = keep_ref.shape[1]
    total = right_ref.shape[1]
    for ref, which in ((keep_ref, side), (send_ref, 1 - side)):
        base = which * (total - half)
        for at in range(0, half, CHUNK):
            size = min(CHUNK, half - at)
            cols = pl.ds(pl.multiple_of(base + at, 128), size)
            ref[:, pl.ds(at, size)] = nn(left, right_ref[:, cols]).astype(low)


def split_narrow(side, keep_ref, send_ref, left_ref, right_ref):
    half = keep_ref.shape[1]

    def chunk(at):
        rows = pl.ds(at, CHUNK)
        both = nn(left_ref[rows, :], right_ref[...]).astype(low)
        near, far = both[:, :half], both[:, half:]
        keep_ref[rows, :] = jnp.where(side == 0, near, far)
        send_ref[rows, :] = jnp.where(side == 0, far, near)

    each(left_ref.shape[0], chunk)


def back_ffn_kernel(
    place_ref, lengths_ref, side_ref, wdown_ref, grad_ref, hidden_t_ref, fslope_ref, normed_t_ref,
    down_keep_ref, down_send_ref, up_keep_ref, up_send_ref, g_ref, dffn_ref, small_ref,
):
    width, ff = g_ref.shape[1], wdown_ref.shape[0]
    for n in range(grad_ref.shape[1]):
        part = wide_block(grad_ref, n)
        part = jnp.where(live_lanes(place_ref, lengths_ref, n, part.shape), part, jnp.zeros_like(part))
        g_ref[pl.ds(n * GROUP, GROUP), :] = part.T
    small_ref[:, pl.ds(0, width)] = column_sum(g_ref[...])
    split_narrow(side_ref[0], down_keep_ref, down_send_ref, hidden_t_ref, g_ref)

    def lift(at):
        part = pl.ds(at, CHUNK)
        pulled = (nt(g_ref[...], wdown_ref[part, :]) * fslope_ref[:, part].astype(f32)).astype(low)
        dffn_ref[:, part] = pulled
        small_ref[:, pl.ds(width + at, CHUNK)] = column_sum(pulled)

    each(ff, lift)
    split_product(side_ref[0], up_keep_ref, up_send_ref, normed_t_ref[...], dffn_ref)


def back_ffn(place, lengths, side, grad, hidden_t, fslope, normed_t, w_down, after=()):
    ff, width = w_down.shape
    count = fslope.shape[0]
    outs = [((ff, width // 2), low)] * 2 + [((width, ff // 2), low)] * 2
    outs += [((count, width), low), ((count, ff), low), ((1, width + ff), f32)]
    return call(
        back_ffn_kernel,
        outs,
        (place, lengths, side, w_down, grad, hidden_t, fslope, normed_t),
        smem=3,
        mib=MIB[2],
        after=after,
        flops=6 * count * width * ff,
        moved=8 * width * ff + 20 * count * width,
    )


def back_norm_kernel(
    base, wup_ref, g_ref, dffn_ref, unit_ref, rstd_ref, vec_ref, hslope_ref, uslope_ref, kept_ref,
    dh_ref, du_ref, direct_ref, small_ref, dn_ref,
):
    width = wup_ref.shape[0]

    def drop(at):
        part = pl.ds(at, CHUNK)
        pulled = g_ref[:, part].astype(f32) + nt(dffn_ref[...], wup_ref[part, :])
        dn_ref[:, part] = pulled
        small_ref[:, part] = column_sum(pulled * unit_ref[:, part].astype(f32))
        small_ref[:, pl.ds(width + at, CHUNK)] = column_sum(pulled)

    each(width, drop)
    for n in range(g_ref.shape[0] // GROUP):
        rows = pl.ds(n * GROUP, GROUP)
        unit = unit_ref[rows, :].astype(f32)
        pulled = dn_ref[rows, :] * piece(vec_ref, base, 0, width)
        inner = jnp.mean(pulled * unit, axis=-1, keepdims=True)
        blend = pulled - jnp.mean(pulled, axis=-1, keepdims=True) - unit * inner
        blend = blend * rstd_ref[rows, :][:, :1]
        dh_ref[rows, :] = (blend * hslope_ref[rows, :].astype(f32)).astype(low)
        du_ref[rows, :] = (blend * uslope_ref[rows, :].astype(f32)).astype(low)
        direct_ref[rows, :] = (blend * kept_ref[rows, :].astype(f32)).astype(low)


def back_norm(g, dffn, unit, rstd, vec, where, hslope, uslope, kept, w_up, after=()):
    width = w_up.shape[0]
    narrow = g.shape
    return call(
        functools.partial(back_norm_kernel, where["gain"]),
        [(narrow, low)] * 3 + [((1, 2 * width), f32)],
        (w_up, g, dffn, unit, rstd, vec, hslope, uslope, kept),
        mib=MIB[3],
        after=after,
        scratch=[pltpu.VMEM(narrow, f32)],
        flops=2 * dffn.size * width,
        moved=2 * w_up.size + 20 * g.size,
    )


def back_attend_kernel(
    wout_ref, wmix_ref, wvalue_ref,
    dh_ref, du_ref, direct_ref, reset_ref, turned_ref, values_ref, vslope_ref, probs_ref,
    query_ref, key_ref, shared_ref, qslope_ref, qscale_ref, small_ffn_ref, small_norm_ref,
    dmix_ref, dvalue_ref, mixed_ref, resid_ref,
    table_ref,
    datt_ref,
):
    vwidth, width = wout_ref.shape
    zwidth = qscale_ref.shape[1]
    count = dh_ref.shape[0]
    seqs = count // GROUP
    dmix_ref[:, pl.ds(0, width)] = du_ref[...]
    dmix_ref[:, pl.ds(width + zwidth + vwidth, width)] = dh_ref[...]

    def gate(at):
        part = pl.ds(at, CHUNK)
        pulled = nt(dh_ref[...], wout_ref[part, :])
        dmix_ref[:, pl.ds(width + zwidth + at, CHUNK)] = (
            pulled * turned_ref[:, part].astype(f32)
        ).astype(low)
        datt_ref[:, part] = (pulled * reset_ref[:, part].astype(f32)).astype(low)

    each(vwidth, gate)
    scale = zwidth**-0.5
    q_scale, k_scale = qscale_ref[pl.ds(0, 1), :], qscale_ref[pl.ds(1, 1), :]
    zero = jnp.zeros((1, zwidth), f32)
    sums = [zero, zero, zero, zero]
    for n in range(seqs):
        rows = pl.ds(n * GROUP, GROUP)
        probs = probs_ref[rows, :]
        pulled = nt(datt_ref[rows, :], values_ref[rows, :])
        pulled = probs * (pulled - jnp.sum(pulled * probs, axis=-1, keepdims=True))
        pulled = pulled.astype(low)
        d_query = nn(pulled, key_ref[rows, :]) * scale
        d_key = nn(pulled.T, query_ref[rows, :]) * scale
        probs_t = probs.astype(low).T
        shared = shared_ref[rows, :]
        found = (d_query * shared, d_key * shared, d_query, d_key)
        sums = [a + jnp.sum(b, axis=0, keepdims=True) for a, b in zip(sums, found)]
        dmix_ref[rows, pl.ds(width, zwidth)] = (
            (d_query * q_scale + d_key * k_scale) * qslope_ref[rows, :]
        ).astype(low)
        dvalue_ref[rows, :] = (nn(probs_t, datt_ref[rows, :]) * vslope_ref[rows, :].astype(f32)).astype(low)

    def turn(result, ref, n):
        ref[:, n] = result.astype(low).T.reshape(ref.shape[0], ref.shape[2], GROUP)

    for n in range(0, seqs, 2):
        result = nt(dmix_ref[pl.ds(n * GROUP, 2 * GROUP), :], wmix_ref[...])
        turn(result[:GROUP], mixed_ref, n)
        turn(result[GROUP:], mixed_ref, n + 1)
    for n in range(0, seqs, 2):
        rows = pl.ds(n * GROUP, 2 * GROUP)
        result = direct_ref[rows, :].astype(f32) + nt(dvalue_ref[rows, :], wvalue_ref[...])
        turn(result[:GROUP], resid_ref, n)
        turn(result[GROUP:], resid_ref, n + 1)
    ff = small_ffn_ref.shape[1] - width
    found = (
        column_sum(dmix_ref[...]), column_sum(dvalue_ref[...]), column_sum(dh_ref[...]),
        sums[0], sums[1], sums[2], sums[3], small_norm_ref[:, :width], small_norm_ref[:, width:],
        small_ffn_ref[:, width:], small_ffn_ref[:, :width],
    )
    lines = []
    for part in found:
        for at in range(0, part.shape[1], TABLE):
            line = part[:, at : at + TABLE]
            lack = TABLE - line.shape[1]
            lines.append(line if lack == 0 else jnp.concatenate([line, jnp.zeros((1, lack), f32)], axis=1))
    lines.append(jnp.zeros((table_ref.shape[0] - len(lines), TABLE), f32))
    table_ref[...] = jnp.concatenate(lines, axis=0).astype(low)


def back_attend(folded, dh, du, direct, reset, turned, values, vslope, probs, query, key, shared, qslope, qk_scale, small_ffn, small_norm, w_out, w_mix, w_value, after=()):
    vwidth, width = w_out.shape
    mwidth = w_mix.shape[1]
    count = dh.shape[0]
    outs = [((count, mwidth), low), ((count, vwidth), low)]
    outs += [(folded, low)] * 2 + [((64, TABLE), low)]
    scratch = [pltpu.VMEM((count, vwidth), low)]
    macs = w_out.size + w_mix.size + w_value.size
    return call(
        back_attend_kernel,
        outs,
        (w_out, w_mix, w_value, dh, du, direct, reset, turned, values, vslope, probs, query, key, shared, qslope, qk_scale, small_ffn, small_norm),
        mib=MIB[4],
        after=after,
        scratch=scratch,
        flops=2 * count * macs,
        moved=2 * macs + 20 * count * width,
    )


def turned_side(ref, side_t_ref):
    for n in range(ref.shape[1]):
        side_t_ref[:, pl.ds(n * GROUP, GROUP)] = wide_block(ref, n)
    return side_t_ref[...]


def back_mid_kernel(
    side_ref, gated_t_ref, dh_ref, x_ref, dvalue_ref,
    out_keep_ref, out_send_ref, value_keep_ref, value_send_ref, side_t_ref,
):
    split_narrow(side_ref[0], out_keep_ref, out_send_ref, gated_t_ref, dh_ref)
    split_product(side_ref[0], value_keep_ref, value_send_ref, turned_side(x_ref, side_t_ref), dvalue_ref)


def back_mid(side, gated_t, dh, x, dvalue, after=()):
    count, width = dh.shape
    vwidth = dvalue.shape[1]
    return call(
        back_mid_kernel,
        [((vwidth, width // 2), low)] * 2 + [((width, vwidth // 2), low)] * 2,
        (side, gated_t, dh, x, dvalue),
        smem=1,
        mib=MIB[5],
        after=after,
        scratch=[pltpu.VMEM((width, count), low)],
        flops=4 * count * width * vwidth,
        moved=4 * width * vwidth,
    )


def back_mix_kernel(side_ref, mixed_ref, dmix_ref, keep_ref, send_ref, side_t_ref):
    split_product(side_ref[0], keep_ref, send_ref, turned_side(mixed_ref, side_t_ref), dmix_ref)


def back_mix_weight(side, mixed, dmix, after=()):
    count, mwidth = dmix.shape
    width = mixed.shape[0] * mixed.shape[2]
    half = -(-mwidth // 256) * 128
    return call(
        back_mix_kernel,
        [((width, half), low)] * 2,
        (side, mixed, dmix),
        smem=1,
        mib=MIB[6],
        after=after,
        scratch=[pltpu.VMEM((width, count), low)],
        flops=2 * count * width * mwidth,
        moved=2 * width * mwidth,
    )


def runs_of(part, columns):
    return [part[:, at : at + columns] for at in range(0, part.shape[1], columns)]


def halve_kernel(pieces, mine_ref, *refs):
    kept, arrived, (sent_ref, stay_ref) = refs[:pieces], refs[pieces : 2 * pieces], refs[2 * pieces :]
    outer, inner, _, columns = sent_ref.shape
    for ref, which in ((sent_ref, 1 - mine_ref[0]), (stay_ref, mine_ref[0])):
        for a in range(outer):
            for b in range(inner):
                row = 0
                for left, right in zip(kept, arrived):
                    total = left[a, which, b].astype(f32) + right[a, which, b].astype(f32)
                    for run in runs_of(total.astype(low), columns):
                        ref[a, b, pl.ds(row, run.shape[0]), :] = run
                        row += run.shape[0]


def halve(kept, arrived, mine, at, after=()):
    dims = kept[0].shape[:-2]
    outer, inner = 1 << at, 1 << (len(dims) - at - 1)
    columns = min(part.shape[-1] for part in kept)
    rows = sum(part.shape[-2] * part.shape[-1] for part in kept) // columns

    def shaped(part):
        return part.reshape((outer, 2, inner) + part.shape[-2:])

    sent, stay = call(
        functools.partial(halve_kernel, len(kept)),
        [((outer, inner, rows, columns), low)] * 2,
        (mine[None], *map(shaped, kept), *map(shaped, arrived)),
        smem=1,
        mib=MIB[7],
        after=after,
        moved=6 * outer * inner * rows * columns,
    )
    rest = dims[:at] + dims[at + 1 :] + (rows, columns)
    return sent.reshape(rest), stay.reshape(rest)


def finish_pair_kernel(tok_ref, *refs):
    shares, (tall_ref, wide_ref) = refs[:-2], refs[-2:]
    columns = shares[0].shape[1]
    cut = tall_ref.shape[0] * 2 // len(shares)
    lone = wide_ref.shape[0] * 2 // len(shares)
    for k, ref in enumerate(shares):
        at = tok_ref[0] ^ k
        high, side = at >> 1, at & 1
        tall_ref[pl.ds(pl.multiple_of(high * cut, 8), cut), pl.ds(pl.multiple_of(side * columns, 128), columns)] = ref[
            pl.ds(0, cut), :
        ].astype(f32)
        runs = wide_ref.shape[1] // 2 // columns
        for run in range(runs):
            wide_ref[
                pl.ds(pl.multiple_of(high * lone, 8), lone),
                pl.ds(pl.multiple_of((side * runs + run) * columns, 128), columns),
            ] = ref[pl.ds(cut + run * lone, lone), :].astype(f32)


def finish_pair(place, shares, tall, wide, after=()):
    return call(
        finish_pair_kernel, [(tall, f32), (wide, f32)], (place, *shares), smem=1, mib=MIB[8], after=after
    )


def finish_mix_kernel(tok_ref, *refs):
    shares, out_ref = refs[:-1], refs[-1]
    half, mwidth = shares[0].shape[1], out_ref.shape[1]
    common = 2 * half - mwidth
    lone = out_ref.shape[0] * 2 // len(shares)
    for k, ref in enumerate(shares):
        at = tok_ref[0] ^ k
        rows = pl.ds(pl.multiple_of((at >> 1) * lone, 8), lone)
        base = pl.multiple_of(common + (at & 1) * (mwidth - half), 128)
        out_ref[rows, pl.ds(base, half - common)] = ref[:, common:].astype(f32)
        if common:

            @pl.when(at & 1 == 0)
            def _():
                out_ref[rows, pl.ds(0, common)] = ref[:, :common].astype(f32)


def finish_mix(place, shares, shape, after=()):
    return call(finish_mix_kernel, [(shape, f32)], (place, *shares), smem=1, mib=MIB[9], after=after)[0]


Y_FIRST = (("tok", 1), ("ch", 0))
X_FIRST = (("ch", 0), ("tok", 1))


def bits_of(axis):
    return lax.axis_size(axis).bit_length() - 1


def exchange(part, axis, bit):
    size = lax.axis_size(axis)
    return lax.ppermute(part, axis, [(i, i ^ (1 << bit)) for i in range(size)])


def side_of(axis, bit):
    return (lax.axis_index(axis) >> bit) & 1


def by_owner(grad):
    dims = (2,) * (bits_of("ch") + bits_of("tok") - 1)
    return grad.reshape(dims + (-1, grad.shape[-1]))


def fold(part, columns):
    runs = [part[..., at : at + columns] for at in range(0, part.shape[-1], columns)]
    return jnp.concatenate(runs, axis=-2)


def add(left, right):
    return (left.astype(f32) + right.astype(f32)).astype(low)


def plain_halve(kept, arrived, mine, at):
    columns = min(part.shape[-1] for part in kept)

    def pick(which):
        def one(part):
            return lax.dynamic_index_in_dim(part, which, at, keepdims=False)

        return jnp.concatenate([fold(add(one(a), one(b)), columns) for a, b in zip(kept, arrived)], axis=-2)

    return pick(1 - mine), pick(mine)


class Sum:
    def __init__(self, kept, sent, order):
        self.names = [("ch", k) for k in reversed(range(bits_of("ch")))]
        self.names += [("tok", k) for k in reversed(range(1, bits_of("tok")))]
        self.stages = list(order) + [name for name in reversed(self.names) if name not in order]
        self.kept = [by_owner(part) for part in kept]
        self.arrived = [by_owner(exchange(part, "tok", 0)) for part in sent]

    def step(self, after=()):
        axis, bit = self.stages.pop(0)
        at = self.names.index((axis, bit))
        self.names.remove((axis, bit))
        mine = side_of(axis, bit).astype(jnp.int32)
        if all(part.shape[-2] % 16 == 0 for part in self.kept):
            sent, stay = halve(self.kept, self.arrived, mine, at, after)
        else:
            sent, stay = plain_halve(self.kept, self.arrived, mine, at)
        self.kept, self.arrived = [stay], [exchange(sent, axis, bit)]
        return stay

    def shares(self):
        found = [add(self.kept[0], self.arrived[0])]
        for bit in reversed(range(1, bits_of("tok"))):
            found += [exchange(part, "tok", bit) for part in found]
        lower = [exchange(part, "tok", 0) for part in found]
        size = bits_of("tok") - 1
        order = [sum(((k >> (size - 1 - i)) & 1) << i for i in range(size)) for k in range(len(found))]
        found = [part for k in order for part in (found[k], lower[k])]
        return found


def in_order(shares, place):
    bit = 1
    while bit < len(shares):
        swapped = (place & bit) != 0
        shares = [jnp.where(swapped, shares[k ^ bit], shares[k]) for k in range(len(shares))]
        bit *= 2
    return jnp.stack(shares)


def plain_pair(place, shares, tall, wide):
    whole = in_order(shares, place).astype(f32)
    high = len(shares) // 2
    cut, lone = tall[0] // high, wide[0] // high
    whole = whole.reshape((high, 2) + whole.shape[1:])
    first = whole[:, :, :cut].transpose(0, 2, 1, 3).reshape(tall)
    second = whole[:, :, cut:].reshape(high, 2, -1, lone, whole.shape[-1])
    return first, second.transpose(0, 3, 1, 2, 4).reshape(wide)


def plain_mix(place, shares, shape):
    whole = in_order(shares, place).astype(f32)
    half = whole.shape[-1]
    whole = whole.reshape((len(shares) // 2, 2) + whole.shape[1:])
    whole = jnp.concatenate([whole[:, 0], whole[:, 1, :, 2 * half - shape[1] :]], axis=-1)
    return whole.reshape(shape)


def sum_tok(part):
    for bit in range(bits_of("tok")):
        part = part + exchange(part, "tok", bit)
    return part


def swap(parts):
    return lax.all_to_all(parts, "ch", split_axis=0, concat_axis=0, tiled=True)


def folded(parts):
    devices, count, channels, span = parts.shape
    if channels % 16 == 0:
        return parts
    return parts.transpose(1, 0, 2, 3).reshape(1, count, devices * channels, span)


def unfolded(parts, devices):
    if parts.shape[0] == devices:
        return parts
    _, count, channels, span = parts.shape
    return parts.reshape(count, devices, channels // devices, span).transpose(1, 0, 2, 3)


def local(
    inputs,
    out_grad,
    seq_lengths,
    ema_alpha,
    ema_delta,
    ema_beta,
    ema_eta,
    ema_omega,
    w_mix,
    b_mix,
    w_value,
    b_value,
    w_out,
    b_out,
    qk_scale,
    qk_shift,
    ln_gain,
    ln_bias,
    w_up,
    b_up,
    w_down,
    b_down,
):
    count, channels, local_len = inputs.shape
    width, mwidth = w_mix.shape
    vwidth, ff = w_value.shape[1], w_up.shape[1]
    devices = lax.axis_size("ch")
    columns = count * channels
    span = local_len // devices
    tok_index = lax.axis_index("tok").astype(jnp.int32)
    first = (tok_index * local_len + lax.axis_index("ch").astype(jnp.int32) * span)[None]
    side = (tok_index & 1)[None]
    place = tok_index[None]

    def by_block(part):
        return part.reshape(count, channels, devices, span).transpose(2, 0, 1, 3)

    def by_column(parts):
        return pad_to_lanes(unfolded(parts, devices).reshape(devices, columns, span), 1)

    where = vectors(width, mwidth, vwidth, ff)
    vec = jnp.concatenate([b_mix, b_value, b_out, ln_gain, ln_bias, b_up, b_down])[None]
    params = ema_params(ema_alpha, ema_delta, ema_beta, ema_eta, count)
    omega = pad_to_lanes(jnp.tile(ema_omega, count)[None], 1)

    recv_in = folded(swap(by_block(inputs)))
    xs, ends, total = ema_ends(pad_to_lanes(inputs.reshape(columns, local_len), 0), params)
    totals = lax.all_gather(total, "tok")
    mixed, slope, entry = ema_mix(place, xs, ends, params, omega, totals)
    mixed = mixed[:, :columns].reshape(devices, count, channels, span)
    mixed, recv_in = lax.optimization_barrier((mixed, recv_in))
    recv_mix = folded(swap(mixed))
    x, values, vslope = value_part(recv_in, w_value, vec, where, (entry,))
    blocks, recv_mix = lax.optimization_barrier((by_block(out_grad), recv_mix))
    recv_grad = folded(swap(blocks))
    (
        result, query, key, shared, qslope, probs, reset, turned, gated_t,
        hslope, uslope, keep, unit, rstd, normed_t, hidden_t, fslope,
    ) = forward_part(
        first, seq_lengths, recv_mix, x, values, w_mix, w_out, w_up, w_down, vec, where, qk_scale, qk_shift
    )
    result, recv_grad = lax.optimization_barrier((unfolded(result, devices), recv_grad))
    output = swap(result)
    down_kept, down_sent, up_kept, up_sent, g, dffn, small_ffn = back_ffn(
        first, seq_lengths, side, recv_grad, hidden_t, fslope, normed_t, w_down
    )
    ffn = Sum([down_kept, up_kept], [down_sent, up_sent], Y_FIRST)
    dh, du, direct, small_norm = back_norm(g, dffn, unit, rstd, vec, where, hslope, uslope, keep, w_up)
    last = ffn.step((small_norm,))
    dmix, dvalue, back_mix, back_resid, table = back_attend(
        recv_mix.shape, dh, du, direct, reset, turned, values, vslope, probs, query, key, shared, qslope,
        qk_scale, small_ffn, small_norm, w_out, w_mix, w_value, (last,),
    )
    back_mix, output = lax.optimization_barrier((unfolded(back_mix, devices), output))
    output = output.transpose(1, 2, 0, 3).reshape(inputs.shape)
    back_mix = swap(back_mix)
    back_resid, back_mix = lax.optimization_barrier((unfolded(back_resid, devices), back_mix))
    back_resid = swap(back_resid)
    out_kept, out_sent, value_kept, value_sent = back_mid(side, gated_t, dh, recv_in, dvalue, (table,))
    tok_size = lax.axis_size("tok")
    table = table.reshape(tok_size // 2, 2, -1, TABLE)

    def to_owners(which):
        part = lax.dynamic_index_in_dim(table, which, 1, keepdims=False)
        return jnp.broadcast_to(part[None], (devices,) + part.shape).reshape(-1, TABLE)

    mid = Sum(
        [out_kept, value_kept, to_owners(side[0])], [out_sent, value_sent, to_owners(1 - side[0])], X_FIRST
    )
    mix_kept, mix_sent = back_mix_weight(side, recv_mix, dmix, (value_kept,))
    mix = Sum([mix_kept], [mix_sent], Y_FIRST)
    last = mid.step((mix_kept,))
    last = ffn.step((last,))
    last = mix.step((last,))
    pull, heads, total = ema_back(by_column(back_mix), slope, params, (last,))
    totals = lax.all_gather(total, "tok")
    last = mid.step((total,))
    last = ffn.step((last,))
    input_grad, enter = ema_finish(
        place, pull, heads, params, omega, totals, by_column(back_resid), (last,)
    )
    input_grad = input_grad[:columns].reshape(inputs.shape)
    last = mix.step((enter,))
    last = mid.step((last,))
    last = ffn.step((last,))
    sums = ema_sums(xs, pull, entry, enter, params, (last,))
    ema_grads = ema_param_grads(sum_tok(sums), ema_alpha, ema_delta, ema_beta, ema_eta, count)
    while mid.stages:
        last = mid.step((last,))
    while ffn.stages:
        last = ffn.step((last,))
    while mix.stages:
        last = mix.step((last,))

    tall, wide, across = (vwidth // devices, width), (width // devices, vwidth), (width // devices, mwidth)
    shares = mid.shares()
    lines = table.shape[2]
    table = in_order([part[-lines:] for part in shares], tok_index).astype(f32).reshape(-1)
    if tall[0] * 2 // tok_size % 16 == 0 and wide[0] * 2 // tok_size % 16 == 0:
        g_out, g_value = finish_pair(place, shares, tall, wide)
        g_down, g_up = finish_pair(place, ffn.shares(), tall, wide)
        g_mix = finish_mix(place, mix.shares(), across)
    else:
        shares = [part[:-lines] for part in shares]
        g_out, g_value = plain_pair(tok_index, shares, tall, wide)
        g_down, g_up = plain_pair(tok_index, ffn.shares(), tall, wide)
        g_mix = plain_mix(tok_index, mix.shares(), across)
    found, at = [], 0
    half = qk_scale.shape[1]
    for size in (mwidth, vwidth, width, half, half, half, half, width, width, ff, width):
        found.append(table[at : at + size])
        at += -(-size // TABLE) * TABLE
    g_bmix, g_bvalue, g_bout, scale_q, scale_k, shift_q, shift_k, g_gain, g_lnbias, g_bup, g_bdown = found
    g_qscale, g_qshift = jnp.stack([scale_q, scale_k]), jnp.stack([shift_q, shift_k])
    return (
        output,
        input_grad,
        *ema_grads,
        g_mix,
        g_bmix,
        g_value,
        g_bvalue,
        g_out,
        g_bout,
        g_qscale,
        g_qshift,
        g_gain,
        g_lnbias,
        g_up,
        g_bup,
        g_down,
        g_bdown,
    )


def solution(mesh):
    by_ch = P("ch", None)
    placed = P(None, "ch", "tok")
    return jax.shard_map(
        local,
        mesh=mesh,
        in_specs=(placed, placed, P()) + (by_ch,) * 4 + (P("ch"),) + (P(),) * 14,
        out_specs=(
            (placed, placed)
            + (by_ch,) * 4
            + (P("ch"), by_ch, P(), by_ch, P(), by_ch)
            + (P(),) * 5
            + (by_ch, P(), by_ch, P())
        ),
        check_vma=False,
    )
```

```python
import functools
import jax
import jax.numpy as jnp
from jax import lax
from jax.experimental import pallas as pl
from jax.experimental.pallas import tpu as pltpu
from jax.sharding import PartitionSpec as P

GROUP = 128
SUB = 8
LANES = 128
f32 = jnp.float32


def by_tile(shape, dim):
    block = tuple(LANES if k == dim else size for k, size in enumerate(shape))
    return pl.BlockSpec(block, lambda i: tuple(i if k == dim else 0 for k in range(len(shape))))


def in_smem():
    return pl.BlockSpec(memory_space=pltpu.SMEM)


def roomy(mib=5):
    return pltpu.CompilerParams(vmem_limit_bytes=mib * 1024 * 1024)


def work(flops, moved, exps=0):
    return pl.CostEstimate(flops=1, bytes_accessed=1, transcendentals=0)


def launch(kernel, outs, ins, in_specs, out_specs, after=(), grid=(), scratch=(), mib=5, cost=None):
    count = len(ins)

    def run(*refs):
        kernel(*refs[:count], *refs[count + len(after) :])

    return pl.pallas_call(
        run,
        grid=grid,
        out_shape=tuple(jax.ShapeDtypeStruct(shape, kind) for shape, kind in outs),
        in_specs=list(in_specs) + [pl.BlockSpec(memory_space=pl.ANY)] * len(after),
        out_specs=tuple(out_specs),
        scratch_shapes=list(scratch),
        compiler_params=roomy(mib),
        cost_estimate=cost,
    )(*ins, *after)


def rates(params_ref):
    rate = jax.nn.sigmoid(params_ref[0])
    drop = rate * jax.nn.sigmoid(params_ref[1])
    weight = params_ref[3] * rate * params_ref[2]
    return 1.0 - drop, jnp.log1p(-drop), weight


def spread(ref, j):
    return jnp.broadcast_to(ref[pl.ds(j, 1), :], (SUB, LANES))


def tree_sum(parts):
    while len(parts) > 1:
        parts = [a + b for a, b in zip(parts[::2], parts[1::2])] + parts[len(parts) & ~1 :]
    return parts[0]


def block_rows(g, t):
    return pl.ds(g * GROUP + t, SUB, stride=GROUP)


def state_rows(g, j, expand):
    return pl.ds(g * expand + j, SUB, stride=expand)


def blocks_kernel(spot_ref, first_ref, second_ref, out_ref):
    for b in range(out_ref.shape[0]):
        cols = pl.ds(b * GROUP, GROUP)
        out_ref[b, 0] = first_ref[:, cols]
        out_ref[b, 1] = second_ref[:, cols]


def by_blocks(spot, first, second):
    columns, length = first.shape
    shape = (length // GROUP, 2, columns, GROUP)
    whole = pl.BlockSpec(memory_space=pltpu.VMEM)
    mib = 5 * max(1, length // 1024)
    return launch(
        blocks_kernel, [(shape, first.dtype)], (spot, first, second), [in_smem(), whole, whole], [whole], mib=mib
    )[0]


def columns_kernel(parts_ref, out_ref):
    for b in range(parts_ref.shape[0]):
        out_ref[:, pl.ds(b * GROUP, GROUP)] = parts_ref[b]


def by_columns(parts):
    blocks, columns, _ = parts.shape
    whole = pl.BlockSpec(memory_space=pltpu.VMEM)
    out = ((columns, blocks * GROUP), parts.dtype)
    return launch(columns_kernel, [out], (parts,), [whole], [whole], mib=5 * max(1, blocks // 8))[0]


def ema_ends_kernel(x_ref, params_ref, xs_ref, ends_ref, total_ref, decay_ref):
    length = x_ref.shape[1]
    expand = params_ref.shape[1]
    blocks = length // GROUP
    decay, log_decay, _ = rates(params_ref)
    decay_ref[...] = decay
    for b in range(blocks):
        rows = pl.ds(b * GROUP, GROUP)
        xs_ref[rows, :] = x_ref[:, rows].astype(f32).T
    factors = [spread(decay_ref, j) for j in range(expand)]
    for g in range(0, blocks, SUB):

        def step(t, states):
            now = xs_ref[block_rows(g, t), :]
            return tuple(f * s + now for f, s in zip(factors, states))

        states = (jnp.zeros((SUB, LANES), f32),) * expand
        states = lax.fori_loop(0, GROUP, step, states, unroll=8)
        for j in range(expand):
            ends_ref[state_rows(g, j, expand), :] = states[j]
    jump = jnp.exp(GROUP * log_decay)
    carry = jnp.zeros_like(jump)
    for b in range(blocks):
        carry = jump * carry + ends_ref[pl.ds(b * expand, expand), :]
    total_ref[...] = carry


def ema_ends(x, params, after=()):
    columns, length = x.shape
    expand = params.shape[1]
    shapes = ((length, columns), (length // GROUP * expand, columns), (expand, columns))
    return launch(
        ema_ends_kernel,
        [(shape, f32) for shape in shapes],
        (x, params),
        [by_tile(x.shape, 0), by_tile(params.shape, 2)],
        [by_tile(shape, 1) for shape in shapes],
        after=after,
        grid=(columns // LANES,),
        scratch=[pltpu.VMEM((expand, LANES), f32)],
        mib=5 * max(1, length // 1024),
        cost=work(2 * expand * length * columns, 6 * length * columns),
    )


def ema_mix_kernel(
    spot_ref, xs_ref, ends_ref, params_ref, omega_ref, totals_ref, *refs
):
    mixed_refs, (slope_ref, entry_ref, decay_ref, weight_ref, smooth_ref) = refs[:-5], refs[-5:]
    length = xs_ref.shape[0]
    expand = params_ref.shape[1]
    blocks = length // GROUP
    decay, log_decay, weight = rates(params_ref)
    decay_ref[...] = decay
    weight_ref[...] = weight
    whole = jnp.exp(length * log_decay)
    jump = jnp.exp(GROUP * log_decay)
    carry = jnp.zeros_like(jump)
    for k in range(totals_ref.shape[0]):
        carry = jnp.where(k < spot_ref[2], whole * carry + totals_ref[k], carry)
    for b in range(blocks):
        rows = pl.ds(b * expand, expand)
        entry_ref[rows, :] = carry
        carry = jump * carry + ends_ref[rows, :]
    factors = [spread(decay_ref, j) for j in range(expand)]
    weights = [spread(weight_ref, j) for j in range(expand)]
    for g in range(0, blocks, SUB):

        def step(t, states):
            now = xs_ref[block_rows(g, t), :]
            states = tuple(f * s + now for f, s in zip(factors, states))
            smooth_ref[block_rows(g, t), :] = tree_sum([w * s for w, s in zip(weights, states)])
            return states

        start = tuple(entry_ref[state_rows(g, j, expand), :] for j in range(expand))
        lax.fori_loop(0, GROUP, step, start, unroll=8)
    for k in range(blocks):
        rows = pl.ds(pl.multiple_of((spot_ref[1] ^ k) * GROUP, GROUP), GROUP)
        pre = smooth_ref[rows, :] + omega_ref[...] * xs_ref[rows, :]
        sigma = jax.nn.sigmoid(pre)
        block = (pre * sigma).T.astype(jnp.bfloat16)
        if len(mixed_refs) == 1:
            mixed_refs[0][spot_ref[1] ^ k] = block
        else:
            mixed_refs[k][...] = block
        slope_ref[rows, :] = (sigma * (1.0 + pre * (1.0 - sigma))).astype(slope_ref.dtype)


def ema_mix(spot, xs, ends, params, omega, totals, apart, after=()):
    length, columns = xs.shape
    expand = params.shape[1]
    blocks = length // GROUP
    mixed = [(columns, GROUP)] * blocks if apart else [(blocks, columns, GROUP)]
    *found, slope, entry = launch(
        ema_mix_kernel,
        [(shape, jnp.bfloat16) for shape in mixed] + [(xs.shape, jnp.bfloat16), (ends.shape, f32)],
        (spot, xs, ends, params, omega, totals),
        [
            in_smem(), by_tile(xs.shape, 1), by_tile(ends.shape, 1), by_tile(params.shape, 2),
            by_tile(omega.shape, 1), by_tile(totals.shape, 2),
        ],
        [by_tile(shape, len(shape) - 2) for shape in mixed] + [by_tile(xs.shape, 1), by_tile(ends.shape, 1)],
        after=after,
        grid=(columns // LANES,),
        scratch=[
            pltpu.VMEM((expand, LANES), f32),
            pltpu.VMEM((expand, LANES), f32),
            pltpu.VMEM((length, LANES), f32),
        ],
        mib=5 * max(1, length // 1024),
        cost=work(4 * expand * length * columns, 10 * length * columns, length * columns),
    )
    return found, slope, entry


def ema_back_kernel(dmix_ref, slope_ref, params_ref, pull_ref, heads_ref, total_ref, decay_ref):
    length = slope_ref.shape[0]
    expand = params_ref.shape[1]
    blocks = length // GROUP
    decay, log_decay, _ = rates(params_ref)
    decay_ref[...] = decay
    for b in range(blocks):
        rows = pl.ds(b * GROUP, GROUP)
        pull_ref[rows, :] = dmix_ref[b].astype(f32).T * slope_ref[rows, :].astype(f32)
    factors = [spread(decay_ref, j) for j in range(expand)]
    for g in range(0, blocks, SUB):

        def step(t, states):
            now = pull_ref[block_rows(g, GROUP - 1 - t), :]
            return tuple(f * s + now for f, s in zip(factors, states))

        states = (jnp.zeros((SUB, LANES), f32),) * expand
        states = lax.fori_loop(0, GROUP, step, states, unroll=8)
        for j in range(expand):
            heads_ref[state_rows(g, j, expand), :] = states[j]
    jump = jnp.exp(GROUP * log_decay)
    carry = jnp.zeros_like(jump)
    for b in reversed(range(blocks)):
        carry = jump * carry + heads_ref[pl.ds(b * expand, expand), :]
    total_ref[...] = carry


def ema_back(dmix, slope, params, after=()):
    length, columns = slope.shape
    expand = params.shape[1]
    shapes = ((length, columns), (length // GROUP * expand, columns), (expand, columns))
    return launch(
        ema_back_kernel,
        [(shape, f32) for shape in shapes],
        (dmix, slope, params),
        [by_tile(dmix.shape, 1), by_tile(slope.shape, 1), by_tile(params.shape, 2)],
        [by_tile(shape, 1) for shape in shapes],
        after=after,
        grid=(columns // LANES,),
        scratch=[pltpu.VMEM((expand, LANES), f32)],
        mib=5 * max(1, length // 1024),
        cost=work(2 * expand * length * columns, 8 * length * columns),
    )


def enter_from_later(spot_ref, heads_ref, totals_ref, enter_ref, log_decay, length):
    expand = log_decay.shape[0]
    whole = jnp.exp(length * log_decay)
    jump = jnp.exp(GROUP * log_decay)
    carry = jnp.zeros_like(jump)
    for k in reversed(range(totals_ref.shape[0])):
        carry = jnp.where(k > spot_ref[2], whole * carry + totals_ref[k], carry)
    for b in reversed(range(length // GROUP)):
        rows = pl.ds(b * expand, expand)
        enter_ref[rows, :] = carry
        carry = jump * carry + heads_ref[rows, :]


def ema_finish_kernel(
    spot_ref, pull_ref, heads_ref, params_ref, omega_ref, totals_ref, direct_ref,
    grad_ref, decay_ref, weight_ref, enter_ref, smooth_ref,
):
    length = pull_ref.shape[0]
    expand = params_ref.shape[1]
    blocks = length // GROUP
    decay, log_decay, weight = rates(params_ref)
    decay_ref[...] = decay
    weight_ref[...] = weight
    enter_from_later(spot_ref, heads_ref, totals_ref, enter_ref, log_decay, length)
    factors = [spread(decay_ref, j) for j in range(expand)]
    weights = [spread(weight_ref, j) for j in range(expand)]
    for g in range(0, blocks, SUB):

        def step(t, states):
            now = pull_ref[block_rows(g, GROUP - 1 - t), :]
            states = tuple(f * s + now for f, s in zip(factors, states))
            back = tree_sum([w * s for w, s in zip(weights, states)])
            smooth_ref[block_rows(g, GROUP - 1 - t), :] = back
            return states

        start = tuple(enter_ref[state_rows(g, j, expand), :] for j in range(expand))
        lax.fori_loop(0, GROUP, step, start, unroll=8)
    for b in range(blocks):
        rows = pl.ds(b * GROUP, GROUP)
        back = smooth_ref[rows, :] + omega_ref[...] * pull_ref[rows, :]
        grad_ref[:, rows] = back.T + direct_ref[b].astype(f32)


def ema_finish(spot, pull, heads, params, omega, totals, direct, after=()):
    length, columns = pull.shape
    expand = params.shape[1]
    return launch(
        ema_finish_kernel,
        [((columns, length), f32)],
        (spot, pull, heads, params, omega, totals, direct),
        [
            in_smem(), by_tile(pull.shape, 1), by_tile(heads.shape, 1), by_tile(params.shape, 2),
            by_tile(omega.shape, 1), by_tile(totals.shape, 2), by_tile(direct.shape, 1),
        ],
        [by_tile((columns, length), 0)],
        after=after,
        grid=(columns // LANES,),
        scratch=[
            pltpu.VMEM((expand, LANES), f32),
            pltpu.VMEM((expand, LANES), f32),
            pltpu.VMEM((heads.shape[0], LANES), f32),
            pltpu.VMEM((length, LANES), f32),
        ],
        mib=5 * max(1, length // 1024),
        cost=work(4 * expand * length * columns, 14 * length * columns),
    )[0]


def ema_sums_kernel(spot_ref, xs_ref, pull_ref, entry_ref, heads_ref, totals_ref, params_ref, sums_ref, decay_ref, enter_ref):
    length = xs_ref.shape[0]
    expand = params_ref.shape[1]
    blocks = length // GROUP
    half = expand // 2
    decay, log_decay, _ = rates(params_ref)
    decay_ref[...] = decay
    enter_from_later(spot_ref, heads_ref, totals_ref, enter_ref, log_decay, length)
    for low in range(0, expand, half):
        factors = [spread(decay_ref, low + j) for j in range(half)]
        zero = (jnp.zeros((SUB, LANES), f32),) * half
        plain, turned = zero, zero
        for g in range(0, blocks, SUB):

            def step(t, held):
                states, slants, plain, turned = held
                now, pull = xs_ref[block_rows(g, t), :], pull_ref[block_rows(g, t), :]
                slants = tuple(f * p + s for f, p, s in zip(factors, slants, states))
                states = tuple(f * s + now for f, s in zip(factors, states))
                plain = tuple(a + pull * s for a, s in zip(plain, states))
                turned = tuple(a + pull * p for a, p in zip(turned, slants))
                return states, slants, plain, turned

            start = tuple(entry_ref[state_rows(g, low + j, expand), :] for j in range(half))
            held = (start, zero, plain, turned)
            _, slants, plain, turned = lax.fori_loop(0, GROUP, step, held, unroll=4)
            turned = tuple(
                a + f * p * enter_ref[state_rows(g, low + j, expand), :]
                for j, (a, f, p) in enumerate(zip(turned, factors, slants))
            )
        for j in range(half):
            sums_ref[pl.ds(low + j, 1), :] = jnp.sum(plain[j], axis=0, keepdims=True)
            sums_ref[pl.ds(expand + low + j, 1), :] = jnp.sum(turned[j], axis=0, keepdims=True)
    straight = jnp.zeros((SUB, LANES), f32)
    for b in range(0, length, SUB):
        straight = straight + xs_ref[pl.ds(b, SUB), :] * pull_ref[pl.ds(b, SUB), :]
    sums_ref[pl.ds(2 * expand, SUB), :] = straight


def ema_sums(spot, xs, pull, entry, heads, totals, params, after=()):
    length, columns = xs.shape
    expand = params.shape[1]
    shape = (2 * expand + SUB, columns)
    return launch(
        ema_sums_kernel,
        [(shape, f32)],
        (spot, xs, pull, entry, heads, totals, params),
        [
            in_smem(), by_tile(xs.shape, 1), by_tile(xs.shape, 1), by_tile(entry.shape, 1), by_tile(entry.shape, 1),
            by_tile(totals.shape, 2), by_tile(params.shape, 2),
        ],
        [by_tile(shape, 1)],
        after=after,
        grid=(columns // LANES,),
        scratch=[pltpu.VMEM((expand, LANES), f32), pltpu.VMEM((entry.shape[0], LANES), f32)],
        mib=5 * max(1, length // 1024),
        cost=work(8 * expand * length * columns, 8 * length * columns),
    )[0]


def pad_to_lanes(part, dim):
    extra = -part.shape[dim] % LANES
    if extra == 0:
        return part
    return jnp.pad(part, [(0, extra if k == dim else 0) for k in range(part.ndim)])


def ema_params(alpha, delta, beta, eta, count):
    packed = jnp.swapaxes(jnp.stack([alpha, delta, beta, eta]), 1, 2)
    return pad_to_lanes(jnp.tile(packed, (1, 1, count)), 2)


def ema_param_grads(total, alpha, delta, beta, eta, count):
    channels, expand = alpha.shape
    summed = jnp.sum(total[:, : count * channels].reshape(-1, count, channels), axis=1)
    plain, turned = summed[:expand].T, summed[expand : 2 * expand].T
    omega = jnp.sum(summed[2 * expand :], axis=0)
    rate, damp = jax.nn.sigmoid(alpha), jax.nn.sigmoid(delta)
    g_alpha = eta * beta * rate * (1.0 - rate) * (plain - damp * rate * turned)
    g_delta = -(eta * beta * rate * rate * damp * (1.0 - damp)) * turned
    return g_alpha, g_delta, rate * eta * plain, rate * beta * plain, omega


low = jnp.bfloat16
CHUNK = 256
MIB = (3, 11, 8, 5, 6, 8, 8, 6, 4, 4)
TABLE = 384


def nn(left, right):
    return jnp.dot(left, right, preferred_element_type=f32)


def nt(left, right):
    return lax.dot_general(left, right, (((1,), (1,)), ((), ())), preferred_element_type=f32)


def silu_pair(pre):
    sigma = jax.nn.sigmoid(pre)
    return pre * sigma, sigma * (1.0 + pre * (1.0 - sigma))


def each(width, body, size=CHUNK):
    for at in range(0, width, size):
        body(at)


def wide_block(ref, which, n):
    part = ref[:, which, n]
    return part.reshape(part.shape[0] * part.shape[1], part.shape[2])


def live_lanes(spot_ref, lengths_ref, n, shape):
    return spot_ref[0] + lax.broadcasted_iota(jnp.int32, shape, 1) < lengths_ref[n]


def span_of(ref, n):
    return pl.ds(n * GROUP, GROUP)


def call(kernel, outs, ins, smem=0, scratch=(), moved=1, mib=16, after=()):
    spaces = [pltpu.SMEM] * smem + [pltpu.VMEM] * (len(ins) - smem)
    return launch(
        kernel,
        outs,
        ins,
        [pl.BlockSpec(memory_space=space) for space in spaces],
        [pl.BlockSpec(memory_space=pltpu.VMEM) for _ in outs],
        after=after,
        scratch=scratch,
        mib=mib,
        cost=pl.CostEstimate(flops=1, bytes_accessed=moved, transcendentals=0),
    )


def vectors(width, mwidth, vwidth, ff):
    sizes = (
        ("mix", mwidth), ("value", vwidth), ("out", width), ("gain", width),
        ("shift", width), ("up", ff), ("down", width),
    )
    place, at = {}, 0
    for name, size in sizes:
        place[name] = at
        at += size
    return place


def piece(ref, base, at, size):
    return ref[:, pl.ds(base + at, size)]


def value_kernel(base, w_ref, x_ref, vec_ref, rows_ref, values_ref, slope_ref, rows_t_ref):
    for n in range(x_ref.shape[2]):
        rows = pl.ds(n * GROUP, GROUP)
        block = wide_block(x_ref, 0, n)
        rows_t_ref[:, rows] = block
        rows_ref[rows, :] = block.T

    def chunk(at):
        cols = pl.ds(at, CHUNK)
        act, slope = silu_pair(nn(rows_ref[...], w_ref[:, cols]) + piece(vec_ref, base, at, CHUNK))
        values_ref[:, cols] = act.astype(low)
        slope_ref[:, cols] = slope.astype(low)

    each(w_ref.shape[1], chunk)


def value_part(x, w_value, vec, where, after=()):
    width, vwidth = w_value.shape
    count = x.shape[2] * GROUP
    return call(
        functools.partial(value_kernel, where["value"]),
        [((count, width), low), ((count, vwidth), low), ((count, vwidth), low), ((width, count), low)],
        (w_value, x, vec),
        mib=MIB[0],
        after=after,
    )


def forward_kernel(
    pieces, where, spot_ref, lengths_ref, wmix_ref, wout_ref, wup_ref, wdown_ref,
    x_ref, values_ref, vec_ref, qscale_ref, qshift_ref, *refs
):
    forward_rows(spot_ref, refs[:pieces], refs[pieces], refs[-6])
    forward_body(
        where, spot_ref, lengths_ref, wmix_ref, wout_ref, wup_ref, wdown_ref,
        x_ref, values_ref, vec_ref, qscale_ref, qshift_ref, *refs[pieces + 1 :]
    )


def forward_rows(spot_ref, mixed_refs, mixed_t_ref, m_ref):
    for k, ref in enumerate(mixed_refs):
        seqs, channels, _ = ref.shape
        at = pl.multiple_of((spot_ref[1] ^ k) * channels, 16) if len(mixed_refs) > 1 else 0
        for n in range(seqs):
            mixed_t_ref[pl.ds(at, channels), pl.ds(n * GROUP, GROUP)] = ref[n]
    for n in range(m_ref.shape[0] // GROUP):
        rows = pl.ds(n * GROUP, GROUP)
        m_ref[rows, :] = mixed_t_ref[:, rows].T


def forward_body(
    where, spot_ref, lengths_ref, wmix_ref, wout_ref, wup_ref, wdown_ref,
    x_ref, values_ref, vec_ref, qscale_ref, qshift_ref,
    out_ref, query_ref, key_ref, shared_ref, qslope_ref, probs_ref, reset_ref, turned_ref, gated_t_ref,
    hslope_ref, uslope_ref, keep_ref, unit_ref, rstd_ref, normed_t_ref, hidden_t_ref, fslope_ref,
    m_ref, update_ref, gated_ref, blend_ref, normed_ref, ffn_ref,
):
    width, vwidth = wout_ref.shape[1], wout_ref.shape[0]
    zwidth = qscale_ref.shape[1]
    seqs = x_ref.shape[0] // GROUP

    def mix(at, size=CHUNK):
        cols = pl.ds(at, size)
        return nn(m_ref[...], wmix_ref[:, cols]) + piece(vec_ref, where["mix"], at, size)

    shared, qslope = silu_pair(mix(width, zwidth))
    shared_ref[...] = shared
    qslope_ref[...] = qslope
    query_ref[...] = (shared * qscale_ref[pl.ds(0, 1), :] + qshift_ref[pl.ds(0, 1), :]).astype(low)
    key_ref[...] = (shared * qscale_ref[pl.ds(1, 1), :] + qshift_ref[pl.ds(1, 1), :]).astype(low)
    causal = lax.broadcasted_iota(jnp.int32, (GROUP, GROUP), 0) >= lax.broadcasted_iota(
        jnp.int32, (GROUP, GROUP), 1
    )
    for n in range(seqs):
        rows = pl.ds(n * GROUP, GROUP)
        scores = jnp.where(causal, nt(query_ref[rows, :], key_ref[rows, :]) * zwidth**-0.5, -1e30)
        scores = jnp.exp(scores - jnp.max(scores, axis=-1, keepdims=True))
        probs_ref[rows, :] = scores / jnp.sum(scores, axis=-1, keepdims=True)

    def gate(at):
        update_ref[:, pl.ds(at, CHUNK)] = jax.nn.sigmoid(mix(at))

    each(width, gate)

    def attend(at):
        cols = pl.ds(at, CHUNK)
        reset, slope = silu_pair(mix(width + zwidth + at))
        attended = jnp.concatenate(
            [
                nn(probs_ref[pl.ds(n * GROUP, GROUP), :].astype(low), values_ref[pl.ds(n * GROUP, GROUP), cols])
                for n in range(seqs)
            ],
            axis=0,
        )
        reset_ref[:, cols] = reset.astype(low)
        turned_ref[:, cols] = (attended * slope).astype(low)
        gated = (reset * attended).astype(low)
        gated_ref[:, cols] = gated
        gated_t_ref[cols, :] = gated.T

    each(vwidth, attend)

    def hide(at):
        cols = pl.ds(at, CHUNK)
        pre = mix(width + zwidth + vwidth + at)
        pre = pre + nn(gated_ref[...], wout_ref[:, cols]) + piece(vec_ref, where["out"], at, CHUNK)
        hidden, slope = silu_pair(pre)
        update = update_ref[:, cols]
        keep = 1.0 - update
        resid = x_ref[:, cols].astype(f32)
        hslope_ref[:, cols] = (update * slope).astype(low)
        uslope_ref[:, cols] = ((hidden - resid) * update * keep).astype(low)
        keep_ref[:, cols] = keep.astype(low)
        blend_ref[:, cols] = update * hidden + keep * resid

    each(width, hide)
    for n in range(seqs):
        rows = pl.ds(n * GROUP, GROUP)
        blend = blend_ref[rows, :]
        centered = blend - jnp.mean(blend, axis=-1, keepdims=True)
        rstd = lax.rsqrt(jnp.mean(centered * centered, axis=-1, keepdims=True) + 1e-05)
        unit = centered * rstd
        unit_ref[rows, :] = unit.astype(low)
        rstd_ref[rows, :] = jnp.broadcast_to(rstd, (GROUP, LANES))
        normed = unit * piece(vec_ref, where["gain"], 0, width) + piece(vec_ref, where["shift"], 0, width)
        blend_ref[rows, :] = normed
        normed_ref[rows, :] = normed.astype(low)
        normed_t_ref[:, rows] = normed.astype(low).T

    def lift(at):
        cols = pl.ds(at, CHUNK)
        act, slope = silu_pair(nn(normed_ref[...], wup_ref[:, cols]) + piece(vec_ref, where["up"], at, CHUNK))
        fslope_ref[:, cols] = slope.astype(low)
        act = act.astype(low)
        ffn_ref[:, cols] = act
        hidden_t_ref[cols, :] = act.T

    each(wup_ref.shape[1], lift)

    def drop(at):
        cols = pl.ds(at, CHUNK)
        blend_ref[:, cols] = blend_ref[:, cols] + nn(ffn_ref[...], wdown_ref[:, cols]) + piece(vec_ref, where["down"], at, CHUNK)

    each(width, drop)
    for n in range(seqs):
        result = blend_ref[pl.ds(n * GROUP, GROUP), :].astype(low).T
        result = jnp.where(live_lanes(spot_ref, lengths_ref, n, result.shape), result, jnp.zeros_like(result))
        out_ref[:, n] = result.reshape(out_ref.shape[0], out_ref.shape[2], GROUP)


def forward_part(spot, lengths, folded, mixed, x, values, w_mix, w_out, w_up, w_down, vec, where, qk_scale, qk_shift, after=()):
    vwidth, width = w_out.shape
    zwidth = qk_scale.shape[1]
    ff = w_up.shape[1]
    count = x.shape[0]
    narrow, wide = (count, width), (count, vwidth)
    outs = [
        ((width, count), low), (folded, low), ((count, zwidth), low), ((count, zwidth), low), ((count, zwidth), f32),
        ((count, zwidth), f32), ((count, GROUP), f32), (wide, low), (wide, low), ((vwidth, count), low),
        (narrow, low), (narrow, low), (narrow, low), (narrow, low), ((count, LANES), f32),
        ((width, count), low), ((ff, count), low), ((count, ff), low),
    ]
    scratch = [pltpu.VMEM(narrow, low), pltpu.VMEM(narrow, f32), pltpu.VMEM(wide, low)]
    scratch += [pltpu.VMEM(narrow, f32), pltpu.VMEM(narrow, low), pltpu.VMEM((count, ff), low)]
    macs = w_mix.size + w_out.size + w_up.size + w_down.size
    return call(
        functools.partial(forward_kernel, len(mixed), where),
        outs,
        (spot, lengths, w_mix, w_out, w_up, w_down, x, values, vec, qk_scale, qk_shift, *mixed),
        smem=2,
        mib=MIB[1],
        after=after,
        scratch=scratch,
    )


def column_sum(part):
    return jnp.sum(part.astype(f32), axis=0, keepdims=True)


def put(ref, row, value, columns):
    if len(ref.shape) == 2:
        ref[...] = value
        return
    owners = ref.shape[0]
    lone = value.shape[0] // owners
    for owner in range(owners):
        part = value[owner * lone : (owner + 1) * lone]
        for i, at in enumerate(range(0, value.shape[1], columns)):
            ref[owner, pl.ds(row + i * lone, lone), :] = part[:, at : at + columns]


def split_product(side, keep_ref, send_ref, left, right_ref, half, columns, row=0):
    total = right_ref.shape[1]
    for ref, which in ((keep_ref, side), (send_ref, 1 - side)):
        base = which * (total - half)
        parts = []
        for at in range(0, half, CHUNK):
            cols = pl.ds(pl.multiple_of(base + at, 128), min(CHUNK, half - at))
            parts.append(nn(left, right_ref[:, cols]).astype(low))
        put(ref, row, jnp.concatenate(parts, axis=1), columns)


def split_narrow(side, keep_ref, send_ref, left_ref, right_ref):
    both = [nn(left_ref[pl.ds(at, CHUNK), :], right_ref[...]).astype(low) for at in range(0, left_ref.shape[0], CHUNK)]
    both = jnp.concatenate(both, axis=0)
    half = both.shape[1] // 2
    near, far = both[:, :half], both[:, half:]
    put(keep_ref, 0, jnp.where(side == 0, near, far), half)
    put(send_ref, 0, jnp.where(side == 0, far, near), half)


def pair_outs(tall, wide, owners, lines=0):
    if not owners:
        return [((tall[0], tall[1] // 2), low)] * 2 + [((wide[0], wide[1] // 2), low)] * 2
    rows = (tall[0] * tall[1] + wide[0] * wide[1]) // (tall[1] * owners) + lines
    return [((owners, rows, tall[1] // 2), low)] * 2


def back_ffn_kernel(
    spot_ref, lengths_ref, wdown_ref, grad_ref, hidden_t_ref, fslope_ref, normed_t_ref, *refs
):
    halves, (g_ref, dffn_ref, small_ref) = refs[:-3], refs[-3:]
    width, ff = g_ref.shape[1], wdown_ref.shape[0]
    for n in range(grad_ref.shape[2]):
        part = wide_block(grad_ref, 1, n)
        part = jnp.where(live_lanes(spot_ref, lengths_ref, n, part.shape), part, jnp.zeros_like(part))
        g_ref[pl.ds(n * GROUP, GROUP), :] = part.T
    small_ref[:, pl.ds(0, width)] = column_sum(g_ref[...])
    side = spot_ref[2] & 1
    split_narrow(side, halves[0], halves[1], hidden_t_ref, g_ref)

    def lift(at):
        part = pl.ds(at, CHUNK)
        pulled = (nt(g_ref[...], wdown_ref[part, :]) * fslope_ref[:, part].astype(f32)).astype(low)
        dffn_ref[:, part] = pulled
        small_ref[:, pl.ds(width + at, CHUNK)] = column_sum(pulled)

    each(ff, lift)
    split_product(side, halves[-2], halves[-1], normed_t_ref[...], dffn_ref, ff // 2, halves[-2].shape[-1], halves[0].shape[-2] // 2)


def back_ffn(spot, lengths, owners, grad, hidden_t, fslope, normed_t, w_down, after=()):
    ff, width = w_down.shape
    count = fslope.shape[0]
    outs = pair_outs((ff, width), (width, ff), owners)
    outs += [((count, width), low), ((count, ff), low), ((1, width + ff), f32)]
    *halves, g, dffn, small = call(
        back_ffn_kernel,
        outs,
        (spot, lengths, w_down, grad, hidden_t, fslope, normed_t),
        smem=2,
        mib=MIB[2],
        after=after,
    )
    return halves, g, dffn, small


def back_norm_kernel(
    base, wup_ref, g_ref, dffn_ref, unit_ref, rstd_ref, vec_ref, hslope_ref, uslope_ref, kept_ref,
    dh_ref, du_ref, direct_ref, small_ref, dn_ref,
):
    width = wup_ref.shape[0]

    def drop(at):
        part = pl.ds(at, CHUNK)
        pulled = g_ref[:, part].astype(f32) + nt(dffn_ref[...], wup_ref[part, :])
        dn_ref[:, part] = pulled
        small_ref[:, part] = column_sum(pulled * unit_ref[:, part].astype(f32))
        small_ref[:, pl.ds(width + at, CHUNK)] = column_sum(pulled)

    each(width, drop)
    for n in range(g_ref.shape[0] // GROUP):
        rows = pl.ds(n * GROUP, GROUP)
        unit = unit_ref[rows, :].astype(f32)
        pulled = dn_ref[rows, :] * piece(vec_ref, base, 0, width)
        inner = jnp.mean(pulled * unit, axis=-1, keepdims=True)
        blend = pulled - jnp.mean(pulled, axis=-1, keepdims=True) - unit * inner
        blend = blend * rstd_ref[rows, :][:, :1]
        dh_ref[rows, :] = (blend * hslope_ref[rows, :].astype(f32)).astype(low)
        du_ref[rows, :] = (blend * uslope_ref[rows, :].astype(f32)).astype(low)
        direct_ref[rows, :] = (blend * kept_ref[rows, :].astype(f32)).astype(low)


def back_norm(g, dffn, unit, rstd, vec, where, hslope, uslope, kept, w_up, after=()):
    width = w_up.shape[0]
    narrow = g.shape
    return call(
        functools.partial(back_norm_kernel, where["gain"]),
        [(narrow, low)] * 3 + [((1, 2 * width), f32)],
        (w_up, g, dffn, unit, rstd, vec, hslope, uslope, kept),
        mib=MIB[3],
        after=after,
        scratch=[pltpu.VMEM(narrow, f32)],
    )


def back_attend_kernel(
    wout_ref, wmix_ref, wvalue_ref,
    dh_ref, du_ref, direct_ref, reset_ref, turned_ref, values_ref, vslope_ref, probs_ref,
    query_ref, key_ref, shared_ref, qslope_ref, qscale_ref, small_ffn_ref, small_norm_ref,
    dmix_ref, dvalue_ref, mixed_ref, resid_ref,
    table_ref,
    datt_ref,
):
    vwidth, width = wout_ref.shape
    zwidth = qscale_ref.shape[1]
    count = dh_ref.shape[0]
    seqs = count // GROUP
    dmix_ref[:, pl.ds(0, width)] = du_ref[...]
    dmix_ref[:, pl.ds(width + zwidth + vwidth, width)] = dh_ref[...]

    def gate(at):
        part = pl.ds(at, CHUNK)
        pulled = nt(dh_ref[...], wout_ref[part, :])
        dmix_ref[:, pl.ds(width + zwidth + at, CHUNK)] = (
            pulled * turned_ref[:, part].astype(f32)
        ).astype(low)
        datt_ref[:, part] = (pulled * reset_ref[:, part].astype(f32)).astype(low)

    each(vwidth, gate)
    scale = zwidth**-0.5
    q_scale, k_scale = qscale_ref[pl.ds(0, 1), :], qscale_ref[pl.ds(1, 1), :]
    zero = jnp.zeros((1, zwidth), f32)
    sums = [zero, zero, zero, zero]
    for n in range(seqs):
        rows = pl.ds(n * GROUP, GROUP)
        probs = probs_ref[rows, :]
        pulled = nt(datt_ref[rows, :], values_ref[rows, :])
        pulled = probs * (pulled - jnp.sum(pulled * probs, axis=-1, keepdims=True))
        pulled = pulled.astype(low)
        d_query = nn(pulled, key_ref[rows, :]) * scale
        d_key = nn(pulled.T, query_ref[rows, :]) * scale
        probs_t = probs.astype(low).T
        shared = shared_ref[rows, :]
        found = (d_query * shared, d_key * shared, d_query, d_key)
        sums = [a + jnp.sum(b, axis=0, keepdims=True) for a, b in zip(sums, found)]
        dmix_ref[rows, pl.ds(width, zwidth)] = (
            (d_query * q_scale + d_key * k_scale) * qslope_ref[rows, :]
        ).astype(low)
        dvalue_ref[rows, :] = (nn(probs_t, datt_ref[rows, :]) * vslope_ref[rows, :].astype(f32)).astype(low)

    def turn(result):
        devices, _, channels, _ = mixed_ref.shape
        return result.astype(low).T.reshape(devices, channels, GROUP)

    for n in range(0, seqs, 2):
        result = nt(dmix_ref[pl.ds(n * GROUP, 2 * GROUP), :], wmix_ref[...])
        mixed_ref[:, n] = turn(result[:GROUP])
        mixed_ref[:, n + 1] = turn(result[GROUP:])
    for n in range(0, seqs, 2):
        rows = pl.ds(n * GROUP, 2 * GROUP)
        result = direct_ref[rows, :].astype(f32) + nt(dvalue_ref[rows, :], wvalue_ref[...])
        resid_ref[:, n] = turn(result[:GROUP])
        resid_ref[:, n + 1] = turn(result[GROUP:])
    ff = small_ffn_ref.shape[1] - width
    found = (
        column_sum(dmix_ref[...]), column_sum(dvalue_ref[...]), column_sum(dh_ref[...]),
        sums[0], sums[1], sums[2], sums[3], small_norm_ref[:, :width], small_norm_ref[:, width:],
        small_ffn_ref[:, width:], small_ffn_ref[:, :width],
    )
    lines = []
    for part in found:
        for at in range(0, part.shape[1], TABLE):
            line = part[:, at : at + TABLE]
            lack = TABLE - line.shape[1]
            lines.append(line if lack == 0 else jnp.concatenate([line, jnp.zeros((1, lack), f32)], axis=1))
    lines.append(jnp.zeros((table_ref.shape[0] - len(lines), TABLE), f32))
    table_ref[...] = jnp.concatenate(lines, axis=0).astype(low)


def back_attend(dh, du, direct, reset, turned, values, vslope, probs, query, key, shared, qslope, qk_scale, small_ffn, small_norm, folded, w_out, w_mix, w_value, after=()):
    vwidth, width = w_out.shape
    mwidth = w_mix.shape[1]
    count = dh.shape[0]
    outs = [((count, mwidth), low), ((count, vwidth), low)]
    outs += [(folded, low), (folded, low)]
    outs += [((64, TABLE), low)]
    scratch = [pltpu.VMEM((count, vwidth), low)]
    macs = w_out.size + w_mix.size + w_value.size
    return call(
        back_attend_kernel,
        outs,
        (w_out, w_mix, w_value, dh, du, direct, reset, turned, values, vslope, probs, query, key, shared, qslope, qk_scale, small_ffn, small_norm),
        mib=MIB[4],
        after=after,
        scratch=scratch,
    )


def back_mid_kernel(spot_ref, gated_t_ref, dh_ref, x_t_ref, dvalue_ref, table_ref, *halves):
    side = spot_ref[2] & 1
    if len(halves) == 4:
        (kept, sent, wide_kept, wide_sent), tall = halves, 0
    else:
        kept, sent = halves
        wide_kept, wide_sent, tall = kept, sent, gated_t_ref.shape[0] // kept.shape[0]
    split_narrow(side, kept, sent, gated_t_ref, dh_ref)
    split_product(
        side, wide_kept, wide_sent, x_t_ref[...], dvalue_ref, dvalue_ref.shape[1] // 2, wide_kept.shape[-1], tall
    )
    if len(halves) == 4:
        return
    lines = kept.shape[1] - 2 * tall
    high = table_ref.shape[0] // (2 * lines)
    for ref, which in ((kept, side), (sent, 1 - side)):
        for owner in range(ref.shape[0]):
            at = pl.multiple_of((2 * (owner % high) + which) * lines, 16)
            ref[owner, pl.ds(2 * tall, lines), :] = table_ref[pl.ds(at, lines), :]


def back_mid(spot, owners, gated_t, dh, x_t, dvalue, table, lines, after=()):
    count, width = dh.shape
    vwidth = dvalue.shape[1]
    outs = pair_outs((vwidth, width), (width, vwidth), owners, lines)
    found = call(
        back_mid_kernel,
        outs,
        (spot, gated_t, dh, x_t, dvalue, table),
        smem=1,
        mib=MIB[5],
        after=after,
    )
    if owners:
        return [found[0]], [found[1]]
    return [found[0], found[2]], [found[1], found[3]]


def back_mix_kernel(spot_ref, mixed_t_ref, dmix_ref, keep_ref, send_ref):
    half = keep_ref.shape[-1]
    split_product(spot_ref[2] & 1, keep_ref, send_ref, mixed_t_ref[...], dmix_ref, half, half)


def back_mix_weight(spot, mixed_t, dmix, after=()):
    mwidth = dmix.shape[1]
    width, count = mixed_t.shape
    half = -(-mwidth // 256) * 128
    kept, sent = call(
        back_mix_kernel,
        [((width, half), low)] * 2,
        (spot, mixed_t, dmix),
        smem=1,
        mib=MIB[6],
        after=after,
    )
    return [kept], [sent]


def halve_kernel(index, bit, spot_ref, kept_ref, *refs):
    arrived, (sent_ref, stay_ref) = refs[:-2], refs[-2:]
    outer, inner, _, _ = sent_ref.shape
    lone = outer // len(arrived)
    mine = (spot_ref[index] >> bit) & 1
    for ref, which in ((sent_ref, 1 - mine), (stay_ref, mine)):
        for a in range(outer):
            for b in range(inner):
                total = kept_ref[a, which, b].astype(f32) + arrived[a // lone][a % lone, which, b].astype(f32)
                ref[a, b] = total.astype(low)


def halve(spot, kept, arrived, index, bit, at, after=()):
    dims = kept.shape[:-2]
    outer, inner = 1 << at, 1 << (len(dims) - at - 1)
    block = kept.shape[-2:]

    def shaped(part):
        return part.reshape((-1, 2, inner) + block)

    sent, stay = call(
        functools.partial(halve_kernel, index, bit),
        [((outer, inner) + block, low)] * 2,
        (spot, shaped(kept), *map(shaped, arrived)),
        smem=1,
        mib=MIB[7],
        after=after,

    )
    rest = dims[:at] + dims[at + 1 :] + block
    return sent.reshape(rest), stay.reshape(rest)


def finish_pair_kernel(lines, spot_ref, *refs):
    outs = 3 if lines else 2
    shares, (tall_ref, wide_ref) = refs[:-outs], refs[len(refs) - outs :][:2]
    columns = shares[0].shape[1]
    cut = tall_ref.shape[0] * 2 // len(shares)
    lone = wide_ref.shape[0] * 2 // len(shares)
    for k, ref in enumerate(shares):
        at = spot_ref[2] ^ k
        high, side = at >> 1, at & 1
        tall_ref[pl.ds(pl.multiple_of(high * cut, 8), cut), pl.ds(pl.multiple_of(side * columns, 128), columns)] = ref[
            pl.ds(0, cut), :
        ].astype(f32)
        runs = wide_ref.shape[1] // 2 // columns
        for run in range(runs):
            wide_ref[
                pl.ds(pl.multiple_of(high * lone, 8), lone),
                pl.ds(pl.multiple_of((side * runs + run) * columns, 128), columns),
            ] = ref[pl.ds(cut + run * lone, lone), :].astype(f32)
        if lines:
            refs[-1][pl.ds(pl.multiple_of(at * lines, 8), lines), :] = ref[pl.ds(ref.shape[0] - lines, lines), :].astype(f32)


def finish_pair(spot, shares, tall, wide, lines=0, after=()):
    outs = [(tall, f32), (wide, f32)]
    if lines:
        outs.append(((len(shares) * lines, shares[0].shape[1]), f32))
    return call(
        functools.partial(finish_pair_kernel, lines), outs, (spot, *shares), smem=1, mib=MIB[8], after=after
    )


def finish_mix_kernel(spot_ref, *refs):
    shares, out_ref = refs[:-1], refs[-1]
    half, mwidth = shares[0].shape[1], out_ref.shape[1]
    common = 2 * half - mwidth
    lone = out_ref.shape[0] * 2 // len(shares)
    for k, ref in enumerate(shares):
        at = spot_ref[2] ^ k
        rows = pl.ds(pl.multiple_of((at >> 1) * lone, 8), lone)
        base = pl.multiple_of(common + (at & 1) * (mwidth - half), 128)
        out_ref[rows, pl.ds(base, half - common)] = ref[:, common:].astype(f32)
        if common:

            @pl.when(at & 1 == 0)
            def _():
                out_ref[rows, pl.ds(0, common)] = ref[:, :common].astype(f32)


def finish_mix(spot, shares, shape, after=()):
    return call(finish_mix_kernel, [(shape, f32)], (spot, *shares), smem=1, mib=MIB[9], after=after)[0]


Y_FIRST = (("tok", 1), ("ch", 0))
Z_FIRST = (("ch", 1), ("tok", 1), ("ch", 0))
X_FIRST = (("ch", 0), ("tok", 1))


def bits_of(axis):
    return lax.axis_size(axis).bit_length() - 1


def across(part, axis, turn):
    return lax.ppermute(part, axis, [(i, i ^ turn) for i in range(lax.axis_size(axis))])


def exchange(part, axis, bit):
    return across(part, axis, 1 << bit)


def side_of(axis, bit):
    return (lax.axis_index(axis) >> bit) & 1


def by_owner(grad):
    dims = (2,) * (bits_of("ch") + bits_of("tok") - 1)
    return grad.reshape(dims + (-1, grad.shape[-1]))


def fold(part, columns):
    runs = [part[..., at : at + columns] for at in range(0, part.shape[-1], columns)]
    return jnp.concatenate(runs, axis=-2)


def add(left, right):
    return (left.astype(f32) + right.astype(f32)).astype(low)


def plain_halve(kept, arrived, mine, at):
    columns = min(part.shape[-1] for part in kept)

    def pick(which):
        def one(part):
            return lax.dynamic_index_in_dim(part, which, at, keepdims=False)

        return jnp.concatenate([fold(add(one(a), one(b)), columns) for a, b in zip(kept, arrived)], axis=-2)

    return pick(1 - mine), pick(mine)


class Sum:
    def __init__(self, spot, kept, sent, order):
        self.spot = spot
        self.names = [("ch", k) for k in reversed(range(bits_of("ch")))]
        self.names += [("tok", k) for k in reversed(range(1, bits_of("tok")))]
        self.stages = list(order) + [name for name in reversed(self.names) if name not in order]
        self.kept = [by_owner(part) for part in kept]
        self.arrived = [by_owner(exchange(part, "tok", 0)) for part in sent]

    def step(self, after=()):
        axis, bit = self.stages.pop(0)
        at = self.names.index((axis, bit))
        self.names.remove((axis, bit))
        if len(self.kept) == 1 and self.kept[0].shape[-2] % 16 == 0:
            index = 1 if axis == "ch" else 2
            sent, stay = halve(self.spot, self.kept[0], self.arrived, index, bit, at, after)
        else:
            sent, stay = plain_halve(self.kept, self.arrived, side_of(axis, bit), at)
        self.kept, self.arrived = [stay], [exchange(sent, axis, bit)]
        return stay

    def shares(self):
        found = [add(self.kept[0], self.arrived[0])]
        for bit in reversed(range(1, bits_of("tok"))):
            found += [exchange(part, "tok", bit) for part in found]
        lower = [exchange(part, "tok", 0) for part in found]
        size = bits_of("tok") - 1
        order = [sum(((k >> (size - 1 - i)) & 1) << i for i in range(size)) for k in range(len(found))]
        found = [part for k in order for part in (found[k], lower[k])]
        return found


def in_order(shares, place):
    bit = 1
    while bit < len(shares):
        swapped = (place & bit) != 0
        shares = [jnp.where(swapped, shares[k ^ bit], shares[k]) for k in range(len(shares))]
        bit *= 2
    return jnp.stack(shares)


def plain_pair(place, shares, tall, wide):
    whole = in_order(shares, place).astype(f32)
    high = len(shares) // 2
    cut, lone = tall[0] // high, wide[0] // high
    whole = whole.reshape((high, 2) + whole.shape[1:])
    first = whole[:, :, :cut].transpose(0, 2, 1, 3).reshape(tall)
    second = whole[:, :, cut:].reshape(high, 2, -1, lone, whole.shape[-1])
    return first, second.transpose(0, 3, 1, 2, 4).reshape(wide)


def plain_mix(place, shares, shape):
    whole = in_order(shares, place).astype(f32)
    half = whole.shape[-1]
    whole = whole.reshape((len(shares) // 2, 2) + whole.shape[1:])
    whole = jnp.concatenate([whole[:, 0], whole[:, 1, :, 2 * half - shape[1] :]], axis=-1)
    return whole.reshape(shape)


def sum_tok(part):
    for bit in range(bits_of("tok")):
        part = part + exchange(part, "tok", bit)
    return part


def swap(parts):
    return lax.all_to_all(parts, "ch", split_axis=0, concat_axis=0, tiled=True)


def folded(parts):
    devices, channels, span = parts.shape[0], parts.shape[-2], parts.shape[-1]
    if channels % 16 == 0:
        return parts
    return jnp.moveaxis(parts, 0, -3).reshape((1,) + parts.shape[1:-2] + (devices * channels, span))


def unfolded(parts, devices):
    if parts.shape[0] == devices:
        return parts
    channels, span = parts.shape[-2] // devices, parts.shape[-1]
    return jnp.moveaxis(parts.reshape(parts.shape[1:-2] + (devices, channels, span)), -3, 0)


def local(
    inputs,
    out_grad,
    seq_lengths,
    ema_alpha,
    ema_delta,
    ema_beta,
    ema_eta,
    ema_omega,
    w_mix,
    b_mix,
    w_value,
    b_value,
    w_out,
    b_out,
    qk_scale,
    qk_shift,
    ln_gain,
    ln_bias,
    w_up,
    b_up,
    w_down,
    b_down,
):
    count, channels, local_len = inputs.shape
    width, mwidth = w_mix.shape
    vwidth, ff = w_value.shape[1], w_up.shape[1]
    devices, tok_size = lax.axis_size("ch"), lax.axis_size("tok")
    columns = count * channels
    span = local_len // devices
    tok_index = lax.axis_index("tok").astype(jnp.int32)
    ch_index = lax.axis_index("ch").astype(jnp.int32)
    spot = jnp.stack([tok_index * local_len + ch_index * span, ch_index, tok_index])
    apart = devices <= 8 and channels % 16 == 0

    def by_column(parts):
        whole = unfolded(parts, devices)
        return pad_to_lanes(whole.reshape(whole.shape[:-3] + (columns, span)), whole.ndim - 3)

    where = vectors(width, mwidth, vwidth, ff)
    vec = jnp.concatenate([b_mix, b_value, b_out, ln_gain, ln_bias, b_up, b_down])[None]
    params = ema_params(ema_alpha, ema_delta, ema_beta, ema_eta, count)
    omega = pad_to_lanes(jnp.tile(ema_omega, count)[None], 1)

    flat = inputs.reshape(columns, local_len)
    raw = by_blocks(spot, flat, out_grad.reshape(columns, local_len))
    raw = folded(swap(raw.reshape(devices, 2, count, channels, span)))
    xs, ends, total = ema_ends(pad_to_lanes(flat, 0), params)
    totals = lax.all_gather(total, "tok")
    mixed, slope, entry = ema_mix(spot, xs, ends, params, omega, totals, apart)
    if apart:
        mixed = [part.reshape(count, channels, span) for part in mixed]
        mixed = [part if k == 0 else across(part, "ch", k) for k, part in enumerate(mixed)]
    else:
        mixed = folded(swap(mixed[0][:, :columns].reshape(devices, count, channels, span)))
        mixed = [mixed[0]] if mixed.shape[0] == 1 else [mixed.transpose(1, 0, 2, 3).reshape(count, width, span)]
    x, values, vslope, x_t = value_part(raw, w_value, vec, where, (entry,))
    (
        mixed_t, result, query, key, shared, qslope, probs, reset, turned, gated_t,
        hslope, uslope, keep, unit, rstd, normed_t, hidden_t, fslope,
    ) = forward_part(
        spot, seq_lengths, raw.shape[:1] + raw.shape[2:], mixed, x, values, w_mix, w_out, w_up, w_down, vec,
        where, qk_scale, qk_shift,
    )
    owners = devices * tok_size // 2
    joined = owners if width // owners % 16 == 0 else 0
    halves, g, dffn, small_ffn = back_ffn(
        spot, seq_lengths, joined, raw, hidden_t, fslope, normed_t, w_down
    )
    ffn = Sum(spot, halves[::2], halves[1::2], Y_FIRST)
    dh, du, direct, small_norm = back_norm(g, dffn, unit, rstd, vec, where, hslope, uslope, keep, w_up)
    last = ffn.step((small_norm,))
    dmix, dvalue, back_mix, back_resid, table = back_attend(
        dh, du, direct, reset, turned, values, vslope, probs, query, key, shared, qslope,
        qk_scale, small_ffn, small_norm, result.shape, w_out, w_mix, w_value, (last,),
    )
    kept, sent = back_mix_weight(spot, mixed_t, dmix, (table,))
    mix = Sum(spot, kept, sent, X_FIRST)
    lines = table.shape[0] // tok_size
    kept, sent = back_mid(spot, joined, gated_t, dh, x_t, dvalue, table, lines, (kept[0],))
    last = kept[0]
    back_mix = swap(unfolded(back_mix, devices))
    if not joined:
        table = table.reshape(tok_size // 2, 2, lines, TABLE)
        for group, which in ((kept, side_of("tok", 0)), (sent, 1 - side_of("tok", 0))):
            part = lax.dynamic_index_in_dim(table, which, 1, keepdims=False)
            part = jnp.broadcast_to(part[None], (devices,) + part.shape).reshape(-1, TABLE)
            group.append(part)
    mid = Sum(spot, kept, sent, Z_FIRST)
    last = mix.step((last,))
    last = mid.step((last,))
    last = ffn.step((last,))
    back_resid, back_mix, _ = lax.optimization_barrier((unfolded(back_resid, devices), back_mix, last))
    back_resid = swap(back_resid)
    pull, heads, total = ema_back(by_column(back_mix), slope, params, (last,))
    totals = lax.all_gather(total, "tok")
    last = mix.step((total,))
    last = mid.step((last,))
    last = ffn.step((last,))
    sums = ema_sums(spot, xs, pull, entry, heads, totals, params, (last,))
    last = mix.step((sums,))
    last = mid.step((last,))
    last = ffn.step((last,))
    result, back_resid = lax.optimization_barrier((unfolded(result, devices), back_resid))
    result = swap(result)
    input_grad = ema_finish(spot, pull, heads, params, omega, totals, by_column(back_resid), (last,))
    input_grad = input_grad[:columns].reshape(inputs.shape)
    output = by_columns(by_column(result))[:columns].reshape(inputs.shape)
    ema_grads = ema_param_grads(sum_tok(sums), ema_alpha, ema_delta, ema_beta, ema_eta, count)
    last = input_grad
    while mix.stages:
        last = mix.step((last,))
    while mid.stages:
        last = mid.step((last,))
    while ffn.stages:
        last = ffn.step((last,))

    tall, wide = (vwidth // devices, width), (width // devices, vwidth)
    shares = mid.shares()
    across_mix = (width // devices, mwidth)
    if joined:
        g_out, g_value, table = finish_pair(spot, shares, tall, wide, lines)
        g_down, g_up = finish_pair(spot, ffn.shares(), tall, wide)
        g_mix = finish_mix(spot, mix.shares(), across_mix)
    else:
        table = in_order([part[-lines:] for part in shares], tok_index).astype(f32)
        shares = [part[:-lines] for part in shares]
        g_out, g_value = plain_pair(tok_index, shares, tall, wide)
        g_down, g_up = plain_pair(tok_index, ffn.shares(), tall, wide)
        g_mix = plain_mix(tok_index, mix.shares(), across_mix)
    table = table.reshape(-1)
    found, at = [], 0
    half = qk_scale.shape[1]
    for size in (mwidth, vwidth, width, half, half, half, half, width, width, ff, width):
        found.append(table[at : at + size])
        at += -(-size // TABLE) * TABLE
    g_bmix, g_bvalue, g_bout, scale_q, scale_k, shift_q, shift_k, g_gain, g_lnbias, g_bup, g_bdown = found
    g_qscale, g_qshift = jnp.stack([scale_q, scale_k]), jnp.stack([shift_q, shift_k])
    return (
        output,
        input_grad,
        *ema_grads,
        g_mix,
        g_bmix,
        g_value,
        g_bvalue,
        g_out,
        g_bout,
        g_qscale,
        g_qshift,
        g_gain,
        g_lnbias,
        g_up,
        g_bup,
        g_down,
        g_bdown,
    )


def solution(mesh):
    by_ch = P("ch", None)
    placed = P(None, "ch", "tok")
    return jax.shard_map(
        local,
        mesh=mesh,
        in_specs=(placed, placed, P()) + (by_ch,) * 4 + (P("ch"),) + (P(),) * 14,
        out_specs=(
            (placed, placed)
            + (by_ch,) * 4
            + (P("ch"), by_ch, P(), by_ch, P(), by_ch)
            + (P(),) * 5
            + (by_ch, P(), by_ch, P())
        ),
        check_vma=False,
    )
```

```python
import functools
import jax
import jax.numpy as jnp
from jax import lax
from jax.experimental import pallas as pl
from jax.experimental.pallas import tpu as pltpu
from jax.sharding import PartitionSpec as P

GROUP = 128
SUB = 8
LANES = 128
f32 = jnp.float32


def by_tile(shape, dim):
    block = tuple(LANES if k == dim else size for k, size in enumerate(shape))
    return pl.BlockSpec(block, lambda i: tuple(i if k == dim else 0 for k in range(len(shape))))


def in_smem():
    return pl.BlockSpec(memory_space=pltpu.SMEM)


def roomy(mib=5):
    return pltpu.CompilerParams(vmem_limit_bytes=mib * 1024 * 1024)


def work(flops, moved, exps=0):
    return pl.CostEstimate(flops=1, bytes_accessed=1, transcendentals=0)


def launch(kernel, outs, ins, in_specs, out_specs, after=(), grid=(), scratch=(), mib=5, cost=None):
    count = len(ins)

    def run(*refs):
        kernel(*refs[:count], *refs[count + len(after) :])

    return pl.pallas_call(
        run,
        grid=grid,
        out_shape=tuple(jax.ShapeDtypeStruct(shape, kind) for shape, kind in outs),
        in_specs=list(in_specs) + [pl.BlockSpec(memory_space=pl.ANY)] * len(after),
        out_specs=tuple(out_specs),
        scratch_shapes=list(scratch),
        compiler_params=roomy(mib),
        cost_estimate=cost,
    )(*ins, *after)


def rates(params_ref):
    rate = jax.nn.sigmoid(params_ref[0])
    drop = rate * jax.nn.sigmoid(params_ref[1])
    weight = params_ref[3] * rate * params_ref[2]
    return 1.0 - drop, jnp.log1p(-drop), weight


def spread(ref, j):
    return jnp.broadcast_to(ref[pl.ds(j, 1), :], (SUB, LANES))


def tree_sum(parts):
    while len(parts) > 1:
        parts = [a + b for a, b in zip(parts[::2], parts[1::2])] + parts[len(parts) & ~1 :]
    return parts[0]


def block_rows(g, t):
    return pl.ds(g * GROUP + t, SUB, stride=GROUP)


def state_rows(g, j, expand):
    return pl.ds(g * expand + j, SUB, stride=expand)


def blocks_kernel(spot_ref, first_ref, second_ref, out_ref, sems):
    copies = []
    for b in range(out_ref.shape[0]):
        cols = pl.ds(b * GROUP, GROUP)
        for which, ref in enumerate((first_ref, second_ref)):
            copies.append(pltpu.make_async_copy(ref.at[:, cols], out_ref.at[b, which], sems.at[2 * b + which]))
    for copy in copies:
        copy.start()
    for copy in copies:
        copy.wait()


def by_blocks(spot, first, second):
    columns, length = first.shape
    blocks = length // GROUP
    anywhere = pl.BlockSpec(memory_space=pl.ANY)
    return launch(
        blocks_kernel,
        [((blocks, 2, columns, GROUP), first.dtype)],
        (spot, first, second),
        [in_smem(), anywhere, anywhere],
        [anywhere],
        scratch=[pltpu.SemaphoreType.DMA((2 * blocks,))],
        mib=1,
    )[0]


def ema_ends_kernel(x_ref, params_ref, xs_ref, ends_ref, total_ref, decay_ref):
    length = x_ref.shape[1]
    expand = params_ref.shape[1]
    blocks = length // GROUP
    decay, log_decay, _ = rates(params_ref)
    decay_ref[...] = decay
    for b in range(blocks):
        rows = pl.ds(b * GROUP, GROUP)
        xs_ref[rows, :] = x_ref[:, rows].astype(f32).T
    factors = [spread(decay_ref, j) for j in range(expand)]
    for g in range(0, blocks, SUB):

        def step(t, states):
            now = xs_ref[block_rows(g, t), :]
            return tuple(f * s + now for f, s in zip(factors, states))

        states = (jnp.zeros((SUB, LANES), f32),) * expand
        states = lax.fori_loop(0, GROUP, step, states, unroll=8)
        for j in range(expand):
            ends_ref[state_rows(g, j, expand), :] = states[j]
    jump = jnp.exp(GROUP * log_decay)
    carry = jnp.zeros_like(jump)
    for b in range(blocks):
        carry = jump * carry + ends_ref[pl.ds(b * expand, expand), :]
    total_ref[...] = carry


def ema_ends(x, params, after=()):
    columns, length = x.shape
    expand = params.shape[1]
    shapes = ((length, columns), (length // GROUP * expand, columns), (expand, columns))
    return launch(
        ema_ends_kernel,
        [(shape, f32) for shape in shapes],
        (x, params),
        [by_tile(x.shape, 0), by_tile(params.shape, 2)],
        [by_tile(shape, 1) for shape in shapes],
        after=after,
        grid=(columns // LANES,),
        scratch=[pltpu.VMEM((expand, LANES), f32)],
        mib=5 * max(1, length // 1024),
        cost=work(2 * expand * length * columns, 6 * length * columns),
    )


def ema_mix_kernel(
    spot_ref, xs_ref, ends_ref, params_ref, omega_ref, totals_ref, *refs
):
    mixed_refs, (slope_ref, entry_ref, decay_ref, weight_ref, smooth_ref) = refs[:-5], refs[-5:]
    length = xs_ref.shape[0]
    expand = params_ref.shape[1]
    blocks = length // GROUP
    decay, log_decay, weight = rates(params_ref)
    decay_ref[...] = decay
    weight_ref[...] = weight
    whole = jnp.exp(length * log_decay)
    jump = jnp.exp(GROUP * log_decay)
    carry = jnp.zeros_like(jump)
    for k in range(totals_ref.shape[0]):
        carry = jnp.where(k < spot_ref[2], whole * carry + totals_ref[k], carry)
    for b in range(blocks):
        rows = pl.ds(b * expand, expand)
        entry_ref[rows, :] = carry
        carry = jump * carry + ends_ref[rows, :]
    factors = [spread(decay_ref, j) for j in range(expand)]
    weights = [spread(weight_ref, j) for j in range(expand)]
    for g in range(0, blocks, SUB):

        def step(t, states):
            now = xs_ref[block_rows(g, t), :]
            states = tuple(f * s + now for f, s in zip(factors, states))
            smooth_ref[block_rows(g, t), :] = tree_sum([w * s for w, s in zip(weights, states)])
            return states

        start = tuple(entry_ref[state_rows(g, j, expand), :] for j in range(expand))
        lax.fori_loop(0, GROUP, step, start, unroll=8)
    for k in range(blocks):
        rows = pl.ds(pl.multiple_of((spot_ref[1] ^ k) * GROUP, GROUP), GROUP)
        pre = smooth_ref[rows, :] + omega_ref[...] * xs_ref[rows, :]
        sigma = jax.nn.sigmoid(pre)
        block = (pre * sigma).T.astype(jnp.bfloat16)
        if len(mixed_refs) == 1:
            mixed_refs[0][spot_ref[1] ^ k] = block
        else:
            mixed_refs[k][...] = block
        slope_ref[rows, :] = (sigma * (1.0 + pre * (1.0 - sigma))).astype(slope_ref.dtype)


def ema_mix(spot, xs, ends, params, omega, totals, apart, after=()):
    length, columns = xs.shape
    expand = params.shape[1]
    blocks = length // GROUP
    mixed = [(columns, GROUP)] * blocks if apart else [(blocks, columns, GROUP)]
    *found, slope, entry = launch(
        ema_mix_kernel,
        [(shape, jnp.bfloat16) for shape in mixed] + [(xs.shape, jnp.bfloat16), (ends.shape, f32)],
        (spot, xs, ends, params, omega, totals),
        [
            in_smem(), by_tile(xs.shape, 1), by_tile(ends.shape, 1), by_tile(params.shape, 2),
            by_tile(omega.shape, 1), by_tile(totals.shape, 2),
        ],
        [by_tile(shape, len(shape) - 2) for shape in mixed] + [by_tile(xs.shape, 1), by_tile(ends.shape, 1)],
        after=after,
        grid=(columns // LANES,),
        scratch=[
            pltpu.VMEM((expand, LANES), f32),
            pltpu.VMEM((expand, LANES), f32),
            pltpu.VMEM((length, LANES), f32),
        ],
        mib=5 * max(1, length // 1024),
        cost=work(4 * expand * length * columns, 10 * length * columns, length * columns),
    )
    return found, slope, entry


def ema_back_kernel(dmix_ref, slope_ref, params_ref, pull_ref, heads_ref, total_ref, decay_ref):
    length = slope_ref.shape[0]
    expand = params_ref.shape[1]
    blocks = length // GROUP
    decay, log_decay, _ = rates(params_ref)
    decay_ref[...] = decay
    for b in range(blocks):
        rows = pl.ds(b * GROUP, GROUP)
        pull_ref[rows, :] = dmix_ref[b].astype(f32).T * slope_ref[rows, :].astype(f32)
    factors = [spread(decay_ref, j) for j in range(expand)]
    for g in range(0, blocks, SUB):

        def step(t, states):
            now = pull_ref[block_rows(g, GROUP - 1 - t), :]
            return tuple(f * s + now for f, s in zip(factors, states))

        states = (jnp.zeros((SUB, LANES), f32),) * expand
        states = lax.fori_loop(0, GROUP, step, states, unroll=8)
        for j in range(expand):
            heads_ref[state_rows(g, j, expand), :] = states[j]
    jump = jnp.exp(GROUP * log_decay)
    carry = jnp.zeros_like(jump)
    for b in reversed(range(blocks)):
        carry = jump * carry + heads_ref[pl.ds(b * expand, expand), :]
    total_ref[...] = carry


def ema_back(dmix, slope, params, after=()):
    length, columns = slope.shape
    expand = params.shape[1]
    shapes = ((length, columns), (length // GROUP * expand, columns), (expand, columns))
    return launch(
        ema_back_kernel,
        [(shape, f32) for shape in shapes],
        (dmix, slope, params),
        [by_tile(dmix.shape, 1), by_tile(slope.shape, 1), by_tile(params.shape, 2)],
        [by_tile(shape, 1) for shape in shapes],
        after=after,
        grid=(columns // LANES,),
        scratch=[pltpu.VMEM((expand, LANES), f32)],
        mib=5 * max(1, length // 1024),
        cost=work(2 * expand * length * columns, 8 * length * columns),
    )


def enter_from_later(spot_ref, heads_ref, totals_ref, enter_ref, log_decay, length):
    expand = log_decay.shape[0]
    whole = jnp.exp(length * log_decay)
    jump = jnp.exp(GROUP * log_decay)
    carry = jnp.zeros_like(jump)
    for k in reversed(range(totals_ref.shape[0])):
        carry = jnp.where(k > spot_ref[2], whole * carry + totals_ref[k], carry)
    for b in reversed(range(length // GROUP)):
        rows = pl.ds(b * expand, expand)
        enter_ref[rows, :] = carry
        carry = jump * carry + heads_ref[rows, :]


def ema_finish_kernel(
    spot_ref, pull_ref, heads_ref, params_ref, omega_ref, totals_ref, direct_ref, result_ref,
    grad_ref, output_ref, decay_ref, weight_ref, enter_ref, smooth_ref,
):
    length = pull_ref.shape[0]
    expand = params_ref.shape[1]
    blocks = length // GROUP
    decay, log_decay, weight = rates(params_ref)
    decay_ref[...] = decay
    weight_ref[...] = weight
    enter_from_later(spot_ref, heads_ref, totals_ref, enter_ref, log_decay, length)
    factors = [spread(decay_ref, j) for j in range(expand)]
    weights = [spread(weight_ref, j) for j in range(expand)]
    for g in range(0, blocks, SUB):

        def step(t, states):
            now = pull_ref[block_rows(g, GROUP - 1 - t), :]
            states = tuple(f * s + now for f, s in zip(factors, states))
            back = tree_sum([w * s for w, s in zip(weights, states)])
            smooth_ref[block_rows(g, GROUP - 1 - t), :] = back
            return states

        start = tuple(enter_ref[state_rows(g, j, expand), :] for j in range(expand))
        lax.fori_loop(0, GROUP, step, start, unroll=8)
    for b in range(blocks):
        rows = pl.ds(b * GROUP, GROUP)
        back = smooth_ref[rows, :] + omega_ref[...] * pull_ref[rows, :]
        grad_ref[:, rows] = back.T + direct_ref[b, 0].astype(f32)
        output_ref[:, rows] = result_ref[b, 0]


def ema_finish(spot, pull, heads, params, omega, totals, joint, after=()):
    length, columns = pull.shape

    def part(which):
        return pl.BlockSpec((length // GROUP, 1, LANES, GROUP), lambda i: (0, which, i, 0))

    expand = params.shape[1]
    return launch(
        ema_finish_kernel,
        [((columns, length), f32), ((columns, length), joint.dtype)],
        (spot, pull, heads, params, omega, totals, joint, joint),
        [
            in_smem(), by_tile(pull.shape, 1), by_tile(heads.shape, 1), by_tile(params.shape, 2),
            by_tile(omega.shape, 1), by_tile(totals.shape, 2), part(0), part(1),
        ],
        [by_tile((columns, length), 0)] * 2,
        after=after,
        grid=(columns // LANES,),
        scratch=[
            pltpu.VMEM((expand, LANES), f32),
            pltpu.VMEM((expand, LANES), f32),
            pltpu.VMEM((heads.shape[0], LANES), f32),
            pltpu.VMEM((length, LANES), f32),
        ],
        mib=5 * max(1, length // 1024),
        cost=work(4 * expand * length * columns, 14 * length * columns),
    )


def ema_sums_kernel(spot_ref, xs_ref, pull_ref, entry_ref, heads_ref, totals_ref, params_ref, sums_ref, decay_ref, enter_ref):
    length = xs_ref.shape[0]
    expand = params_ref.shape[1]
    blocks = length // GROUP
    half = expand // 2
    decay, log_decay, _ = rates(params_ref)
    decay_ref[...] = decay
    enter_from_later(spot_ref, heads_ref, totals_ref, enter_ref, log_decay, length)
    for low in range(0, expand, half):
        factors = [spread(decay_ref, low + j) for j in range(half)]
        zero = (jnp.zeros((SUB, LANES), f32),) * half
        plain, turned = zero, zero
        for g in range(0, blocks, SUB):

            def step(t, held):
                states, slants, plain, turned = held
                now, pull = xs_ref[block_rows(g, t), :], pull_ref[block_rows(g, t), :]
                slants = tuple(f * p + s for f, p, s in zip(factors, slants, states))
                states = tuple(f * s + now for f, s in zip(factors, states))
                plain = tuple(a + pull * s for a, s in zip(plain, states))
                turned = tuple(a + pull * p for a, p in zip(turned, slants))
                return states, slants, plain, turned

            start = tuple(entry_ref[state_rows(g, low + j, expand), :] for j in range(half))
            held = (start, zero, plain, turned)
            _, slants, plain, turned = lax.fori_loop(0, GROUP, step, held, unroll=4)
            turned = tuple(
                a + f * p * enter_ref[state_rows(g, low + j, expand), :]
                for j, (a, f, p) in enumerate(zip(turned, factors, slants))
            )
        for j in range(half):
            sums_ref[pl.ds(low + j, 1), :] = jnp.sum(plain[j], axis=0, keepdims=True)
            sums_ref[pl.ds(expand + low + j, 1), :] = jnp.sum(turned[j], axis=0, keepdims=True)
    straight = jnp.zeros((SUB, LANES), f32)
    for b in range(0, length, SUB):
        straight = straight + xs_ref[pl.ds(b, SUB), :] * pull_ref[pl.ds(b, SUB), :]
    sums_ref[pl.ds(2 * expand, SUB), :] = straight


def ema_sums(spot, xs, pull, entry, heads, totals, params, after=()):
    length, columns = xs.shape
    expand = params.shape[1]
    shape = (2 * expand + SUB, columns)
    return launch(
        ema_sums_kernel,
        [(shape, f32)],
        (spot, xs, pull, entry, heads, totals, params),
        [
            in_smem(), by_tile(xs.shape, 1), by_tile(xs.shape, 1), by_tile(entry.shape, 1), by_tile(entry.shape, 1),
            by_tile(totals.shape, 2), by_tile(params.shape, 2),
        ],
        [by_tile(shape, 1)],
        after=after,
        grid=(columns // LANES,),
        scratch=[pltpu.VMEM((expand, LANES), f32), pltpu.VMEM((entry.shape[0], LANES), f32)],
        mib=5 * max(1, length // 1024),
        cost=work(8 * expand * length * columns, 8 * length * columns),
    )[0]


def pad_to_lanes(part, dim):
    extra = -part.shape[dim] % LANES
    if extra == 0:
        return part
    return jnp.pad(part, [(0, extra if k == dim else 0) for k in range(part.ndim)])


def ema_params(alpha, delta, beta, eta, count):
    packed = jnp.swapaxes(jnp.stack([alpha, delta, beta, eta]), 1, 2)
    return pad_to_lanes(jnp.tile(packed, (1, 1, count)), 2)


def ema_param_grads(total, alpha, delta, beta, eta, count):
    channels, expand = alpha.shape
    summed = jnp.sum(total[:, : count * channels].reshape(-1, count, channels), axis=1)
    plain, turned = summed[:expand].T, summed[expand : 2 * expand].T
    omega = jnp.sum(summed[2 * expand :], axis=0)
    rate, damp = jax.nn.sigmoid(alpha), jax.nn.sigmoid(delta)
    g_alpha = eta * beta * rate * (1.0 - rate) * (plain - damp * rate * turned)
    g_delta = -(eta * beta * rate * rate * damp * (1.0 - damp)) * turned
    return g_alpha, g_delta, rate * eta * plain, rate * beta * plain, omega


low = jnp.bfloat16
CHUNK = 256
MIB = (3, 18, 8, 5, 6, 8, 8, 6, 4, 4)
TABLE = 384


def nn(left, right):
    return jnp.dot(left, right, preferred_element_type=f32)


def nt(left, right):
    return lax.dot_general(left, right, (((1,), (1,)), ((), ())), preferred_element_type=f32)


def silu_pair(pre):
    sigma = jax.nn.sigmoid(pre)
    return pre * sigma, sigma * (1.0 + pre * (1.0 - sigma))


def each(width, body, size=CHUNK):
    for at in range(0, width, size):
        body(at)


def wide_block(ref, which, n):
    part = ref[:, which, n]
    return part.reshape(part.shape[0] * part.shape[1], part.shape[2])


def live_lanes(spot_ref, lengths_ref, n, shape):
    return spot_ref[0] + lax.broadcasted_iota(jnp.int32, shape, 1) < lengths_ref[n]


def span_of(ref, n):
    return pl.ds(n * GROUP, GROUP)


def call(kernel, outs, ins, smem=0, hbm=0, scratch=(), moved=1, mib=16, after=()):
    spaces = [pltpu.SMEM] * smem + [pl.ANY] * hbm + [pltpu.VMEM] * (len(ins) - smem - hbm)
    return launch(
        kernel,
        outs,
        ins,
        [pl.BlockSpec(memory_space=space) for space in spaces],
        [pl.BlockSpec(memory_space=pltpu.VMEM) for _ in outs],
        after=after,
        scratch=scratch,
        mib=mib,
        cost=pl.CostEstimate(flops=1, bytes_accessed=moved, transcendentals=0),
    )


def vectors(width, mwidth, vwidth, ff):
    sizes = (
        ("mix", mwidth), ("value", vwidth), ("out", width), ("gain", width),
        ("shift", width), ("up", ff), ("down", width),
    )
    place, at = {}, 0
    for name, size in sizes:
        place[name] = at
        at += size
    return place


def piece(ref, base, at, size):
    return ref[:, pl.ds(base + at, size)]


def value_kernel(base, w_ref, x_ref, vec_ref, rows_ref, values_ref, slope_ref, rows_t_ref):
    for n in range(x_ref.shape[2]):
        rows = pl.ds(n * GROUP, GROUP)
        block = wide_block(x_ref, 0, n)
        rows_t_ref[:, rows] = block
        rows_ref[rows, :] = block.T

    def chunk(at):
        cols = pl.ds(at, CHUNK)
        act, slope = silu_pair(nn(rows_ref[...], w_ref[:, cols]) + piece(vec_ref, base, at, CHUNK))
        values_ref[:, cols] = act.astype(low)
        slope_ref[:, cols] = slope.astype(low)

    each(w_ref.shape[1], chunk)


def value_part(x, w_value, vec, where, after=()):
    width, vwidth = w_value.shape
    count = x.shape[2] * GROUP
    return call(
        functools.partial(value_kernel, where["value"]),
        [((count, width), low), ((count, vwidth), low), ((count, vwidth), low), ((width, count), low)],
        (w_value, x, vec),
        mib=MIB[0],
        after=after,
    )


def forward_kernel(
    pieces, where, spot_ref, lengths_ref, wout_hbm, wup_hbm, wdown_hbm, wmix_ref,
    x_ref, values_ref, vec_ref, qscale_ref, qshift_ref, *refs
):
    mixed_refs, refs = refs[:pieces], refs[pieces:]
    mixed_t_ref, refs, (wout_ref, wup_ref, wdown_ref, sems) = refs[0], refs[1:-4], refs[-4:]
    pairs = ((wout_hbm, wout_ref), (wup_hbm, wup_ref), (wdown_hbm, wdown_ref))
    copies = [pltpu.make_async_copy(src, dst, sems.at[k]) for k, (src, dst) in enumerate(pairs)]
    for copy in copies:
        copy.start()
    forward_rows(spot_ref, mixed_refs, mixed_t_ref, refs[-6])
    forward_body(
        copies, where, spot_ref, lengths_ref, wmix_ref, wout_ref, wup_ref, wdown_ref,
        x_ref, values_ref, vec_ref, qscale_ref, qshift_ref, *refs
    )


def forward_rows(spot_ref, mixed_refs, mixed_t_ref, m_ref):
    for k, ref in enumerate(mixed_refs):
        seqs, channels, _ = ref.shape
        at = pl.multiple_of((spot_ref[1] ^ k) * channels, 16) if len(mixed_refs) > 1 else 0
        for n in range(seqs):
            mixed_t_ref[pl.ds(at, channels), pl.ds(n * GROUP, GROUP)] = ref[n]
    for n in range(m_ref.shape[0] // GROUP):
        rows = pl.ds(n * GROUP, GROUP)
        m_ref[rows, :] = mixed_t_ref[:, rows].T


def forward_body(
    copies, where, spot_ref, lengths_ref, wmix_ref, wout_ref, wup_ref, wdown_ref,
    x_ref, values_ref, vec_ref, qscale_ref, qshift_ref,
    out_ref, query_ref, key_ref, shared_ref, qslope_ref, probs_ref, reset_ref, turned_ref, gated_t_ref,
    hslope_ref, uslope_ref, keep_ref, unit_ref, rstd_ref, normed_t_ref, hidden_t_ref, fslope_ref,
    m_ref, update_ref, gated_ref, blend_ref, normed_ref, ffn_ref,
):
    width, vwidth = wout_ref.shape[1], wout_ref.shape[0]
    zwidth = qscale_ref.shape[1]
    seqs = x_ref.shape[0] // GROUP

    def mix(at, size=CHUNK):
        cols = pl.ds(at, size)
        return nn(m_ref[...], wmix_ref[:, cols]) + piece(vec_ref, where["mix"], at, size)

    shared, qslope = silu_pair(mix(width, zwidth))
    shared_ref[...] = shared
    qslope_ref[...] = qslope
    query_ref[...] = (shared * qscale_ref[pl.ds(0, 1), :] + qshift_ref[pl.ds(0, 1), :]).astype(low)
    key_ref[...] = (shared * qscale_ref[pl.ds(1, 1), :] + qshift_ref[pl.ds(1, 1), :]).astype(low)
    causal = lax.broadcasted_iota(jnp.int32, (GROUP, GROUP), 0) >= lax.broadcasted_iota(
        jnp.int32, (GROUP, GROUP), 1
    )
    for n in range(seqs):
        rows = pl.ds(n * GROUP, GROUP)
        scores = jnp.where(causal, nt(query_ref[rows, :], key_ref[rows, :]) * zwidth**-0.5, -1e30)
        scores = jnp.exp(scores - jnp.max(scores, axis=-1, keepdims=True))
        probs_ref[rows, :] = scores / jnp.sum(scores, axis=-1, keepdims=True)

    def gate(at):
        update_ref[:, pl.ds(at, CHUNK)] = jax.nn.sigmoid(mix(at))

    each(width, gate)

    def attend(at):
        cols = pl.ds(at, CHUNK)
        reset, slope = silu_pair(mix(width + zwidth + at))
        attended = jnp.concatenate(
            [
                nn(probs_ref[pl.ds(n * GROUP, GROUP), :].astype(low), values_ref[pl.ds(n * GROUP, GROUP), cols])
                for n in range(seqs)
            ],
            axis=0,
        )
        reset_ref[:, cols] = reset.astype(low)
        turned_ref[:, cols] = (attended * slope).astype(low)
        gated = (reset * attended).astype(low)
        gated_ref[:, cols] = gated
        gated_t_ref[cols, :] = gated.T

    each(vwidth, attend)
    copies[0].wait()

    def hide(at):
        cols = pl.ds(at, CHUNK)
        pre = mix(width + zwidth + vwidth + at)
        pre = pre + nn(gated_ref[...], wout_ref[:, cols]) + piece(vec_ref, where["out"], at, CHUNK)
        hidden, slope = silu_pair(pre)
        update = update_ref[:, cols]
        keep = 1.0 - update
        resid = x_ref[:, cols].astype(f32)
        hslope_ref[:, cols] = (update * slope).astype(low)
        uslope_ref[:, cols] = ((hidden - resid) * update * keep).astype(low)
        keep_ref[:, cols] = keep.astype(low)
        blend_ref[:, cols] = update * hidden + keep * resid

    each(width, hide)
    copies[1].wait()
    for n in range(seqs):
        rows = pl.ds(n * GROUP, GROUP)
        blend = blend_ref[rows, :]
        centered = blend - jnp.mean(blend, axis=-1, keepdims=True)
        rstd = lax.rsqrt(jnp.mean(centered * centered, axis=-1, keepdims=True) + 1e-05)
        unit = centered * rstd
        unit_ref[rows, :] = unit.astype(low)
        rstd_ref[rows, :] = jnp.broadcast_to(rstd, (GROUP, LANES))
        normed = unit * piece(vec_ref, where["gain"], 0, width) + piece(vec_ref, where["shift"], 0, width)
        blend_ref[rows, :] = normed
        normed_ref[rows, :] = normed.astype(low)
        normed_t_ref[:, rows] = normed.astype(low).T

    def lift(at):
        cols = pl.ds(at, CHUNK)
        act, slope = silu_pair(nn(normed_ref[...], wup_ref[:, cols]) + piece(vec_ref, where["up"], at, CHUNK))
        fslope_ref[:, cols] = slope.astype(low)
        act = act.astype(low)
        ffn_ref[:, cols] = act
        hidden_t_ref[cols, :] = act.T

    each(wup_ref.shape[1], lift)
    copies[2].wait()

    def drop(at):
        cols = pl.ds(at, CHUNK)
        blend_ref[:, cols] = blend_ref[:, cols] + nn(ffn_ref[...], wdown_ref[:, cols]) + piece(vec_ref, where["down"], at, CHUNK)

    each(width, drop)
    for n in range(seqs):
        result = blend_ref[pl.ds(n * GROUP, GROUP), :].astype(low).T
        result = jnp.where(live_lanes(spot_ref, lengths_ref, n, result.shape), result, jnp.zeros_like(result))
        out_ref[:, n] = result.reshape(out_ref.shape[0], out_ref.shape[2], GROUP)


def forward_part(spot, lengths, folded, mixed, x, values, w_mix, w_out, w_up, w_down, vec, where, qk_scale, qk_shift, after=()):
    vwidth, width = w_out.shape
    zwidth = qk_scale.shape[1]
    ff = w_up.shape[1]
    count = x.shape[0]
    narrow, wide = (count, width), (count, vwidth)
    outs = [
        ((width, count), low), (folded, low), ((count, zwidth), low), ((count, zwidth), low), ((count, zwidth), f32),
        ((count, zwidth), f32), ((count, GROUP), f32), (wide, low), (wide, low), ((vwidth, count), low),
        (narrow, low), (narrow, low), (narrow, low), (narrow, low), ((count, LANES), f32),
        ((width, count), low), ((ff, count), low), ((count, ff), low),
    ]
    scratch = [pltpu.VMEM(narrow, low), pltpu.VMEM(narrow, f32), pltpu.VMEM(wide, low)]
    scratch += [pltpu.VMEM(narrow, f32), pltpu.VMEM(narrow, low), pltpu.VMEM((count, ff), low)]
    scratch += [pltpu.VMEM(w.shape, low) for w in (w_out, w_up, w_down)] + [pltpu.SemaphoreType.DMA((3,))]
    macs = w_mix.size + w_out.size + w_up.size + w_down.size
    return call(
        functools.partial(forward_kernel, len(mixed), where),
        outs,
        (spot, lengths, w_out, w_up, w_down, w_mix, x, values, vec, qk_scale, qk_shift, *mixed),
        smem=2,
        hbm=3,
        mib=MIB[1],
        after=after,
        scratch=scratch,
    )


def column_sum(part):
    return jnp.sum(part.astype(f32), axis=0, keepdims=True)


def put(ref, row, value, columns):
    if isinstance(ref, tuple):
        lone = value.shape[0] // len(ref)
        for k, one in enumerate(ref):
            put(one, row, value[k * lone : (k + 1) * lone], columns)
        return
    if len(ref.shape) == 2:
        ref[...] = value
        return
    owners = ref.shape[0]
    lone = value.shape[0] // owners
    for owner in range(owners):
        part = value[owner * lone : (owner + 1) * lone]
        for i, at in enumerate(range(0, value.shape[1], columns)):
            ref[owner, pl.ds(row + i * lone, lone), :] = part[:, at : at + columns]


def split_product(side, keep_ref, send_ref, left, right_ref, half, columns, row=0):
    total = right_ref.shape[1]
    for ref, which in ((keep_ref, side), (send_ref, 1 - side)):
        base = which * (total - half)
        parts = []
        for at in range(0, half, CHUNK):
            cols = pl.ds(pl.multiple_of(base + at, 128), min(CHUNK, half - at))
            parts.append(nn(left, right_ref[:, cols]).astype(low))
        put(ref, row, jnp.concatenate(parts, axis=1), columns)


def split_narrow(side, keep_ref, send_ref, left_ref, right_ref):
    both = [nn(left_ref[pl.ds(at, CHUNK), :], right_ref[...]).astype(low) for at in range(0, left_ref.shape[0], CHUNK)]
    both = jnp.concatenate(both, axis=0)
    half = both.shape[1] // 2
    near, far = both[:, :half], both[:, half:]
    put(keep_ref, 0, jnp.where(side == 0, near, far), half)
    put(send_ref, 0, jnp.where(side == 0, far, near), half)


def pair_outs(tall, wide, owners, lines=0):
    if not owners:
        return [((tall[0], tall[1] // 2), low)] * 2 + [((wide[0], wide[1] // 2), low)] * 2
    rows = (tall[0] * tall[1] + wide[0] * wide[1]) // (tall[1] * owners) + lines
    return [((owners, rows, tall[1] // 2), low)] * 2


def back_ffn_kernel(
    spot_ref, lengths_ref, wdown_ref, grad_ref, hidden_t_ref, fslope_ref, normed_t_ref, *refs
):
    halves, (g_ref, dffn_ref, small_ref) = refs[:-3], refs[-3:]
    width, ff = g_ref.shape[1], wdown_ref.shape[0]
    for n in range(grad_ref.shape[2]):
        part = wide_block(grad_ref, 1, n)
        part = jnp.where(live_lanes(spot_ref, lengths_ref, n, part.shape), part, jnp.zeros_like(part))
        g_ref[pl.ds(n * GROUP, GROUP), :] = part.T
    small_ref[:, pl.ds(0, width)] = column_sum(g_ref[...])
    side = spot_ref[2] & 1
    split_narrow(side, halves[0], halves[1], hidden_t_ref, g_ref)

    def lift(at):
        part = pl.ds(at, CHUNK)
        pulled = (nt(g_ref[...], wdown_ref[part, :]) * fslope_ref[:, part].astype(f32)).astype(low)
        dffn_ref[:, part] = pulled
        small_ref[:, pl.ds(width + at, CHUNK)] = column_sum(pulled)

    each(ff, lift)
    tall = hidden_t_ref.shape[0] // halves[0].shape[0]
    split_product(side, halves[-2], halves[-1], normed_t_ref[...], dffn_ref, ff // 2, halves[-2].shape[-1], tall)
    if len(halves) == 2:
        for ref in halves:
            owners, rows, columns = ref.shape
            ref[:, pl.ds(2 * tall, rows - 2 * tall), :] = jnp.zeros((owners, rows - 2 * tall, columns), low)


def back_ffn(spot, lengths, owners, lines, grad, hidden_t, fslope, normed_t, w_down, after=()):
    ff, width = w_down.shape
    count = fslope.shape[0]
    outs = pair_outs((ff, width), (width, ff), owners, lines)
    outs += [((count, width), low), ((count, ff), low), ((1, width + ff), f32)]
    *halves, g, dffn, small = call(
        back_ffn_kernel,
        outs,
        (spot, lengths, w_down, grad, hidden_t, fslope, normed_t),
        smem=2,
        mib=MIB[2],
        after=after,
    )
    return halves, g, dffn, small


def back_norm_kernel(
    base, wup_ref, g_ref, dffn_ref, unit_ref, rstd_ref, vec_ref, hslope_ref, uslope_ref, kept_ref,
    dh_ref, du_ref, direct_ref, small_ref, dn_ref,
):
    width = wup_ref.shape[0]

    def drop(at):
        part = pl.ds(at, CHUNK)
        pulled = g_ref[:, part].astype(f32) + nt(dffn_ref[...], wup_ref[part, :])
        dn_ref[:, part] = pulled
        small_ref[:, part] = column_sum(pulled * unit_ref[:, part].astype(f32))
        small_ref[:, pl.ds(width + at, CHUNK)] = column_sum(pulled)

    each(width, drop)
    for n in range(g_ref.shape[0] // GROUP):
        rows = pl.ds(n * GROUP, GROUP)
        unit = unit_ref[rows, :].astype(f32)
        pulled = dn_ref[rows, :] * piece(vec_ref, base, 0, width)
        inner = jnp.mean(pulled * unit, axis=-1, keepdims=True)
        blend = pulled - jnp.mean(pulled, axis=-1, keepdims=True) - unit * inner
        blend = blend * rstd_ref[rows, :][:, :1]
        dh_ref[rows, :] = (blend * hslope_ref[rows, :].astype(f32)).astype(low)
        du_ref[rows, :] = (blend * uslope_ref[rows, :].astype(f32)).astype(low)
        direct_ref[rows, :] = (blend * kept_ref[rows, :].astype(f32)).astype(low)


def back_norm(g, dffn, unit, rstd, vec, where, hslope, uslope, kept, w_up, after=()):
    width = w_up.shape[0]
    narrow = g.shape
    return call(
        functools.partial(back_norm_kernel, where["gain"]),
        [(narrow, low)] * 3 + [((1, 2 * width), f32)],
        (w_up, g, dffn, unit, rstd, vec, hslope, uslope, kept),
        mib=MIB[3],
        after=after,
        scratch=[pltpu.VMEM(narrow, f32)],
    )


def back_attend_kernel(
    wout_ref, wmix_ref, wvalue_ref,
    dh_ref, du_ref, direct_ref, reset_ref, turned_ref, values_ref, vslope_ref, probs_ref,
    query_ref, key_ref, shared_ref, qslope_ref, qscale_ref, small_ffn_ref, small_norm_ref, result_ref,
    dmix_ref, dvalue_ref, mixed_ref, joint_ref,
    table_ref,
    datt_ref,
):
    vwidth, width = wout_ref.shape
    zwidth = qscale_ref.shape[1]
    count = dh_ref.shape[0]
    seqs = count // GROUP
    dmix_ref[:, pl.ds(0, width)] = du_ref[...]
    dmix_ref[:, pl.ds(width + zwidth + vwidth, width)] = dh_ref[...]

    def gate(at):
        part = pl.ds(at, CHUNK)
        pulled = nt(dh_ref[...], wout_ref[part, :])
        dmix_ref[:, pl.ds(width + zwidth + at, CHUNK)] = (
            pulled * turned_ref[:, part].astype(f32)
        ).astype(low)
        datt_ref[:, part] = (pulled * reset_ref[:, part].astype(f32)).astype(low)

    each(vwidth, gate)
    scale = zwidth**-0.5
    q_scale, k_scale = qscale_ref[pl.ds(0, 1), :], qscale_ref[pl.ds(1, 1), :]
    zero = jnp.zeros((1, zwidth), f32)
    sums = [zero, zero, zero, zero]
    for n in range(seqs):
        rows = pl.ds(n * GROUP, GROUP)
        probs = probs_ref[rows, :]
        pulled = nt(datt_ref[rows, :], values_ref[rows, :])
        pulled = probs * (pulled - jnp.sum(pulled * probs, axis=-1, keepdims=True))
        pulled = pulled.astype(low)
        d_query = nn(pulled, key_ref[rows, :]) * scale
        d_key = nn(pulled.T, query_ref[rows, :]) * scale
        probs_t = probs.astype(low).T
        shared = shared_ref[rows, :]
        found = (d_query * shared, d_key * shared, d_query, d_key)
        sums = [a + jnp.sum(b, axis=0, keepdims=True) for a, b in zip(sums, found)]
        dmix_ref[rows, pl.ds(width, zwidth)] = (
            (d_query * q_scale + d_key * k_scale) * qslope_ref[rows, :]
        ).astype(low)
        dvalue_ref[rows, :] = (nn(probs_t, datt_ref[rows, :]) * vslope_ref[rows, :].astype(f32)).astype(low)

    def turn(result):
        devices, _, channels, _ = mixed_ref.shape
        return result.astype(low).T.reshape(devices, channels, GROUP)

    for n in range(0, seqs, 2):
        result = nt(dmix_ref[pl.ds(n * GROUP, 2 * GROUP), :], wmix_ref[...])
        mixed_ref[:, n] = turn(result[:GROUP])
        mixed_ref[:, n + 1] = turn(result[GROUP:])
    for n in range(0, seqs, 2):
        rows = pl.ds(n * GROUP, 2 * GROUP)
        result = direct_ref[rows, :].astype(f32) + nt(dvalue_ref[rows, :], wvalue_ref[...])
        joint_ref[:, 0, n] = turn(result[:GROUP])
        joint_ref[:, 0, n + 1] = turn(result[GROUP:])
    joint_ref[:, 1] = result_ref[...]
    ff = small_ffn_ref.shape[1] - width
    found = (
        column_sum(dmix_ref[...]), column_sum(dvalue_ref[...]), column_sum(dh_ref[...]),
        sums[0], sums[1], sums[2], sums[3], small_norm_ref[:, :width], small_norm_ref[:, width:],
        small_ffn_ref[:, width:], small_ffn_ref[:, :width],
    )
    lines = []
    for part in found:
        for at in range(0, part.shape[1], TABLE):
            line = part[:, at : at + TABLE]
            lack = TABLE - line.shape[1]
            lines.append(line if lack == 0 else jnp.concatenate([line, jnp.zeros((1, lack), f32)], axis=1))
    lines.append(jnp.zeros((table_ref.shape[0] - len(lines), TABLE), f32))
    table_ref[...] = jnp.concatenate(lines, axis=0).astype(low)


def back_attend(dh, du, direct, reset, turned, values, vslope, probs, query, key, shared, qslope, qk_scale, small_ffn, small_norm, result, w_out, w_mix, w_value, after=()):
    vwidth, width = w_out.shape
    mwidth = w_mix.shape[1]
    count = dh.shape[0]
    outs = [((count, mwidth), low), ((count, vwidth), low)]
    outs += [(result.shape, low), (result.shape[:1] + (2,) + result.shape[1:], low), ((64, TABLE), low)]
    scratch = [pltpu.VMEM((count, vwidth), low)]
    macs = w_out.size + w_mix.size + w_value.size
    return call(
        back_attend_kernel,
        outs,
        (w_out, w_mix, w_value, dh, du, direct, reset, turned, values, vslope, probs, query, key, shared, qslope, qk_scale, small_ffn, small_norm, result),
        mib=MIB[4],
        after=after,
        scratch=scratch,
    )


def back_mid_kernel(spot_ref, gated_t_ref, dh_ref, x_t_ref, dvalue_ref, table_ref, *halves):
    side = spot_ref[2] & 1
    if len(halves) == 4:
        (kept, sent, wide_kept, wide_sent), tall = halves, 0
    else:
        kept, sent = halves[0], halves[1:]
        wide_kept, wide_sent, tall = kept, sent, gated_t_ref.shape[0] // kept.shape[0]
    split_narrow(side, kept, sent, gated_t_ref, dh_ref)
    split_product(
        side, wide_kept, wide_sent, x_t_ref[...], dvalue_ref, dvalue_ref.shape[1] // 2, wide_kept.shape[-1], tall
    )
    if len(halves) == 4:
        return
    lines = kept.shape[1] - 2 * tall
    high = table_ref.shape[0] // (2 * lines)
    for refs, which in (((kept,), side), (sent, 1 - side)):
        for ref in refs:
            for owner in range(ref.shape[0]):
                at = pl.multiple_of((2 * (owner % high) + which) * lines, 16)
                ref[owner, pl.ds(2 * tall, lines), :] = table_ref[pl.ds(at, lines), :]


def halved(outs):
    (kept, kind), (sent, _) = outs
    return [(kept, kind)] + [((sent[0] // 2,) + sent[1:], kind)] * 2


def back_mid(spot, owners, gated_t, dh, x_t, dvalue, table, lines, after=()):
    count, width = dh.shape
    vwidth = dvalue.shape[1]
    outs = pair_outs((vwidth, width), (width, vwidth), owners, lines)
    found = call(
        back_mid_kernel,
        halved(outs) if owners else outs,
        (spot, gated_t, dh, x_t, dvalue, table),
        smem=1,
        mib=MIB[5],
        after=after,
    )
    if owners:
        return [found[0]], [list(found[1:])]
    return [found[0], found[2]], [[found[1]], [found[3]]]


def back_mix_kernel(spot_ref, mixed_t_ref, dmix_ref, keep_ref, *send_refs):
    half = keep_ref.shape[-1]
    split_product(spot_ref[2] & 1, keep_ref, send_refs, mixed_t_ref[...], dmix_ref, half, half)


def back_mix_weight(spot, owners, mixed_t, dmix, after=()):
    mwidth = dmix.shape[1]
    width, count = mixed_t.shape
    half = -(-mwidth // 256) * 128
    outs = [((width, half), low)] * 2
    kept, *sent = call(
        back_mix_kernel,
        halved(outs) if owners else outs,
        (spot, mixed_t, dmix),
        smem=1,
        mib=MIB[6],
        after=after,
    )
    return [kept], [sent]


def halve_kernel(index, bit, spot_ref, kept_ref, *refs):
    arrived, (sent_ref, stay_ref) = refs[:-2], refs[-2:]
    outer, inner, _, _ = sent_ref.shape
    lone = outer // len(arrived)
    mine = (spot_ref[index] >> bit) & 1
    for ref, which in ((sent_ref, 1 - mine), (stay_ref, mine)):
        for a in range(outer):
            for b in range(inner):
                total = kept_ref[a, which, b].astype(f32) + arrived[a // lone][a % lone, which, b].astype(f32)
                ref[a, b] = total.astype(low)


def halve(spot, kept, arrived, index, bit, at, after=()):
    dims = kept.shape[:-2]
    outer, inner = 1 << at, 1 << (len(dims) - at - 1)
    block = kept.shape[-2:]

    def shaped(part):
        return part.reshape((-1, 2, inner) + block)

    sent, stay = call(
        functools.partial(halve_kernel, index, bit),
        [((outer, inner) + block, low)] * 2,
        (spot, shaped(kept), *map(shaped, arrived)),
        smem=1,
        mib=MIB[7],
        after=after,

    )
    rest = dims[:at] + dims[at + 1 :] + block
    return sent.reshape(rest), stay.reshape(rest)


def finish_pair_kernel(lines, spot_ref, *refs):
    outs = 3 if lines else 2
    shares, (tall_ref, wide_ref) = refs[:-outs], refs[len(refs) - outs :][:2]
    columns = shares[0].shape[1]
    cut = tall_ref.shape[0] * 2 // len(shares)
    lone = wide_ref.shape[0] * 2 // len(shares)
    for k, ref in enumerate(shares):
        at = spot_ref[2] ^ k
        high, side = at >> 1, at & 1
        tall_ref[pl.ds(pl.multiple_of(high * cut, 8), cut), pl.ds(pl.multiple_of(side * columns, 128), columns)] = ref[
            pl.ds(0, cut), :
        ].astype(f32)
        runs = wide_ref.shape[1] // 2 // columns
        for run in range(runs):
            wide_ref[
                pl.ds(pl.multiple_of(high * lone, 8), lone),
                pl.ds(pl.multiple_of((side * runs + run) * columns, 128), columns),
            ] = ref[pl.ds(cut + run * lone, lone), :].astype(f32)
        if lines:
            refs[-1][pl.ds(pl.multiple_of(at * lines, 8), lines), :] = ref[pl.ds(ref.shape[0] - lines, lines), :].astype(f32)


def finish_pair(spot, shares, tall, wide, lines=0, after=()):
    outs = [(tall, f32), (wide, f32)]
    if lines:
        outs.append(((len(shares) * lines, shares[0].shape[1]), f32))
    return call(
        functools.partial(finish_pair_kernel, lines), outs, (spot, *shares), smem=1, mib=MIB[8], after=after
    )


def finish_mix_kernel(spot_ref, *refs):
    shares, out_ref = refs[:-1], refs[-1]
    half, mwidth = shares[0].shape[1], out_ref.shape[1]
    common = 2 * half - mwidth
    lone = out_ref.shape[0] * 2 // len(shares)
    for k, ref in enumerate(shares):
        at = spot_ref[2] ^ k
        rows = pl.ds(pl.multiple_of((at >> 1) * lone, 8), lone)
        base = pl.multiple_of(common + (at & 1) * (mwidth - half), 128)
        out_ref[rows, pl.ds(base, half - common)] = ref[:, common:].astype(f32)
        if common:

            @pl.when(at & 1 == 0)
            def _():
                out_ref[rows, pl.ds(0, common)] = ref[:, :common].astype(f32)


def finish_mix(spot, shares, shape, after=()):
    return call(finish_mix_kernel, [(shape, f32)], (spot, *shares), smem=1, mib=MIB[9], after=after)[0]


Y_FIRST = (("tok", 1), ("ch", 0))
Y_THEN_Z = (("tok", 1), ("ch", 1), ("ch", 0))
X_FIRST = (("ch", 0), ("tok", 1))


def bits_of(axis):
    return lax.axis_size(axis).bit_length() - 1


def across(part, axis, turn):
    return lax.ppermute(part, axis, [(i, i ^ turn) for i in range(lax.axis_size(axis))])


def exchange(part, axis, bit):
    return across(part, axis, 1 << bit)


def side_of(axis, bit):
    return (lax.axis_index(axis) >> bit) & 1


def by_owner(grad):
    dims = (2,) * (bits_of("ch") + bits_of("tok") - 1)
    return grad.reshape(dims + (-1, grad.shape[-1]))


def fold(part, columns):
    runs = [part[..., at : at + columns] for at in range(0, part.shape[-1], columns)]
    return jnp.concatenate(runs, axis=-2)


def add(left, right):
    return (left.astype(f32) + right.astype(f32)).astype(low)


def plain_halve(kept, arrived, mine, at):
    columns = min(part.shape[-1] for part in kept)

    def pick(which):
        def one(part):
            return lax.dynamic_index_in_dim(part, which, at, keepdims=False)

        return jnp.concatenate([fold(add(one(a), one(b)), columns) for a, b in zip(kept, arrived)], axis=-2)

    return pick(1 - mine), pick(mine)


class Sum:
    def __init__(self, spot, kept, sent, order):
        self.spot = spot
        self.names = [("ch", k) for k in reversed(range(bits_of("ch")))]
        self.names += [("tok", k) for k in reversed(range(1, bits_of("tok")))]
        self.stages = list(order) + [name for name in reversed(self.names) if name not in order]
        self.kept = [by_owner(part) for part in kept]
        arrived = [[exchange(piece, "tok", 0) for piece in part] for part in sent]
        self.arrived = arrived[0] if self.by_kernel() else [by_owner(part) for part, in arrived]

    def by_kernel(self):
        return len(self.kept) == 1 and self.kept[0].shape[-2] % 16 == 0

    def step(self, after=()):
        axis, bit = self.stages.pop(0)
        at = self.names.index((axis, bit))
        self.names.remove((axis, bit))
        if self.by_kernel():
            index = 1 if axis == "ch" else 2
            sent, stay = halve(self.spot, self.kept[0], self.arrived, index, bit, at, after)
        else:
            sent, stay = plain_halve(self.kept, self.arrived, side_of(axis, bit), at)
        self.kept, self.arrived = [stay], [exchange(sent, axis, bit)]
        return stay

    def shares(self):
        found = [add(self.kept[0], self.arrived[0])]
        for bit in reversed(range(1, bits_of("tok"))):
            found += [exchange(part, "tok", bit) for part in found]
        lower = [exchange(part, "tok", 0) for part in found]
        size = bits_of("tok") - 1
        order = [sum(((k >> (size - 1 - i)) & 1) << i for i in range(size)) for k in range(len(found))]
        found = [part for k in order for part in (found[k], lower[k])]
        return found


def in_order(shares, place):
    bit = 1
    while bit < len(shares):
        swapped = (place & bit) != 0
        shares = [jnp.where(swapped, shares[k ^ bit], shares[k]) for k in range(len(shares))]
        bit *= 2
    return jnp.stack(shares)


def plain_pair(place, shares, tall, wide):
    whole = in_order(shares, place).astype(f32)
    high = len(shares) // 2
    cut, lone = tall[0] // high, wide[0] // high
    whole = whole.reshape((high, 2) + whole.shape[1:])
    first = whole[:, :, :cut].transpose(0, 2, 1, 3).reshape(tall)
    second = whole[:, :, cut:].reshape(high, 2, -1, lone, whole.shape[-1])
    return first, second.transpose(0, 3, 1, 2, 4).reshape(wide)


def plain_mix(place, shares, shape):
    whole = in_order(shares, place).astype(f32)
    half = whole.shape[-1]
    whole = whole.reshape((len(shares) // 2, 2) + whole.shape[1:])
    whole = jnp.concatenate([whole[:, 0], whole[:, 1, :, 2 * half - shape[1] :]], axis=-1)
    return whole.reshape(shape)


def sum_tok(part):
    for bit in range(bits_of("tok")):
        part = part + exchange(part, "tok", bit)
    return part


def swap(parts):
    return lax.all_to_all(parts, "ch", split_axis=0, concat_axis=0, tiled=True)


def folded(parts):
    devices, channels, span = parts.shape[0], parts.shape[-2], parts.shape[-1]
    if channels % 16 == 0:
        return parts
    return jnp.moveaxis(parts, 0, -3).reshape((1,) + parts.shape[1:-2] + (devices * channels, span))


def unfolded(parts, devices):
    if parts.shape[0] == devices:
        return parts
    channels, span = parts.shape[-2] // devices, parts.shape[-1]
    return jnp.moveaxis(parts.reshape(parts.shape[1:-2] + (devices, channels, span)), -3, 0)


def local(
    inputs,
    out_grad,
    seq_lengths,
    ema_alpha,
    ema_delta,
    ema_beta,
    ema_eta,
    ema_omega,
    w_mix,
    b_mix,
    w_value,
    b_value,
    w_out,
    b_out,
    qk_scale,
    qk_shift,
    ln_gain,
    ln_bias,
    w_up,
    b_up,
    w_down,
    b_down,
):
    count, channels, local_len = inputs.shape
    width, mwidth = w_mix.shape
    vwidth, ff = w_value.shape[1], w_up.shape[1]
    devices, tok_size = lax.axis_size("ch"), lax.axis_size("tok")
    columns = count * channels
    span = local_len // devices
    tok_index = lax.axis_index("tok").astype(jnp.int32)
    ch_index = lax.axis_index("ch").astype(jnp.int32)
    spot = jnp.stack([tok_index * local_len + ch_index * span, ch_index, tok_index])
    apart = devices <= 8 and channels % 16 == 0

    def by_column(parts):
        whole = unfolded(parts, devices)
        return pad_to_lanes(whole.reshape(whole.shape[:-3] + (columns, span)), whole.ndim - 3)

    where = vectors(width, mwidth, vwidth, ff)
    vec = jnp.concatenate([b_mix, b_value, b_out, ln_gain, ln_bias, b_up, b_down])[None]
    params = ema_params(ema_alpha, ema_delta, ema_beta, ema_eta, count)
    omega = pad_to_lanes(jnp.tile(ema_omega, count)[None], 1)

    flat = inputs.reshape(columns, local_len)
    raw = by_blocks(spot, flat, out_grad.reshape(columns, local_len))
    raw = folded(swap(raw.reshape(devices, 2, count, channels, span)))
    xs, ends, total = ema_ends(pad_to_lanes(flat, 0), params)
    totals = lax.all_gather(total, "tok")
    mixed, slope, entry = ema_mix(spot, xs, ends, params, omega, totals, apart)
    if apart:
        mixed = [part.reshape(count, channels, span) for part in mixed]
        mixed = [part if k == 0 else across(part, "ch", k) for k, part in enumerate(mixed)]
    else:
        mixed = folded(swap(mixed[0][:, :columns].reshape(devices, count, channels, span)))
        mixed = [mixed[0]] if mixed.shape[0] == 1 else [mixed.transpose(1, 0, 2, 3).reshape(count, width, span)]
    x, values, vslope, x_t = value_part(raw, w_value, vec, where, (entry,))
    (
        mixed_t, result, query, key, shared, qslope, probs, reset, turned, gated_t,
        hslope, uslope, keep, unit, rstd, normed_t, hidden_t, fslope,
    ) = forward_part(
        spot, seq_lengths, raw.shape[:1] + raw.shape[2:], mixed, x, values, w_mix, w_out, w_up, w_down, vec,
        where, qk_scale, qk_shift,
    )
    owners = devices * tok_size // 2
    joined = owners if width // owners % 16 == 0 else 0
    lines = 64 // tok_size
    halves, g, dffn, small_ffn = back_ffn(
        spot, seq_lengths, joined, lines, raw, hidden_t, fslope, normed_t, w_down
    )
    ffn = Sum(spot, halves[::2], [[part] for part in halves[1::2]], Y_THEN_Z)
    dh, du, direct, small_norm = back_norm(g, dffn, unit, rstd, vec, where, hslope, uslope, keep, w_up)
    last = ffn.step((small_norm,))
    dmix, dvalue, back_mix, joint, table = back_attend(
        dh, du, direct, reset, turned, values, vslope, probs, query, key, shared, qslope,
        qk_scale, small_ffn, small_norm, result, w_out, w_mix, w_value, (last,),
    )
    kept, sent = back_mix_weight(spot, joined, mixed_t, dmix, (table,))
    mix = Sum(spot, kept, sent, X_FIRST)
    kept, sent = back_mid(spot, joined, gated_t, dh, x_t, dvalue, table, lines, (kept[0],))
    last = kept[0]
    back_mix = swap(unfolded(back_mix, devices))
    if not joined:
        table = table.reshape(tok_size // 2, 2, lines, TABLE)
        for group, which in ((kept, side_of("tok", 0)), (sent, 1 - side_of("tok", 0))):
            part = lax.dynamic_index_in_dim(table, which, 1, keepdims=False)
            part = jnp.broadcast_to(part[None], (devices,) + part.shape).reshape(-1, TABLE)
            group.append(part if group is kept else [part])
    mid = Sum(spot, kept, sent, Y_FIRST)
    last = ffn.step((last,))
    last = mix.step((last,))
    last = mid.step((last,))
    joint, back_mix, _ = lax.optimization_barrier((unfolded(joint, devices), back_mix, last))
    joint = swap(joint)
    pull, heads, total = ema_back(by_column(back_mix), slope, params, (last,))
    totals = lax.all_gather(total, "tok")
    last = mix.step((totals,))
    last = mid.step((last,))
    last = ffn.step((last,))
    sums = ema_sums(spot, xs, pull, entry, heads, totals, params, (last,))
    last = sums
    while mix.stages:
        for group in (mix, mid, ffn):
            last = group.step((last,)) if group.stages else last
    input_grad, output = ema_finish(spot, pull, heads, params, omega, totals, by_column(joint), (last,))
    input_grad = input_grad[:columns].reshape(inputs.shape)
    output = output[:columns].reshape(inputs.shape)
    ema_grads = ema_param_grads(sum_tok(sums), ema_alpha, ema_delta, ema_beta, ema_eta, count)

    tall, wide = (vwidth // devices, width), (width // devices, vwidth)
    shares = mid.shares()
    across_mix = (width // devices, mwidth)
    if joined:
        g_out, g_value, table = finish_pair(spot, shares, tall, wide, lines)
        g_down, g_up = finish_pair(spot, ffn.shares(), tall, wide)
        g_mix = finish_mix(spot, mix.shares(), across_mix)
    else:
        table = in_order([part[-lines:] for part in shares], tok_index).astype(f32)
        shares = [part[:-lines] for part in shares]
        g_out, g_value = plain_pair(tok_index, shares, tall, wide)
        g_down, g_up = plain_pair(tok_index, ffn.shares(), tall, wide)
        g_mix = plain_mix(tok_index, mix.shares(), across_mix)
    table = table.reshape(-1)
    found, at = [], 0
    half = qk_scale.shape[1]
    for size in (mwidth, vwidth, width, half, half, half, half, width, width, ff, width):
        found.append(table[at : at + size])
        at += -(-size // TABLE) * TABLE
    g_bmix, g_bvalue, g_bout, scale_q, scale_k, shift_q, shift_k, g_gain, g_lnbias, g_bup, g_bdown = found
    g_qscale, g_qshift = jnp.stack([scale_q, scale_k]), jnp.stack([shift_q, shift_k])
    return (
        output,
        input_grad,
        *ema_grads,
        g_mix,
        g_bmix,
        g_value,
        g_bvalue,
        g_out,
        g_bout,
        g_qscale,
        g_qshift,
        g_gain,
        g_lnbias,
        g_up,
        g_bup,
        g_down,
        g_bdown,
    )


def solution(mesh):
    by_ch = P("ch", None)
    placed = P(None, "ch", "tok")
    return jax.shard_map(
        local,
        mesh=mesh,
        in_specs=(placed, placed, P()) + (by_ch,) * 4 + (P("ch"),) + (P(),) * 14,
        out_specs=(
            (placed, placed)
            + (by_ch,) * 4
            + (P("ch"), by_ch, P(), by_ch, P(), by_ch)
            + (P(),) * 5
            + (by_ch, P(), by_ch, P())
        ),
        check_vma=False,
    )
```

```python
import functools
import jax
import jax.numpy as jnp
from jax import lax
from jax.experimental import pallas as pl
from jax.experimental.pallas import tpu as pltpu
from jax.sharding import PartitionSpec as P

GROUP = 128
SUB = 8
LANES = 128
f32 = jnp.float32


def by_tile(shape, dim):
    block = tuple(LANES if k == dim else size for k, size in enumerate(shape))
    return pl.BlockSpec(block, lambda i: tuple(i if k == dim else 0 for k in range(len(shape))))


def in_smem():
    return pl.BlockSpec(memory_space=pltpu.SMEM)


def roomy(mib=5):
    return pltpu.CompilerParams(vmem_limit_bytes=mib * 1024 * 1024)


def work(flops, moved, exps=0):
    return pl.CostEstimate(flops=1, bytes_accessed=1, transcendentals=0)


def launch(kernel, outs, ins, in_specs, out_specs, after=(), grid=(), scratch=(), mib=5, cost=None):
    count = len(ins)

    def run(*refs):
        kernel(*refs[:count], *refs[count + len(after) :])

    return pl.pallas_call(
        run,
        grid=grid,
        out_shape=tuple(jax.ShapeDtypeStruct(shape, kind) for shape, kind in outs),
        in_specs=list(in_specs) + [pl.BlockSpec(memory_space=pl.ANY)] * len(after),
        out_specs=tuple(out_specs),
        scratch_shapes=list(scratch),
        compiler_params=roomy(mib),
        cost_estimate=cost,
    )(*ins, *after)


def rates(params_ref):
    rate = jax.nn.sigmoid(params_ref[0])
    drop = rate * jax.nn.sigmoid(params_ref[1])
    weight = params_ref[3] * rate * params_ref[2]
    return 1.0 - drop, jnp.log1p(-drop), weight


def spread(ref, j):
    return jnp.broadcast_to(ref[pl.ds(j, 1), :], (SUB, LANES))


def tree_sum(parts):
    while len(parts) > 1:
        parts = [a + b for a, b in zip(parts[::2], parts[1::2])] + parts[len(parts) & ~1 :]
    return parts[0]


def block_rows(g, t):
    return pl.ds(g * GROUP + t, SUB, stride=GROUP)


def state_rows(g, j, expand):
    return pl.ds(g * expand + j, SUB, stride=expand)


def blocks_kernel(spot_ref, first_ref, second_ref, out_ref, sems):
    copies = []
    for b in range(out_ref.shape[0]):
        cols = pl.ds(b * GROUP, GROUP)
        for which, ref in enumerate((first_ref, second_ref)):
            copies.append(pltpu.make_async_copy(ref.at[:, cols], out_ref.at[b, which], sems.at[2 * b + which]))
    for copy in copies:
        copy.start()
    for copy in copies:
        copy.wait()


def by_blocks(spot, first, second):
    columns, length = first.shape
    blocks = length // GROUP
    anywhere = pl.BlockSpec(memory_space=pl.ANY)
    return launch(
        blocks_kernel,
        [((blocks, 2, columns, GROUP), first.dtype)],
        (spot, first, second),
        [in_smem(), anywhere, anywhere],
        [anywhere],
        scratch=[pltpu.SemaphoreType.DMA((2 * blocks,))],
        mib=1,
    )[0]


def ema_ends_kernel(x_ref, params_ref, xs_ref, ends_ref, total_ref, decay_ref):
    length = x_ref.shape[1]
    expand = params_ref.shape[1]
    blocks = length // GROUP
    decay, log_decay, _ = rates(params_ref)
    decay_ref[...] = decay
    for b in range(blocks):
        rows = pl.ds(b * GROUP, GROUP)
        xs_ref[rows, :] = x_ref[:, rows].astype(f32).T
    factors = [spread(decay_ref, j) for j in range(expand)]
    for g in range(0, blocks, SUB):

        def step(t, states):
            now = xs_ref[block_rows(g, t), :]
            return tuple(f * s + now for f, s in zip(factors, states))

        states = (jnp.zeros((SUB, LANES), f32),) * expand
        states = lax.fori_loop(0, GROUP, step, states, unroll=8)
        for j in range(expand):
            ends_ref[state_rows(g, j, expand), :] = states[j]
    jump = jnp.exp(GROUP * log_decay)
    carry = jnp.zeros_like(jump)
    for b in range(blocks):
        carry = jump * carry + ends_ref[pl.ds(b * expand, expand), :]
    total_ref[...] = carry


def ema_ends(x, params, after=()):
    columns, length = x.shape
    expand = params.shape[1]
    shapes = ((length, columns), (length // GROUP * expand, columns), (expand, columns))
    return launch(
        ema_ends_kernel,
        [(shape, f32) for shape in shapes],
        (x, params),
        [by_tile(x.shape, 0), by_tile(params.shape, 2)],
        [by_tile(shape, 1) for shape in shapes],
        after=after,
        grid=(columns // LANES,),
        scratch=[pltpu.VMEM((expand, LANES), f32)],
        mib=5 * max(1, length // 1024),
        cost=work(2 * expand * length * columns, 6 * length * columns),
    )


def ema_mix_kernel(
    spot_ref, xs_ref, ends_ref, params_ref, omega_ref, totals_ref, *refs
):
    mixed_refs, (slope_ref, entry_ref, decay_ref, weight_ref, smooth_ref) = refs[:-5], refs[-5:]
    length = xs_ref.shape[0]
    expand = params_ref.shape[1]
    blocks = length // GROUP
    decay, log_decay, weight = rates(params_ref)
    decay_ref[...] = decay
    weight_ref[...] = weight
    whole = jnp.exp(length * log_decay)
    jump = jnp.exp(GROUP * log_decay)
    carry = jnp.zeros_like(jump)
    for k in range(totals_ref.shape[0]):
        carry = jnp.where(k < spot_ref[2], whole * carry + totals_ref[k], carry)
    for b in range(blocks):
        rows = pl.ds(b * expand, expand)
        entry_ref[rows, :] = carry
        carry = jump * carry + ends_ref[rows, :]
    factors = [spread(decay_ref, j) for j in range(expand)]
    weights = [spread(weight_ref, j) for j in range(expand)]
    for g in range(0, blocks, SUB):

        def step(t, states):
            now = xs_ref[block_rows(g, t), :]
            states = tuple(f * s + now for f, s in zip(factors, states))
            smooth_ref[block_rows(g, t), :] = tree_sum([w * s for w, s in zip(weights, states)])
            return states

        start = tuple(entry_ref[state_rows(g, j, expand), :] for j in range(expand))
        lax.fori_loop(0, GROUP, step, start, unroll=8)
    for k in range(blocks):
        rows = pl.ds(pl.multiple_of((spot_ref[1] ^ k) * GROUP, GROUP), GROUP)
        pre = smooth_ref[rows, :] + omega_ref[...] * xs_ref[rows, :]
        sigma = jax.nn.sigmoid(pre)
        block = (pre * sigma).T.astype(jnp.bfloat16)
        if len(mixed_refs) == 1:
            mixed_refs[0][spot_ref[1] ^ k] = block
        else:
            mixed_refs[k][...] = block
        slope_ref[rows, :] = (sigma * (1.0 + pre * (1.0 - sigma))).astype(slope_ref.dtype)


def ema_mix(spot, xs, ends, params, omega, totals, apart, after=()):
    length, columns = xs.shape
    expand = params.shape[1]
    blocks = length // GROUP
    mixed = [(columns, GROUP)] * blocks if apart else [(blocks, columns, GROUP)]
    *found, slope, entry = launch(
        ema_mix_kernel,
        [(shape, jnp.bfloat16) for shape in mixed] + [(xs.shape, jnp.bfloat16), (ends.shape, f32)],
        (spot, xs, ends, params, omega, totals),
        [
            in_smem(), by_tile(xs.shape, 1), by_tile(ends.shape, 1), by_tile(params.shape, 2),
            by_tile(omega.shape, 1), by_tile(totals.shape, 2),
        ],
        [by_tile(shape, len(shape) - 2) for shape in mixed] + [by_tile(xs.shape, 1), by_tile(ends.shape, 1)],
        after=after,
        grid=(columns // LANES,),
        scratch=[
            pltpu.VMEM((expand, LANES), f32),
            pltpu.VMEM((expand, LANES), f32),
            pltpu.VMEM((length, LANES), f32),
        ],
        mib=5 * max(1, length // 1024),
        cost=work(4 * expand * length * columns, 10 * length * columns, length * columns),
    )
    return found, slope, entry


def ema_back_kernel(dmix_ref, slope_ref, params_ref, pull_ref, heads_ref, total_ref, decay_ref):
    length = slope_ref.shape[0]
    expand = params_ref.shape[1]
    blocks = length // GROUP
    decay, log_decay, _ = rates(params_ref)
    decay_ref[...] = decay
    for b in range(blocks):
        rows = pl.ds(b * GROUP, GROUP)
        pull_ref[rows, :] = dmix_ref[b].astype(f32).T * slope_ref[rows, :].astype(f32)
    factors = [spread(decay_ref, j) for j in range(expand)]
    for g in range(0, blocks, SUB):

        def step(t, states):
            now = pull_ref[block_rows(g, GROUP - 1 - t), :]
            return tuple(f * s + now for f, s in zip(factors, states))

        states = (jnp.zeros((SUB, LANES), f32),) * expand
        states = lax.fori_loop(0, GROUP, step, states, unroll=8)
        for j in range(expand):
            heads_ref[state_rows(g, j, expand), :] = states[j]
    jump = jnp.exp(GROUP * log_decay)
    carry = jnp.zeros_like(jump)
    for b in reversed(range(blocks)):
        carry = jump * carry + heads_ref[pl.ds(b * expand, expand), :]
    total_ref[...] = carry


def ema_back(dmix, slope, params, after=()):
    length, columns = slope.shape
    expand = params.shape[1]
    shapes = ((length, columns), (length // GROUP * expand, columns), (expand, columns))
    return launch(
        ema_back_kernel,
        [(shape, f32) for shape in shapes],
        (dmix, slope, params),
        [by_tile(dmix.shape, 1), by_tile(slope.shape, 1), by_tile(params.shape, 2)],
        [by_tile(shape, 1) for shape in shapes],
        after=after,
        grid=(columns // LANES,),
        scratch=[pltpu.VMEM((expand, LANES), f32)],
        mib=5 * max(1, length // 1024),
        cost=work(2 * expand * length * columns, 8 * length * columns),
    )


def enter_from_later(spot_ref, heads_ref, totals_ref, enter_ref, log_decay, length):
    expand = log_decay.shape[0]
    whole = jnp.exp(length * log_decay)
    jump = jnp.exp(GROUP * log_decay)
    carry = jnp.zeros_like(jump)
    for k in reversed(range(totals_ref.shape[0])):
        carry = jnp.where(k > spot_ref[2], whole * carry + totals_ref[k], carry)
    for b in reversed(range(length // GROUP)):
        rows = pl.ds(b * expand, expand)
        enter_ref[rows, :] = carry
        carry = jump * carry + heads_ref[rows, :]


def ema_finish_kernel(
    spot_ref, pull_ref, heads_ref, params_ref, omega_ref, totals_ref, direct_ref, result_ref,
    grad_ref, output_ref, decay_ref, weight_ref, enter_ref, smooth_ref,
):
    length = pull_ref.shape[0]
    expand = params_ref.shape[1]
    blocks = length // GROUP
    decay, log_decay, weight = rates(params_ref)
    decay_ref[...] = decay
    weight_ref[...] = weight
    enter_from_later(spot_ref, heads_ref, totals_ref, enter_ref, log_decay, length)
    factors = [spread(decay_ref, j) for j in range(expand)]
    weights = [spread(weight_ref, j) for j in range(expand)]
    for g in range(0, blocks, SUB):

        def step(t, states):
            now = pull_ref[block_rows(g, GROUP - 1 - t), :]
            states = tuple(f * s + now for f, s in zip(factors, states))
            back = tree_sum([w * s for w, s in zip(weights, states)])
            smooth_ref[block_rows(g, GROUP - 1 - t), :] = back
            return states

        start = tuple(enter_ref[state_rows(g, j, expand), :] for j in range(expand))
        lax.fori_loop(0, GROUP, step, start, unroll=8)
    for b in range(blocks):
        rows = pl.ds(b * GROUP, GROUP)
        back = smooth_ref[rows, :] + omega_ref[...] * pull_ref[rows, :]
        grad_ref[:, rows] = back.T + direct_ref[b, 0].astype(f32)
        output_ref[:, rows] = result_ref[b, 0]


def ema_finish(spot, pull, heads, params, omega, totals, joint, after=()):
    length, columns = pull.shape

    def part(which):
        return pl.BlockSpec((length // GROUP, 1, LANES, GROUP), lambda i: (0, which, i, 0))

    expand = params.shape[1]
    return launch(
        ema_finish_kernel,
        [((columns, length), f32), ((columns, length), joint.dtype)],
        (spot, pull, heads, params, omega, totals, joint, joint),
        [
            in_smem(), by_tile(pull.shape, 1), by_tile(heads.shape, 1), by_tile(params.shape, 2),
            by_tile(omega.shape, 1), by_tile(totals.shape, 2), part(0), part(1),
        ],
        [by_tile((columns, length), 0)] * 2,
        after=after,
        grid=(columns // LANES,),
        scratch=[
            pltpu.VMEM((expand, LANES), f32),
            pltpu.VMEM((expand, LANES), f32),
            pltpu.VMEM((heads.shape[0], LANES), f32),
            pltpu.VMEM((length, LANES), f32),
        ],
        mib=5 * max(1, length // 1024),
        cost=work(4 * expand * length * columns, 14 * length * columns),
    )


def ema_sums_kernel(spot_ref, xs_ref, pull_ref, entry_ref, heads_ref, totals_ref, params_ref, sums_ref, decay_ref, enter_ref):
    length = xs_ref.shape[0]
    expand = params_ref.shape[1]
    blocks = length // GROUP
    half = expand // 2
    decay, log_decay, _ = rates(params_ref)
    decay_ref[...] = decay
    enter_from_later(spot_ref, heads_ref, totals_ref, enter_ref, log_decay, length)
    for low in range(0, expand, half):
        factors = [spread(decay_ref, low + j) for j in range(half)]
        zero = (jnp.zeros((SUB, LANES), f32),) * half
        plain, turned = zero, zero
        for g in range(0, blocks, SUB):

            def step(t, held):
                states, slants, plain, turned = held
                now, pull = xs_ref[block_rows(g, t), :], pull_ref[block_rows(g, t), :]
                slants = tuple(f * p + s for f, p, s in zip(factors, slants, states))
                states = tuple(f * s + now for f, s in zip(factors, states))
                plain = tuple(a + pull * s for a, s in zip(plain, states))
                turned = tuple(a + pull * p for a, p in zip(turned, slants))
                return states, slants, plain, turned

            start = tuple(entry_ref[state_rows(g, low + j, expand), :] for j in range(half))
            held = (start, zero, plain, turned)
            _, slants, plain, turned = lax.fori_loop(0, GROUP, step, held, unroll=4)
            turned = tuple(
                a + f * p * enter_ref[state_rows(g, low + j, expand), :]
                for j, (a, f, p) in enumerate(zip(turned, factors, slants))
            )
        for j in range(half):
            sums_ref[pl.ds(low + j, 1), :] = jnp.sum(plain[j], axis=0, keepdims=True)
            sums_ref[pl.ds(expand + low + j, 1), :] = jnp.sum(turned[j], axis=0, keepdims=True)
    straight = jnp.zeros((SUB, LANES), f32)
    for b in range(0, length, SUB):
        straight = straight + xs_ref[pl.ds(b, SUB), :] * pull_ref[pl.ds(b, SUB), :]
    sums_ref[pl.ds(2 * expand, SUB), :] = straight


def ema_sums(spot, xs, pull, entry, heads, totals, params, after=()):
    length, columns = xs.shape
    expand = params.shape[1]
    shape = (2 * expand + SUB, columns)
    return launch(
        ema_sums_kernel,
        [(shape, f32)],
        (spot, xs, pull, entry, heads, totals, params),
        [
            in_smem(), by_tile(xs.shape, 1), by_tile(xs.shape, 1), by_tile(entry.shape, 1), by_tile(entry.shape, 1),
            by_tile(totals.shape, 2), by_tile(params.shape, 2),
        ],
        [by_tile(shape, 1)],
        after=after,
        grid=(columns // LANES,),
        scratch=[pltpu.VMEM((expand, LANES), f32), pltpu.VMEM((entry.shape[0], LANES), f32)],
        mib=5 * max(1, length // 1024),
        cost=work(8 * expand * length * columns, 8 * length * columns),
    )[0]


def pad_to_lanes(part, dim):
    extra = -part.shape[dim] % LANES
    if extra == 0:
        return part
    return jnp.pad(part, [(0, extra if k == dim else 0) for k in range(part.ndim)])


def ema_params(alpha, delta, beta, eta, count):
    packed = jnp.swapaxes(jnp.stack([alpha, delta, beta, eta]), 1, 2)
    return pad_to_lanes(jnp.tile(packed, (1, 1, count)), 2)


def ema_param_grads(total, alpha, delta, beta, eta, count):
    channels, expand = alpha.shape
    summed = jnp.sum(total[:, : count * channels].reshape(-1, count, channels), axis=1)
    plain, turned = summed[:expand].T, summed[expand : 2 * expand].T
    omega = jnp.sum(summed[2 * expand :], axis=0)
    rate, damp = jax.nn.sigmoid(alpha), jax.nn.sigmoid(delta)
    g_alpha = eta * beta * rate * (1.0 - rate) * (plain - damp * rate * turned)
    g_delta = -(eta * beta * rate * rate * damp * (1.0 - damp)) * turned
    return g_alpha, g_delta, rate * eta * plain, rate * beta * plain, omega


low = jnp.bfloat16
CHUNK = 256
MIB = (3, 11, 8, 5, 6, 8, 8, 6, 4, 4)
TABLE = 384


def nn(left, right):
    return jnp.dot(left, right, preferred_element_type=f32)


def nt(left, right):
    return lax.dot_general(left, right, (((1,), (1,)), ((), ())), preferred_element_type=f32)


def silu_pair(pre):
    sigma = jax.nn.sigmoid(pre)
    return pre * sigma, sigma * (1.0 + pre * (1.0 - sigma))


def each(width, body, size=CHUNK):
    for at in range(0, width, size):
        body(at)


def wide_block(ref, which, n):
    part = ref[:, which, n]
    return part.reshape(part.shape[0] * part.shape[1], part.shape[2])


def live_lanes(spot_ref, lengths_ref, n, shape):
    return spot_ref[0] + lax.broadcasted_iota(jnp.int32, shape, 1) < lengths_ref[n]


def span_of(ref, n):
    return pl.ds(n * GROUP, GROUP)


def call(kernel, outs, ins, smem=0, hbm=0, scratch=(), moved=1, mib=16, after=()):
    spaces = [pltpu.SMEM] * smem + [pl.ANY] * hbm + [pltpu.VMEM] * (len(ins) - smem - hbm)
    return launch(
        kernel,
        outs,
        ins,
        [pl.BlockSpec(memory_space=space) for space in spaces],
        [pl.BlockSpec(memory_space=pltpu.VMEM) for _ in outs],
        after=after,
        scratch=scratch,
        mib=mib,
        cost=pl.CostEstimate(flops=1, bytes_accessed=moved, transcendentals=0),
    )


def vectors(width, mwidth, vwidth, ff):
    sizes = (
        ("mix", mwidth), ("value", vwidth), ("out", width), ("gain", width),
        ("shift", width), ("up", ff), ("down", width),
    )
    place, at = {}, 0
    for name, size in sizes:
        place[name] = at
        at += size
    return place


def piece(ref, base, at, size):
    return ref[:, pl.ds(base + at, size)]


def value_kernel(base, w_ref, x_ref, vec_ref, rows_ref, values_ref, slope_ref, rows_t_ref):
    for n in range(x_ref.shape[2]):
        rows = pl.ds(n * GROUP, GROUP)
        block = wide_block(x_ref, 0, n)
        rows_t_ref[:, rows] = block
        rows_ref[rows, :] = block.T

    def chunk(at):
        cols = pl.ds(at, CHUNK)
        act, slope = silu_pair(nn(rows_ref[...], w_ref[:, cols]) + piece(vec_ref, base, at, CHUNK))
        values_ref[:, cols] = act.astype(low)
        slope_ref[:, cols] = slope.astype(low)

    each(w_ref.shape[1], chunk)


def value_part(x, w_value, vec, where, after=()):
    width, vwidth = w_value.shape
    count = x.shape[2] * GROUP
    return call(
        functools.partial(value_kernel, where["value"]),
        [((count, width), low), ((count, vwidth), low), ((count, vwidth), low), ((width, count), low)],
        (w_value, x, vec),
        mib=MIB[0],
        after=after,
    )


def forward_kernel(
    pieces, where, spot_ref, lengths_ref, wmix_ref, wout_ref, wup_ref, wdown_ref,
    x_ref, values_ref, vec_ref, qscale_ref, qshift_ref, *refs
):
    forward_rows(spot_ref, refs[:pieces], refs[pieces], refs[-6])
    forward_body(
        where, spot_ref, lengths_ref, wmix_ref, wout_ref, wup_ref, wdown_ref,
        x_ref, values_ref, vec_ref, qscale_ref, qshift_ref, *refs[pieces + 1 :]
    )


def forward_rows(spot_ref, mixed_refs, mixed_t_ref, m_ref):
    for k, ref in enumerate(mixed_refs):
        seqs, channels, _ = ref.shape
        at = pl.multiple_of((spot_ref[1] ^ k) * channels, 16) if len(mixed_refs) > 1 else 0
        for n in range(seqs):
            mixed_t_ref[pl.ds(at, channels), pl.ds(n * GROUP, GROUP)] = ref[n]
    for n in range(m_ref.shape[0] // GROUP):
        rows = pl.ds(n * GROUP, GROUP)
        m_ref[rows, :] = mixed_t_ref[:, rows].T


def forward_body(
    where, spot_ref, lengths_ref, wmix_ref, wout_ref, wup_ref, wdown_ref,
    x_ref, values_ref, vec_ref, qscale_ref, qshift_ref,
    out_ref, query_ref, key_ref, shared_ref, qslope_ref, probs_ref, reset_ref, turned_ref, gated_t_ref,
    hslope_ref, uslope_ref, keep_ref, unit_ref, rstd_ref, normed_t_ref, hidden_t_ref, fslope_ref,
    m_ref, update_ref, gated_ref, blend_ref, normed_ref, ffn_ref,
):
    width, vwidth = wout_ref.shape[1], wout_ref.shape[0]
    zwidth = qscale_ref.shape[1]
    seqs = x_ref.shape[0] // GROUP

    def mix(at, size=CHUNK):
        cols = pl.ds(at, size)
        return nn(m_ref[...], wmix_ref[:, cols]) + piece(vec_ref, where["mix"], at, size)

    shared, qslope = silu_pair(mix(width, zwidth))
    shared_ref[...] = shared
    qslope_ref[...] = qslope
    query_ref[...] = (shared * qscale_ref[pl.ds(0, 1), :] + qshift_ref[pl.ds(0, 1), :]).astype(low)
    key_ref[...] = (shared * qscale_ref[pl.ds(1, 1), :] + qshift_ref[pl.ds(1, 1), :]).astype(low)
    causal = lax.broadcasted_iota(jnp.int32, (GROUP, GROUP), 0) >= lax.broadcasted_iota(
        jnp.int32, (GROUP, GROUP), 1
    )
    for n in range(seqs):
        rows = pl.ds(n * GROUP, GROUP)
        scores = jnp.where(causal, nt(query_ref[rows, :], key_ref[rows, :]) * zwidth**-0.5, -1e30)
        scores = jnp.exp(scores - jnp.max(scores, axis=-1, keepdims=True))
        probs_ref[rows, :] = scores / jnp.sum(scores, axis=-1, keepdims=True)

    def gate(at):
        update_ref[:, pl.ds(at, CHUNK)] = jax.nn.sigmoid(mix(at))

    each(width, gate)

    def attend(at):
        cols = pl.ds(at, CHUNK)
        reset, slope = silu_pair(mix(width + zwidth + at))
        attended = jnp.concatenate(
            [
                nn(probs_ref[pl.ds(n * GROUP, GROUP), :].astype(low), values_ref[pl.ds(n * GROUP, GROUP), cols])
                for n in range(seqs)
            ],
            axis=0,
        )
        reset_ref[:, cols] = reset.astype(low)
        turned_ref[:, cols] = (attended * slope).astype(low)
        gated = (reset * attended).astype(low)
        gated_ref[:, cols] = gated
        gated_t_ref[cols, :] = gated.T

    each(vwidth, attend)

    def hide(at):
        cols = pl.ds(at, CHUNK)
        pre = mix(width + zwidth + vwidth + at)
        pre = pre + nn(gated_ref[...], wout_ref[:, cols]) + piece(vec_ref, where["out"], at, CHUNK)
        hidden, slope = silu_pair(pre)
        update = update_ref[:, cols]
        keep = 1.0 - update
        resid = x_ref[:, cols].astype(f32)
        hslope_ref[:, cols] = (update * slope).astype(low)
        uslope_ref[:, cols] = ((hidden - resid) * update * keep).astype(low)
        keep_ref[:, cols] = keep.astype(low)
        blend_ref[:, cols] = update * hidden + keep * resid

    each(width, hide)
    for n in range(seqs):
        rows = pl.ds(n * GROUP, GROUP)
        blend = blend_ref[rows, :]
        centered = blend - jnp.mean(blend, axis=-1, keepdims=True)
        rstd = lax.rsqrt(jnp.mean(centered * centered, axis=-1, keepdims=True) + 1e-05)
        unit = centered * rstd
        unit_ref[rows, :] = unit.astype(low)
        rstd_ref[rows, :] = jnp.broadcast_to(rstd, (GROUP, LANES))
        normed = unit * piece(vec_ref, where["gain"], 0, width) + piece(vec_ref, where["shift"], 0, width)
        blend_ref[rows, :] = normed
        normed_ref[rows, :] = normed.astype(low)
        normed_t_ref[:, rows] = normed.astype(low).T

    def lift(at):
        cols = pl.ds(at, CHUNK)
        act, slope = silu_pair(nn(normed_ref[...], wup_ref[:, cols]) + piece(vec_ref, where["up"], at, CHUNK))
        fslope_ref[:, cols] = slope.astype(low)
        act = act.astype(low)
        ffn_ref[:, cols] = act
        hidden_t_ref[cols, :] = act.T

    each(wup_ref.shape[1], lift)

    def drop(at):
        cols = pl.ds(at, CHUNK)
        blend_ref[:, cols] = blend_ref[:, cols] + nn(ffn_ref[...], wdown_ref[:, cols]) + piece(vec_ref, where["down"], at, CHUNK)

    each(width, drop)
    for n in range(seqs):
        result = blend_ref[pl.ds(n * GROUP, GROUP), :].astype(low).T
        result = jnp.where(live_lanes(spot_ref, lengths_ref, n, result.shape), result, jnp.zeros_like(result))
        out_ref[:, n] = result.reshape(out_ref.shape[0], out_ref.shape[2], GROUP)


def forward_part(spot, lengths, folded, mixed, x, values, w_mix, w_out, w_up, w_down, vec, where, qk_scale, qk_shift, after=()):
    vwidth, width = w_out.shape
    zwidth = qk_scale.shape[1]
    ff = w_up.shape[1]
    count = x.shape[0]
    narrow, wide = (count, width), (count, vwidth)
    outs = [
        ((width, count), low), (folded, low), ((count, zwidth), low), ((count, zwidth), low), ((count, zwidth), f32),
        ((count, zwidth), f32), ((count, GROUP), f32), (wide, low), (wide, low), ((vwidth, count), low),
        (narrow, low), (narrow, low), (narrow, low), (narrow, low), ((count, LANES), f32),
        ((width, count), low), ((ff, count), low), ((count, ff), low),
    ]
    scratch = [pltpu.VMEM(narrow, low), pltpu.VMEM(narrow, f32), pltpu.VMEM(wide, low)]
    scratch += [pltpu.VMEM(narrow, f32), pltpu.VMEM(narrow, low), pltpu.VMEM((count, ff), low)]
    macs = w_mix.size + w_out.size + w_up.size + w_down.size
    return call(
        functools.partial(forward_kernel, len(mixed), where),
        outs,
        (spot, lengths, w_mix, w_out, w_up, w_down, x, values, vec, qk_scale, qk_shift, *mixed),
        smem=2,
        mib=MIB[1],
        after=after,
        scratch=scratch,
    )


def column_sum(part):
    return jnp.sum(part.astype(f32), axis=0, keepdims=True)


def put(ref, row, value, columns):
    if isinstance(ref, tuple):
        lone = value.shape[0] // len(ref)
        for k, one in enumerate(ref):
            put(one, row, value[k * lone : (k + 1) * lone], columns)
        return
    if len(ref.shape) == 2:
        ref[...] = value
        return
    owners = ref.shape[0]
    lone = value.shape[0] // owners
    for owner in range(owners):
        part = value[owner * lone : (owner + 1) * lone]
        for i, at in enumerate(range(0, value.shape[1], columns)):
            ref[owner, pl.ds(row + i * lone, lone), :] = part[:, at : at + columns]


def split_product(side, keep_ref, send_ref, left, right_ref, half, columns, row=0):
    total = right_ref.shape[1]
    for ref, which in ((keep_ref, side), (send_ref, 1 - side)):
        base = which * (total - half)
        parts = []
        for at in range(0, half, CHUNK):
            cols = pl.ds(pl.multiple_of(base + at, 128), min(CHUNK, half - at))
            parts.append(nn(left, right_ref[:, cols]).astype(low))
        put(ref, row, jnp.concatenate(parts, axis=1), columns)


def split_narrow(side, keep_ref, send_ref, left_ref, right_ref):
    both = [nn(left_ref[pl.ds(at, CHUNK), :], right_ref[...]).astype(low) for at in range(0, left_ref.shape[0], CHUNK)]
    both = jnp.concatenate(both, axis=0)
    half = both.shape[1] // 2
    near, far = both[:, :half], both[:, half:]
    put(keep_ref, 0, jnp.where(side == 0, near, far), half)
    put(send_ref, 0, jnp.where(side == 0, far, near), half)


def pair_outs(tall, wide, owners, lines=0):
    if not owners:
        return [((tall[0], tall[1] // 2), low)] * 2 + [((wide[0], wide[1] // 2), low)] * 2
    rows = (tall[0] * tall[1] + wide[0] * wide[1]) // (tall[1] * owners) + lines
    return [((owners, rows, tall[1] // 2), low)] * 2


def back_ffn_kernel(
    spot_ref, lengths_ref, wdown_ref, grad_ref, hidden_t_ref, fslope_ref, normed_t_ref, *refs
):
    halves, (g_ref, dffn_ref, small_ref) = refs[:-3], refs[-3:]
    width, ff = g_ref.shape[1], wdown_ref.shape[0]
    for n in range(grad_ref.shape[2]):
        part = wide_block(grad_ref, 1, n)
        part = jnp.where(live_lanes(spot_ref, lengths_ref, n, part.shape), part, jnp.zeros_like(part))
        g_ref[pl.ds(n * GROUP, GROUP), :] = part.T
    small_ref[:, pl.ds(0, width)] = column_sum(g_ref[...])
    side = spot_ref[2] & 1
    split_narrow(side, halves[0], halves[1], hidden_t_ref, g_ref)

    def lift(at):
        part = pl.ds(at, CHUNK)
        pulled = (nt(g_ref[...], wdown_ref[part, :]) * fslope_ref[:, part].astype(f32)).astype(low)
        dffn_ref[:, part] = pulled
        small_ref[:, pl.ds(width + at, CHUNK)] = column_sum(pulled)

    each(ff, lift)
    tall = hidden_t_ref.shape[0] // halves[0].shape[0]
    split_product(side, halves[-2], halves[-1], normed_t_ref[...], dffn_ref, ff // 2, halves[-2].shape[-1], tall)
    if len(halves) == 2:
        for ref in halves:
            owners, rows, columns = ref.shape
            ref[:, pl.ds(2 * tall, rows - 2 * tall), :] = jnp.zeros((owners, rows - 2 * tall, columns), low)


def back_ffn(spot, lengths, owners, lines, grad, hidden_t, fslope, normed_t, w_down, after=()):
    ff, width = w_down.shape
    count = fslope.shape[0]
    outs = pair_outs((ff, width), (width, ff), owners, lines)
    outs += [((count, width), low), ((count, ff), low), ((1, width + ff), f32)]
    *halves, g, dffn, small = call(
        back_ffn_kernel,
        outs,
        (spot, lengths, w_down, grad, hidden_t, fslope, normed_t),
        smem=2,
        mib=MIB[2],
        after=after,
    )
    return halves, g, dffn, small


def back_norm_kernel(
    base, wup_ref, g_ref, dffn_ref, unit_ref, rstd_ref, vec_ref, hslope_ref, uslope_ref, kept_ref,
    dh_ref, du_ref, direct_ref, small_ref, dn_ref,
):
    width = wup_ref.shape[0]

    def drop(at):
        part = pl.ds(at, CHUNK)
        pulled = g_ref[:, part].astype(f32) + nt(dffn_ref[...], wup_ref[part, :])
        dn_ref[:, part] = pulled
        small_ref[:, part] = column_sum(pulled * unit_ref[:, part].astype(f32))
        small_ref[:, pl.ds(width + at, CHUNK)] = column_sum(pulled)

    each(width, drop)
    for n in range(g_ref.shape[0] // GROUP):
        rows = pl.ds(n * GROUP, GROUP)
        unit = unit_ref[rows, :].astype(f32)
        pulled = dn_ref[rows, :] * piece(vec_ref, base, 0, width)
        inner = jnp.mean(pulled * unit, axis=-1, keepdims=True)
        blend = pulled - jnp.mean(pulled, axis=-1, keepdims=True) - unit * inner
        blend = blend * rstd_ref[rows, :][:, :1]
        dh_ref[rows, :] = (blend * hslope_ref[rows, :].astype(f32)).astype(low)
        du_ref[rows, :] = (blend * uslope_ref[rows, :].astype(f32)).astype(low)
        direct_ref[rows, :] = (blend * kept_ref[rows, :].astype(f32)).astype(low)


def back_norm(g, dffn, unit, rstd, vec, where, hslope, uslope, kept, w_up, after=()):
    width = w_up.shape[0]
    narrow = g.shape
    return call(
        functools.partial(back_norm_kernel, where["gain"]),
        [(narrow, low)] * 3 + [((1, 2 * width), f32)],
        (w_up, g, dffn, unit, rstd, vec, hslope, uslope, kept),
        mib=MIB[3],
        after=after,
        scratch=[pltpu.VMEM(narrow, f32)],
    )


def back_attend_kernel(
    wout_ref, wmix_ref, wvalue_ref,
    dh_ref, du_ref, direct_ref, reset_ref, turned_ref, values_ref, vslope_ref, probs_ref,
    query_ref, key_ref, shared_ref, qslope_ref, qscale_ref, small_ffn_ref, small_norm_ref, result_ref,
    dmix_ref, dvalue_ref, mixed_ref, joint_ref,
    table_ref,
    datt_ref,
):
    vwidth, width = wout_ref.shape
    zwidth = qscale_ref.shape[1]
    count = dh_ref.shape[0]
    seqs = count // GROUP
    dmix_ref[:, pl.ds(0, width)] = du_ref[...]
    dmix_ref[:, pl.ds(width + zwidth + vwidth, width)] = dh_ref[...]

    def gate(at):
        part = pl.ds(at, CHUNK)
        pulled = nt(dh_ref[...], wout_ref[part, :])
        dmix_ref[:, pl.ds(width + zwidth + at, CHUNK)] = (
            pulled * turned_ref[:, part].astype(f32)
        ).astype(low)
        datt_ref[:, part] = (pulled * reset_ref[:, part].astype(f32)).astype(low)

    each(vwidth, gate)
    scale = zwidth**-0.5
    q_scale, k_scale = qscale_ref[pl.ds(0, 1), :], qscale_ref[pl.ds(1, 1), :]
    zero = jnp.zeros((1, zwidth), f32)
    sums = [zero, zero, zero, zero]
    for n in range(seqs):
        rows = pl.ds(n * GROUP, GROUP)
        probs = probs_ref[rows, :]
        pulled = nt(datt_ref[rows, :], values_ref[rows, :])
        pulled = probs * (pulled - jnp.sum(pulled * probs, axis=-1, keepdims=True))
        pulled = pulled.astype(low)
        d_query = nn(pulled, key_ref[rows, :]) * scale
        d_key = nn(pulled.T, query_ref[rows, :]) * scale
        probs_t = probs.astype(low).T
        shared = shared_ref[rows, :]
        found = (d_query * shared, d_key * shared, d_query, d_key)
        sums = [a + jnp.sum(b, axis=0, keepdims=True) for a, b in zip(sums, found)]
        dmix_ref[rows, pl.ds(width, zwidth)] = (
            (d_query * q_scale + d_key * k_scale) * qslope_ref[rows, :]
        ).astype(low)
        dvalue_ref[rows, :] = (nn(probs_t, datt_ref[rows, :]) * vslope_ref[rows, :].astype(f32)).astype(low)

    def turn(result):
        devices, _, channels, _ = mixed_ref.shape
        return result.astype(low).T.reshape(devices, channels, GROUP)

    for n in range(0, seqs, 2):
        result = nt(dmix_ref[pl.ds(n * GROUP, 2 * GROUP), :], wmix_ref[...])
        mixed_ref[:, n] = turn(result[:GROUP])
        mixed_ref[:, n + 1] = turn(result[GROUP:])
    for n in range(0, seqs, 2):
        rows = pl.ds(n * GROUP, 2 * GROUP)
        result = direct_ref[rows, :].astype(f32) + nt(dvalue_ref[rows, :], wvalue_ref[...])
        joint_ref[:, 0, n] = turn(result[:GROUP])
        joint_ref[:, 0, n + 1] = turn(result[GROUP:])
    joint_ref[:, 1] = result_ref[...]
    ff = small_ffn_ref.shape[1] - width
    found = (
        column_sum(dmix_ref[...]), column_sum(dvalue_ref[...]), column_sum(dh_ref[...]),
        sums[0], sums[1], sums[2], sums[3], small_norm_ref[:, :width], small_norm_ref[:, width:],
        small_ffn_ref[:, width:], small_ffn_ref[:, :width],
    )
    lines = []
    for part in found:
        for at in range(0, part.shape[1], TABLE):
            line = part[:, at : at + TABLE]
            lack = TABLE - line.shape[1]
            lines.append(line if lack == 0 else jnp.concatenate([line, jnp.zeros((1, lack), f32)], axis=1))
    lines.append(jnp.zeros((table_ref.shape[0] - len(lines), TABLE), f32))
    table_ref[...] = jnp.concatenate(lines, axis=0).astype(low)


def back_attend(dh, du, direct, reset, turned, values, vslope, probs, query, key, shared, qslope, qk_scale, small_ffn, small_norm, result, w_out, w_mix, w_value, after=()):
    vwidth, width = w_out.shape
    mwidth = w_mix.shape[1]
    count = dh.shape[0]
    outs = [((count, mwidth), low), ((count, vwidth), low)]
    outs += [(result.shape, low), (result.shape[:1] + (2,) + result.shape[1:], low), ((64, TABLE), low)]
    scratch = [pltpu.VMEM((count, vwidth), low)]
    macs = w_out.size + w_mix.size + w_value.size
    return call(
        back_attend_kernel,
        outs,
        (w_out, w_mix, w_value, dh, du, direct, reset, turned, values, vslope, probs, query, key, shared, qslope, qk_scale, small_ffn, small_norm, result),
        mib=MIB[4],
        after=after,
        scratch=scratch,
    )


def back_mid_kernel(spot_ref, gated_t_ref, dh_ref, x_t_ref, dvalue_ref, table_ref, *halves):
    side = spot_ref[2] & 1
    if len(halves) == 4:
        (kept, sent, wide_kept, wide_sent), tall = halves, 0
    else:
        kept, sent = halves[0], halves[1:]
        wide_kept, wide_sent, tall = kept, sent, gated_t_ref.shape[0] // kept.shape[0]
    split_narrow(side, kept, sent, gated_t_ref, dh_ref)
    split_product(
        side, wide_kept, wide_sent, x_t_ref[...], dvalue_ref, dvalue_ref.shape[1] // 2, wide_kept.shape[-1], tall
    )
    if len(halves) == 4:
        return
    lines = kept.shape[1] - 2 * tall
    high = table_ref.shape[0] // (2 * lines)
    for refs, which in (((kept,), side), (sent, 1 - side)):
        for ref in refs:
            for owner in range(ref.shape[0]):
                at = pl.multiple_of((2 * (owner % high) + which) * lines, 16)
                ref[owner, pl.ds(2 * tall, lines), :] = table_ref[pl.ds(at, lines), :]


def halved(outs):
    (kept, kind), (sent, _) = outs
    return [(kept, kind)] + [((sent[0] // 2,) + sent[1:], kind)] * 2


def back_mid(spot, owners, gated_t, dh, x_t, dvalue, table, lines, after=()):
    count, width = dh.shape
    vwidth = dvalue.shape[1]
    outs = pair_outs((vwidth, width), (width, vwidth), owners, lines)
    found = call(
        back_mid_kernel,
        halved(outs) if owners else outs,
        (spot, gated_t, dh, x_t, dvalue, table),
        smem=1,
        mib=MIB[5],
        after=after,
    )
    if owners:
        return [found[0]], [list(found[1:])]
    return [found[0], found[2]], [[found[1]], [found[3]]]


def back_mix_kernel(spot_ref, mixed_t_ref, dmix_ref, keep_ref, *send_refs):
    half = keep_ref.shape[-1]
    split_product(spot_ref[2] & 1, keep_ref, send_refs, mixed_t_ref[...], dmix_ref, half, half)


def back_mix_weight(spot, owners, mixed_t, dmix, after=()):
    mwidth = dmix.shape[1]
    width, count = mixed_t.shape
    half = -(-mwidth // 256) * 128
    outs = [((width, half), low)] * 2
    kept, *sent = call(
        back_mix_kernel,
        halved(outs) if owners else outs,
        (spot, mixed_t, dmix),
        smem=1,
        mib=MIB[6],
        after=after,
    )
    return [kept], [sent]


def halve_kernel(index, bit, spot_ref, kept_ref, *refs):
    arrived, (sent_ref, stay_ref) = refs[:-2], refs[-2:]
    outer, inner, _, _ = sent_ref.shape
    lone = outer // len(arrived)
    mine = (spot_ref[index] >> bit) & 1
    for ref, which in ((sent_ref, 1 - mine), (stay_ref, mine)):
        for a in range(outer):
            for b in range(inner):
                total = kept_ref[a, which, b].astype(f32) + arrived[a // lone][a % lone, which, b].astype(f32)
                ref[a, b] = total.astype(low)


def halve(spot, kept, arrived, index, bit, at, after=()):
    dims = kept.shape[:-2]
    outer, inner = 1 << at, 1 << (len(dims) - at - 1)
    block = kept.shape[-2:]

    def shaped(part):
        return part.reshape((-1, 2, inner) + block)

    sent, stay = call(
        functools.partial(halve_kernel, index, bit),
        [((outer, inner) + block, low)] * 2,
        (spot, shaped(kept), *map(shaped, arrived)),
        smem=1,
        mib=MIB[7],
        after=after,

    )
    rest = dims[:at] + dims[at + 1 :] + block
    return sent.reshape(rest), stay.reshape(rest)


def finish_pair_kernel(count, lines, spot_ref, *refs):
    shares, outs = refs[:count], refs[count:]
    tall_ref, wide_ref = outs[:2]
    columns = shares[0].shape[1]
    cut = tall_ref.shape[0] * 2 // len(shares)
    lone = wide_ref.shape[0] * 2 // len(shares)
    for k, ref in enumerate(shares):
        at = spot_ref[2] ^ k
        high, side = at >> 1, at & 1
        tall_ref[pl.ds(pl.multiple_of(high * cut, 8), cut), pl.ds(pl.multiple_of(side * columns, 128), columns)] = ref[
            pl.ds(0, cut), :
        ].astype(f32)
        runs = wide_ref.shape[1] // 2 // columns
        for run in range(runs):
            wide_ref[
                pl.ds(pl.multiple_of(high * lone, 8), lone),
                pl.ds(pl.multiple_of((side * runs + run) * columns, 128), columns),
            ] = ref[pl.ds(cut + run * lone, lone), :].astype(f32)
        if lines:
            outs[-1][pl.ds(pl.multiple_of(at * lines, 8), lines), :] = ref[pl.ds(2 * cut, lines), :].astype(f32)
    if lines:
        row = 0
        for ref in outs[2:-1]:
            if len(ref.shape) == 2:
                for k in range(ref.shape[0]):
                    ref[pl.ds(k, 1), :] = outs[-1][pl.ds(row, 1), :][:, : ref.shape[1]]
                    row += 1
                continue
            for at in range(0, ref.shape[0], columns):
                size = min(columns, ref.shape[0] - at)
                ref[pl.ds(at, size)] = outs[-1][row, :size]
                row += 1


def finish_pair(spot, shares, tall, wide, lines=0, vectors=(), after=()):
    outs = [(tall, f32), (wide, f32)] + [(shape, f32) for shape in vectors]
    count = len(shares)
    scratch = [pltpu.VMEM((count * lines, shares[0].shape[1]), f32)] if lines else []
    kernel = functools.partial(finish_pair_kernel, count, lines)
    return call(kernel, outs, (spot, *shares), smem=1, mib=MIB[8], scratch=scratch, after=after)


def finish_mix_kernel(spot_ref, *refs):
    shares, out_ref = refs[:-1], refs[-1]
    half, mwidth = shares[0].shape[1], out_ref.shape[1]
    common = 2 * half - mwidth
    lone = out_ref.shape[0] * 2 // len(shares)
    for k, ref in enumerate(shares):
        at = spot_ref[2] ^ k
        rows = pl.ds(pl.multiple_of((at >> 1) * lone, 8), lone)
        base = pl.multiple_of(common + (at & 1) * (mwidth - half), 128)
        out_ref[rows, pl.ds(base, half - common)] = ref[:, common:].astype(f32)
        if common:

            @pl.when(at & 1 == 0)
            def _():
                out_ref[rows, pl.ds(0, common)] = ref[:, :common].astype(f32)


def finish_mix(spot, shares, shape, after=()):
    return call(finish_mix_kernel, [(shape, f32)], (spot, *shares), smem=1, mib=MIB[9], after=after)[0]


Y_FIRST = (("tok", 1), ("ch", 0))
Z_FIRST = (("ch", 1), ("tok", 1), ("ch", 0))
X_FIRST = (("ch", 0), ("tok", 1))


def bits_of(axis):
    return lax.axis_size(axis).bit_length() - 1


def across(part, axis, turn):
    return lax.ppermute(part, axis, [(i, i ^ turn) for i in range(lax.axis_size(axis))])


def exchange(part, axis, bit):
    return across(part, axis, 1 << bit)


def side_of(axis, bit):
    return (lax.axis_index(axis) >> bit) & 1


def by_owner(grad):
    dims = (2,) * (bits_of("ch") + bits_of("tok") - 1)
    return grad.reshape(dims + (-1, grad.shape[-1]))


def fold(part, columns):
    runs = [part[..., at : at + columns] for at in range(0, part.shape[-1], columns)]
    return jnp.concatenate(runs, axis=-2)


def add(left, right):
    return (left.astype(f32) + right.astype(f32)).astype(low)


def plain_halve(kept, arrived, mine, at):
    columns = min(part.shape[-1] for part in kept)

    def pick(which):
        def one(part):
            return lax.dynamic_index_in_dim(part, which, at, keepdims=False)

        return jnp.concatenate([fold(add(one(a), one(b)), columns) for a, b in zip(kept, arrived)], axis=-2)

    return pick(1 - mine), pick(mine)


class Sum:
    def __init__(self, spot, kept, sent, order):
        self.spot = spot
        self.names = [("ch", k) for k in reversed(range(bits_of("ch")))]
        self.names += [("tok", k) for k in reversed(range(1, bits_of("tok")))]
        self.stages = list(order) + [name for name in reversed(self.names) if name not in order]
        self.kept = [by_owner(part) for part in kept]
        arrived = [[exchange(piece, "tok", 0) for piece in part] for part in sent]
        self.arrived = arrived[0] if self.by_kernel() else [by_owner(part) for part, in arrived]

    def by_kernel(self):
        return len(self.kept) == 1 and self.kept[0].shape[-2] % 16 == 0

    def step(self, after=()):
        axis, bit = self.stages.pop(0)
        at = self.names.index((axis, bit))
        self.names.remove((axis, bit))
        if self.by_kernel():
            index = 1 if axis == "ch" else 2
            sent, stay = halve(self.spot, self.kept[0], self.arrived, index, bit, at, after)
        else:
            sent, stay = plain_halve(self.kept, self.arrived, side_of(axis, bit), at)
        self.kept, self.arrived = [stay], [exchange(sent, axis, bit)]
        return stay

    def shares(self):
        found = [add(self.kept[0], self.arrived[0])]
        for bit in reversed(range(1, bits_of("tok"))):
            found += [exchange(part, "tok", bit) for part in found]
        lower = [exchange(part, "tok", 0) for part in found]
        size = bits_of("tok") - 1
        order = [sum(((k >> (size - 1 - i)) & 1) << i for i in range(size)) for k in range(len(found))]
        found = [part for k in order for part in (found[k], lower[k])]
        return found


def in_order(shares, place):
    bit = 1
    while bit < len(shares):
        swapped = (place & bit) != 0
        shares = [jnp.where(swapped, shares[k ^ bit], shares[k]) for k in range(len(shares))]
        bit *= 2
    return jnp.stack(shares)


def plain_pair(place, shares, tall, wide):
    whole = in_order(shares, place).astype(f32)
    high = len(shares) // 2
    cut, lone = tall[0] // high, wide[0] // high
    whole = whole.reshape((high, 2) + whole.shape[1:])
    first = whole[:, :, :cut].transpose(0, 2, 1, 3).reshape(tall)
    second = whole[:, :, cut:].reshape(high, 2, -1, lone, whole.shape[-1])
    return first, second.transpose(0, 3, 1, 2, 4).reshape(wide)


def plain_mix(place, shares, shape):
    whole = in_order(shares, place).astype(f32)
    half = whole.shape[-1]
    whole = whole.reshape((len(shares) // 2, 2) + whole.shape[1:])
    whole = jnp.concatenate([whole[:, 0], whole[:, 1, :, 2 * half - shape[1] :]], axis=-1)
    return whole.reshape(shape)


def sum_tok(part):
    for bit in range(bits_of("tok")):
        part = part + exchange(part, "tok", bit)
    return part


def swap(parts):
    return lax.all_to_all(parts, "ch", split_axis=0, concat_axis=0, tiled=True)


def folded(parts):
    devices, channels, span = parts.shape[0], parts.shape[-2], parts.shape[-1]
    if channels % 16 == 0:
        return parts
    return jnp.moveaxis(parts, 0, -3).reshape((1,) + parts.shape[1:-2] + (devices * channels, span))


def unfolded(parts, devices):
    if parts.shape[0] == devices:
        return parts
    channels, span = parts.shape[-2] // devices, parts.shape[-1]
    return jnp.moveaxis(parts.reshape(parts.shape[1:-2] + (devices, channels, span)), -3, 0)


def local(
    inputs,
    out_grad,
    seq_lengths,
    ema_alpha,
    ema_delta,
    ema_beta,
    ema_eta,
    ema_omega,
    w_mix,
    b_mix,
    w_value,
    b_value,
    w_out,
    b_out,
    qk_scale,
    qk_shift,
    ln_gain,
    ln_bias,
    w_up,
    b_up,
    w_down,
    b_down,
):
    count, channels, local_len = inputs.shape
    width, mwidth = w_mix.shape
    vwidth, ff = w_value.shape[1], w_up.shape[1]
    devices, tok_size = lax.axis_size("ch"), lax.axis_size("tok")
    columns = count * channels
    span = local_len // devices
    tok_index = lax.axis_index("tok").astype(jnp.int32)
    ch_index = lax.axis_index("ch").astype(jnp.int32)
    spot = jnp.stack([tok_index * local_len + ch_index * span, ch_index, tok_index])
    apart = devices <= 8 and channels % 16 == 0

    def by_column(parts):
        whole = unfolded(parts, devices)
        return pad_to_lanes(whole.reshape(whole.shape[:-3] + (columns, span)), whole.ndim - 3)

    where = vectors(width, mwidth, vwidth, ff)
    vec = jnp.concatenate([b_mix, b_value, b_out, ln_gain, ln_bias, b_up, b_down])[None]
    params = ema_params(ema_alpha, ema_delta, ema_beta, ema_eta, count)
    omega = pad_to_lanes(jnp.tile(ema_omega, count)[None], 1)

    flat = inputs.reshape(columns, local_len)
    raw = by_blocks(spot, flat, out_grad.reshape(columns, local_len))
    raw = folded(swap(raw.reshape(devices, 2, count, channels, span)))
    xs, ends, total = ema_ends(pad_to_lanes(flat, 0), params)
    totals = lax.all_gather(total, "tok")
    mixed, slope, entry = ema_mix(spot, xs, ends, params, omega, totals, apart)
    if apart:
        mixed = [part.reshape(count, channels, span) for part in mixed]
        mixed = [part if k == 0 else across(part, "ch", k) for k, part in enumerate(mixed)]
    else:
        mixed = folded(swap(mixed[0][:, :columns].reshape(devices, count, channels, span)))
        mixed = [mixed[0]] if mixed.shape[0] == 1 else [mixed.transpose(1, 0, 2, 3).reshape(count, width, span)]
    x, values, vslope, x_t = value_part(raw, w_value, vec, where, (entry,))
    (
        mixed_t, result, query, key, shared, qslope, probs, reset, turned, gated_t,
        hslope, uslope, keep, unit, rstd, normed_t, hidden_t, fslope,
    ) = forward_part(
        spot, seq_lengths, raw.shape[:1] + raw.shape[2:], mixed, x, values, w_mix, w_out, w_up, w_down, vec,
        where, qk_scale, qk_shift,
    )
    owners = devices * tok_size // 2
    joined = owners if width // owners % 16 == 0 else 0
    lines = 64 // tok_size
    halves, g, dffn, small_ffn = back_ffn(
        spot, seq_lengths, joined, lines, raw, hidden_t, fslope, normed_t, w_down
    )
    ffn = Sum(spot, halves[::2], [[part] for part in halves[1::2]], Y_FIRST)
    dh, du, direct, small_norm = back_norm(g, dffn, unit, rstd, vec, where, hslope, uslope, keep, w_up)
    last = ffn.step((small_norm,))
    dmix, dvalue, back_mix, joint, table = back_attend(
        dh, du, direct, reset, turned, values, vslope, probs, query, key, shared, qslope,
        qk_scale, small_ffn, small_norm, result, w_out, w_mix, w_value, (last,),
    )
    kept, sent = back_mix_weight(spot, joined, mixed_t, dmix, (table,))
    mix = Sum(spot, kept, sent, X_FIRST)
    kept, sent = back_mid(spot, joined, gated_t, dh, x_t, dvalue, table, lines, (kept[0],))
    last = kept[0]
    back_mix = swap(unfolded(back_mix, devices))
    if not joined:
        table = table.reshape(tok_size // 2, 2, lines, TABLE)
        for group, which in ((kept, side_of("tok", 0)), (sent, 1 - side_of("tok", 0))):
            part = lax.dynamic_index_in_dim(table, which, 1, keepdims=False)
            part = jnp.broadcast_to(part[None], (devices,) + part.shape).reshape(-1, TABLE)
            group.append(part if group is kept else [part])
    mid = Sum(spot, kept, sent, Z_FIRST)
    last = ffn.step((last,))
    last = mix.step((last,))
    last = mid.step((last,))
    joint, back_mix, _ = lax.optimization_barrier((unfolded(joint, devices), back_mix, last))
    joint = swap(joint)
    pull, heads, total = ema_back(by_column(back_mix), slope, params, (last,))
    totals = lax.all_gather(total, "tok")
    last = mix.step((totals,))
    last = mid.step((last,))
    sums = ema_sums(spot, xs, pull, entry, heads, totals, params, (last,))
    last = mix.step((sums,))
    last = mid.step((last,))
    last = ffn.step((last,))
    last = mix.step((last,))
    while len(mid.stages) + len(mix.stages) + len(ffn.stages):
        for group in (mid, ffn, mix):
            last = group.step((last,)) if group.stages else last
    input_grad, output = ema_finish(spot, pull, heads, params, omega, totals, by_column(joint), (last,))
    mix.arrived[0], output = lax.optimization_barrier((mix.arrived[0], output))
    last = output
    input_grad = input_grad[:columns].reshape(inputs.shape)
    output = output[:columns].reshape(inputs.shape)
    ema_grads = ema_param_grads(sum_tok(sums), ema_alpha, ema_delta, ema_beta, ema_eta, count)

    tall, wide = (vwidth // devices, width), (width // devices, vwidth)
    shares = mid.shares()
    half = qk_scale.shape[1]
    across_mix = (width // devices, mwidth)
    if joined:
        vectors_of = [(mwidth,), (vwidth,), (width,), qk_scale.shape, qk_scale.shape, (width,), (width,), (ff,), (width,)]
        g_down, g_up = finish_pair(spot, ffn.shares(), tall, wide, after=(last,))
        g_out, g_value, *found = finish_pair(spot, shares, tall, wide, lines, vectors_of, (last,))
        g_mix = finish_mix(spot, mix.shares(), across_mix, (last,))
    else:
        table = in_order([part[-lines:] for part in shares], tok_index).astype(f32).reshape(-1)
        shares = [part[:-lines] for part in shares]
        g_out, g_value = plain_pair(tok_index, shares, tall, wide)
        g_down, g_up = plain_pair(tok_index, ffn.shares(), tall, wide)
        g_mix = plain_mix(tok_index, mix.shares(), across_mix)
        found, at = [], 0
        for size in (mwidth, vwidth, width, half, half, half, half, width, width, ff, width):
            found.append(table[at : at + size])
            at += -(-size // TABLE) * TABLE
        found = found[:3] + [jnp.stack(found[3:5]), jnp.stack(found[5:7])] + found[7:]
    g_bmix, g_bvalue, g_bout, g_qscale, g_qshift, g_gain, g_lnbias, g_bup, g_bdown = found
    return (
        output,
        input_grad,
        *ema_grads,
        g_mix,
        g_bmix,
        g_value,
        g_bvalue,
        g_out,
        g_bout,
        g_qscale,
        g_qshift,
        g_gain,
        g_lnbias,
        g_up,
        g_bup,
        g_down,
        g_bdown,
    )


def solution(mesh):
    by_ch = P("ch", None)
    placed = P(None, "ch", "tok")
    return jax.shard_map(
        local,
        mesh=mesh,
        in_specs=(placed, placed, P()) + (by_ch,) * 4 + (P("ch"),) + (P(),) * 14,
        out_specs=(
            (placed, placed)
            + (by_ch,) * 4
            + (P("ch"), by_ch, P(), by_ch, P(), by_ch)
            + (P(),) * 5
            + (by_ch, P(), by_ch, P())
        ),
        check_vma=False,
    )
```

```python
import functools
import jax
import jax.numpy as jnp
from jax import lax
from jax.experimental import pallas as pl
from jax.experimental.pallas import tpu as pltpu
from jax.sharding import PartitionSpec as P

GROUP = 128
SUB = 8
LANES = 128
f32 = jnp.float32


def by_tile(shape, dim):
    block = tuple(LANES if k == dim else size for k, size in enumerate(shape))
    return pl.BlockSpec(block, lambda i: tuple(i if k == dim else 0 for k in range(len(shape))))


def in_smem():
    return pl.BlockSpec(memory_space=pltpu.SMEM)


def roomy(mib=5):
    return pltpu.CompilerParams(vmem_limit_bytes=mib * 1024 * 1024)


def work(flops, moved, exps=0):
    return pl.CostEstimate(flops=1, bytes_accessed=1, transcendentals=0)


def launch(kernel, outs, ins, in_specs, out_specs, after=(), grid=(), scratch=(), mib=5, cost=None):
    count = len(ins)

    def run(*refs):
        kernel(*refs[:count], *refs[count + len(after) :])

    return pl.pallas_call(
        run,
        grid=grid,
        out_shape=tuple(jax.ShapeDtypeStruct(shape, kind) for shape, kind in outs),
        in_specs=list(in_specs) + [pl.BlockSpec(memory_space=pl.ANY)] * len(after),
        out_specs=tuple(out_specs),
        scratch_shapes=list(scratch),
        compiler_params=roomy(mib),
        cost_estimate=cost,
    )(*ins, *after)


def rates(params_ref):
    rate = jax.nn.sigmoid(params_ref[0])
    drop = rate * jax.nn.sigmoid(params_ref[1])
    weight = params_ref[3] * rate * params_ref[2]
    return 1.0 - drop, jnp.log1p(-drop), weight


def spread(ref, j):
    return jnp.broadcast_to(ref[pl.ds(j, 1), :], (SUB, LANES))


def tree_sum(parts):
    while len(parts) > 1:
        parts = [a + b for a, b in zip(parts[::2], parts[1::2])] + parts[len(parts) & ~1 :]
    return parts[0]


def block_rows(g, t):
    return pl.ds(g * GROUP + t, SUB, stride=GROUP)


def state_rows(g, j, expand):
    return pl.ds(g * expand + j, SUB, stride=expand)


def blocks_kernel(spot_ref, first_ref, second_ref, out_ref, sems):
    copies = []
    for b in range(out_ref.shape[0]):
        cols = pl.ds(b * GROUP, GROUP)
        for which, ref in enumerate((first_ref, second_ref)):
            copies.append(pltpu.make_async_copy(ref.at[:, cols], out_ref.at[b, which], sems.at[2 * b + which]))
    for copy in copies:
        copy.start()
    for copy in copies:
        copy.wait()


def by_blocks(spot, first, second):
    columns, length = first.shape
    blocks = length // GROUP
    anywhere = pl.BlockSpec(memory_space=pl.ANY)
    return launch(
        blocks_kernel,
        [((blocks, 2, columns, GROUP), first.dtype)],
        (spot, first, second),
        [in_smem(), anywhere, anywhere],
        [anywhere],
        scratch=[pltpu.SemaphoreType.DMA((2 * blocks,))],
        mib=1,
    )[0]


def ema_ends_kernel(x_ref, params_ref, xs_ref, ends_ref, total_ref, decay_ref):
    length = x_ref.shape[1]
    expand = params_ref.shape[1]
    blocks = length // GROUP
    decay, log_decay, _ = rates(params_ref)
    decay_ref[...] = decay
    for b in range(blocks):
        rows = pl.ds(b * GROUP, GROUP)
        xs_ref[rows, :] = x_ref[:, rows].astype(f32).T
    factors = [spread(decay_ref, j) for j in range(expand)]
    for g in range(0, blocks, SUB):

        def step(t, states):
            now = xs_ref[block_rows(g, t), :]
            return tuple(f * s + now for f, s in zip(factors, states))

        states = (jnp.zeros((SUB, LANES), f32),) * expand
        states = lax.fori_loop(0, GROUP, step, states, unroll=8)
        for j in range(expand):
            ends_ref[state_rows(g, j, expand), :] = states[j]
    jump = jnp.exp(GROUP * log_decay)
    carry = jnp.zeros_like(jump)
    for b in range(blocks):
        carry = jump * carry + ends_ref[pl.ds(b * expand, expand), :]
    total_ref[...] = carry


def ema_ends(x, params, after=()):
    columns, length = x.shape
    expand = params.shape[1]
    shapes = ((length, columns), (length // GROUP * expand, columns), (expand, columns))
    return launch(
        ema_ends_kernel,
        [(shape, f32) for shape in shapes],
        (x, params),
        [by_tile(x.shape, 0), by_tile(params.shape, 2)],
        [by_tile(shape, 1) for shape in shapes],
        after=after,
        grid=(columns // LANES,),
        scratch=[pltpu.VMEM((expand, LANES), f32)],
        mib=5 * max(1, length // 1024),
        cost=work(2 * expand * length * columns, 6 * length * columns),
    )


def ema_mix_kernel(
    spot_ref, xs_ref, ends_ref, params_ref, omega_ref, totals_ref, *refs
):
    mixed_refs, (slope_ref, entry_ref, decay_ref, weight_ref, smooth_ref) = refs[:-5], refs[-5:]
    length = xs_ref.shape[0]
    expand = params_ref.shape[1]
    blocks = length // GROUP
    decay, log_decay, weight = rates(params_ref)
    decay_ref[...] = decay
    weight_ref[...] = weight
    whole = jnp.exp(length * log_decay)
    jump = jnp.exp(GROUP * log_decay)
    carry = jnp.zeros_like(jump)
    for k in range(totals_ref.shape[0]):
        carry = jnp.where(k < spot_ref[2], whole * carry + totals_ref[k], carry)
    for b in range(blocks):
        rows = pl.ds(b * expand, expand)
        entry_ref[rows, :] = carry
        carry = jump * carry + ends_ref[rows, :]
    factors = [spread(decay_ref, j) for j in range(expand)]
    weights = [spread(weight_ref, j) for j in range(expand)]
    for g in range(0, blocks, SUB):

        def step(t, states):
            now = xs_ref[block_rows(g, t), :]
            states = tuple(f * s + now for f, s in zip(factors, states))
            smooth_ref[block_rows(g, t), :] = tree_sum([w * s for w, s in zip(weights, states)])
            return states

        start = tuple(entry_ref[state_rows(g, j, expand), :] for j in range(expand))
        lax.fori_loop(0, GROUP, step, start, unroll=8)
    for k in range(blocks):
        rows = pl.ds(pl.multiple_of((spot_ref[1] ^ k) * GROUP, GROUP), GROUP)
        pre = smooth_ref[rows, :] + omega_ref[...] * xs_ref[rows, :]
        sigma = jax.nn.sigmoid(pre)
        block = (pre * sigma).T.astype(jnp.bfloat16)
        if len(mixed_refs) == 1:
            mixed_refs[0][spot_ref[1] ^ k] = block
        else:
            mixed_refs[k][...] = block
        slope_ref[rows, :] = (sigma * (1.0 + pre * (1.0 - sigma))).astype(slope_ref.dtype)


def ema_mix(spot, xs, ends, params, omega, totals, apart, after=()):
    length, columns = xs.shape
    expand = params.shape[1]
    blocks = length // GROUP
    mixed = [(columns, GROUP)] * blocks if apart else [(blocks, columns, GROUP)]
    *found, slope, entry = launch(
        ema_mix_kernel,
        [(shape, jnp.bfloat16) for shape in mixed] + [(xs.shape, jnp.bfloat16), (ends.shape, f32)],
        (spot, xs, ends, params, omega, totals),
        [
            in_smem(), by_tile(xs.shape, 1), by_tile(ends.shape, 1), by_tile(params.shape, 2),
            by_tile(omega.shape, 1), by_tile(totals.shape, 2),
        ],
        [by_tile(shape, len(shape) - 2) for shape in mixed] + [by_tile(xs.shape, 1), by_tile(ends.shape, 1)],
        after=after,
        grid=(columns // LANES,),
        scratch=[
            pltpu.VMEM((expand, LANES), f32),
            pltpu.VMEM((expand, LANES), f32),
            pltpu.VMEM((length, LANES), f32),
        ],
        mib=5 * max(1, length // 1024),
        cost=work(4 * expand * length * columns, 10 * length * columns, length * columns),
    )
    return found, slope, entry


def ema_back_kernel(dmix_ref, slope_ref, params_ref, pull_ref, heads_ref, total_ref, decay_ref):
    length = slope_ref.shape[0]
    expand = params_ref.shape[1]
    blocks = length // GROUP
    decay, log_decay, _ = rates(params_ref)
    decay_ref[...] = decay
    for b in range(blocks):
        rows = pl.ds(b * GROUP, GROUP)
        pull_ref[rows, :] = dmix_ref[b].astype(f32).T * slope_ref[rows, :].astype(f32)
    factors = [spread(decay_ref, j) for j in range(expand)]
    for g in range(0, blocks, SUB):

        def step(t, states):
            now = pull_ref[block_rows(g, GROUP - 1 - t), :]
            return tuple(f * s + now for f, s in zip(factors, states))

        states = (jnp.zeros((SUB, LANES), f32),) * expand
        states = lax.fori_loop(0, GROUP, step, states, unroll=8)
        for j in range(expand):
            heads_ref[state_rows(g, j, expand), :] = states[j]
    jump = jnp.exp(GROUP * log_decay)
    carry = jnp.zeros_like(jump)
    for b in reversed(range(blocks)):
        carry = jump * carry + heads_ref[pl.ds(b * expand, expand), :]
    total_ref[...] = carry


def ema_back(dmix, slope, params, after=()):
    length, columns = slope.shape
    expand = params.shape[1]
    shapes = ((length, columns), (length // GROUP * expand, columns), (expand, columns))
    return launch(
        ema_back_kernel,
        [(shape, f32) for shape in shapes],
        (dmix, slope, params),
        [by_tile(dmix.shape, 1), by_tile(slope.shape, 1), by_tile(params.shape, 2)],
        [by_tile(shape, 1) for shape in shapes],
        after=after,
        grid=(columns // LANES,),
        scratch=[pltpu.VMEM((expand, LANES), f32)],
        mib=5 * max(1, length // 1024),
        cost=work(2 * expand * length * columns, 8 * length * columns),
    )


def enter_from_later(spot_ref, heads_ref, totals_ref, enter_ref, log_decay, length):
    expand = log_decay.shape[0]
    whole = jnp.exp(length * log_decay)
    jump = jnp.exp(GROUP * log_decay)
    carry = jnp.zeros_like(jump)
    for k in reversed(range(totals_ref.shape[0])):
        carry = jnp.where(k > spot_ref[2], whole * carry + totals_ref[k], carry)
    for b in reversed(range(length // GROUP)):
        rows = pl.ds(b * expand, expand)
        enter_ref[rows, :] = carry
        carry = jump * carry + heads_ref[rows, :]


def ema_finish_kernel(
    spot_ref, pull_ref, heads_ref, params_ref, omega_ref, totals_ref, direct_ref, result_ref,
    grad_ref, output_ref, decay_ref, weight_ref, enter_ref, smooth_ref,
):
    length = pull_ref.shape[0]
    expand = params_ref.shape[1]
    blocks = length // GROUP
    decay, log_decay, weight = rates(params_ref)
    decay_ref[...] = decay
    weight_ref[...] = weight
    enter_from_later(spot_ref, heads_ref, totals_ref, enter_ref, log_decay, length)
    factors = [spread(decay_ref, j) for j in range(expand)]
    weights = [spread(weight_ref, j) for j in range(expand)]
    for g in range(0, blocks, SUB):

        def step(t, states):
            now = pull_ref[block_rows(g, GROUP - 1 - t), :]
            states = tuple(f * s + now for f, s in zip(factors, states))
            back = tree_sum([w * s for w, s in zip(weights, states)])
            smooth_ref[block_rows(g, GROUP - 1 - t), :] = back
            return states

        start = tuple(enter_ref[state_rows(g, j, expand), :] for j in range(expand))
        lax.fori_loop(0, GROUP, step, start, unroll=8)
    for b in range(blocks):
        rows = pl.ds(b * GROUP, GROUP)
        back = smooth_ref[rows, :] + omega_ref[...] * pull_ref[rows, :]
        grad_ref[:, rows] = back.T + direct_ref[b, 0].astype(f32)
        output_ref[:, rows] = result_ref[b, 0]


def ema_finish(spot, pull, heads, params, omega, totals, joint, after=()):
    length, columns = pull.shape

    def part(which):
        return pl.BlockSpec((length // GROUP, 1, LANES, GROUP), lambda i: (0, which, i, 0))

    expand = params.shape[1]
    return launch(
        ema_finish_kernel,
        [((columns, length), f32), ((columns, length), joint.dtype)],
        (spot, pull, heads, params, omega, totals, joint, joint),
        [
            in_smem(), by_tile(pull.shape, 1), by_tile(heads.shape, 1), by_tile(params.shape, 2),
            by_tile(omega.shape, 1), by_tile(totals.shape, 2), part(0), part(1),
        ],
        [by_tile((columns, length), 0)] * 2,
        after=after,
        grid=(columns // LANES,),
        scratch=[
            pltpu.VMEM((expand, LANES), f32),
            pltpu.VMEM((expand, LANES), f32),
            pltpu.VMEM((heads.shape[0], LANES), f32),
            pltpu.VMEM((length, LANES), f32),
        ],
        mib=5 * max(1, length // 1024),
        cost=work(4 * expand * length * columns, 14 * length * columns),
    )


def ema_sums_kernel(spot_ref, xs_ref, pull_ref, entry_ref, heads_ref, totals_ref, params_ref, sums_ref, decay_ref, enter_ref):
    length = xs_ref.shape[0]
    expand = params_ref.shape[1]
    blocks = length // GROUP
    half = expand // 2
    decay, log_decay, _ = rates(params_ref)
    decay_ref[...] = decay
    enter_from_later(spot_ref, heads_ref, totals_ref, enter_ref, log_decay, length)
    for low in range(0, expand, half):
        factors = [spread(decay_ref, low + j) for j in range(half)]
        zero = (jnp.zeros((SUB, LANES), f32),) * half
        plain, turned = zero, zero
        for g in range(0, blocks, SUB):

            def step(t, held):
                states, slants, plain, turned = held
                now, pull = xs_ref[block_rows(g, t), :], pull_ref[block_rows(g, t), :]
                slants = tuple(f * p + s for f, p, s in zip(factors, slants, states))
                states = tuple(f * s + now for f, s in zip(factors, states))
                plain = tuple(a + pull * s for a, s in zip(plain, states))
                turned = tuple(a + pull * p for a, p in zip(turned, slants))
                return states, slants, plain, turned

            start = tuple(entry_ref[state_rows(g, low + j, expand), :] for j in range(half))
            held = (start, zero, plain, turned)
            _, slants, plain, turned = lax.fori_loop(0, GROUP, step, held, unroll=4)
            turned = tuple(
                a + f * p * enter_ref[state_rows(g, low + j, expand), :]
                for j, (a, f, p) in enumerate(zip(turned, factors, slants))
            )
        for j in range(half):
            sums_ref[pl.ds(low + j, 1), :] = jnp.sum(plain[j], axis=0, keepdims=True)
            sums_ref[pl.ds(expand + low + j, 1), :] = jnp.sum(turned[j], axis=0, keepdims=True)
    straight = jnp.zeros((SUB, LANES), f32)
    for b in range(0, length, SUB):
        straight = straight + xs_ref[pl.ds(b, SUB), :] * pull_ref[pl.ds(b, SUB), :]
    sums_ref[pl.ds(2 * expand, SUB), :] = straight


def ema_sums(spot, xs, pull, entry, heads, totals, params, after=()):
    length, columns = xs.shape
    expand = params.shape[1]
    shape = (2 * expand + SUB, columns)
    return launch(
        ema_sums_kernel,
        [(shape, f32)],
        (spot, xs, pull, entry, heads, totals, params),
        [
            in_smem(), by_tile(xs.shape, 1), by_tile(xs.shape, 1), by_tile(entry.shape, 1), by_tile(entry.shape, 1),
            by_tile(totals.shape, 2), by_tile(params.shape, 2),
        ],
        [by_tile(shape, 1)],
        after=after,
        grid=(columns // LANES,),
        scratch=[pltpu.VMEM((expand, LANES), f32), pltpu.VMEM((entry.shape[0], LANES), f32)],
        mib=5 * max(1, length // 1024),
        cost=work(8 * expand * length * columns, 8 * length * columns),
    )[0]


def pad_to_lanes(part, dim):
    extra = -part.shape[dim] % LANES
    if extra == 0:
        return part
    return jnp.pad(part, [(0, extra if k == dim else 0) for k in range(part.ndim)])


def ema_params(alpha, delta, beta, eta, count):
    packed = jnp.swapaxes(jnp.stack([alpha, delta, beta, eta]), 1, 2)
    return pad_to_lanes(jnp.tile(packed, (1, 1, count)), 2)


def ema_param_grads(total, alpha, delta, beta, eta, count):
    channels, expand = alpha.shape
    summed = jnp.sum(total[:, : count * channels].reshape(-1, count, channels), axis=1)
    plain, turned = summed[:expand].T, summed[expand : 2 * expand].T
    omega = jnp.sum(summed[2 * expand :], axis=0)
    rate, damp = jax.nn.sigmoid(alpha), jax.nn.sigmoid(delta)
    g_alpha = eta * beta * rate * (1.0 - rate) * (plain - damp * rate * turned)
    g_delta = -(eta * beta * rate * rate * damp * (1.0 - damp)) * turned
    return g_alpha, g_delta, rate * eta * plain, rate * beta * plain, omega


low = jnp.bfloat16
CHUNK = 256
MIB = (3, 11, 8, 5, 6, 8, 8, 6, 4, 4)
TABLE = 384


def nn(left, right):
    return jnp.dot(left, right, preferred_element_type=f32)


def nt(left, right):
    return lax.dot_general(left, right, (((1,), (1,)), ((), ())), preferred_element_type=f32)


def silu_pair(pre):
    sigma = jax.nn.sigmoid(pre)
    return pre * sigma, sigma * (1.0 + pre * (1.0 - sigma))


def each(width, body, size=CHUNK):
    for at in range(0, width, size):
        body(at)


def wide_block(ref, which, n):
    part = ref[:, which, n]
    return part.reshape(part.shape[0] * part.shape[1], part.shape[2])


def live_lanes(spot_ref, lengths_ref, n, shape):
    return spot_ref[0] + lax.broadcasted_iota(jnp.int32, shape, 1) < lengths_ref[n]


def span_of(ref, n):
    return pl.ds(n * GROUP, GROUP)


def call(kernel, outs, ins, smem=0, hbm=0, scratch=(), moved=1, mib=16, after=()):
    spaces = [pltpu.SMEM] * smem + [pl.ANY] * hbm + [pltpu.VMEM] * (len(ins) - smem - hbm)
    return launch(
        kernel,
        outs,
        ins,
        [pl.BlockSpec(memory_space=space) for space in spaces],
        [pl.BlockSpec(memory_space=pltpu.VMEM) for _ in outs],
        after=after,
        scratch=scratch,
        mib=mib,
        cost=pl.CostEstimate(flops=1, bytes_accessed=moved, transcendentals=0),
    )


def vectors(width, mwidth, vwidth, ff):
    sizes = (
        ("mix", mwidth), ("value", vwidth), ("out", width), ("gain", width),
        ("shift", width), ("up", ff), ("down", width),
    )
    place, at = {}, 0
    for name, size in sizes:
        place[name] = at
        at += size
    return place


def piece(ref, base, at, size):
    return ref[:, pl.ds(base + at, size)]


def value_kernel(base, w_ref, x_ref, vec_ref, rows_ref, values_ref, slope_ref, rows_t_ref):
    for n in range(x_ref.shape[2]):
        rows = pl.ds(n * GROUP, GROUP)
        block = wide_block(x_ref, 0, n)
        rows_t_ref[:, rows] = block
        rows_ref[rows, :] = block.T

    def chunk(at):
        cols = pl.ds(at, CHUNK)
        act, slope = silu_pair(nn(rows_ref[...], w_ref[:, cols]) + piece(vec_ref, base, at, CHUNK))
        values_ref[:, cols] = act.astype(low)
        slope_ref[:, cols] = slope.astype(low)

    each(w_ref.shape[1], chunk)


def value_part(x, w_value, vec, where, after=()):
    width, vwidth = w_value.shape
    count = x.shape[2] * GROUP
    return call(
        functools.partial(value_kernel, where["value"]),
        [((count, width), low), ((count, vwidth), low), ((count, vwidth), low), ((width, count), low)],
        (w_value, x, vec),
        mib=MIB[0],
        after=after,
    )


def forward_kernel(
    pieces, where, spot_ref, lengths_ref, wmix_ref, wout_ref, wup_ref, wdown_ref,
    x_ref, values_ref, vec_ref, qscale_ref, qshift_ref, *refs
):
    forward_rows(spot_ref, refs[:pieces], refs[pieces], refs[-6])
    forward_body(
        where, spot_ref, lengths_ref, wmix_ref, wout_ref, wup_ref, wdown_ref,
        x_ref, values_ref, vec_ref, qscale_ref, qshift_ref, *refs[pieces + 1 :]
    )


def forward_rows(spot_ref, mixed_refs, mixed_t_ref, m_ref):
    for k, ref in enumerate(mixed_refs):
        seqs, channels, _ = ref.shape
        at = pl.multiple_of((spot_ref[1] ^ k) * channels, 16) if len(mixed_refs) > 1 else 0
        for n in range(seqs):
            mixed_t_ref[pl.ds(at, channels), pl.ds(n * GROUP, GROUP)] = ref[n]
    for n in range(m_ref.shape[0] // GROUP):
        rows = pl.ds(n * GROUP, GROUP)
        m_ref[rows, :] = mixed_t_ref[:, rows].T


def forward_body(
    where, spot_ref, lengths_ref, wmix_ref, wout_ref, wup_ref, wdown_ref,
    x_ref, values_ref, vec_ref, qscale_ref, qshift_ref,
    out_ref, query_ref, key_ref, shared_ref, qslope_ref, probs_ref, reset_ref, turned_ref, gated_t_ref,
    hslope_ref, uslope_ref, keep_ref, unit_ref, rstd_ref, normed_t_ref, hidden_t_ref, fslope_ref,
    m_ref, update_ref, gated_ref, blend_ref, normed_ref, ffn_ref,
):
    width, vwidth = wout_ref.shape[1], wout_ref.shape[0]
    zwidth = qscale_ref.shape[1]
    seqs = x_ref.shape[0] // GROUP

    def mix(at, size=CHUNK):
        cols = pl.ds(at, size)
        return nn(m_ref[...], wmix_ref[:, cols]) + piece(vec_ref, where["mix"], at, size)

    shared, qslope = silu_pair(mix(width, zwidth))
    shared_ref[...] = shared
    qslope_ref[...] = qslope
    query_ref[...] = (shared * qscale_ref[pl.ds(0, 1), :] + qshift_ref[pl.ds(0, 1), :]).astype(low)
    key_ref[...] = (shared * qscale_ref[pl.ds(1, 1), :] + qshift_ref[pl.ds(1, 1), :]).astype(low)
    causal = lax.broadcasted_iota(jnp.int32, (GROUP, GROUP), 0) >= lax.broadcasted_iota(
        jnp.int32, (GROUP, GROUP), 1
    )
    for n in range(seqs):
        rows = pl.ds(n * GROUP, GROUP)
        scores = jnp.where(causal, nt(query_ref[rows, :], key_ref[rows, :]) * zwidth**-0.5, -1e30)
        scores = jnp.exp(scores - jnp.max(scores, axis=-1, keepdims=True))
        probs_ref[rows, :] = scores / jnp.sum(scores, axis=-1, keepdims=True)

    def gate(at):
        update_ref[:, pl.ds(at, CHUNK)] = jax.nn.sigmoid(mix(at))

    each(width, gate)

    def attend(at):
        cols = pl.ds(at, CHUNK)
        reset, slope = silu_pair(mix(width + zwidth + at))
        attended = jnp.concatenate(
            [
                nn(probs_ref[pl.ds(n * GROUP, GROUP), :].astype(low), values_ref[pl.ds(n * GROUP, GROUP), cols])
                for n in range(seqs)
            ],
            axis=0,
        )
        reset_ref[:, cols] = reset.astype(low)
        turned_ref[:, cols] = (attended * slope).astype(low)
        gated = (reset * attended).astype(low)
        gated_ref[:, cols] = gated
        gated_t_ref[cols, :] = gated.T

    each(vwidth, attend)

    def hide(at):
        cols = pl.ds(at, CHUNK)
        pre = mix(width + zwidth + vwidth + at)
        pre = pre + nn(gated_ref[...], wout_ref[:, cols]) + piece(vec_ref, where["out"], at, CHUNK)
        hidden, slope = silu_pair(pre)
        update = update_ref[:, cols]
        keep = 1.0 - update
        resid = x_ref[:, cols].astype(f32)
        hslope_ref[:, cols] = (update * slope).astype(low)
        uslope_ref[:, cols] = ((hidden - resid) * update * keep).astype(low)
        keep_ref[:, cols] = keep.astype(low)
        blend_ref[:, cols] = update * hidden + keep * resid

    each(width, hide)
    for n in range(seqs):
        rows = pl.ds(n * GROUP, GROUP)
        blend = blend_ref[rows, :]
        centered = blend - jnp.mean(blend, axis=-1, keepdims=True)
        rstd = lax.rsqrt(jnp.mean(centered * centered, axis=-1, keepdims=True) + 1e-05)
        unit = centered * rstd
        unit_ref[rows, :] = unit.astype(low)
        rstd_ref[rows, :] = jnp.broadcast_to(rstd, (GROUP, LANES))
        normed = unit * piece(vec_ref, where["gain"], 0, width) + piece(vec_ref, where["shift"], 0, width)
        blend_ref[rows, :] = normed
        normed_ref[rows, :] = normed.astype(low)
        normed_t_ref[:, rows] = normed.astype(low).T

    def lift(at):
        cols = pl.ds(at, CHUNK)
        act, slope = silu_pair(nn(normed_ref[...], wup_ref[:, cols]) + piece(vec_ref, where["up"], at, CHUNK))
        fslope_ref[:, cols] = slope.astype(low)
        act = act.astype(low)
        ffn_ref[:, cols] = act
        hidden_t_ref[cols, :] = act.T

    each(wup_ref.shape[1], lift)

    def drop(at):
        cols = pl.ds(at, CHUNK)
        blend_ref[:, cols] = blend_ref[:, cols] + nn(ffn_ref[...], wdown_ref[:, cols]) + piece(vec_ref, where["down"], at, CHUNK)

    each(width, drop)
    for n in range(seqs):
        result = blend_ref[pl.ds(n * GROUP, GROUP), :].astype(low).T
        result = jnp.where(live_lanes(spot_ref, lengths_ref, n, result.shape), result, jnp.zeros_like(result))
        out_ref[:, n] = result.reshape(out_ref.shape[0], out_ref.shape[2], GROUP)


def forward_part(spot, lengths, folded, mixed, x, values, w_mix, w_out, w_up, w_down, vec, where, qk_scale, qk_shift, after=()):
    vwidth, width = w_out.shape
    zwidth = qk_scale.shape[1]
    ff = w_up.shape[1]
    count = x.shape[0]
    narrow, wide = (count, width), (count, vwidth)
    outs = [
        ((width, count), low), (folded, low), ((count, zwidth), low), ((count, zwidth), low), ((count, zwidth), f32),
        ((count, zwidth), f32), ((count, GROUP), f32), (wide, low), (wide, low), ((vwidth, count), low),
        (narrow, low), (narrow, low), (narrow, low), (narrow, low), ((count, LANES), f32),
        ((width, count), low), ((ff, count), low), ((count, ff), low),
    ]
    scratch = [pltpu.VMEM(narrow, low), pltpu.VMEM(narrow, f32), pltpu.VMEM(wide, low)]
    scratch += [pltpu.VMEM(narrow, f32), pltpu.VMEM(narrow, low), pltpu.VMEM((count, ff), low)]
    macs = w_mix.size + w_out.size + w_up.size + w_down.size
    return call(
        functools.partial(forward_kernel, len(mixed), where),
        outs,
        (spot, lengths, w_mix, w_out, w_up, w_down, x, values, vec, qk_scale, qk_shift, *mixed),
        smem=2,
        mib=MIB[1],
        after=after,
        scratch=scratch,
    )


def column_sum(part):
    return jnp.sum(part.astype(f32), axis=0, keepdims=True)


def put(ref, row, value, columns):
    if isinstance(ref, tuple):
        lone = value.shape[0] // len(ref)
        for k, one in enumerate(ref):
            put(one, row, value[k * lone : (k + 1) * lone], columns)
        return
    if len(ref.shape) == 2:
        ref[...] = value
        return
    owners = ref.shape[0]
    lone = value.shape[0] // owners
    for owner in range(owners):
        part = value[owner * lone : (owner + 1) * lone]
        for i, at in enumerate(range(0, value.shape[1], columns)):
            ref[owner, pl.ds(row + i * lone, lone), :] = part[:, at : at + columns]


def split_product(side, keep_ref, send_ref, left, right_ref, half, columns, row=0):
    total = right_ref.shape[1]
    for ref, which in ((keep_ref, side), (send_ref, 1 - side)):
        base = which * (total - half)
        parts = []
        for at in range(0, half, CHUNK):
            cols = pl.ds(pl.multiple_of(base + at, 128), min(CHUNK, half - at))
            parts.append(nn(left, right_ref[:, cols]).astype(low))
        put(ref, row, jnp.concatenate(parts, axis=1), columns)


def split_narrow(side, keep_ref, send_ref, left_ref, right_ref):
    both = [nn(left_ref[pl.ds(at, CHUNK), :], right_ref[...]).astype(low) for at in range(0, left_ref.shape[0], CHUNK)]
    both = jnp.concatenate(both, axis=0)
    half = both.shape[1] // 2
    near, far = both[:, :half], both[:, half:]
    put(keep_ref, 0, jnp.where(side == 0, near, far), half)
    put(send_ref, 0, jnp.where(side == 0, far, near), half)


def pair_outs(tall, wide, owners, lines=0):
    if not owners:
        return [((tall[0], tall[1] // 2), low)] * 2 + [((wide[0], wide[1] // 2), low)] * 2
    rows = (tall[0] * tall[1] + wide[0] * wide[1]) // (tall[1] * owners) + lines
    return [((owners, rows, tall[1] // 2), low)] * 2


def back_ffn_kernel(
    spot_ref, lengths_ref, wdown_ref, grad_ref, hidden_t_ref, fslope_ref, normed_t_ref, *refs
):
    halves, (g_ref, dffn_ref, small_ref) = refs[:-3], refs[-3:]
    width, ff = g_ref.shape[1], wdown_ref.shape[0]
    for n in range(grad_ref.shape[2]):
        part = wide_block(grad_ref, 1, n)
        part = jnp.where(live_lanes(spot_ref, lengths_ref, n, part.shape), part, jnp.zeros_like(part))
        g_ref[pl.ds(n * GROUP, GROUP), :] = part.T
    small_ref[:, pl.ds(0, width)] = column_sum(g_ref[...])
    side = spot_ref[2] & 1
    split_narrow(side, halves[0], halves[1], hidden_t_ref, g_ref)

    def lift(at):
        part = pl.ds(at, CHUNK)
        pulled = (nt(g_ref[...], wdown_ref[part, :]) * fslope_ref[:, part].astype(f32)).astype(low)
        dffn_ref[:, part] = pulled
        small_ref[:, pl.ds(width + at, CHUNK)] = column_sum(pulled)

    each(ff, lift)
    tall = hidden_t_ref.shape[0] // halves[0].shape[0]
    split_product(side, halves[-2], halves[-1], normed_t_ref[...], dffn_ref, ff // 2, halves[-2].shape[-1], tall)
    if len(halves) == 2:
        for ref in halves:
            owners, rows, columns = ref.shape
            ref[:, pl.ds(2 * tall, rows - 2 * tall), :] = jnp.zeros((owners, rows - 2 * tall, columns), low)


def back_ffn(spot, lengths, owners, lines, grad, hidden_t, fslope, normed_t, w_down, after=()):
    ff, width = w_down.shape
    count = fslope.shape[0]
    outs = pair_outs((ff, width), (width, ff), owners, lines)
    outs += [((count, width), low), ((count, ff), low), ((1, width + ff), f32)]
    *halves, g, dffn, small = call(
        back_ffn_kernel,
        outs,
        (spot, lengths, w_down, grad, hidden_t, fslope, normed_t),
        smem=2,
        mib=MIB[2],
        after=after,
    )
    return halves, g, dffn, small


def back_norm_kernel(
    base, wup_ref, g_ref, dffn_ref, unit_ref, rstd_ref, vec_ref, hslope_ref, uslope_ref, kept_ref,
    dh_ref, du_ref, direct_ref, small_ref, dn_ref,
):
    width = wup_ref.shape[0]

    def drop(at):
        part = pl.ds(at, CHUNK)
        pulled = g_ref[:, part].astype(f32) + nt(dffn_ref[...], wup_ref[part, :])
        dn_ref[:, part] = pulled
        small_ref[:, part] = column_sum(pulled * unit_ref[:, part].astype(f32))
        small_ref[:, pl.ds(width + at, CHUNK)] = column_sum(pulled)

    each(width, drop)
    for n in range(g_ref.shape[0] // GROUP):
        rows = pl.ds(n * GROUP, GROUP)
        unit = unit_ref[rows, :].astype(f32)
        pulled = dn_ref[rows, :] * piece(vec_ref, base, 0, width)
        inner = jnp.mean(pulled * unit, axis=-1, keepdims=True)
        blend = pulled - jnp.mean(pulled, axis=-1, keepdims=True) - unit * inner
        blend = blend * rstd_ref[rows, :][:, :1]
        dh_ref[rows, :] = (blend * hslope_ref[rows, :].astype(f32)).astype(low)
        du_ref[rows, :] = (blend * uslope_ref[rows, :].astype(f32)).astype(low)
        direct_ref[rows, :] = (blend * kept_ref[rows, :].astype(f32)).astype(low)


def back_norm(g, dffn, unit, rstd, vec, where, hslope, uslope, kept, w_up, after=()):
    width = w_up.shape[0]
    narrow = g.shape
    return call(
        functools.partial(back_norm_kernel, where["gain"]),
        [(narrow, low)] * 3 + [((1, 2 * width), f32)],
        (w_up, g, dffn, unit, rstd, vec, hslope, uslope, kept),
        mib=MIB[3],
        after=after,
        scratch=[pltpu.VMEM(narrow, f32)],
    )


def back_attend_kernel(
    wout_ref, wmix_ref, wvalue_ref,
    dh_ref, du_ref, direct_ref, reset_ref, turned_ref, values_ref, vslope_ref, probs_ref,
    query_ref, key_ref, shared_ref, qslope_ref, qscale_ref, small_ffn_ref, small_norm_ref, result_ref,
    dmix_ref, dvalue_ref, mixed_ref, joint_ref,
    table_ref,
    datt_ref,
):
    vwidth, width = wout_ref.shape
    zwidth = qscale_ref.shape[1]
    count = dh_ref.shape[0]
    seqs = count // GROUP
    dmix_ref[:, pl.ds(0, width)] = du_ref[...]
    dmix_ref[:, pl.ds(width + zwidth + vwidth, width)] = dh_ref[...]

    def gate(at):
        part = pl.ds(at, CHUNK)
        pulled = nt(dh_ref[...], wout_ref[part, :])
        dmix_ref[:, pl.ds(width + zwidth + at, CHUNK)] = (
            pulled * turned_ref[:, part].astype(f32)
        ).astype(low)
        datt_ref[:, part] = (pulled * reset_ref[:, part].astype(f32)).astype(low)

    each(vwidth, gate)
    scale = zwidth**-0.5
    q_scale, k_scale = qscale_ref[pl.ds(0, 1), :], qscale_ref[pl.ds(1, 1), :]
    zero = jnp.zeros((1, zwidth), f32)
    sums = [zero, zero, zero, zero]
    for n in range(seqs):
        rows = pl.ds(n * GROUP, GROUP)
        probs = probs_ref[rows, :]
        pulled = nt(datt_ref[rows, :], values_ref[rows, :])
        pulled = probs * (pulled - jnp.sum(pulled * probs, axis=-1, keepdims=True))
        pulled = pulled.astype(low)
        d_query = nn(pulled, key_ref[rows, :]) * scale
        d_key = nn(pulled.T, query_ref[rows, :]) * scale
        probs_t = probs.astype(low).T
        shared = shared_ref[rows, :]
        found = (d_query * shared, d_key * shared, d_query, d_key)
        sums = [a + jnp.sum(b, axis=0, keepdims=True) for a, b in zip(sums, found)]
        dmix_ref[rows, pl.ds(width, zwidth)] = (
            (d_query * q_scale + d_key * k_scale) * qslope_ref[rows, :]
        ).astype(low)
        dvalue_ref[rows, :] = (nn(probs_t, datt_ref[rows, :]) * vslope_ref[rows, :].astype(f32)).astype(low)

    def turn(result):
        devices, _, channels, _ = mixed_ref.shape
        return result.astype(low).T.reshape(devices, channels, GROUP)

    for n in range(0, seqs, 2):
        result = nt(dmix_ref[pl.ds(n * GROUP, 2 * GROUP), :], wmix_ref[...])
        mixed_ref[:, n] = turn(result[:GROUP])
        mixed_ref[:, n + 1] = turn(result[GROUP:])
    for n in range(0, seqs, 2):
        rows = pl.ds(n * GROUP, 2 * GROUP)
        result = direct_ref[rows, :].astype(f32) + nt(dvalue_ref[rows, :], wvalue_ref[...])
        joint_ref[:, 0, n] = turn(result[:GROUP])
        joint_ref[:, 0, n + 1] = turn(result[GROUP:])
    joint_ref[:, 1] = result_ref[...]
    ff = small_ffn_ref.shape[1] - width
    found = (
        column_sum(dmix_ref[...]), column_sum(dvalue_ref[...]), column_sum(dh_ref[...]),
        sums[0], sums[1], sums[2], sums[3], small_norm_ref[:, :width], small_norm_ref[:, width:],
        small_ffn_ref[:, width:], small_ffn_ref[:, :width],
    )
    lines = []
    for part in found:
        for at in range(0, part.shape[1], TABLE):
            line = part[:, at : at + TABLE]
            lack = TABLE - line.shape[1]
            lines.append(line if lack == 0 else jnp.concatenate([line, jnp.zeros((1, lack), f32)], axis=1))
    lines.append(jnp.zeros((table_ref.shape[0] - len(lines), TABLE), f32))
    table_ref[...] = jnp.concatenate(lines, axis=0).astype(low)


def back_attend(dh, du, direct, reset, turned, values, vslope, probs, query, key, shared, qslope, qk_scale, small_ffn, small_norm, result, w_out, w_mix, w_value, after=()):
    vwidth, width = w_out.shape
    mwidth = w_mix.shape[1]
    count = dh.shape[0]
    outs = [((count, mwidth), low), ((count, vwidth), low)]
    outs += [(result.shape, low), (result.shape[:1] + (2,) + result.shape[1:], low), ((64, TABLE), low)]
    scratch = [pltpu.VMEM((count, vwidth), low)]
    macs = w_out.size + w_mix.size + w_value.size
    return call(
        back_attend_kernel,
        outs,
        (w_out, w_mix, w_value, dh, du, direct, reset, turned, values, vslope, probs, query, key, shared, qslope, qk_scale, small_ffn, small_norm, result),
        mib=MIB[4],
        after=after,
        scratch=scratch,
    )


def back_mid_kernel(spot_ref, gated_t_ref, dh_ref, x_t_ref, dvalue_ref, table_ref, *halves):
    side = spot_ref[2] & 1
    if len(halves) == 4:
        (kept, sent, wide_kept, wide_sent), tall = halves, 0
    else:
        kept, sent = halves[0], halves[1:]
        wide_kept, wide_sent, tall = kept, sent, gated_t_ref.shape[0] // kept.shape[0]
    split_narrow(side, kept, sent, gated_t_ref, dh_ref)
    split_product(
        side, wide_kept, wide_sent, x_t_ref[...], dvalue_ref, dvalue_ref.shape[1] // 2, wide_kept.shape[-1], tall
    )
    if len(halves) == 4:
        return
    lines = kept.shape[1] - 2 * tall
    high = table_ref.shape[0] // (2 * lines)
    for refs, which in (((kept,), side), (sent, 1 - side)):
        for ref in refs:
            for owner in range(ref.shape[0]):
                at = pl.multiple_of((2 * (owner % high) + which) * lines, 16)
                ref[owner, pl.ds(2 * tall, lines), :] = table_ref[pl.ds(at, lines), :]


def halved(outs):
    (kept, kind), (sent, _) = outs
    return [(kept, kind)] + [((sent[0] // 2,) + sent[1:], kind)] * 2


def back_mid(spot, owners, gated_t, dh, x_t, dvalue, table, lines, after=()):
    count, width = dh.shape
    vwidth = dvalue.shape[1]
    outs = pair_outs((vwidth, width), (width, vwidth), owners, lines)
    found = call(
        back_mid_kernel,
        halved(outs) if owners else outs,
        (spot, gated_t, dh, x_t, dvalue, table),
        smem=1,
        mib=MIB[5],
        after=after,
    )
    if owners:
        return [found[0]], [list(found[1:])]
    return [found[0], found[2]], [[found[1]], [found[3]]]


def back_mix_kernel(spot_ref, mixed_t_ref, dmix_ref, keep_ref, *send_refs):
    half = keep_ref.shape[-1]
    split_product(spot_ref[2] & 1, keep_ref, send_refs, mixed_t_ref[...], dmix_ref, half, half)


def back_mix_weight(spot, owners, mixed_t, dmix, after=()):
    mwidth = dmix.shape[1]
    width, count = mixed_t.shape
    half = -(-mwidth // 256) * 128
    outs = [((width, half), low)] * 2
    kept, *sent = call(
        back_mix_kernel,
        halved(outs) if owners else outs,
        (spot, mixed_t, dmix),
        smem=1,
        mib=MIB[6],
        after=after,
    )
    return [kept], [sent]


def halve_kernel(index, bit, spot_ref, kept_ref, *refs):
    arrived, (sent_ref, stay_ref) = refs[:-2], refs[-2:]
    outer, inner, _, _ = sent_ref.shape
    lone = outer // len(arrived)
    mine = (spot_ref[index] >> bit) & 1
    for ref, which in ((sent_ref, 1 - mine), (stay_ref, mine)):
        for a in range(outer):
            for b in range(inner):
                total = kept_ref[a, which, b].astype(f32) + arrived[a // lone][a % lone, which, b].astype(f32)
                ref[a, b] = total.astype(low)


def halve(spot, kept, arrived, index, bit, at, after=()):
    dims = kept.shape[:-2]
    outer, inner = 1 << at, 1 << (len(dims) - at - 1)
    block = kept.shape[-2:]

    def shaped(part):
        return part.reshape((-1, 2, inner) + block)

    sent, stay = call(
        functools.partial(halve_kernel, index, bit),
        [((outer, inner) + block, low)] * 2,
        (spot, shaped(kept), *map(shaped, arrived)),
        smem=1,
        mib=MIB[7],
        after=after,

    )
    rest = dims[:at] + dims[at + 1 :] + block
    return sent.reshape(rest), stay.reshape(rest)


def finish_pair_kernel(count, lines, spot_ref, *refs):
    shares, outs = refs[:count], refs[count:]
    tall_ref, wide_ref = outs[:2]
    columns = shares[0].shape[1]
    cut = tall_ref.shape[0] * 2 // len(shares)
    lone = wide_ref.shape[0] * 2 // len(shares)
    for k, ref in enumerate(shares):
        at = spot_ref[2] ^ k
        high, side = at >> 1, at & 1
        tall_ref[pl.ds(pl.multiple_of(high * cut, 8), cut), pl.ds(pl.multiple_of(side * columns, 128), columns)] = ref[
            pl.ds(0, cut), :
        ].astype(f32)
        runs = wide_ref.shape[1] // 2 // columns
        for run in range(runs):
            wide_ref[
                pl.ds(pl.multiple_of(high * lone, 8), lone),
                pl.ds(pl.multiple_of((side * runs + run) * columns, 128), columns),
            ] = ref[pl.ds(cut + run * lone, lone), :].astype(f32)
        if lines:
            outs[-1][pl.ds(pl.multiple_of(at * lines, 8), lines), :] = ref[pl.ds(2 * cut, lines), :].astype(f32)
    if lines:
        row = 0
        for ref in outs[2:-1]:
            if len(ref.shape) == 2:
                for k in range(ref.shape[0]):
                    ref[pl.ds(k, 1), :] = outs[-1][pl.ds(row, 1), :][:, : ref.shape[1]]
                    row += 1
                continue
            for at in range(0, ref.shape[0], columns):
                size = min(columns, ref.shape[0] - at)
                ref[pl.ds(at, size)] = outs[-1][row, :size]
                row += 1


def finish_pair(spot, shares, tall, wide, lines=0, vectors=(), after=()):
    outs = [(tall, f32), (wide, f32)] + [(shape, f32) for shape in vectors]
    count = len(shares)
    scratch = [pltpu.VMEM((count * lines, shares[0].shape[1]), f32)] if lines else []
    kernel = functools.partial(finish_pair_kernel, count, lines)
    return call(kernel, outs, (spot, *shares), smem=1, mib=MIB[8], scratch=scratch, after=after)


def finish_mix_kernel(spot_ref, *refs):
    shares, out_ref = refs[:-1], refs[-1]
    half, mwidth = shares[0].shape[1], out_ref.shape[1]
    common = 2 * half - mwidth
    lone = out_ref.shape[0] * 2 // len(shares)
    for k, ref in enumerate(shares):
        at = spot_ref[2] ^ k
        rows = pl.ds(pl.multiple_of((at >> 1) * lone, 8), lone)
        base = pl.multiple_of(common + (at & 1) * (mwidth - half), 128)
        out_ref[rows, pl.ds(base, half - common)] = ref[:, common:].astype(f32)
        if common:

            @pl.when(at & 1 == 0)
            def _():
                out_ref[rows, pl.ds(0, common)] = ref[:, :common].astype(f32)


def finish_mix(spot, shares, shape, after=()):
    return call(finish_mix_kernel, [(shape, f32)], (spot, *shares), smem=1, mib=MIB[9], after=after)[0]


Y_FIRST = (("tok", 1), ("ch", 0))
Y_THEN_Z = (("tok", 1), ("ch", 1), ("ch", 0))
X_FIRST = (("ch", 0), ("tok", 1))


def bits_of(axis):
    return lax.axis_size(axis).bit_length() - 1


def across(part, axis, turn):
    return lax.ppermute(part, axis, [(i, i ^ turn) for i in range(lax.axis_size(axis))])


def exchange(part, axis, bit):
    return across(part, axis, 1 << bit)


def side_of(axis, bit):
    return (lax.axis_index(axis) >> bit) & 1


def by_owner(grad):
    dims = (2,) * (bits_of("ch") + bits_of("tok") - 1)
    return grad.reshape(dims + (-1, grad.shape[-1]))


def fold(part, columns):
    runs = [part[..., at : at + columns] for at in range(0, part.shape[-1], columns)]
    return jnp.concatenate(runs, axis=-2)


def add(left, right):
    return (left.astype(f32) + right.astype(f32)).astype(low)


def plain_halve(kept, arrived, mine, at):
    columns = min(part.shape[-1] for part in kept)

    def pick(which):
        def one(part):
            return lax.dynamic_index_in_dim(part, which, at, keepdims=False)

        return jnp.concatenate([fold(add(one(a), one(b)), columns) for a, b in zip(kept, arrived)], axis=-2)

    return pick(1 - mine), pick(mine)


class Sum:
    def __init__(self, spot, kept, sent, order):
        self.spot = spot
        self.names = [("ch", k) for k in reversed(range(bits_of("ch")))]
        self.names += [("tok", k) for k in reversed(range(1, bits_of("tok")))]
        self.stages = list(order) + [name for name in reversed(self.names) if name not in order]
        self.kept = [by_owner(part) for part in kept]
        arrived = [[exchange(piece, "tok", 0) for piece in part] for part in sent]
        self.arrived = arrived[0] if self.by_kernel() else [by_owner(part) for part, in arrived]

    def by_kernel(self):
        return len(self.kept) == 1 and self.kept[0].shape[-2] % 16 == 0

    def step(self, after=()):
        axis, bit = self.stages.pop(0)
        at = self.names.index((axis, bit))
        self.names.remove((axis, bit))
        if self.by_kernel():
            index = 1 if axis == "ch" else 2
            sent, stay = halve(self.spot, self.kept[0], self.arrived, index, bit, at, after)
        else:
            sent, stay = plain_halve(self.kept, self.arrived, side_of(axis, bit), at)
        self.kept, self.arrived = [stay], [exchange(sent, axis, bit)]
        return stay

    def shares(self):
        found = [add(self.kept[0], self.arrived[0])]
        for bit in reversed(range(1, bits_of("tok"))):
            found += [exchange(part, "tok", bit) for part in found]
        lower = [exchange(part, "tok", 0) for part in found]
        size = bits_of("tok") - 1
        order = [sum(((k >> (size - 1 - i)) & 1) << i for i in range(size)) for k in range(len(found))]
        found = [part for k in order for part in (found[k], lower[k])]
        return found


def in_order(shares, place):
    bit = 1
    while bit < len(shares):
        swapped = (place & bit) != 0
        shares = [jnp.where(swapped, shares[k ^ bit], shares[k]) for k in range(len(shares))]
        bit *= 2
    return jnp.stack(shares)


def plain_pair(place, shares, tall, wide):
    whole = in_order(shares, place).astype(f32)
    high = len(shares) // 2
    cut, lone = tall[0] // high, wide[0] // high
    whole = whole.reshape((high, 2) + whole.shape[1:])
    first = whole[:, :, :cut].transpose(0, 2, 1, 3).reshape(tall)
    second = whole[:, :, cut:].reshape(high, 2, -1, lone, whole.shape[-1])
    return first, second.transpose(0, 3, 1, 2, 4).reshape(wide)


def plain_mix(place, shares, shape):
    whole = in_order(shares, place).astype(f32)
    half = whole.shape[-1]
    whole = whole.reshape((len(shares) // 2, 2) + whole.shape[1:])
    whole = jnp.concatenate([whole[:, 0], whole[:, 1, :, 2 * half - shape[1] :]], axis=-1)
    return whole.reshape(shape)


def sum_tok(part):
    for bit in range(bits_of("tok")):
        part = part + exchange(part, "tok", bit)
    return part


def swap(parts):
    return lax.all_to_all(parts, "ch", split_axis=0, concat_axis=0, tiled=True)


def folded(parts):
    devices, channels, span = parts.shape[0], parts.shape[-2], parts.shape[-1]
    if channels % 16 == 0:
        return parts
    return jnp.moveaxis(parts, 0, -3).reshape((1,) + parts.shape[1:-2] + (devices * channels, span))


def unfolded(parts, devices):
    if parts.shape[0] == devices:
        return parts
    channels, span = parts.shape[-2] // devices, parts.shape[-1]
    return jnp.moveaxis(parts.reshape(parts.shape[1:-2] + (devices, channels, span)), -3, 0)


def local(
    inputs,
    out_grad,
    seq_lengths,
    ema_alpha,
    ema_delta,
    ema_beta,
    ema_eta,
    ema_omega,
    w_mix,
    b_mix,
    w_value,
    b_value,
    w_out,
    b_out,
    qk_scale,
    qk_shift,
    ln_gain,
    ln_bias,
    w_up,
    b_up,
    w_down,
    b_down,
):
    count, channels, local_len = inputs.shape
    width, mwidth = w_mix.shape
    vwidth, ff = w_value.shape[1], w_up.shape[1]
    devices, tok_size = lax.axis_size("ch"), lax.axis_size("tok")
    columns = count * channels
    span = local_len // devices
    tok_index = lax.axis_index("tok").astype(jnp.int32)
    ch_index = lax.axis_index("ch").astype(jnp.int32)
    spot = jnp.stack([tok_index * local_len + ch_index * span, ch_index, tok_index])
    apart = devices <= 8 and channels % 16 == 0

    def by_column(parts):
        whole = unfolded(parts, devices)
        return pad_to_lanes(whole.reshape(whole.shape[:-3] + (columns, span)), whole.ndim - 3)

    where = vectors(width, mwidth, vwidth, ff)
    vec = jnp.concatenate([b_mix, b_value, b_out, ln_gain, ln_bias, b_up, b_down])[None]
    params = ema_params(ema_alpha, ema_delta, ema_beta, ema_eta, count)
    omega = pad_to_lanes(jnp.tile(ema_omega, count)[None], 1)

    flat = inputs.reshape(columns, local_len)
    raw = by_blocks(spot, flat, out_grad.reshape(columns, local_len))
    raw = folded(swap(raw.reshape(devices, 2, count, channels, span)))
    xs, ends, total = ema_ends(pad_to_lanes(flat, 0), params)
    totals = lax.all_gather(total, "tok")
    mixed, slope, entry = ema_mix(spot, xs, ends, params, omega, totals, apart)
    if apart:
        mixed = [part.reshape(count, channels, span) for part in mixed]
        mixed = [part if k == 0 else across(part, "ch", k) for k, part in enumerate(mixed)]
    else:
        mixed = folded(swap(mixed[0][:, :columns].reshape(devices, count, channels, span)))
        mixed = [mixed[0]] if mixed.shape[0] == 1 else [mixed.transpose(1, 0, 2, 3).reshape(count, width, span)]
    x, values, vslope, x_t = value_part(raw, w_value, vec, where, (entry,))
    (
        mixed_t, result, query, key, shared, qslope, probs, reset, turned, gated_t,
        hslope, uslope, keep, unit, rstd, normed_t, hidden_t, fslope,
    ) = forward_part(
        spot, seq_lengths, raw.shape[:1] + raw.shape[2:], mixed, x, values, w_mix, w_out, w_up, w_down, vec,
        where, qk_scale, qk_shift,
    )
    owners = devices * tok_size // 2
    joined = owners if width // owners % 16 == 0 else 0
    lines = 64 // tok_size
    halves, g, dffn, small_ffn = back_ffn(
        spot, seq_lengths, joined, lines, raw, hidden_t, fslope, normed_t, w_down
    )
    ffn = Sum(spot, halves[::2], [[part] for part in halves[1::2]], Y_THEN_Z)
    dh, du, direct, small_norm = back_norm(g, dffn, unit, rstd, vec, where, hslope, uslope, keep, w_up)
    last = ffn.step((small_norm,))
    dmix, dvalue, back_mix, joint, table = back_attend(
        dh, du, direct, reset, turned, values, vslope, probs, query, key, shared, qslope,
        qk_scale, small_ffn, small_norm, result, w_out, w_mix, w_value, (last,),
    )
    kept, sent = back_mix_weight(spot, joined, mixed_t, dmix, (table,))
    mix = Sum(spot, kept, sent, X_FIRST)
    kept, sent = back_mid(spot, joined, gated_t, dh, x_t, dvalue, table, lines, (kept[0],))
    last = kept[0]
    back_mix = swap(unfolded(back_mix, devices))
    if not joined:
        table = table.reshape(tok_size // 2, 2, lines, TABLE)
        for group, which in ((kept, side_of("tok", 0)), (sent, 1 - side_of("tok", 0))):
            part = lax.dynamic_index_in_dim(table, which, 1, keepdims=False)
            part = jnp.broadcast_to(part[None], (devices,) + part.shape).reshape(-1, TABLE)
            group.append(part if group is kept else [part])
    mid = Sum(spot, kept, sent, Y_FIRST)
    last = ffn.step((last,))
    last = mix.step((last,))
    last = mid.step((last,))
    joint, back_mix, _ = lax.optimization_barrier((unfolded(joint, devices), back_mix, last))
    joint = swap(joint)
    pull, heads, total = ema_back(by_column(back_mix), slope, params, (last,))
    totals = lax.all_gather(total, "tok")
    last = mix.step((totals,))
    last = mid.step((last,))
    sums = ema_sums(spot, xs, pull, entry, heads, totals, params, (last,))
    last = mix.step((sums,))
    last = mid.step((last,))
    last = ffn.step((last,))
    last = mix.step((last,))
    while len(mid.stages) + len(mix.stages) + len(ffn.stages):
        for group in (mid, ffn, mix):
            last = group.step((last,)) if group.stages else last
    input_grad, output = ema_finish(spot, pull, heads, params, omega, totals, by_column(joint), (last,))
    ema_grads = ema_param_grads(sum_tok(sums), ema_alpha, ema_delta, ema_beta, ema_eta, count)
    mix.arrived[0], output, ema_grads = lax.optimization_barrier((mix.arrived[0], output, ema_grads))
    last = output
    input_grad = input_grad[:columns].reshape(inputs.shape)
    output = output[:columns].reshape(inputs.shape)

    tall, wide = (vwidth // devices, width), (width // devices, vwidth)
    shares = mid.shares()
    half = qk_scale.shape[1]
    across_mix = (width // devices, mwidth)
    if joined:
        vectors_of = [(mwidth,), (vwidth,), (width,), qk_scale.shape, qk_scale.shape, (width,), (width,), (ff,), (width,)]
        g_down, g_up = finish_pair(spot, ffn.shares(), tall, wide, after=(last,))
        g_out, g_value, *found = finish_pair(spot, shares, tall, wide, lines, vectors_of, (last,))
        g_mix = finish_mix(spot, mix.shares(), across_mix, (last,))
    else:
        table = in_order([part[-lines:] for part in shares], tok_index).astype(f32).reshape(-1)
        shares = [part[:-lines] for part in shares]
        g_out, g_value = plain_pair(tok_index, shares, tall, wide)
        g_down, g_up = plain_pair(tok_index, ffn.shares(), tall, wide)
        g_mix = plain_mix(tok_index, mix.shares(), across_mix)
        found, at = [], 0
        for size in (mwidth, vwidth, width, half, half, half, half, width, width, ff, width):
            found.append(table[at : at + size])
            at += -(-size // TABLE) * TABLE
        found = found[:3] + [jnp.stack(found[3:5]), jnp.stack(found[5:7])] + found[7:]
    g_bmix, g_bvalue, g_bout, g_qscale, g_qshift, g_gain, g_lnbias, g_bup, g_bdown = found
    return (
        output,
        input_grad,
        *ema_grads,
        g_mix,
        g_bmix,
        g_value,
        g_bvalue,
        g_out,
        g_bout,
        g_qscale,
        g_qshift,
        g_gain,
        g_lnbias,
        g_up,
        g_bup,
        g_down,
        g_bdown,
    )


def solution(mesh):
    by_ch = P("ch", None)
    placed = P(None, "ch", "tok")
    return jax.shard_map(
        local,
        mesh=mesh,
        in_specs=(placed, placed, P()) + (by_ch,) * 4 + (P("ch"),) + (P(),) * 14,
        out_specs=(
            (placed, placed)
            + (by_ch,) * 4
            + (P("ch"), by_ch, P(), by_ch, P(), by_ch)
            + (P(),) * 5
            + (by_ch, P(), by_ch, P())
        ),
        check_vma=False,
    )
```

```python
import functools
import jax
import jax.numpy as jnp
from jax import lax
from jax.experimental import pallas as pl
from jax.experimental.pallas import tpu as pltpu
from jax.sharding import PartitionSpec as P

GROUP = 128
SUB = 8
LANES = 128
f32 = jnp.float32


def by_tile(shape, dim):
    block = tuple(LANES if k == dim else size for k, size in enumerate(shape))
    return pl.BlockSpec(block, lambda i: tuple(i if k == dim else 0 for k in range(len(shape))))


def in_smem():
    return pl.BlockSpec(memory_space=pltpu.SMEM)


def roomy(mib=5):
    return pltpu.CompilerParams(vmem_limit_bytes=mib * 1024 * 1024)


def work(flops, moved, exps=0):
    return pl.CostEstimate(flops=1, bytes_accessed=1, transcendentals=0)


def launch(kernel, outs, ins, in_specs, out_specs, after=(), grid=(), scratch=(), mib=5, cost=None):
    count = len(ins)

    def run(*refs):
        kernel(*refs[:count], *refs[count + len(after) :])

    return pl.pallas_call(
        run,
        grid=grid,
        out_shape=tuple(jax.ShapeDtypeStruct(shape, kind) for shape, kind in outs),
        in_specs=list(in_specs) + [pl.BlockSpec(memory_space=pl.ANY)] * len(after),
        out_specs=tuple(out_specs),
        scratch_shapes=list(scratch),
        compiler_params=roomy(mib),
        cost_estimate=cost,
    )(*ins, *after)


def rates(params_ref):
    rate = jax.nn.sigmoid(params_ref[0])
    drop = rate * jax.nn.sigmoid(params_ref[1])
    weight = params_ref[3] * rate * params_ref[2]
    return 1.0 - drop, jnp.log1p(-drop), weight


def spread(ref, j):
    return jnp.broadcast_to(ref[pl.ds(j, 1), :], (SUB, LANES))


def tree_sum(parts):
    while len(parts) > 1:
        parts = [a + b for a, b in zip(parts[::2], parts[1::2])] + parts[len(parts) & ~1 :]
    return parts[0]


def block_rows(g, t):
    return pl.ds(g * GROUP + t, SUB, stride=GROUP)


def state_rows(g, j, expand):
    return pl.ds(g * expand + j, SUB, stride=expand)


def blocks_kernel(spot_ref, first_ref, second_ref, blocks_ref, near_ref, far_ref, sems):
    side = spot_ref[1] & 1
    copies = []
    for b in range(blocks_ref.shape[0]):
        cols = pl.ds(b * GROUP, GROUP)
        copies.append(pltpu.make_async_copy(first_ref.at[:, cols], blocks_ref.at[b], sems.at[b]))
    for z in range(near_ref.shape[0]):
        for k, (ref, which) in enumerate(((near_ref, side), (far_ref, 1 - side))):
            cols = pl.ds(pl.multiple_of((2 * z + which) * GROUP, GROUP), GROUP)
            at = blocks_ref.shape[0] + 2 * z + k
            copies.append(pltpu.make_async_copy(second_ref.at[:, cols], ref.at[z], sems.at[at]))
    for copy in copies:
        copy.start()
    for copy in copies:
        copy.wait()


def by_blocks(spot, first, second):
    columns, length = first.shape
    blocks = length // GROUP
    half = (blocks // 2, columns, GROUP)
    anywhere = pl.BlockSpec(memory_space=pltpu.HBM)
    return launch(
        blocks_kernel,
        [((blocks, columns, GROUP), first.dtype), (half, first.dtype), (half, first.dtype)],
        (spot, first, second),
        [in_smem(), anywhere, anywhere],
        [anywhere] * 3,
        scratch=[pltpu.SemaphoreType.DMA((2 * blocks,))],
        mib=1,
    )


def pairs_kernel(spot_ref, near_ref, arrived_ref, *refs):
    side, place = spot_ref[1] & 1, spot_ref[1] >> 1
    for k, ref in enumerate(refs):
        ref[side] = near_ref[place ^ k]
        ref[1 - side] = arrived_ref[place ^ k]


def by_partner(spot, near, arrived, after=()):
    high, columns, _ = near.shape
    whole = pl.BlockSpec(memory_space=pltpu.VMEM)
    outs = [((2, columns, GROUP), near.dtype)] * high
    return launch(pairs_kernel, outs, (spot, near, arrived), [in_smem(), whole, whole], [whole] * high, after=after, mib=4)


def ema_ends_kernel(x_ref, params_ref, xs_ref, ends_ref, total_ref, decay_ref):
    length = x_ref.shape[1]
    expand = params_ref.shape[1]
    blocks = length // GROUP
    decay, log_decay, _ = rates(params_ref)
    decay_ref[...] = decay
    for b in range(blocks):
        rows = pl.ds(b * GROUP, GROUP)
        xs_ref[rows, :] = x_ref[:, rows].astype(f32).T
    factors = [spread(decay_ref, j) for j in range(expand)]
    for g in range(0, blocks, SUB):

        def step(t, states):
            now = xs_ref[block_rows(g, t), :]
            return tuple(f * s + now for f, s in zip(factors, states))

        states = (jnp.zeros((SUB, LANES), f32),) * expand
        states = lax.fori_loop(0, GROUP, step, states, unroll=8)
        for j in range(expand):
            ends_ref[state_rows(g, j, expand), :] = states[j]
    jump = jnp.exp(GROUP * log_decay)
    carry = jnp.zeros_like(jump)
    for b in range(blocks):
        carry = jump * carry + ends_ref[pl.ds(b * expand, expand), :]
    total_ref[...] = carry


def ema_ends(x, params, after=()):
    columns, length = x.shape
    expand = params.shape[1]
    shapes = ((length, columns), (length // GROUP * expand, columns), (expand, columns))
    return launch(
        ema_ends_kernel,
        [(shape, f32) for shape in shapes],
        (x, params),
        [by_tile(x.shape, 0), by_tile(params.shape, 2)],
        [by_tile(shape, 1) for shape in shapes],
        after=after,
        grid=(columns // LANES,),
        scratch=[pltpu.VMEM((expand, LANES), f32)],
        mib=5 * max(1, length // 1024),
        cost=work(2 * expand * length * columns, 6 * length * columns),
    )


def ema_mix_kernel(
    spot_ref, xs_ref, ends_ref, params_ref, omega_ref, totals_ref, *refs
):
    mixed_refs, (slope_ref, entry_ref, decay_ref, weight_ref, smooth_ref) = refs[:-5], refs[-5:]
    length = xs_ref.shape[0]
    expand = params_ref.shape[1]
    blocks = length // GROUP
    decay, log_decay, weight = rates(params_ref)
    decay_ref[...] = decay
    weight_ref[...] = weight
    whole = jnp.exp(length * log_decay)
    jump = jnp.exp(GROUP * log_decay)
    carry = jnp.zeros_like(jump)
    for k in range(totals_ref.shape[0]):
        carry = jnp.where(k < spot_ref[2], whole * carry + totals_ref[k], carry)
    for b in range(blocks):
        rows = pl.ds(b * expand, expand)
        entry_ref[rows, :] = carry
        carry = jump * carry + ends_ref[rows, :]
    factors = [spread(decay_ref, j) for j in range(expand)]
    weights = [spread(weight_ref, j) for j in range(expand)]
    for g in range(0, blocks, SUB):

        def step(t, states):
            now = xs_ref[block_rows(g, t), :]
            states = tuple(f * s + now for f, s in zip(factors, states))
            smooth_ref[block_rows(g, t), :] = tree_sum([w * s for w, s in zip(weights, states)])
            return states

        start = tuple(entry_ref[state_rows(g, j, expand), :] for j in range(expand))
        lax.fori_loop(0, GROUP, step, start, unroll=8)
    for k in range(blocks):
        rows = pl.ds(pl.multiple_of((spot_ref[1] ^ k) * GROUP, GROUP), GROUP)
        pre = smooth_ref[rows, :] + omega_ref[...] * xs_ref[rows, :]
        sigma = jax.nn.sigmoid(pre)
        block = (pre * sigma).T.astype(jnp.bfloat16)
        if len(mixed_refs) == 1:
            mixed_refs[0][spot_ref[1] ^ k] = block
        else:
            mixed_refs[k][...] = block
        slope_ref[rows, :] = (sigma * (1.0 + pre * (1.0 - sigma))).astype(slope_ref.dtype)


def ema_mix(spot, xs, ends, params, omega, totals, apart, after=()):
    length, columns = xs.shape
    expand = params.shape[1]
    blocks = length // GROUP
    mixed = [(columns, GROUP)] * blocks if apart else [(blocks, columns, GROUP)]
    *found, slope, entry = launch(
        ema_mix_kernel,
        [(shape, jnp.bfloat16) for shape in mixed] + [(xs.shape, jnp.bfloat16), (ends.shape, f32)],
        (spot, xs, ends, params, omega, totals),
        [
            in_smem(), by_tile(xs.shape, 1), by_tile(ends.shape, 1), by_tile(params.shape, 2),
            by_tile(omega.shape, 1), by_tile(totals.shape, 2),
        ],
        [by_tile(shape, len(shape) - 2) for shape in mixed] + [by_tile(xs.shape, 1), by_tile(ends.shape, 1)],
        after=after,
        grid=(columns // LANES,),
        scratch=[
            pltpu.VMEM((expand, LANES), f32),
            pltpu.VMEM((expand, LANES), f32),
            pltpu.VMEM((length, LANES), f32),
        ],
        mib=5 * max(1, length // 1024),
        cost=work(4 * expand * length * columns, 10 * length * columns, length * columns),
    )
    return found, slope, entry


def ema_back_kernel(dmix_ref, slope_ref, params_ref, pull_ref, heads_ref, total_ref, decay_ref):
    length = slope_ref.shape[0]
    expand = params_ref.shape[1]
    blocks = length // GROUP
    decay, log_decay, _ = rates(params_ref)
    decay_ref[...] = decay
    for b in range(blocks):
        rows = pl.ds(b * GROUP, GROUP)
        pull_ref[rows, :] = dmix_ref[b].astype(f32).T * slope_ref[rows, :].astype(f32)
    factors = [spread(decay_ref, j) for j in range(expand)]
    for g in range(0, blocks, SUB):

        def step(t, states):
            now = pull_ref[block_rows(g, GROUP - 1 - t), :]
            return tuple(f * s + now for f, s in zip(factors, states))

        states = (jnp.zeros((SUB, LANES), f32),) * expand
        states = lax.fori_loop(0, GROUP, step, states, unroll=8)
        for j in range(expand):
            heads_ref[state_rows(g, j, expand), :] = states[j]
    jump = jnp.exp(GROUP * log_decay)
    carry = jnp.zeros_like(jump)
    for b in reversed(range(blocks)):
        carry = jump * carry + heads_ref[pl.ds(b * expand, expand), :]
    total_ref[...] = carry


def ema_back(dmix, slope, params, after=()):
    length, columns = slope.shape
    expand = params.shape[1]
    shapes = ((length, columns), (length // GROUP * expand, columns), (expand, columns))
    return launch(
        ema_back_kernel,
        [(shape, f32) for shape in shapes],
        (dmix, slope, params),
        [by_tile(dmix.shape, 1), by_tile(slope.shape, 1), by_tile(params.shape, 2)],
        [by_tile(shape, 1) for shape in shapes],
        after=after,
        grid=(columns // LANES,),
        scratch=[pltpu.VMEM((expand, LANES), f32)],
        mib=5 * max(1, length // 1024),
        cost=work(2 * expand * length * columns, 8 * length * columns),
    )


def enter_from_later(spot_ref, heads_ref, totals_ref, enter_ref, log_decay, length):
    expand = log_decay.shape[0]
    whole = jnp.exp(length * log_decay)
    jump = jnp.exp(GROUP * log_decay)
    carry = jnp.zeros_like(jump)
    for k in reversed(range(totals_ref.shape[0])):
        carry = jnp.where(k > spot_ref[2], whole * carry + totals_ref[k], carry)
    for b in reversed(range(length // GROUP)):
        rows = pl.ds(b * expand, expand)
        enter_ref[rows, :] = carry
        carry = jump * carry + heads_ref[rows, :]


def ema_finish_kernel(
    spot_ref, pull_ref, heads_ref, params_ref, omega_ref, totals_ref, direct_ref, result_ref,
    grad_ref, output_ref, decay_ref, weight_ref, enter_ref, smooth_ref,
):
    length = pull_ref.shape[0]
    expand = params_ref.shape[1]
    blocks = length // GROUP
    decay, log_decay, weight = rates(params_ref)
    decay_ref[...] = decay
    weight_ref[...] = weight
    enter_from_later(spot_ref, heads_ref, totals_ref, enter_ref, log_decay, length)
    factors = [spread(decay_ref, j) for j in range(expand)]
    weights = [spread(weight_ref, j) for j in range(expand)]
    for g in range(0, blocks, SUB):

        def step(t, states):
            now = pull_ref[block_rows(g, GROUP - 1 - t), :]
            states = tuple(f * s + now for f, s in zip(factors, states))
            back = tree_sum([w * s for w, s in zip(weights, states)])
            smooth_ref[block_rows(g, GROUP - 1 - t), :] = back
            return states

        start = tuple(enter_ref[state_rows(g, j, expand), :] for j in range(expand))
        lax.fori_loop(0, GROUP, step, start, unroll=8)
    for b in range(blocks):
        rows = pl.ds(b * GROUP, GROUP)
        back = smooth_ref[rows, :] + omega_ref[...] * pull_ref[rows, :]
        grad_ref[:, rows] = back.T + direct_ref[b, 0].astype(f32)
        output_ref[:, rows] = result_ref[b, 0]


def ema_finish(spot, pull, heads, params, omega, totals, joint, after=()):
    length, columns = pull.shape

    def part(which):
        return pl.BlockSpec((length // GROUP, 1, LANES, GROUP), lambda i: (0, which, i, 0))

    expand = params.shape[1]
    return launch(
        ema_finish_kernel,
        [((columns, length), f32), ((columns, length), joint.dtype)],
        (spot, pull, heads, params, omega, totals, joint, joint),
        [
            in_smem(), by_tile(pull.shape, 1), by_tile(heads.shape, 1), by_tile(params.shape, 2),
            by_tile(omega.shape, 1), by_tile(totals.shape, 2), part(0), part(1),
        ],
        [by_tile((columns, length), 0)] * 2,
        after=after,
        grid=(columns // LANES,),
        scratch=[
            pltpu.VMEM((expand, LANES), f32),
            pltpu.VMEM((expand, LANES), f32),
            pltpu.VMEM((heads.shape[0], LANES), f32),
            pltpu.VMEM((length, LANES), f32),
        ],
        mib=5 * max(1, length // 1024),
        cost=work(4 * expand * length * columns, 14 * length * columns),
    )


def ema_sums_kernel(spot_ref, xs_ref, pull_ref, entry_ref, heads_ref, totals_ref, params_ref, sums_ref, decay_ref, enter_ref):
    length = xs_ref.shape[0]
    expand = params_ref.shape[1]
    blocks = length // GROUP
    half = expand // 2
    decay, log_decay, _ = rates(params_ref)
    decay_ref[...] = decay
    enter_from_later(spot_ref, heads_ref, totals_ref, enter_ref, log_decay, length)
    for low in range(0, expand, half):
        factors = [spread(decay_ref, low + j) for j in range(half)]
        zero = (jnp.zeros((SUB, LANES), f32),) * half
        plain, turned = zero, zero
        for g in range(0, blocks, SUB):

            def step(t, held):
                states, slants, plain, turned = held
                now, pull = xs_ref[block_rows(g, t), :], pull_ref[block_rows(g, t), :]
                slants = tuple(f * p + s for f, p, s in zip(factors, slants, states))
                states = tuple(f * s + now for f, s in zip(factors, states))
                plain = tuple(a + pull * s for a, s in zip(plain, states))
                turned = tuple(a + pull * p for a, p in zip(turned, slants))
                return states, slants, plain, turned

            start = tuple(entry_ref[state_rows(g, low + j, expand), :] for j in range(half))
            held = (start, zero, plain, turned)
            _, slants, plain, turned = lax.fori_loop(0, GROUP, step, held, unroll=4)
            turned = tuple(
                a + f * p * enter_ref[state_rows(g, low + j, expand), :]
                for j, (a, f, p) in enumerate(zip(turned, factors, slants))
            )
        for j in range(half):
            sums_ref[pl.ds(low + j, 1), :] = jnp.sum(plain[j], axis=0, keepdims=True)
            sums_ref[pl.ds(expand + low + j, 1), :] = jnp.sum(turned[j], axis=0, keepdims=True)
    straight = jnp.zeros((SUB, LANES), f32)
    for b in range(0, length, SUB):
        straight = straight + xs_ref[pl.ds(b, SUB), :] * pull_ref[pl.ds(b, SUB), :]
    sums_ref[pl.ds(2 * expand, SUB), :] = straight


def ema_sums(spot, xs, pull, entry, heads, totals, params, after=()):
    length, columns = xs.shape
    expand = params.shape[1]
    shape = (2 * expand + SUB, columns)
    return launch(
        ema_sums_kernel,
        [(shape, f32)],
        (spot, xs, pull, entry, heads, totals, params),
        [
            in_smem(), by_tile(xs.shape, 1), by_tile(xs.shape, 1), by_tile(entry.shape, 1), by_tile(entry.shape, 1),
            by_tile(totals.shape, 2), by_tile(params.shape, 2),
        ],
        [by_tile(shape, 1)],
        after=after,
        grid=(columns // LANES,),
        scratch=[pltpu.VMEM((expand, LANES), f32), pltpu.VMEM((entry.shape[0], LANES), f32)],
        mib=5 * max(1, length // 1024),
        cost=work(8 * expand * length * columns, 8 * length * columns),
    )[0]


def pad_to_lanes(part, dim):
    extra = -part.shape[dim] % LANES
    if extra == 0:
        return part
    return jnp.pad(part, [(0, extra if k == dim else 0) for k in range(part.ndim)])


def ema_params(alpha, delta, beta, eta, count):
    packed = jnp.swapaxes(jnp.stack([alpha, delta, beta, eta]), 1, 2)
    return pad_to_lanes(jnp.tile(packed, (1, 1, count)), 2)


def ema_param_grads(total, alpha, delta, beta, eta, count):
    channels, expand = alpha.shape
    summed = jnp.sum(total[:, : count * channels].reshape(-1, count, channels), axis=1)
    plain, turned = summed[:expand].T, summed[expand : 2 * expand].T
    omega = jnp.sum(summed[2 * expand :], axis=0)
    rate, damp = jax.nn.sigmoid(alpha), jax.nn.sigmoid(delta)
    g_alpha = eta * beta * rate * (1.0 - rate) * (plain - damp * rate * turned)
    g_delta = -(eta * beta * rate * rate * damp * (1.0 - damp)) * turned
    return g_alpha, g_delta, rate * eta * plain, rate * beta * plain, omega


low = jnp.bfloat16
CHUNK = 256
MIB = (3, 11, 8, 5, 6, 8, 8, 6, 4, 4)
TABLE = 384


def nn(left, right):
    return jnp.dot(left, right, preferred_element_type=f32)


def nt(left, right):
    return lax.dot_general(left, right, (((1,), (1,)), ((), ())), preferred_element_type=f32)


def silu_pair(pre):
    sigma = jax.nn.sigmoid(pre)
    return pre * sigma, sigma * (1.0 + pre * (1.0 - sigma))


def each(width, body, size=CHUNK):
    for at in range(0, width, size):
        body(at)


def wide_block(ref, n):
    part = ref[:, n]
    return part.reshape(part.shape[0] * part.shape[1], part.shape[2])


def live_lanes(spot_ref, lengths_ref, n, shape):
    return spot_ref[0] + lax.broadcasted_iota(jnp.int32, shape, 1) < lengths_ref[n]


def span_of(ref, n):
    return pl.ds(n * GROUP, GROUP)


def call(kernel, outs, ins, smem=0, hbm=0, scratch=(), moved=1, mib=16, after=()):
    spaces = [pltpu.SMEM] * smem + [pl.ANY] * hbm + [pltpu.VMEM] * (len(ins) - smem - hbm)
    return launch(
        kernel,
        outs,
        ins,
        [pl.BlockSpec(memory_space=space) for space in spaces],
        [pl.BlockSpec(memory_space=pltpu.VMEM) for _ in outs],
        after=after,
        scratch=scratch,
        mib=mib,
        cost=pl.CostEstimate(flops=1, bytes_accessed=moved, transcendentals=0),
    )


def vectors(width, mwidth, vwidth, ff):
    sizes = (
        ("mix", mwidth), ("value", vwidth), ("out", width), ("gain", width),
        ("shift", width), ("up", ff), ("down", width),
    )
    place, at = {}, 0
    for name, size in sizes:
        place[name] = at
        at += size
    return place


def piece(ref, base, at, size):
    return ref[:, pl.ds(base + at, size)]


def value_kernel(base, w_ref, x_ref, vec_ref, rows_ref, values_ref, slope_ref, rows_t_ref):
    for n in range(x_ref.shape[1]):
        rows = pl.ds(n * GROUP, GROUP)
        block = wide_block(x_ref, n)
        rows_t_ref[:, rows] = block
        rows_ref[rows, :] = block.T

    def chunk(at):
        cols = pl.ds(at, CHUNK)
        act, slope = silu_pair(nn(rows_ref[...], w_ref[:, cols]) + piece(vec_ref, base, at, CHUNK))
        values_ref[:, cols] = act.astype(low)
        slope_ref[:, cols] = slope.astype(low)

    each(w_ref.shape[1], chunk)


def value_part(x, w_value, vec, where, after=()):
    width, vwidth = w_value.shape
    count = x.shape[1] * GROUP
    return call(
        functools.partial(value_kernel, where["value"]),
        [((count, width), low), ((count, vwidth), low), ((count, vwidth), low), ((width, count), low)],
        (w_value, x, vec),
        mib=MIB[0],
        after=after,
    )


def forward_kernel(
    pieces, where, spot_ref, lengths_ref, wmix_ref, wout_ref, wup_ref, wdown_ref,
    x_ref, values_ref, vec_ref, qscale_ref, qshift_ref, *refs
):
    forward_rows(spot_ref, refs[:pieces], refs[pieces], refs[-6])
    forward_body(
        where, spot_ref, lengths_ref, wmix_ref, wout_ref, wup_ref, wdown_ref,
        x_ref, values_ref, vec_ref, qscale_ref, qshift_ref, *refs[pieces + 1 :]
    )


def forward_rows(spot_ref, mixed_refs, mixed_t_ref, m_ref):
    for k, ref in enumerate(mixed_refs):
        seqs, channels, _ = ref.shape
        at = pl.multiple_of((spot_ref[1] ^ k) * channels, 16) if len(mixed_refs) > 1 else 0
        for n in range(seqs):
            mixed_t_ref[pl.ds(at, channels), pl.ds(n * GROUP, GROUP)] = ref[n]
    for n in range(m_ref.shape[0] // GROUP):
        rows = pl.ds(n * GROUP, GROUP)
        m_ref[rows, :] = mixed_t_ref[:, rows].T


def forward_body(
    where, spot_ref, lengths_ref, wmix_ref, wout_ref, wup_ref, wdown_ref,
    x_ref, values_ref, vec_ref, qscale_ref, qshift_ref,
    out_ref, query_ref, key_ref, shared_ref, qslope_ref, probs_ref, reset_ref, turned_ref, gated_t_ref,
    hslope_ref, uslope_ref, keep_ref, unit_ref, rstd_ref, normed_t_ref, hidden_t_ref, fslope_ref,
    m_ref, update_ref, gated_ref, blend_ref, normed_ref, ffn_ref,
):
    width, vwidth = wout_ref.shape[1], wout_ref.shape[0]
    zwidth = qscale_ref.shape[1]
    seqs = x_ref.shape[0] // GROUP

    def mix(at, size=CHUNK):
        cols = pl.ds(at, size)
        return nn(m_ref[...], wmix_ref[:, cols]) + piece(vec_ref, where["mix"], at, size)

    shared, qslope = silu_pair(mix(width, zwidth))
    shared_ref[...] = shared
    qslope_ref[...] = qslope
    query_ref[...] = (shared * qscale_ref[pl.ds(0, 1), :] + qshift_ref[pl.ds(0, 1), :]).astype(low)
    key_ref[...] = (shared * qscale_ref[pl.ds(1, 1), :] + qshift_ref[pl.ds(1, 1), :]).astype(low)
    causal = lax.broadcasted_iota(jnp.int32, (GROUP, GROUP), 0) >= lax.broadcasted_iota(
        jnp.int32, (GROUP, GROUP), 1
    )
    for n in range(seqs):
        rows = pl.ds(n * GROUP, GROUP)
        scores = jnp.where(causal, nt(query_ref[rows, :], key_ref[rows, :]) * zwidth**-0.5, -1e30)
        scores = jnp.exp(scores - jnp.max(scores, axis=-1, keepdims=True))
        probs_ref[rows, :] = scores / jnp.sum(scores, axis=-1, keepdims=True)

    def gate(at):
        update_ref[:, pl.ds(at, CHUNK)] = jax.nn.sigmoid(mix(at))

    each(width, gate)

    def attend(at):
        cols = pl.ds(at, CHUNK)
        reset, slope = silu_pair(mix(width + zwidth + at))
        attended = jnp.concatenate(
            [
                nn(probs_ref[pl.ds(n * GROUP, GROUP), :].astype(low), values_ref[pl.ds(n * GROUP, GROUP), cols])
                for n in range(seqs)
            ],
            axis=0,
        )
        reset_ref[:, cols] = reset.astype(low)
        turned_ref[:, cols] = (attended * slope).astype(low)
        gated = (reset * attended).astype(low)
        gated_ref[:, cols] = gated
        gated_t_ref[cols, :] = gated.T

    each(vwidth, attend)

    def hide(at):
        cols = pl.ds(at, CHUNK)
        pre = mix(width + zwidth + vwidth + at)
        pre = pre + nn(gated_ref[...], wout_ref[:, cols]) + piece(vec_ref, where["out"], at, CHUNK)
        hidden, slope = silu_pair(pre)
        update = update_ref[:, cols]
        keep = 1.0 - update
        resid = x_ref[:, cols].astype(f32)
        hslope_ref[:, cols] = (update * slope).astype(low)
        uslope_ref[:, cols] = ((hidden - resid) * update * keep).astype(low)
        keep_ref[:, cols] = keep.astype(low)
        blend_ref[:, cols] = update * hidden + keep * resid

    each(width, hide)
    for n in range(seqs):
        rows = pl.ds(n * GROUP, GROUP)
        blend = blend_ref[rows, :]
        centered = blend - jnp.mean(blend, axis=-1, keepdims=True)
        rstd = lax.rsqrt(jnp.mean(centered * centered, axis=-1, keepdims=True) + 1e-05)
        unit = centered * rstd
        unit_ref[rows, :] = unit.astype(low)
        rstd_ref[rows, :] = jnp.broadcast_to(rstd, (GROUP, LANES))
        normed = unit * piece(vec_ref, where["gain"], 0, width) + piece(vec_ref, where["shift"], 0, width)
        blend_ref[rows, :] = normed
        normed_ref[rows, :] = normed.astype(low)
        normed_t_ref[:, rows] = normed.astype(low).T

    def lift(at):
        cols = pl.ds(at, CHUNK)
        act, slope = silu_pair(nn(normed_ref[...], wup_ref[:, cols]) + piece(vec_ref, where["up"], at, CHUNK))
        fslope_ref[:, cols] = slope.astype(low)
        act = act.astype(low)
        ffn_ref[:, cols] = act
        hidden_t_ref[cols, :] = act.T

    each(wup_ref.shape[1], lift)

    def drop(at):
        cols = pl.ds(at, CHUNK)
        blend_ref[:, cols] = blend_ref[:, cols] + nn(ffn_ref[...], wdown_ref[:, cols]) + piece(vec_ref, where["down"], at, CHUNK)

    each(width, drop)
    for n in range(seqs):
        result = blend_ref[pl.ds(n * GROUP, GROUP), :].astype(low).T
        result = jnp.where(live_lanes(spot_ref, lengths_ref, n, result.shape), result, jnp.zeros_like(result))
        out_ref[:, n] = result.reshape(out_ref.shape[0], out_ref.shape[2], GROUP)


def forward_part(spot, lengths, folded, mixed, x, values, w_mix, w_out, w_up, w_down, vec, where, qk_scale, qk_shift, after=()):
    vwidth, width = w_out.shape
    zwidth = qk_scale.shape[1]
    ff = w_up.shape[1]
    count = x.shape[0]
    narrow, wide = (count, width), (count, vwidth)
    outs = [
        ((width, count), low), (folded, low), ((count, zwidth), low), ((count, zwidth), low), ((count, zwidth), f32),
        ((count, zwidth), f32), ((count, GROUP), f32), (wide, low), (wide, low), ((vwidth, count), low),
        (narrow, low), (narrow, low), (narrow, low), (narrow, low), ((count, LANES), f32),
        ((width, count), low), ((ff, count), low), ((count, ff), low),
    ]
    scratch = [pltpu.VMEM(narrow, low), pltpu.VMEM(narrow, f32), pltpu.VMEM(wide, low)]
    scratch += [pltpu.VMEM(narrow, f32), pltpu.VMEM(narrow, low), pltpu.VMEM((count, ff), low)]
    macs = w_mix.size + w_out.size + w_up.size + w_down.size
    return call(
        functools.partial(forward_kernel, len(mixed), where),
        outs,
        (spot, lengths, w_mix, w_out, w_up, w_down, x, values, vec, qk_scale, qk_shift, *mixed),
        smem=2,
        mib=MIB[1],
        after=after,
        scratch=scratch,
    )


def column_sum(part):
    return jnp.sum(part.astype(f32), axis=0, keepdims=True)


def put(ref, row, value, columns):
    if isinstance(ref, tuple):
        lone = value.shape[0] // len(ref)
        for k, one in enumerate(ref):
            put(one, row, value[k * lone : (k + 1) * lone], columns)
        return
    if len(ref.shape) == 2:
        ref[...] = value
        return
    owners = ref.shape[0]
    lone = value.shape[0] // owners
    for owner in range(owners):
        part = value[owner * lone : (owner + 1) * lone]
        for i, at in enumerate(range(0, value.shape[1], columns)):
            ref[owner, pl.ds(row + i * lone, lone), :] = part[:, at : at + columns]


def split_product(side, keep_ref, send_ref, left, right_ref, half, columns, row=0):
    total = right_ref.shape[1]
    for ref, which in ((keep_ref, side), (send_ref, 1 - side)):
        base = which * (total - half)
        parts = []
        for at in range(0, half, CHUNK):
            cols = pl.ds(pl.multiple_of(base + at, 128), min(CHUNK, half - at))
            parts.append(nn(left, right_ref[:, cols]).astype(low))
        put(ref, row, jnp.concatenate(parts, axis=1), columns)


def split_narrow(side, keep_ref, send_ref, left_ref, right_ref):
    both = [nn(left_ref[pl.ds(at, CHUNK), :], right_ref[...]).astype(low) for at in range(0, left_ref.shape[0], CHUNK)]
    both = jnp.concatenate(both, axis=0)
    half = both.shape[1] // 2
    near, far = both[:, :half], both[:, half:]
    put(keep_ref, 0, jnp.where(side == 0, near, far), half)
    put(send_ref, 0, jnp.where(side == 0, far, near), half)


def pair_outs(tall, wide, owners, lines=0):
    if not owners:
        return [((tall[0], tall[1] // 2), low)] * 2 + [((wide[0], wide[1] // 2), low)] * 2
    rows = (tall[0] * tall[1] + wide[0] * wide[1]) // (tall[1] * owners) + lines
    return [((owners, rows, tall[1] // 2), low)] * 2


def back_ffn_kernel(
    pieces, spot_ref, lengths_ref, wdown_ref, hidden_t_ref, fslope_ref, normed_t_ref, *refs
):
    grads, halves, (g_ref, dffn_ref, small_ref, turned_ref) = refs[:pieces], refs[pieces:-4], refs[-4:]
    width, ff = g_ref.shape[1], wdown_ref.shape[0]
    for k, ref in enumerate(grads):
        devices, seqs, channels, _ = ref.shape
        base = ((spot_ref[1] >> 1) ^ k) * devices if len(grads) > 1 else 0
        for d in range(devices):
            rows = pl.ds(pl.multiple_of((base + d) * channels, 16), channels)
            for n in range(seqs):
                turned_ref[rows, span_of(ref, n)] = ref[d, n]
    for n in range(g_ref.shape[0] // GROUP):
        part = turned_ref[:, span_of(g_ref, n)]
        part = jnp.where(live_lanes(spot_ref, lengths_ref, n, part.shape), part, jnp.zeros_like(part))
        g_ref[pl.ds(n * GROUP, GROUP), :] = part.T
    small_ref[:, pl.ds(0, width)] = column_sum(g_ref[...])
    side = spot_ref[2] & 1
    split_narrow(side, halves[0], halves[1], hidden_t_ref, g_ref)

    def lift(at):
        part = pl.ds(at, CHUNK)
        pulled = (nt(g_ref[...], wdown_ref[part, :]) * fslope_ref[:, part].astype(f32)).astype(low)
        dffn_ref[:, part] = pulled
        small_ref[:, pl.ds(width + at, CHUNK)] = column_sum(pulled)

    each(ff, lift)
    tall = hidden_t_ref.shape[0] // halves[0].shape[0]
    split_product(side, halves[-2], halves[-1], normed_t_ref[...], dffn_ref, ff // 2, halves[-2].shape[-1], tall)
    if len(halves) == 2:
        for ref in halves:
            owners, rows, columns = ref.shape
            ref[:, pl.ds(2 * tall, rows - 2 * tall), :] = jnp.zeros((owners, rows - 2 * tall, columns), low)


def back_ffn(spot, lengths, owners, lines, grad, hidden_t, fslope, normed_t, w_down, after=()):
    ff, width = w_down.shape
    count = fslope.shape[0]
    outs = pair_outs((ff, width), (width, ff), owners, lines)
    outs += [((count, width), low), ((count, ff), low), ((1, width + ff), f32)]
    *halves, g, dffn, small = call(
        functools.partial(back_ffn_kernel, len(grad)),
        outs,
        (spot, lengths, w_down, hidden_t, fslope, normed_t, *grad),
        smem=2,
        mib=MIB[2],
        scratch=[pltpu.VMEM((width, count), low)],
        after=after,
    )
    return halves, g, dffn, small


def back_norm_kernel(
    base, wup_ref, g_ref, dffn_ref, unit_ref, rstd_ref, vec_ref, hslope_ref, uslope_ref, kept_ref,
    dh_ref, du_ref, direct_ref, small_ref, dn_ref,
):
    width = wup_ref.shape[0]

    def drop(at):
        part = pl.ds(at, CHUNK)
        pulled = g_ref[:, part].astype(f32) + nt(dffn_ref[...], wup_ref[part, :])
        dn_ref[:, part] = pulled
        small_ref[:, part] = column_sum(pulled * unit_ref[:, part].astype(f32))
        small_ref[:, pl.ds(width + at, CHUNK)] = column_sum(pulled)

    each(width, drop)
    for n in range(g_ref.shape[0] // GROUP):
        rows = pl.ds(n * GROUP, GROUP)
        unit = unit_ref[rows, :].astype(f32)
        pulled = dn_ref[rows, :] * piece(vec_ref, base, 0, width)
        inner = jnp.mean(pulled * unit, axis=-1, keepdims=True)
        blend = pulled - jnp.mean(pulled, axis=-1, keepdims=True) - unit * inner
        blend = blend * rstd_ref[rows, :][:, :1]
        dh_ref[rows, :] = (blend * hslope_ref[rows, :].astype(f32)).astype(low)
        du_ref[rows, :] = (blend * uslope_ref[rows, :].astype(f32)).astype(low)
        direct_ref[rows, :] = (blend * kept_ref[rows, :].astype(f32)).astype(low)


def back_norm(g, dffn, unit, rstd, vec, where, hslope, uslope, kept, w_up, after=()):
    width = w_up.shape[0]
    narrow = g.shape
    return call(
        functools.partial(back_norm_kernel, where["gain"]),
        [(narrow, low)] * 3 + [((1, 2 * width), f32)],
        (w_up, g, dffn, unit, rstd, vec, hslope, uslope, kept),
        mib=MIB[3],
        after=after,
        scratch=[pltpu.VMEM(narrow, f32)],
    )


def back_attend_kernel(
    wout_ref, wmix_ref, wvalue_ref,
    dh_ref, du_ref, direct_ref, reset_ref, turned_ref, values_ref, vslope_ref, probs_ref,
    query_ref, key_ref, shared_ref, qslope_ref, qscale_ref, small_ffn_ref, small_norm_ref, result_ref,
    dmix_ref, dvalue_ref, mixed_ref, joint_ref,
    table_ref,
    datt_ref,
):
    vwidth, width = wout_ref.shape
    zwidth = qscale_ref.shape[1]
    count = dh_ref.shape[0]
    seqs = count // GROUP
    dmix_ref[:, pl.ds(0, width)] = du_ref[...]
    dmix_ref[:, pl.ds(width + zwidth + vwidth, width)] = dh_ref[...]

    def gate(at):
        part = pl.ds(at, CHUNK)
        pulled = nt(dh_ref[...], wout_ref[part, :])
        dmix_ref[:, pl.ds(width + zwidth + at, CHUNK)] = (
            pulled * turned_ref[:, part].astype(f32)
        ).astype(low)
        datt_ref[:, part] = (pulled * reset_ref[:, part].astype(f32)).astype(low)

    each(vwidth, gate)
    scale = zwidth**-0.5
    q_scale, k_scale = qscale_ref[pl.ds(0, 1), :], qscale_ref[pl.ds(1, 1), :]
    zero = jnp.zeros((1, zwidth), f32)
    sums = [zero, zero, zero, zero]
    for n in range(seqs):
        rows = pl.ds(n * GROUP, GROUP)
        probs = probs_ref[rows, :]
        pulled = nt(datt_ref[rows, :], values_ref[rows, :])
        pulled = probs * (pulled - jnp.sum(pulled * probs, axis=-1, keepdims=True))
        pulled = pulled.astype(low)
        d_query = nn(pulled, key_ref[rows, :]) * scale
        d_key = nn(pulled.T, query_ref[rows, :]) * scale
        probs_t = probs.astype(low).T
        shared = shared_ref[rows, :]
        found = (d_query * shared, d_key * shared, d_query, d_key)
        sums = [a + jnp.sum(b, axis=0, keepdims=True) for a, b in zip(sums, found)]
        dmix_ref[rows, pl.ds(width, zwidth)] = (
            (d_query * q_scale + d_key * k_scale) * qslope_ref[rows, :]
        ).astype(low)
        dvalue_ref[rows, :] = (nn(probs_t, datt_ref[rows, :]) * vslope_ref[rows, :].astype(f32)).astype(low)

    def turn(result):
        devices, _, channels, _ = mixed_ref.shape
        return result.astype(low).T.reshape(devices, channels, GROUP)

    for n in range(0, seqs, 2):
        result = nt(dmix_ref[pl.ds(n * GROUP, 2 * GROUP), :], wmix_ref[...])
        mixed_ref[:, n] = turn(result[:GROUP])
        mixed_ref[:, n + 1] = turn(result[GROUP:])
    for n in range(0, seqs, 2):
        rows = pl.ds(n * GROUP, 2 * GROUP)
        result = direct_ref[rows, :].astype(f32) + nt(dvalue_ref[rows, :], wvalue_ref[...])
        joint_ref[:, 0, n] = turn(result[:GROUP])
        joint_ref[:, 0, n + 1] = turn(result[GROUP:])
    joint_ref[:, 1] = result_ref[...]
    ff = small_ffn_ref.shape[1] - width
    found = (
        column_sum(dmix_ref[...]), column_sum(dvalue_ref[...]), column_sum(dh_ref[...]),
        sums[0], sums[1], sums[2], sums[3], small_norm_ref[:, :width], small_norm_ref[:, width:],
        small_ffn_ref[:, width:], small_ffn_ref[:, :width],
    )
    lines = []
    for part in found:
        for at in range(0, part.shape[1], TABLE):
            line = part[:, at : at + TABLE]
            lack = TABLE - line.shape[1]
            lines.append(line if lack == 0 else jnp.concatenate([line, jnp.zeros((1, lack), f32)], axis=1))
    lines.append(jnp.zeros((table_ref.shape[0] - len(lines), TABLE), f32))
    table_ref[...] = jnp.concatenate(lines, axis=0).astype(low)


def back_attend(dh, du, direct, reset, turned, values, vslope, probs, query, key, shared, qslope, qk_scale, small_ffn, small_norm, result, w_out, w_mix, w_value, after=()):
    vwidth, width = w_out.shape
    mwidth = w_mix.shape[1]
    count = dh.shape[0]
    outs = [((count, mwidth), low), ((count, vwidth), low)]
    outs += [(result.shape, low), (result.shape[:1] + (2,) + result.shape[1:], low), ((64, TABLE), low)]
    scratch = [pltpu.VMEM((count, vwidth), low)]
    macs = w_out.size + w_mix.size + w_value.size
    return call(
        back_attend_kernel,
        outs,
        (w_out, w_mix, w_value, dh, du, direct, reset, turned, values, vslope, probs, query, key, shared, qslope, qk_scale, small_ffn, small_norm, result),
        mib=MIB[4],
        after=after,
        scratch=scratch,
    )


def back_mid_kernel(spot_ref, gated_t_ref, dh_ref, x_t_ref, dvalue_ref, table_ref, *halves):
    side = spot_ref[2] & 1
    if len(halves) == 4:
        (kept, sent, wide_kept, wide_sent), tall = halves, 0
    else:
        kept, sent = halves[0], halves[1:]
        wide_kept, wide_sent, tall = kept, sent, gated_t_ref.shape[0] // kept.shape[0]
    split_narrow(side, kept, sent, gated_t_ref, dh_ref)
    split_product(
        side, wide_kept, wide_sent, x_t_ref[...], dvalue_ref, dvalue_ref.shape[1] // 2, wide_kept.shape[-1], tall
    )
    if len(halves) == 4:
        return
    lines = kept.shape[1] - 2 * tall
    high = table_ref.shape[0] // (2 * lines)
    for refs, which in (((kept,), side), (sent, 1 - side)):
        for ref in refs:
            for owner in range(ref.shape[0]):
                at = pl.multiple_of((2 * (owner % high) + which) * lines, 16)
                ref[owner, pl.ds(2 * tall, lines), :] = table_ref[pl.ds(at, lines), :]


def halved(outs):
    (kept, kind), (sent, _) = outs
    return [(kept, kind)] + [((sent[0] // 2,) + sent[1:], kind)] * 2


def back_mid(spot, owners, gated_t, dh, x_t, dvalue, table, lines, after=()):
    count, width = dh.shape
    vwidth = dvalue.shape[1]
    outs = pair_outs((vwidth, width), (width, vwidth), owners, lines)
    found = call(
        back_mid_kernel,
        halved(outs) if owners else outs,
        (spot, gated_t, dh, x_t, dvalue, table),
        smem=1,
        mib=MIB[5],
        after=after,
    )
    if owners:
        return [found[0]], [list(found[1:])]
    return [found[0], found[2]], [[found[1]], [found[3]]]


def back_mix_kernel(spot_ref, mixed_t_ref, dmix_ref, keep_ref, *send_refs):
    half = keep_ref.shape[-1]
    split_product(spot_ref[2] & 1, keep_ref, send_refs, mixed_t_ref[...], dmix_ref, half, half)


def back_mix_weight(spot, owners, mixed_t, dmix, after=()):
    mwidth = dmix.shape[1]
    width, count = mixed_t.shape
    half = -(-mwidth // 256) * 128
    outs = [((width, half), low)] * 2
    kept, *sent = call(
        back_mix_kernel,
        halved(outs) if owners else outs,
        (spot, mixed_t, dmix),
        smem=1,
        mib=MIB[6],
        after=after,
    )
    return [kept], [sent]


def halve_kernel(index, bit, spot_ref, kept_ref, *refs):
    arrived, (sent_ref, stay_ref) = refs[:-2], refs[-2:]
    outer, inner, _, _ = sent_ref.shape
    lone = outer // len(arrived)
    mine = (spot_ref[index] >> bit) & 1
    for ref, which in ((sent_ref, 1 - mine), (stay_ref, mine)):
        for a in range(outer):
            for b in range(inner):
                total = kept_ref[a, which, b].astype(f32) + arrived[a // lone][a % lone, which, b].astype(f32)
                ref[a, b] = total.astype(low)


def halve(spot, kept, arrived, index, bit, at, after=()):
    dims = kept.shape[:-2]
    outer, inner = 1 << at, 1 << (len(dims) - at - 1)
    block = kept.shape[-2:]

    def shaped(part):
        return part.reshape((-1, 2, inner) + block)

    sent, stay = call(
        functools.partial(halve_kernel, index, bit),
        [((outer, inner) + block, low)] * 2,
        (spot, shaped(kept), *map(shaped, arrived)),
        smem=1,
        mib=MIB[7],
        after=after,

    )
    rest = dims[:at] + dims[at + 1 :] + block
    return sent.reshape(rest), stay.reshape(rest)


def finish_pair_kernel(count, lines, spot_ref, *refs):
    shares, outs = refs[:count], refs[count:]
    tall_ref, wide_ref = outs[:2]
    columns = shares[0].shape[1]
    cut = tall_ref.shape[0] * 2 // len(shares)
    lone = wide_ref.shape[0] * 2 // len(shares)
    for k, ref in enumerate(shares):
        at = spot_ref[2] ^ k
        high, side = at >> 1, at & 1
        tall_ref[pl.ds(pl.multiple_of(high * cut, 8), cut), pl.ds(pl.multiple_of(side * columns, 128), columns)] = ref[
            pl.ds(0, cut), :
        ].astype(f32)
        runs = wide_ref.shape[1] // 2 // columns
        for run in range(runs):
            wide_ref[
                pl.ds(pl.multiple_of(high * lone, 8), lone),
                pl.ds(pl.multiple_of((side * runs + run) * columns, 128), columns),
            ] = ref[pl.ds(cut + run * lone, lone), :].astype(f32)
        if lines:
            outs[-1][pl.ds(pl.multiple_of(at * lines, 8), lines), :] = ref[pl.ds(2 * cut, lines), :].astype(f32)
    if lines:
        row = 0
        for ref in outs[2:-1]:
            if len(ref.shape) == 2:
                for k in range(ref.shape[0]):
                    ref[pl.ds(k, 1), :] = outs[-1][pl.ds(row, 1), :][:, : ref.shape[1]]
                    row += 1
                continue
            for at in range(0, ref.shape[0], columns):
                size = min(columns, ref.shape[0] - at)
                ref[pl.ds(at, size)] = outs[-1][row, :size]
                row += 1


def finish_pair(spot, shares, tall, wide, lines=0, vectors=(), after=()):
    outs = [(tall, f32), (wide, f32)] + [(shape, f32) for shape in vectors]
    count = len(shares)
    scratch = [pltpu.VMEM((count * lines, shares[0].shape[1]), f32)] if lines else []
    kernel = functools.partial(finish_pair_kernel, count, lines)
    return call(kernel, outs, (spot, *shares), smem=1, mib=MIB[8], scratch=scratch, after=after)


def finish_mix_kernel(spot_ref, *refs):
    shares, out_ref = refs[:-1], refs[-1]
    half, mwidth = shares[0].shape[1], out_ref.shape[1]
    common = 2 * half - mwidth
    lone = out_ref.shape[0] * 2 // len(shares)
    for k, ref in enumerate(shares):
        at = spot_ref[2] ^ k
        rows = pl.ds(pl.multiple_of((at >> 1) * lone, 8), lone)
        base = pl.multiple_of(common + (at & 1) * (mwidth - half), 128)
        out_ref[rows, pl.ds(base, half - common)] = ref[:, common:].astype(f32)
        if common:

            @pl.when(at & 1 == 0)
            def _():
                out_ref[rows, pl.ds(0, common)] = ref[:, :common].astype(f32)


def finish_mix(spot, shares, shape, after=()):
    return call(finish_mix_kernel, [(shape, f32)], (spot, *shares), smem=1, mib=MIB[9], after=after)[0]


Y_FIRST = (("tok", 1), ("ch", 0))
Y_THEN_Z = (("tok", 1), ("ch", 1), ("ch", 0))
X_FIRST = (("ch", 0), ("tok", 1))


def bits_of(axis):
    return lax.axis_size(axis).bit_length() - 1


def across(part, axis, turn):
    return lax.ppermute(part, axis, [(i, i ^ turn) for i in range(lax.axis_size(axis))])


def exchange(part, axis, bit):
    return across(part, axis, 1 << bit)


def side_of(axis, bit):
    return (lax.axis_index(axis) >> bit) & 1


def by_owner(grad):
    dims = (2,) * (bits_of("ch") + bits_of("tok") - 1)
    return grad.reshape(dims + (-1, grad.shape[-1]))


def fold(part, columns):
    runs = [part[..., at : at + columns] for at in range(0, part.shape[-1], columns)]
    return jnp.concatenate(runs, axis=-2)


def add(left, right):
    return (left.astype(f32) + right.astype(f32)).astype(low)


def plain_halve(kept, arrived, mine, at):
    columns = min(part.shape[-1] for part in kept)

    def pick(which):
        def one(part):
            return lax.dynamic_index_in_dim(part, which, at, keepdims=False)

        return jnp.concatenate([fold(add(one(a), one(b)), columns) for a, b in zip(kept, arrived)], axis=-2)

    return pick(1 - mine), pick(mine)


class Sum:
    def __init__(self, spot, kept, sent, order):
        self.spot = spot
        self.names = [("ch", k) for k in reversed(range(bits_of("ch")))]
        self.names += [("tok", k) for k in reversed(range(1, bits_of("tok")))]
        self.stages = list(order) + [name for name in reversed(self.names) if name not in order]
        self.kept = [by_owner(part) for part in kept]
        arrived = [[exchange(piece, "tok", 0) for piece in part] for part in sent]
        self.arrived = arrived[0] if self.by_kernel() else [by_owner(part) for part, in arrived]

    def by_kernel(self):
        return len(self.kept) == 1 and self.kept[0].shape[-2] % 16 == 0

    def step(self, after=()):
        axis, bit = self.stages.pop(0)
        at = self.names.index((axis, bit))
        self.names.remove((axis, bit))
        if self.by_kernel():
            index = 1 if axis == "ch" else 2
            sent, stay = halve(self.spot, self.kept[0], self.arrived, index, bit, at, after)
        else:
            sent, stay = plain_halve(self.kept, self.arrived, side_of(axis, bit), at)
        self.kept, self.arrived = [stay], [exchange(sent, axis, bit)]
        return stay

    def shares(self):
        found = [add(self.kept[0], self.arrived[0])]
        for bit in reversed(range(1, bits_of("tok"))):
            found += [exchange(part, "tok", bit) for part in found]
        lower = [exchange(part, "tok", 0) for part in found]
        size = bits_of("tok") - 1
        order = [sum(((k >> (size - 1 - i)) & 1) << i for i in range(size)) for k in range(len(found))]
        found = [part for k in order for part in (found[k], lower[k])]
        return found


def in_order(shares, place):
    bit = 1
    while bit < len(shares):
        swapped = (place & bit) != 0
        shares = [jnp.where(swapped, shares[k ^ bit], shares[k]) for k in range(len(shares))]
        bit *= 2
    return jnp.stack(shares)


def plain_pair(place, shares, tall, wide):
    whole = in_order(shares, place).astype(f32)
    high = len(shares) // 2
    cut, lone = tall[0] // high, wide[0] // high
    whole = whole.reshape((high, 2) + whole.shape[1:])
    first = whole[:, :, :cut].transpose(0, 2, 1, 3).reshape(tall)
    second = whole[:, :, cut:].reshape(high, 2, -1, lone, whole.shape[-1])
    return first, second.transpose(0, 3, 1, 2, 4).reshape(wide)


def plain_mix(place, shares, shape):
    whole = in_order(shares, place).astype(f32)
    half = whole.shape[-1]
    whole = whole.reshape((len(shares) // 2, 2) + whole.shape[1:])
    whole = jnp.concatenate([whole[:, 0], whole[:, 1, :, 2 * half - shape[1] :]], axis=-1)
    return whole.reshape(shape)


def sum_tok(part):
    for bit in range(bits_of("tok")):
        part = part + exchange(part, "tok", bit)
    return part


def swap(parts):
    return lax.all_to_all(parts, "ch", split_axis=0, concat_axis=0, tiled=True)


def folded(parts):
    devices, channels, span = parts.shape[0], parts.shape[-2], parts.shape[-1]
    if channels % 16 == 0:
        return parts
    return jnp.moveaxis(parts, 0, -3).reshape((1,) + parts.shape[1:-2] + (devices * channels, span))


def unfolded(parts, devices):
    if parts.shape[0] == devices:
        return parts
    channels, span = parts.shape[-2] // devices, parts.shape[-1]
    return jnp.moveaxis(parts.reshape(parts.shape[1:-2] + (devices, channels, span)), -3, 0)


def local(
    inputs,
    out_grad,
    seq_lengths,
    ema_alpha,
    ema_delta,
    ema_beta,
    ema_eta,
    ema_omega,
    w_mix,
    b_mix,
    w_value,
    b_value,
    w_out,
    b_out,
    qk_scale,
    qk_shift,
    ln_gain,
    ln_bias,
    w_up,
    b_up,
    w_down,
    b_down,
):
    count, channels, local_len = inputs.shape
    width, mwidth = w_mix.shape
    vwidth, ff = w_value.shape[1], w_up.shape[1]
    devices, tok_size = lax.axis_size("ch"), lax.axis_size("tok")
    columns = count * channels
    span = local_len // devices
    tok_index = lax.axis_index("tok").astype(jnp.int32)
    ch_index = lax.axis_index("ch").astype(jnp.int32)
    spot = jnp.stack([tok_index * local_len + ch_index * span, ch_index, tok_index])
    apart = devices <= 8 and channels % 16 == 0

    def by_column(parts):
        whole = unfolded(parts, devices)
        return pad_to_lanes(whole.reshape(whole.shape[:-3] + (columns, span)), whole.ndim - 3)

    where = vectors(width, mwidth, vwidth, ff)
    vec = jnp.concatenate([b_mix, b_value, b_out, ln_gain, ln_bias, b_up, b_down])[None]
    params = ema_params(ema_alpha, ema_delta, ema_beta, ema_eta, count)
    omega = pad_to_lanes(jnp.tile(ema_omega, count)[None], 1)

    flat = inputs.reshape(columns, local_len)
    if apart:
        blocks, near, far = by_blocks(spot, flat, out_grad.reshape(columns, local_len))
        recv_in = swap(blocks.reshape(devices, count, channels, span))
        arrived = across(far, "ch", 1)
    else:
        recv_in, recv_grad = (
            folded(swap(part.reshape(count, channels, devices, span).transpose(2, 0, 1, 3))) for part in (inputs, out_grad)
        )
    xs, ends, total = ema_ends(pad_to_lanes(flat, 0), params)
    totals = lax.all_gather(total, "tok")
    mixed, slope, entry = ema_mix(spot, xs, ends, params, omega, totals, apart)
    x, values, vslope, x_t = value_part(recv_in, w_value, vec, where, (entry,))
    if apart:
        grads = by_partner(spot, near, arrived, (x,))
        mixed = [part.reshape(count, channels, span) for part in mixed]
        mixed = [part if k == 0 else across(part, "ch", k) for k, part in enumerate(mixed)]
        grads = [part.reshape(2, count, channels, span) for part in grads]
        grads = [part if k == 0 else across(part, "ch", 2 * k) for k, part in enumerate(grads)]
    else:
        mixed = folded(swap(mixed[0][:, :columns].reshape(devices, count, channels, span)))
        mixed = [mixed[0]] if mixed.shape[0] == 1 else [mixed.transpose(1, 0, 2, 3).reshape(count, width, span)]
        grads = [recv_grad]
    (
        mixed_t, result, query, key, shared, qslope, probs, reset, turned, gated_t,
        hslope, uslope, keep, unit, rstd, normed_t, hidden_t, fslope,
    ) = forward_part(
        spot, seq_lengths, recv_in.shape, mixed, x, values, w_mix, w_out, w_up, w_down, vec,
        where, qk_scale, qk_shift,
    )
    owners = devices * tok_size // 2
    joined = owners if width // owners % 16 == 0 else 0
    lines = 64 // tok_size
    halves, g, dffn, small_ffn = back_ffn(
        spot, seq_lengths, joined, lines, grads, hidden_t, fslope, normed_t, w_down
    )
    ffn = Sum(spot, halves[::2], [[part] for part in halves[1::2]], Y_THEN_Z)
    dh, du, direct, small_norm = back_norm(g, dffn, unit, rstd, vec, where, hslope, uslope, keep, w_up)
    last = ffn.step((small_norm,))
    dmix, dvalue, back_mix, joint, table = back_attend(
        dh, du, direct, reset, turned, values, vslope, probs, query, key, shared, qslope,
        qk_scale, small_ffn, small_norm, result, w_out, w_mix, w_value, (last,),
    )
    kept, sent = back_mix_weight(spot, joined, mixed_t, dmix, (table,))
    mix = Sum(spot, kept, sent, X_FIRST)
    kept, sent = back_mid(spot, joined, gated_t, dh, x_t, dvalue, table, lines, (kept[0],))
    last = kept[0]
    back_mix = swap(unfolded(back_mix, devices))
    if not joined:
        table = table.reshape(tok_size // 2, 2, lines, TABLE)
        for group, which in ((kept, side_of("tok", 0)), (sent, 1 - side_of("tok", 0))):
            part = lax.dynamic_index_in_dim(table, which, 1, keepdims=False)
            part = jnp.broadcast_to(part[None], (devices,) + part.shape).reshape(-1, TABLE)
            group.append(part if group is kept else [part])
    mid = Sum(spot, kept, sent, Y_FIRST)
    last = ffn.step((last,))
    last = mix.step((last,))
    last = mid.step((last,))
    joint, back_mix, _ = lax.optimization_barrier((unfolded(joint, devices), back_mix, last))
    joint = swap(joint)
    pull, heads, total = ema_back(by_column(back_mix), slope, params, (last,))
    totals = lax.all_gather(total, "tok")
    last = mix.step((totals,))
    last = mid.step((last,))
    sums = ema_sums(spot, xs, pull, entry, heads, totals, params, (last,))
    last = mix.step((sums,))
    last = mid.step((last,))
    last = ffn.step((last,))
    last = mix.step((last,))
    while len(mid.stages) + len(mix.stages) + len(ffn.stages):
        for group in (mid, ffn, mix):
            last = group.step((last,)) if group.stages else last
    input_grad, output = ema_finish(spot, pull, heads, params, omega, totals, by_column(joint), (last,))
    ema_grads = ema_param_grads(sum_tok(sums), ema_alpha, ema_delta, ema_beta, ema_eta, count)
    mix.arrived[0], output, ema_grads = lax.optimization_barrier((mix.arrived[0], output, ema_grads))
    last = output
    input_grad = input_grad[:columns].reshape(inputs.shape)
    output = output[:columns].reshape(inputs.shape)

    tall, wide = (vwidth // devices, width), (width // devices, vwidth)
    shares = mid.shares()
    half = qk_scale.shape[1]
    across_mix = (width // devices, mwidth)
    if joined:
        vectors_of = [(mwidth,), (vwidth,), (width,), qk_scale.shape, qk_scale.shape, (width,), (width,), (ff,), (width,)]
        g_down, g_up = finish_pair(spot, ffn.shares(), tall, wide, after=(last,))
        g_out, g_value, *found = finish_pair(spot, shares, tall, wide, lines, vectors_of, (last,))
        g_mix = finish_mix(spot, mix.shares(), across_mix, (last,))
    else:
        table = in_order([part[-lines:] for part in shares], tok_index).astype(f32).reshape(-1)
        shares = [part[:-lines] for part in shares]
        g_out, g_value = plain_pair(tok_index, shares, tall, wide)
        g_down, g_up = plain_pair(tok_index, ffn.shares(), tall, wide)
        g_mix = plain_mix(tok_index, mix.shares(), across_mix)
        found, at = [], 0
        for size in (mwidth, vwidth, width, half, half, half, half, width, width, ff, width):
            found.append(table[at : at + size])
            at += -(-size // TABLE) * TABLE
        found = found[:3] + [jnp.stack(found[3:5]), jnp.stack(found[5:7])] + found[7:]
    g_bmix, g_bvalue, g_bout, g_qscale, g_qshift, g_gain, g_lnbias, g_bup, g_bdown = found
    return (
        output,
        input_grad,
        *ema_grads,
        g_mix,
        g_bmix,
        g_value,
        g_bvalue,
        g_out,
        g_bout,
        g_qscale,
        g_qshift,
        g_gain,
        g_lnbias,
        g_up,
        g_bup,
        g_down,
        g_bdown,
    )


def solution(mesh):
    by_ch = P("ch", None)
    placed = P(None, "ch", "tok")
    return jax.shard_map(
        local,
        mesh=mesh,
        in_specs=(placed, placed, P()) + (by_ch,) * 4 + (P("ch"),) + (P(),) * 14,
        out_specs=(
            (placed, placed)
            + (by_ch,) * 4
            + (P("ch"), by_ch, P(), by_ch, P(), by_ch)
            + (P(),) * 5
            + (by_ch, P(), by_ch, P())
        ),
        check_vma=False,
    )
```

```python
import functools
import jax
import jax.numpy as jnp
from jax import lax
from jax.experimental import pallas as pl
from jax.experimental.pallas import tpu as pltpu
from jax.sharding import PartitionSpec as P

GROUP = 128
SUB = 8
LANES = 128
f32 = jnp.float32


def by_tile(shape, dim):
    block = tuple(LANES if k == dim else size for k, size in enumerate(shape))
    return pl.BlockSpec(block, lambda i: tuple(i if k == dim else 0 for k in range(len(shape))))


def in_smem():
    return pl.BlockSpec(memory_space=pltpu.SMEM)


def roomy(mib=5):
    return pltpu.CompilerParams(vmem_limit_bytes=mib * 1024 * 1024)


def work(flops, moved, exps=0):
    return pl.CostEstimate(flops=1, bytes_accessed=1, transcendentals=0)


def launch(kernel, outs, ins, in_specs, out_specs, after=(), grid=(), scratch=(), mib=5, cost=None):
    count = len(ins)

    def run(*refs):
        kernel(*refs[:count], *refs[count + len(after) :])

    return pl.pallas_call(
        run,
        grid=grid,
        out_shape=tuple(jax.ShapeDtypeStruct(shape, kind) for shape, kind in outs),
        in_specs=list(in_specs) + [pl.BlockSpec(memory_space=pl.ANY)] * len(after),
        out_specs=tuple(out_specs),
        scratch_shapes=list(scratch),
        compiler_params=roomy(mib),
        cost_estimate=cost,
    )(*ins, *after)


def rates(params_ref):
    rate = jax.nn.sigmoid(params_ref[0])
    drop = rate * jax.nn.sigmoid(params_ref[1])
    weight = params_ref[3] * rate * params_ref[2]
    return 1.0 - drop, jnp.log1p(-drop), weight


def spread(ref, j):
    return jnp.broadcast_to(ref[pl.ds(j, 1), :], (SUB, LANES))


def tree_sum(parts):
    while len(parts) > 1:
        parts = [a + b for a, b in zip(parts[::2], parts[1::2])] + parts[len(parts) & ~1 :]
    return parts[0]


def block_rows(g, t):
    return pl.ds(g * GROUP + t, SUB, stride=GROUP)


def state_rows(g, j, expand):
    return pl.ds(g * expand + j, SUB, stride=expand)


def blocks_kernel(spot_ref, first_ref, second_ref, out_ref, sems):
    copies = []
    for b in range(out_ref.shape[0]):
        cols = pl.ds(b * GROUP, GROUP)
        for which, ref in enumerate((first_ref, second_ref)):
            copies.append(pltpu.make_async_copy(ref.at[:, cols], out_ref.at[b, which], sems.at[2 * b + which]))
    for copy in copies:
        copy.start()
    for copy in copies:
        copy.wait()


def by_blocks(spot, first, second):
    columns, length = first.shape
    blocks = length // GROUP
    anywhere = pl.BlockSpec(memory_space=pl.ANY)
    return launch(
        blocks_kernel,
        [((blocks, 2, columns, GROUP), first.dtype)],
        (spot, first, second),
        [in_smem(), anywhere, anywhere],
        [anywhere],
        scratch=[pltpu.SemaphoreType.DMA((2 * blocks,))],
        mib=1,
    )[0]


def ema_ends_kernel(x_ref, params_ref, xs_ref, ends_ref, total_ref, decay_ref):
    length = x_ref.shape[1]
    expand = params_ref.shape[1]
    blocks = length // GROUP
    decay, log_decay, _ = rates(params_ref)
    decay_ref[...] = decay
    for b in range(blocks):
        rows = pl.ds(b * GROUP, GROUP)
        xs_ref[rows, :] = x_ref[:, rows].astype(f32).T
    factors = [spread(decay_ref, j) for j in range(expand)]
    for g in range(0, blocks, SUB):

        def step(t, states):
            now = xs_ref[block_rows(g, t), :]
            return tuple(f * s + now for f, s in zip(factors, states))

        states = (jnp.zeros((SUB, LANES), f32),) * expand
        states = lax.fori_loop(0, GROUP, step, states, unroll=8)
        for j in range(expand):
            ends_ref[state_rows(g, j, expand), :] = states[j]
    jump = jnp.exp(GROUP * log_decay)
    carry = jnp.zeros_like(jump)
    for b in range(blocks):
        carry = jump * carry + ends_ref[pl.ds(b * expand, expand), :]
    total_ref[...] = carry


def ema_ends(x, params, after=()):
    columns, length = x.shape
    expand = params.shape[1]
    shapes = ((length, columns), (length // GROUP * expand, columns), (expand, columns))
    return launch(
        ema_ends_kernel,
        [(shape, f32) for shape in shapes],
        (x, params),
        [by_tile(x.shape, 0), by_tile(params.shape, 2)],
        [by_tile(shape, 1) for shape in shapes],
        after=after,
        grid=(columns // LANES,),
        scratch=[pltpu.VMEM((expand, LANES), f32)],
        mib=5 * max(1, length // 1024),
        cost=work(2 * expand * length * columns, 6 * length * columns),
    )


def ema_mix_kernel(
    spot_ref, xs_ref, ends_ref, params_ref, omega_ref, totals_ref, *refs
):
    mixed_refs, (slope_ref, entry_ref, decay_ref, weight_ref, smooth_ref) = refs[:-5], refs[-5:]
    length = xs_ref.shape[0]
    expand = params_ref.shape[1]
    blocks = length // GROUP
    decay, log_decay, weight = rates(params_ref)
    decay_ref[...] = decay
    weight_ref[...] = weight
    whole = jnp.exp(length * log_decay)
    jump = jnp.exp(GROUP * log_decay)
    carry = jnp.zeros_like(jump)
    for k in range(totals_ref.shape[0]):
        carry = jnp.where(k < spot_ref[2], whole * carry + totals_ref[k], carry)
    for b in range(blocks):
        rows = pl.ds(b * expand, expand)
        entry_ref[rows, :] = carry
        carry = jump * carry + ends_ref[rows, :]
    factors = [spread(decay_ref, j) for j in range(expand)]
    weights = [spread(weight_ref, j) for j in range(expand)]
    for g in range(0, blocks, SUB):

        def step(t, states):
            now = xs_ref[block_rows(g, t), :]
            states = tuple(f * s + now for f, s in zip(factors, states))
            smooth_ref[block_rows(g, t), :] = tree_sum([w * s for w, s in zip(weights, states)])
            return states

        start = tuple(entry_ref[state_rows(g, j, expand), :] for j in range(expand))
        lax.fori_loop(0, GROUP, step, start, unroll=8)
    for k in range(blocks):
        rows = pl.ds(pl.multiple_of((spot_ref[1] ^ k) * GROUP, GROUP), GROUP)
        pre = smooth_ref[rows, :] + omega_ref[...] * xs_ref[rows, :]
        sigma = jax.nn.sigmoid(pre)
        block = (pre * sigma).T.astype(jnp.bfloat16)
        if len(mixed_refs) == 1:
            mixed_refs[0][spot_ref[1] ^ k] = block
        else:
            mixed_refs[k][...] = block
        slope_ref[rows, :] = (sigma * (1.0 + pre * (1.0 - sigma))).astype(slope_ref.dtype)


def ema_mix(spot, xs, ends, params, omega, totals, apart, after=()):
    length, columns = xs.shape
    expand = params.shape[1]
    blocks = length // GROUP
    mixed = [(columns, GROUP)] * blocks if apart else [(blocks, columns, GROUP)]
    *found, slope, entry = launch(
        ema_mix_kernel,
        [(shape, jnp.bfloat16) for shape in mixed] + [(xs.shape, jnp.bfloat16), (ends.shape, f32)],
        (spot, xs, ends, params, omega, totals),
        [
            in_smem(), by_tile(xs.shape, 1), by_tile(ends.shape, 1), by_tile(params.shape, 2),
            by_tile(omega.shape, 1), by_tile(totals.shape, 2),
        ],
        [by_tile(shape, len(shape) - 2) for shape in mixed] + [by_tile(xs.shape, 1), by_tile(ends.shape, 1)],
        after=after,
        grid=(columns // LANES,),
        scratch=[
            pltpu.VMEM((expand, LANES), f32),
            pltpu.VMEM((expand, LANES), f32),
            pltpu.VMEM((length, LANES), f32),
        ],
        mib=5 * max(1, length // 1024),
        cost=work(4 * expand * length * columns, 10 * length * columns, length * columns),
    )
    return found, slope, entry


def ema_back_kernel(dmix_ref, slope_ref, params_ref, pull_ref, heads_ref, total_ref, decay_ref):
    length = slope_ref.shape[0]
    expand = params_ref.shape[1]
    blocks = length // GROUP
    decay, log_decay, _ = rates(params_ref)
    decay_ref[...] = decay
    for b in range(blocks):
        rows = pl.ds(b * GROUP, GROUP)
        pull_ref[rows, :] = dmix_ref[b].astype(f32).T * slope_ref[rows, :].astype(f32)
    factors = [spread(decay_ref, j) for j in range(expand)]
    for g in range(0, blocks, SUB):

        def step(t, states):
            now = pull_ref[block_rows(g, GROUP - 1 - t), :]
            return tuple(f * s + now for f, s in zip(factors, states))

        states = (jnp.zeros((SUB, LANES), f32),) * expand
        states = lax.fori_loop(0, GROUP, step, states, unroll=8)
        for j in range(expand):
            heads_ref[state_rows(g, j, expand), :] = states[j]
    jump = jnp.exp(GROUP * log_decay)
    carry = jnp.zeros_like(jump)
    for b in reversed(range(blocks)):
        carry = jump * carry + heads_ref[pl.ds(b * expand, expand), :]
    total_ref[...] = carry


def ema_back(dmix, slope, params, after=()):
    length, columns = slope.shape
    expand = params.shape[1]
    shapes = ((length, columns), (length // GROUP * expand, columns), (expand, columns))
    return launch(
        ema_back_kernel,
        [(shape, f32) for shape in shapes],
        (dmix, slope, params),
        [by_tile(dmix.shape, 1), by_tile(slope.shape, 1), by_tile(params.shape, 2)],
        [by_tile(shape, 1) for shape in shapes],
        after=after,
        grid=(columns // LANES,),
        scratch=[pltpu.VMEM((expand, LANES), f32)],
        mib=5 * max(1, length // 1024),
        cost=work(2 * expand * length * columns, 8 * length * columns),
    )


def enter_from_later(spot_ref, heads_ref, totals_ref, enter_ref, log_decay, length):
    expand = log_decay.shape[0]
    whole = jnp.exp(length * log_decay)
    jump = jnp.exp(GROUP * log_decay)
    carry = jnp.zeros_like(jump)
    for k in reversed(range(totals_ref.shape[0])):
        carry = jnp.where(k > spot_ref[2], whole * carry + totals_ref[k], carry)
    for b in reversed(range(length // GROUP)):
        rows = pl.ds(b * expand, expand)
        enter_ref[rows, :] = carry
        carry = jump * carry + heads_ref[rows, :]


def ema_finish_kernel(
    spot_ref, pull_ref, heads_ref, params_ref, omega_ref, totals_ref, direct_ref, result_ref,
    grad_ref, output_ref, decay_ref, weight_ref, enter_ref, smooth_ref,
):
    length = pull_ref.shape[0]
    expand = params_ref.shape[1]
    blocks = length // GROUP
    decay, log_decay, weight = rates(params_ref)
    decay_ref[...] = decay
    weight_ref[...] = weight
    enter_from_later(spot_ref, heads_ref, totals_ref, enter_ref, log_decay, length)
    factors = [spread(decay_ref, j) for j in range(expand)]
    weights = [spread(weight_ref, j) for j in range(expand)]
    for g in range(0, blocks, SUB):

        def step(t, states):
            now = pull_ref[block_rows(g, GROUP - 1 - t), :]
            states = tuple(f * s + now for f, s in zip(factors, states))
            back = tree_sum([w * s for w, s in zip(weights, states)])
            smooth_ref[block_rows(g, GROUP - 1 - t), :] = back
            return states

        start = tuple(enter_ref[state_rows(g, j, expand), :] for j in range(expand))
        lax.fori_loop(0, GROUP, step, start, unroll=8)
    for b in range(blocks):
        rows = pl.ds(b * GROUP, GROUP)
        back = smooth_ref[rows, :] + omega_ref[...] * pull_ref[rows, :]
        grad_ref[:, rows] = back.T + direct_ref[b, 0].astype(f32)
        output_ref[:, rows] = result_ref[b, 0]


def ema_finish(spot, pull, heads, params, omega, totals, joint, after=()):
    length, columns = pull.shape

    def part(which):
        return pl.BlockSpec((length // GROUP, 1, LANES, GROUP), lambda i: (0, which, i, 0))

    expand = params.shape[1]
    return launch(
        ema_finish_kernel,
        [((columns, length), f32), ((columns, length), joint.dtype)],
        (spot, pull, heads, params, omega, totals, joint, joint),
        [
            in_smem(), by_tile(pull.shape, 1), by_tile(heads.shape, 1), by_tile(params.shape, 2),
            by_tile(omega.shape, 1), by_tile(totals.shape, 2), part(0), part(1),
        ],
        [by_tile((columns, length), 0)] * 2,
        after=after,
        grid=(columns // LANES,),
        scratch=[
            pltpu.VMEM((expand, LANES), f32),
            pltpu.VMEM((expand, LANES), f32),
            pltpu.VMEM((heads.shape[0], LANES), f32),
            pltpu.VMEM((length, LANES), f32),
        ],
        mib=5 * max(1, length // 1024),
        cost=work(4 * expand * length * columns, 14 * length * columns),
    )


def ema_sums_kernel(spot_ref, xs_ref, pull_ref, entry_ref, heads_ref, totals_ref, params_ref, sums_ref, decay_ref, enter_ref):
    length = xs_ref.shape[0]
    expand = params_ref.shape[1]
    blocks = length // GROUP
    half = expand // 2
    decay, log_decay, _ = rates(params_ref)
    decay_ref[...] = decay
    enter_from_later(spot_ref, heads_ref, totals_ref, enter_ref, log_decay, length)
    for low in range(0, expand, half):
        factors = [spread(decay_ref, low + j) for j in range(half)]
        zero = (jnp.zeros((SUB, LANES), f32),) * half
        plain, turned = zero, zero
        for g in range(0, blocks, SUB):

            def step(t, held):
                states, slants, plain, turned = held
                now, pull = xs_ref[block_rows(g, t), :], pull_ref[block_rows(g, t), :]
                slants = tuple(f * p + s for f, p, s in zip(factors, slants, states))
                states = tuple(f * s + now for f, s in zip(factors, states))
                plain = tuple(a + pull * s for a, s in zip(plain, states))
                turned = tuple(a + pull * p for a, p in zip(turned, slants))
                return states, slants, plain, turned

            start = tuple(entry_ref[state_rows(g, low + j, expand), :] for j in range(half))
            held = (start, zero, plain, turned)
            _, slants, plain, turned = lax.fori_loop(0, GROUP, step, held, unroll=4)
            turned = tuple(
                a + f * p * enter_ref[state_rows(g, low + j, expand), :]
                for j, (a, f, p) in enumerate(zip(turned, factors, slants))
            )
        for j in range(half):
            sums_ref[pl.ds(low + j, 1), :] = jnp.sum(plain[j], axis=0, keepdims=True)
            sums_ref[pl.ds(expand + low + j, 1), :] = jnp.sum(turned[j], axis=0, keepdims=True)
    straight = jnp.zeros((SUB, LANES), f32)
    for b in range(0, length, SUB):
        straight = straight + xs_ref[pl.ds(b, SUB), :] * pull_ref[pl.ds(b, SUB), :]
    sums_ref[pl.ds(2 * expand, SUB), :] = straight


def ema_sums(spot, xs, pull, entry, heads, totals, params, after=()):
    length, columns = xs.shape
    expand = params.shape[1]
    shape = (2 * expand + SUB, columns)
    return launch(
        ema_sums_kernel,
        [(shape, f32)],
        (spot, xs, pull, entry, heads, totals, params),
        [
            in_smem(), by_tile(xs.shape, 1), by_tile(xs.shape, 1), by_tile(entry.shape, 1), by_tile(entry.shape, 1),
            by_tile(totals.shape, 2), by_tile(params.shape, 2),
        ],
        [by_tile(shape, 1)],
        after=after,
        grid=(columns // LANES,),
        scratch=[pltpu.VMEM((expand, LANES), f32), pltpu.VMEM((entry.shape[0], LANES), f32)],
        mib=5 * max(1, length // 1024),
        cost=work(8 * expand * length * columns, 8 * length * columns),
    )[0]


def pad_to_lanes(part, dim):
    extra = -part.shape[dim] % LANES
    if extra == 0:
        return part
    return jnp.pad(part, [(0, extra if k == dim else 0) for k in range(part.ndim)])


def ema_params(alpha, delta, beta, eta, count):
    packed = jnp.swapaxes(jnp.stack([alpha, delta, beta, eta]), 1, 2)
    return pad_to_lanes(jnp.tile(packed, (1, 1, count)), 2)


def ema_param_grads(total, alpha, delta, beta, eta, count):
    channels, expand = alpha.shape
    summed = jnp.sum(total[:, : count * channels].reshape(-1, count, channels), axis=1)
    plain, turned = summed[:expand].T, summed[expand : 2 * expand].T
    omega = jnp.sum(summed[2 * expand :], axis=0)
    rate, damp = jax.nn.sigmoid(alpha), jax.nn.sigmoid(delta)
    g_alpha = eta * beta * rate * (1.0 - rate) * (plain - damp * rate * turned)
    g_delta = -(eta * beta * rate * rate * damp * (1.0 - damp)) * turned
    return g_alpha, g_delta, rate * eta * plain, rate * beta * plain, omega


low = jnp.bfloat16
CHUNK = 256
MIB = (3, 11, 8, 5, 6, 8, 8, 6, 4, 4)
TABLE = 384


def nn(left, right):
    return jnp.dot(left, right, preferred_element_type=f32)


def nt(left, right):
    return lax.dot_general(left, right, (((1,), (1,)), ((), ())), preferred_element_type=f32)


def silu_pair(pre):
    sigma = jax.nn.sigmoid(pre)
    return pre * sigma, sigma * (1.0 + pre * (1.0 - sigma))


def each(width, body, size=CHUNK):
    for at in range(0, width, size):
        body(at)


def wide_block(ref, which, n):
    part = ref[:, which, n]
    return part.reshape(part.shape[0] * part.shape[1], part.shape[2])


def live_lanes(spot_ref, lengths_ref, n, shape):
    return spot_ref[0] + lax.broadcasted_iota(jnp.int32, shape, 1) < lengths_ref[n]


def span_of(ref, n):
    return pl.ds(n * GROUP, GROUP)


def call(kernel, outs, ins, smem=0, hbm=0, scratch=(), moved=1, mib=16, after=()):
    spaces = [pltpu.SMEM] * smem + [pl.ANY] * hbm + [pltpu.VMEM] * (len(ins) - smem - hbm)
    return launch(
        kernel,
        outs,
        ins,
        [pl.BlockSpec(memory_space=space) for space in spaces],
        [pl.BlockSpec(memory_space=pltpu.VMEM) for _ in outs],
        after=after,
        scratch=scratch,
        mib=mib,
        cost=pl.CostEstimate(flops=1, bytes_accessed=moved, transcendentals=0),
    )


def vectors(width, mwidth, vwidth, ff):
    sizes = (
        ("mix", mwidth), ("value", vwidth), ("out", width), ("gain", width),
        ("shift", width), ("up", ff), ("down", width),
    )
    place, at = {}, 0
    for name, size in sizes:
        place[name] = at
        at += size
    return place


def piece(ref, base, at, size):
    return ref[:, pl.ds(base + at, size)]


def value_kernel(base, w_ref, x_ref, vec_ref, rows_ref, values_ref, slope_ref, rows_t_ref):
    for n in range(x_ref.shape[2]):
        rows = pl.ds(n * GROUP, GROUP)
        block = wide_block(x_ref, 0, n)
        rows_t_ref[:, rows] = block
        rows_ref[rows, :] = block.T

    def chunk(at):
        cols = pl.ds(at, CHUNK)
        act, slope = silu_pair(nn(rows_ref[...], w_ref[:, cols]) + piece(vec_ref, base, at, CHUNK))
        values_ref[:, cols] = act.astype(low)
        slope_ref[:, cols] = slope.astype(low)

    each(w_ref.shape[1], chunk)


def value_part(x, w_value, vec, where, after=()):
    width, vwidth = w_value.shape
    count = x.shape[2] * GROUP
    return call(
        functools.partial(value_kernel, where["value"]),
        [((count, width), low), ((count, vwidth), low), ((count, vwidth), low), ((width, count), low)],
        (w_value, x, vec),
        mib=MIB[0],
        after=after,
    )


def forward_kernel(
    pieces, where, spot_ref, lengths_ref, wmix_ref, wout_ref, wup_ref, wdown_ref,
    x_ref, values_ref, vec_ref, qscale_ref, qshift_ref, *refs
):
    forward_rows(spot_ref, refs[:pieces], refs[pieces], refs[-6])
    forward_body(
        where, spot_ref, lengths_ref, wmix_ref, wout_ref, wup_ref, wdown_ref,
        x_ref, values_ref, vec_ref, qscale_ref, qshift_ref, *refs[pieces + 1 :]
    )


def forward_rows(spot_ref, mixed_refs, mixed_t_ref, m_ref):
    for k, ref in enumerate(mixed_refs):
        seqs, channels, _ = ref.shape
        at = pl.multiple_of((spot_ref[1] ^ k) * channels, 16) if len(mixed_refs) > 1 else 0
        for n in range(seqs):
            mixed_t_ref[pl.ds(at, channels), pl.ds(n * GROUP, GROUP)] = ref[n]
    for n in range(m_ref.shape[0] // GROUP):
        rows = pl.ds(n * GROUP, GROUP)
        m_ref[rows, :] = mixed_t_ref[:, rows].T


def forward_body(
    where, spot_ref, lengths_ref, wmix_ref, wout_ref, wup_ref, wdown_ref,
    x_ref, values_ref, vec_ref, qscale_ref, qshift_ref,
    out_ref, query_ref, key_ref, shared_ref, qslope_ref, probs_ref, reset_ref, turned_ref, gated_t_ref,
    hslope_ref, uslope_ref, keep_ref, unit_ref, rstd_ref, normed_t_ref, hidden_t_ref, fslope_ref,
    m_ref, update_ref, gated_ref, blend_ref, normed_ref, ffn_ref,
):
    width, vwidth = wout_ref.shape[1], wout_ref.shape[0]
    zwidth = qscale_ref.shape[1]
    seqs = x_ref.shape[0] // GROUP

    def mix(at, size=CHUNK):
        cols = pl.ds(at, size)
        return nn(m_ref[...], wmix_ref[:, cols]) + piece(vec_ref, where["mix"], at, size)

    shared, qslope = silu_pair(mix(width, zwidth))
    shared_ref[...] = shared
    qslope_ref[...] = qslope
    query_ref[...] = (shared * qscale_ref[pl.ds(0, 1), :] + qshift_ref[pl.ds(0, 1), :]).astype(low)
    key_ref[...] = (shared * qscale_ref[pl.ds(1, 1), :] + qshift_ref[pl.ds(1, 1), :]).astype(low)
    causal = lax.broadcasted_iota(jnp.int32, (GROUP, GROUP), 0) >= lax.broadcasted_iota(
        jnp.int32, (GROUP, GROUP), 1
    )
    for n in range(seqs):
        rows = pl.ds(n * GROUP, GROUP)
        scores = jnp.where(causal, nt(query_ref[rows, :], key_ref[rows, :]) * zwidth**-0.5, -1e30)
        scores = jnp.exp(scores - jnp.max(scores, axis=-1, keepdims=True))
        probs_ref[rows, :] = scores / jnp.sum(scores, axis=-1, keepdims=True)

    def gate(at):
        update_ref[:, pl.ds(at, CHUNK)] = jax.nn.sigmoid(mix(at))

    each(width, gate)

    def attend(at):
        cols = pl.ds(at, CHUNK)
        reset, slope = silu_pair(mix(width + zwidth + at))
        attended = jnp.concatenate(
            [
                nn(probs_ref[pl.ds(n * GROUP, GROUP), :].astype(low), values_ref[pl.ds(n * GROUP, GROUP), cols])
                for n in range(seqs)
            ],
            axis=0,
        )
        reset_ref[:, cols] = reset.astype(low)
        turned_ref[:, cols] = (attended * slope).astype(low)
        gated = (reset * attended).astype(low)
        gated_ref[:, cols] = gated
        gated_t_ref[cols, :] = gated.T

    each(vwidth, attend)

    def hide(at):
        cols = pl.ds(at, CHUNK)
        pre = mix(width + zwidth + vwidth + at)
        pre = pre + nn(gated_ref[...], wout_ref[:, cols]) + piece(vec_ref, where["out"], at, CHUNK)
        hidden, slope = silu_pair(pre)
        update = update_ref[:, cols]
        keep = 1.0 - update
        resid = x_ref[:, cols].astype(f32)
        hslope_ref[:, cols] = (update * slope).astype(low)
        uslope_ref[:, cols] = ((hidden - resid) * update * keep).astype(low)
        keep_ref[:, cols] = keep.astype(low)
        blend_ref[:, cols] = update * hidden + keep * resid

    each(width, hide)
    for n in range(seqs):
        rows = pl.ds(n * GROUP, GROUP)
        blend = blend_ref[rows, :]
        centered = blend - jnp.mean(blend, axis=-1, keepdims=True)
        rstd = lax.rsqrt(jnp.mean(centered * centered, axis=-1, keepdims=True) + 1e-05)
        unit = centered * rstd
        unit_ref[rows, :] = unit.astype(low)
        rstd_ref[rows, :] = jnp.broadcast_to(rstd, (GROUP, LANES))
        normed = unit * piece(vec_ref, where["gain"], 0, width) + piece(vec_ref, where["shift"], 0, width)
        blend_ref[rows, :] = normed
        normed_ref[rows, :] = normed.astype(low)
        normed_t_ref[:, rows] = normed.astype(low).T

    def lift(at):
        cols = pl.ds(at, CHUNK)
        act, slope = silu_pair(nn(normed_ref[...], wup_ref[:, cols]) + piece(vec_ref, where["up"], at, CHUNK))
        fslope_ref[:, cols] = slope.astype(low)
        act = act.astype(low)
        ffn_ref[:, cols] = act
        hidden_t_ref[cols, :] = act.T

    each(wup_ref.shape[1], lift)

    def drop(at):
        cols = pl.ds(at, CHUNK)
        blend_ref[:, cols] = blend_ref[:, cols] + nn(ffn_ref[...], wdown_ref[:, cols]) + piece(vec_ref, where["down"], at, CHUNK)

    each(width, drop)
    for n in range(seqs):
        result = blend_ref[pl.ds(n * GROUP, GROUP), :].astype(low).T
        result = jnp.where(live_lanes(spot_ref, lengths_ref, n, result.shape), result, jnp.zeros_like(result))
        out_ref[:, n] = result.reshape(out_ref.shape[0], out_ref.shape[2], GROUP)


def forward_part(spot, lengths, folded, mixed, x, values, w_mix, w_out, w_up, w_down, vec, where, qk_scale, qk_shift, after=()):
    vwidth, width = w_out.shape
    zwidth = qk_scale.shape[1]
    ff = w_up.shape[1]
    count = x.shape[0]
    narrow, wide = (count, width), (count, vwidth)
    outs = [
        ((width, count), low), (folded, low), ((count, zwidth), low), ((count, zwidth), low), ((count, zwidth), f32),
        ((count, zwidth), f32), ((count, GROUP), f32), (wide, low), (wide, low), ((vwidth, count), low),
        (narrow, low), (narrow, low), (narrow, low), (narrow, low), ((count, LANES), f32),
        ((width, count), low), ((ff, count), low), ((count, ff), low),
    ]
    scratch = [pltpu.VMEM(narrow, low), pltpu.VMEM(narrow, f32), pltpu.VMEM(wide, low)]
    scratch += [pltpu.VMEM(narrow, f32), pltpu.VMEM(narrow, low), pltpu.VMEM((count, ff), low)]
    macs = w_mix.size + w_out.size + w_up.size + w_down.size
    return call(
        functools.partial(forward_kernel, len(mixed), where),
        outs,
        (spot, lengths, w_mix, w_out, w_up, w_down, x, values, vec, qk_scale, qk_shift, *mixed),
        smem=2,
        mib=MIB[1],
        after=after,
        scratch=scratch,
    )


def column_sum(part):
    return jnp.sum(part.astype(f32), axis=0, keepdims=True)


def put(ref, row, value, columns):
    if isinstance(ref, tuple):
        lone = value.shape[0] // len(ref)
        for k, one in enumerate(ref):
            put(one, row, value[k * lone : (k + 1) * lone], columns)
        return
    if len(ref.shape) == 2:
        ref[...] = value
        return
    owners = ref.shape[0]
    lone = value.shape[0] // owners
    for owner in range(owners):
        part = value[owner * lone : (owner + 1) * lone]
        for i, at in enumerate(range(0, value.shape[1], columns)):
            ref[owner, pl.ds(row + i * lone, lone), :] = part[:, at : at + columns]


def split_product(side, keep_ref, send_ref, left, right_ref, half, columns, row=0):
    total = right_ref.shape[1]
    for ref, which in ((keep_ref, side), (send_ref, 1 - side)):
        base = which * (total - half)
        parts = []
        for at in range(0, half, CHUNK):
            cols = pl.ds(pl.multiple_of(base + at, 128), min(CHUNK, half - at))
            parts.append(nn(left, right_ref[:, cols]).astype(low))
        put(ref, row, jnp.concatenate(parts, axis=1), columns)


def split_narrow(side, keep_ref, send_ref, left_ref, right_ref):
    both = [nn(left_ref[pl.ds(at, CHUNK), :], right_ref[...]).astype(low) for at in range(0, left_ref.shape[0], CHUNK)]
    both = jnp.concatenate(both, axis=0)
    half = both.shape[1] // 2
    near, far = both[:, :half], both[:, half:]
    put(keep_ref, 0, jnp.where(side == 0, near, far), half)
    put(send_ref, 0, jnp.where(side == 0, far, near), half)


def pair_outs(tall, wide, owners, lines=0):
    if not owners:
        return [((tall[0], tall[1] // 2), low)] * 2 + [((wide[0], wide[1] // 2), low)] * 2
    rows = (tall[0] * tall[1] + wide[0] * wide[1]) // (tall[1] * owners) + lines
    return [((owners, rows, tall[1] // 2), low)] * 2


def back_ffn_kernel(
    spot_ref, lengths_ref, wdown_ref, grad_ref, hidden_t_ref, fslope_ref, normed_t_ref, *refs
):
    halves, (g_ref, dffn_ref, small_ref) = refs[:-3], refs[-3:]
    width, ff = g_ref.shape[1], wdown_ref.shape[0]
    for n in range(grad_ref.shape[2]):
        part = wide_block(grad_ref, 1, n)
        part = jnp.where(live_lanes(spot_ref, lengths_ref, n, part.shape), part, jnp.zeros_like(part))
        g_ref[pl.ds(n * GROUP, GROUP), :] = part.T
    small_ref[:, pl.ds(0, width)] = column_sum(g_ref[...])
    side = spot_ref[2] & 1
    split_narrow(side, halves[0], halves[1], hidden_t_ref, g_ref)

    def lift(at):
        part = pl.ds(at, CHUNK)
        pulled = (nt(g_ref[...], wdown_ref[part, :]) * fslope_ref[:, part].astype(f32)).astype(low)
        dffn_ref[:, part] = pulled
        small_ref[:, pl.ds(width + at, CHUNK)] = column_sum(pulled)

    each(ff, lift)
    tall = hidden_t_ref.shape[0] // halves[0].shape[0]
    split_product(side, halves[-2], halves[-1], normed_t_ref[...], dffn_ref, ff // 2, halves[-2].shape[-1], tall)
    if len(halves) == 2:
        for ref in halves:
            owners, rows, columns = ref.shape
            ref[:, pl.ds(2 * tall, rows - 2 * tall), :] = jnp.zeros((owners, rows - 2 * tall, columns), low)


def back_ffn(spot, lengths, owners, lines, grad, hidden_t, fslope, normed_t, w_down, after=()):
    ff, width = w_down.shape
    count = fslope.shape[0]
    outs = pair_outs((ff, width), (width, ff), owners, lines)
    outs += [((count, width), low), ((count, ff), low), ((1, width + ff), f32)]
    *halves, g, dffn, small = call(
        back_ffn_kernel,
        outs,
        (spot, lengths, w_down, grad, hidden_t, fslope, normed_t),
        smem=2,
        mib=MIB[2],
        after=after,
    )
    return halves, g, dffn, small


def back_norm_kernel(
    base, wup_ref, g_ref, dffn_ref, unit_ref, rstd_ref, vec_ref, hslope_ref, uslope_ref, kept_ref,
    dh_ref, du_ref, direct_ref, small_ref, dn_ref,
):
    width = wup_ref.shape[0]

    def drop(at):
        part = pl.ds(at, CHUNK)
        pulled = g_ref[:, part].astype(f32) + nt(dffn_ref[...], wup_ref[part, :])
        dn_ref[:, part] = pulled
        small_ref[:, part] = column_sum(pulled * unit_ref[:, part].astype(f32))
        small_ref[:, pl.ds(width + at, CHUNK)] = column_sum(pulled)

    each(width, drop)
    for n in range(g_ref.shape[0] // GROUP):
        rows = pl.ds(n * GROUP, GROUP)
        unit = unit_ref[rows, :].astype(f32)
        pulled = dn_ref[rows, :] * piece(vec_ref, base, 0, width)
        inner = jnp.mean(pulled * unit, axis=-1, keepdims=True)
        blend = pulled - jnp.mean(pulled, axis=-1, keepdims=True) - unit * inner
        blend = blend * rstd_ref[rows, :][:, :1]
        dh_ref[rows, :] = (blend * hslope_ref[rows, :].astype(f32)).astype(low)
        du_ref[rows, :] = (blend * uslope_ref[rows, :].astype(f32)).astype(low)
        direct_ref[rows, :] = (blend * kept_ref[rows, :].astype(f32)).astype(low)


def back_norm(g, dffn, unit, rstd, vec, where, hslope, uslope, kept, w_up, after=()):
    width = w_up.shape[0]
    narrow = g.shape
    return call(
        functools.partial(back_norm_kernel, where["gain"]),
        [(narrow, low)] * 3 + [((1, 2 * width), f32)],
        (w_up, g, dffn, unit, rstd, vec, hslope, uslope, kept),
        mib=MIB[3],
        after=after,
        scratch=[pltpu.VMEM(narrow, f32)],
    )


def back_attend_kernel(
    wout_ref, wmix_ref, wvalue_ref,
    dh_ref, du_ref, direct_ref, reset_ref, turned_ref, values_ref, vslope_ref, probs_ref,
    query_ref, key_ref, shared_ref, qslope_ref, qscale_ref, small_ffn_ref, small_norm_ref, result_ref,
    dmix_ref, dvalue_ref, mixed_ref, joint_ref,
    table_ref,
    datt_ref,
):
    vwidth, width = wout_ref.shape
    zwidth = qscale_ref.shape[1]
    count = dh_ref.shape[0]
    seqs = count // GROUP
    dmix_ref[:, pl.ds(0, width)] = du_ref[...]
    dmix_ref[:, pl.ds(width + zwidth + vwidth, width)] = dh_ref[...]

    def gate(at):
        part = pl.ds(at, CHUNK)
        pulled = nt(dh_ref[...], wout_ref[part, :])
        dmix_ref[:, pl.ds(width + zwidth + at, CHUNK)] = (
            pulled * turned_ref[:, part].astype(f32)
        ).astype(low)
        datt_ref[:, part] = (pulled * reset_ref[:, part].astype(f32)).astype(low)

    each(vwidth, gate)
    scale = zwidth**-0.5
    q_scale, k_scale = qscale_ref[pl.ds(0, 1), :], qscale_ref[pl.ds(1, 1), :]
    zero = jnp.zeros((1, zwidth), f32)
    sums = [zero, zero, zero, zero]
    for n in range(seqs):
        rows = pl.ds(n * GROUP, GROUP)
        probs = probs_ref[rows, :]
        pulled = nt(datt_ref[rows, :], values_ref[rows, :])
        pulled = probs * (pulled - jnp.sum(pulled * probs, axis=-1, keepdims=True))
        pulled = pulled.astype(low)
        d_query = nn(pulled, key_ref[rows, :]) * scale
        d_key = nn(pulled.T, query_ref[rows, :]) * scale
        probs_t = probs.astype(low).T
        shared = shared_ref[rows, :]
        found = (d_query * shared, d_key * shared, d_query, d_key)
        sums = [a + jnp.sum(b, axis=0, keepdims=True) for a, b in zip(sums, found)]
        dmix_ref[rows, pl.ds(width, zwidth)] = (
            (d_query * q_scale + d_key * k_scale) * qslope_ref[rows, :]
        ).astype(low)
        dvalue_ref[rows, :] = (nn(probs_t, datt_ref[rows, :]) * vslope_ref[rows, :].astype(f32)).astype(low)

    def turn(result):
        devices, _, channels, _ = mixed_ref.shape
        return result.astype(low).T.reshape(devices, channels, GROUP)

    for n in range(0, seqs, 2):
        result = nt(dmix_ref[pl.ds(n * GROUP, 2 * GROUP), :], wmix_ref[...])
        mixed_ref[:, n] = turn(result[:GROUP])
        mixed_ref[:, n + 1] = turn(result[GROUP:])
    for n in range(0, seqs, 2):
        rows = pl.ds(n * GROUP, 2 * GROUP)
        result = direct_ref[rows, :].astype(f32) + nt(dvalue_ref[rows, :], wvalue_ref[...])
        joint_ref[:, 0, n] = turn(result[:GROUP])
        joint_ref[:, 0, n + 1] = turn(result[GROUP:])
    joint_ref[:, 1] = result_ref[...]
    ff = small_ffn_ref.shape[1] - width
    found = (
        column_sum(dmix_ref[...]), column_sum(dvalue_ref[...]), column_sum(dh_ref[...]),
        sums[0], sums[1], sums[2], sums[3], small_norm_ref[:, :width], small_norm_ref[:, width:],
        small_ffn_ref[:, width:], small_ffn_ref[:, :width],
    )
    lines = []
    for part in found:
        for at in range(0, part.shape[1], TABLE):
            line = part[:, at : at + TABLE]
            lack = TABLE - line.shape[1]
            lines.append(line if lack == 0 else jnp.concatenate([line, jnp.zeros((1, lack), f32)], axis=1))
    lines.append(jnp.zeros((table_ref.shape[0] - len(lines), TABLE), f32))
    table_ref[...] = jnp.concatenate(lines, axis=0).astype(low)


def back_attend(dh, du, direct, reset, turned, values, vslope, probs, query, key, shared, qslope, qk_scale, small_ffn, small_norm, result, w_out, w_mix, w_value, after=()):
    vwidth, width = w_out.shape
    mwidth = w_mix.shape[1]
    count = dh.shape[0]
    outs = [((count, mwidth), low), ((count, vwidth), low)]
    outs += [(result.shape, low), (result.shape[:1] + (2,) + result.shape[1:], low), ((64, TABLE), low)]
    scratch = [pltpu.VMEM((count, vwidth), low)]
    macs = w_out.size + w_mix.size + w_value.size
    return call(
        back_attend_kernel,
        outs,
        (w_out, w_mix, w_value, dh, du, direct, reset, turned, values, vslope, probs, query, key, shared, qslope, qk_scale, small_ffn, small_norm, result),
        mib=MIB[4],
        after=after,
        scratch=scratch,
    )


def back_mid_kernel(spot_ref, gated_t_ref, dh_ref, x_t_ref, dvalue_ref, table_ref, *halves):
    side = spot_ref[2] & 1
    if len(halves) == 4:
        (kept, sent, wide_kept, wide_sent), tall = halves, 0
    else:
        kept, sent = halves[0], halves[1:]
        wide_kept, wide_sent, tall = kept, sent, gated_t_ref.shape[0] // kept.shape[0]
    split_narrow(side, kept, sent, gated_t_ref, dh_ref)
    split_product(
        side, wide_kept, wide_sent, x_t_ref[...], dvalue_ref, dvalue_ref.shape[1] // 2, wide_kept.shape[-1], tall
    )
    if len(halves) == 4:
        return
    lines = kept.shape[1] - 2 * tall
    high = table_ref.shape[0] // (2 * lines)
    for refs, which in (((kept,), side), (sent, 1 - side)):
        for ref in refs:
            for owner in range(ref.shape[0]):
                at = pl.multiple_of((2 * (owner % high) + which) * lines, 16)
                ref[owner, pl.ds(2 * tall, lines), :] = table_ref[pl.ds(at, lines), :]


def halved(outs):
    (kept, kind), (sent, _) = outs
    return [(kept, kind)] + [((sent[0] // 2,) + sent[1:], kind)] * 2


def back_mid(spot, owners, gated_t, dh, x_t, dvalue, table, lines, after=()):
    count, width = dh.shape
    vwidth = dvalue.shape[1]
    outs = pair_outs((vwidth, width), (width, vwidth), owners, lines)
    found = call(
        back_mid_kernel,
        halved(outs) if owners else outs,
        (spot, gated_t, dh, x_t, dvalue, table),
        smem=1,
        mib=MIB[5],
        after=after,
    )
    if owners:
        return [found[0]], [list(found[1:])]
    return [found[0], found[2]], [[found[1]], [found[3]]]


def back_mix_kernel(spot_ref, mixed_t_ref, dmix_ref, keep_ref, *send_refs):
    half = keep_ref.shape[-1]
    split_product(spot_ref[2] & 1, keep_ref, send_refs, mixed_t_ref[...], dmix_ref, half, half)


def back_mix_weight(spot, owners, mixed_t, dmix, after=()):
    mwidth = dmix.shape[1]
    width, count = mixed_t.shape
    half = -(-mwidth // 256) * 128
    outs = [((width, half), low)] * 2
    kept, *sent = call(
        back_mix_kernel,
        halved(outs) if owners else outs,
        (spot, mixed_t, dmix),
        smem=1,
        mib=MIB[6],
        after=after,
    )
    return [kept], [sent]


def halve_kernel(index, bit, spot_ref, kept_ref, *refs):
    arrived, (sent_ref, stay_ref) = refs[:-2], refs[-2:]
    outer, inner, _, _ = sent_ref.shape
    lone = outer // len(arrived)
    mine = (spot_ref[index] >> bit) & 1
    for ref, which in ((sent_ref, 1 - mine), (stay_ref, mine)):
        for a in range(outer):
            for b in range(inner):
                total = kept_ref[a, which, b].astype(f32) + arrived[a // lone][a % lone, which, b].astype(f32)
                ref[a, b] = total.astype(low)


def halve(spot, kept, arrived, index, bit, at, after=()):
    dims = kept.shape[:-2]
    outer, inner = 1 << at, 1 << (len(dims) - at - 1)
    block = kept.shape[-2:]

    def shaped(part):
        return part.reshape((-1, 2, inner) + block)

    sent, stay = call(
        functools.partial(halve_kernel, index, bit),
        [((outer, inner) + block, low)] * 2,
        (spot, shaped(kept), *map(shaped, arrived)),
        smem=1,
        mib=MIB[7],
        after=after,

    )
    rest = dims[:at] + dims[at + 1 :] + block
    return sent.reshape(rest), stay.reshape(rest)


def finish_pair_kernel(count, lines, spot_ref, *refs):
    shares, outs = refs[:count], refs[count:]
    tall_ref, wide_ref = outs[:2]
    columns = shares[0].shape[1]
    cut = tall_ref.shape[0] * 2 // len(shares)
    lone = wide_ref.shape[0] * 2 // len(shares)
    for k, ref in enumerate(shares):
        at = spot_ref[2] ^ k
        high, side = at >> 1, at & 1
        tall_ref[pl.ds(pl.multiple_of(high * cut, 8), cut), pl.ds(pl.multiple_of(side * columns, 128), columns)] = ref[
            pl.ds(0, cut), :
        ].astype(f32)
        runs = wide_ref.shape[1] // 2 // columns
        for run in range(runs):
            wide_ref[
                pl.ds(pl.multiple_of(high * lone, 8), lone),
                pl.ds(pl.multiple_of((side * runs + run) * columns, 128), columns),
            ] = ref[pl.ds(cut + run * lone, lone), :].astype(f32)
        if lines:
            outs[-1][pl.ds(pl.multiple_of(at * lines, 8), lines), :] = ref[pl.ds(2 * cut, lines), :].astype(f32)
    if lines:
        row = 0
        for ref in outs[2:-1]:
            if len(ref.shape) == 2:
                for k in range(ref.shape[0]):
                    ref[pl.ds(k, 1), :] = outs[-1][pl.ds(row, 1), :][:, : ref.shape[1]]
                    row += 1
                continue
            for at in range(0, ref.shape[0], columns):
                size = min(columns, ref.shape[0] - at)
                ref[pl.ds(at, size)] = outs[-1][row, :size]
                row += 1


def finish_pair(spot, shares, tall, wide, lines=0, vectors=(), after=()):
    outs = [(tall, f32), (wide, f32)] + [(shape, f32) for shape in vectors]
    count = len(shares)
    scratch = [pltpu.VMEM((count * lines, shares[0].shape[1]), f32)] if lines else []
    kernel = functools.partial(finish_pair_kernel, count, lines)
    return call(kernel, outs, (spot, *shares), smem=1, mib=MIB[8], scratch=scratch, after=after)


def finish_mix_kernel(spot_ref, *refs):
    shares, out_ref = refs[:-1], refs[-1]
    half, mwidth = shares[0].shape[1], out_ref.shape[1]
    common = 2 * half - mwidth
    lone = out_ref.shape[0] * 2 // len(shares)
    for k, ref in enumerate(shares):
        at = spot_ref[2] ^ k
        rows = pl.ds(pl.multiple_of((at >> 1) * lone, 8), lone)
        base = pl.multiple_of(common + (at & 1) * (mwidth - half), 128)
        out_ref[rows, pl.ds(base, half - common)] = ref[:, common:].astype(f32)
        if common:

            @pl.when(at & 1 == 0)
            def _():
                out_ref[rows, pl.ds(0, common)] = ref[:, :common].astype(f32)


def finish_mix(spot, shares, shape, after=()):
    return call(finish_mix_kernel, [(shape, f32)], (spot, *shares), smem=1, mib=MIB[9], after=after)[0]


Y_FIRST = (("tok", 1), ("ch", 0))
Y_THEN_Z = (("tok", 1), ("ch", 1), ("ch", 0))
X_FIRST = (("ch", 0), ("tok", 1))


def bits_of(axis):
    return lax.axis_size(axis).bit_length() - 1


def across(part, axis, turn):
    return lax.ppermute(part, axis, [(i, i ^ turn) for i in range(lax.axis_size(axis))])


def exchange(part, axis, bit):
    return across(part, axis, 1 << bit)


def side_of(axis, bit):
    return (lax.axis_index(axis) >> bit) & 1


def by_owner(grad):
    dims = (2,) * (bits_of("ch") + bits_of("tok") - 1)
    return grad.reshape(dims + (-1, grad.shape[-1]))


def fold(part, columns):
    runs = [part[..., at : at + columns] for at in range(0, part.shape[-1], columns)]
    return jnp.concatenate(runs, axis=-2)


def add(left, right):
    return (left.astype(f32) + right.astype(f32)).astype(low)


def plain_halve(kept, arrived, mine, at):
    columns = min(part.shape[-1] for part in kept)

    def pick(which):
        def one(part):
            return lax.dynamic_index_in_dim(part, which, at, keepdims=False)

        return jnp.concatenate([fold(add(one(a), one(b)), columns) for a, b in zip(kept, arrived)], axis=-2)

    return pick(1 - mine), pick(mine)


class Sum:
    def __init__(self, spot, kept, sent, order):
        self.spot = spot
        self.names = [("ch", k) for k in reversed(range(bits_of("ch")))]
        self.names += [("tok", k) for k in reversed(range(1, bits_of("tok")))]
        self.stages = list(order) + [name for name in reversed(self.names) if name not in order]
        self.kept = [by_owner(part) for part in kept]
        arrived = [[exchange(piece, "tok", 0) for piece in part] for part in sent]
        self.arrived = arrived[0] if self.by_kernel() else [by_owner(part) for part, in arrived]

    def by_kernel(self):
        return len(self.kept) == 1 and self.kept[0].shape[-2] % 16 == 0

    def step(self, after=()):
        axis, bit = self.stages.pop(0)
        at = self.names.index((axis, bit))
        self.names.remove((axis, bit))
        if self.by_kernel():
            index = 1 if axis == "ch" else 2
            sent, stay = halve(self.spot, self.kept[0], self.arrived, index, bit, at, after)
        else:
            sent, stay = plain_halve(self.kept, self.arrived, side_of(axis, bit), at)
        self.kept, self.arrived = [stay], [exchange(sent, axis, bit)]
        return stay

    def shares(self):
        found = [add(self.kept[0], self.arrived[0])]
        for bit in reversed(range(1, bits_of("tok"))):
            found += [exchange(part, "tok", bit) for part in found]
        lower = [exchange(part, "tok", 0) for part in found]
        size = bits_of("tok") - 1
        order = [sum(((k >> (size - 1 - i)) & 1) << i for i in range(size)) for k in range(len(found))]
        found = [part for k in order for part in (found[k], lower[k])]
        return found


def in_order(shares, place):
    bit = 1
    while bit < len(shares):
        swapped = (place & bit) != 0
        shares = [jnp.where(swapped, shares[k ^ bit], shares[k]) for k in range(len(shares))]
        bit *= 2
    return jnp.stack(shares)


def plain_pair(place, shares, tall, wide):
    whole = in_order(shares, place).astype(f32)
    high = len(shares) // 2
    cut, lone = tall[0] // high, wide[0] // high
    whole = whole.reshape((high, 2) + whole.shape[1:])
    first = whole[:, :, :cut].transpose(0, 2, 1, 3).reshape(tall)
    second = whole[:, :, cut:].reshape(high, 2, -1, lone, whole.shape[-1])
    return first, second.transpose(0, 3, 1, 2, 4).reshape(wide)


def plain_mix(place, shares, shape):
    whole = in_order(shares, place).astype(f32)
    half = whole.shape[-1]
    whole = whole.reshape((len(shares) // 2, 2) + whole.shape[1:])
    whole = jnp.concatenate([whole[:, 0], whole[:, 1, :, 2 * half - shape[1] :]], axis=-1)
    return whole.reshape(shape)


def sum_tok(part):
    for bit in range(bits_of("tok")):
        part = part + exchange(part, "tok", bit)
    return part


def swap(parts):
    return lax.all_to_all(parts, "ch", split_axis=0, concat_axis=0, tiled=True)


def folded(parts):
    devices, channels, span = parts.shape[0], parts.shape[-2], parts.shape[-1]
    if channels % 16 == 0:
        return parts
    return jnp.moveaxis(parts, 0, -3).reshape((1,) + parts.shape[1:-2] + (devices * channels, span))


def unfolded(parts, devices):
    if parts.shape[0] == devices:
        return parts
    channels, span = parts.shape[-2] // devices, parts.shape[-1]
    return jnp.moveaxis(parts.reshape(parts.shape[1:-2] + (devices, channels, span)), -3, 0)


def local(
    inputs,
    out_grad,
    seq_lengths,
    ema_alpha,
    ema_delta,
    ema_beta,
    ema_eta,
    ema_omega,
    w_mix,
    b_mix,
    w_value,
    b_value,
    w_out,
    b_out,
    qk_scale,
    qk_shift,
    ln_gain,
    ln_bias,
    w_up,
    b_up,
    w_down,
    b_down,
):
    count, channels, local_len = inputs.shape
    width, mwidth = w_mix.shape
    vwidth, ff = w_value.shape[1], w_up.shape[1]
    devices, tok_size = lax.axis_size("ch"), lax.axis_size("tok")
    columns = count * channels
    span = local_len // devices
    tok_index = lax.axis_index("tok").astype(jnp.int32)
    ch_index = lax.axis_index("ch").astype(jnp.int32)
    spot = jnp.stack([tok_index * local_len + ch_index * span, ch_index, tok_index])
    apart = devices <= 8 and channels % 16 == 0

    def by_column(parts):
        whole = unfolded(parts, devices)
        return pad_to_lanes(whole.reshape(whole.shape[:-3] + (columns, span)), whole.ndim - 3)

    where = vectors(width, mwidth, vwidth, ff)
    vec = jnp.concatenate([b_mix, b_value, b_out, ln_gain, ln_bias, b_up, b_down])[None]
    params = ema_params(ema_alpha, ema_delta, ema_beta, ema_eta, count)
    omega = pad_to_lanes(jnp.tile(ema_omega, count)[None], 1)

    flat = inputs.reshape(columns, local_len)
    raw = by_blocks(spot, flat, out_grad.reshape(columns, local_len))
    raw = folded(swap(raw.reshape(devices, 2, count, channels, span)))
    xs, ends, total = ema_ends(pad_to_lanes(flat, 0), params)
    totals = lax.all_gather(total, "tok")
    mixed, slope, entry = ema_mix(spot, xs, ends, params, omega, totals, apart)
    if apart:
        mixed = [part.reshape(count, channels, span) for part in mixed]
        mixed = [part if k == 0 else across(part, "ch", k) for k, part in enumerate(mixed)]
    else:
        mixed = folded(swap(mixed[0][:, :columns].reshape(devices, count, channels, span)))
        mixed = [mixed[0]] if mixed.shape[0] == 1 else [mixed.transpose(1, 0, 2, 3).reshape(count, width, span)]
    x, values, vslope, x_t = value_part(raw, w_value, vec, where, (entry,))
    (
        mixed_t, result, query, key, shared, qslope, probs, reset, turned, gated_t,
        hslope, uslope, keep, unit, rstd, normed_t, hidden_t, fslope,
    ) = forward_part(
        spot, seq_lengths, raw.shape[:1] + raw.shape[2:], mixed, x, values, w_mix, w_out, w_up, w_down, vec,
        where, qk_scale, qk_shift,
    )
    owners = devices * tok_size // 2
    joined = owners if width // owners % 16 == 0 else 0
    lines = 64 // tok_size
    halves, g, dffn, small_ffn = back_ffn(
        spot, seq_lengths, joined, lines, raw, hidden_t, fslope, normed_t, w_down
    )
    ffn = Sum(spot, halves[::2], [[part] for part in halves[1::2]], Y_THEN_Z)
    dh, du, direct, small_norm = back_norm(g, dffn, unit, rstd, vec, where, hslope, uslope, keep, w_up)
    last = ffn.step((small_norm,))
    dmix, dvalue, back_mix, joint, table = back_attend(
        dh, du, direct, reset, turned, values, vslope, probs, query, key, shared, qslope,
        qk_scale, small_ffn, small_norm, result, w_out, w_mix, w_value, (last,),
    )
    kept, sent = back_mix_weight(spot, joined, mixed_t, dmix, (table,))
    mix = Sum(spot, kept, sent, X_FIRST)
    kept, sent = back_mid(spot, joined, gated_t, dh, x_t, dvalue, table, lines, (kept[0],))
    last = kept[0]
    back_mix = swap(unfolded(back_mix, devices))
    if not joined:
        table = table.reshape(tok_size // 2, 2, lines, TABLE)
        for group, which in ((kept, side_of("tok", 0)), (sent, 1 - side_of("tok", 0))):
            part = lax.dynamic_index_in_dim(table, which, 1, keepdims=False)
            part = jnp.broadcast_to(part[None], (devices,) + part.shape).reshape(-1, TABLE)
            group.append(part if group is kept else [part])
    mid = Sum(spot, kept, sent, Y_FIRST)
    last = ffn.step((last,))
    last = mix.step((last,))
    last = mid.step((last,))
    joint, back_mix, _ = lax.optimization_barrier((unfolded(joint, devices), back_mix, last))
    joint = swap(joint)
    pull, heads, total = ema_back(by_column(back_mix), slope, params, (last,))
    totals = lax.all_gather(total, "tok")
    last = ffn.step((totals,))
    last = mix.step((last,))
    last = mid.step((last,))
    sums = ema_sums(spot, xs, pull, entry, heads, totals, params, (last,))
    last = mix.step((sums,))
    last = mid.step((last,))
    while len(mid.stages) + len(mix.stages) + len(ffn.stages):
        for group in (mix, mid, ffn):
            last = group.step((last,)) if group.stages else last
    input_grad, output = ema_finish(spot, pull, heads, params, omega, totals, by_column(joint), (last,))
    ema_grads = ema_param_grads(sum_tok(sums), ema_alpha, ema_delta, ema_beta, ema_eta, count)
    mix.arrived[0], output, ema_grads = lax.optimization_barrier((mix.arrived[0], output, ema_grads))
    last = output
    input_grad = input_grad[:columns].reshape(inputs.shape)
    output = output[:columns].reshape(inputs.shape)

    tall, wide = (vwidth // devices, width), (width // devices, vwidth)
    shares = mid.shares()
    half = qk_scale.shape[1]
    across_mix = (width // devices, mwidth)
    if joined:
        vectors_of = [(mwidth,), (vwidth,), (width,), qk_scale.shape, qk_scale.shape, (width,), (width,), (ff,), (width,)]
        g_down, g_up = finish_pair(spot, ffn.shares(), tall, wide, after=(last,))
        g_out, g_value, *found = finish_pair(spot, shares, tall, wide, lines, vectors_of, (last,))
        g_mix = finish_mix(spot, mix.shares(), across_mix, (last,))
    else:
        table = in_order([part[-lines:] for part in shares], tok_index).astype(f32).reshape(-1)
        shares = [part[:-lines] for part in shares]
        g_out, g_value = plain_pair(tok_index, shares, tall, wide)
        g_down, g_up = plain_pair(tok_index, ffn.shares(), tall, wide)
        g_mix = plain_mix(tok_index, mix.shares(), across_mix)
        found, at = [], 0
        for size in (mwidth, vwidth, width, half, half, half, half, width, width, ff, width):
            found.append(table[at : at + size])
            at += -(-size // TABLE) * TABLE
        found = found[:3] + [jnp.stack(found[3:5]), jnp.stack(found[5:7])] + found[7:]
    g_bmix, g_bvalue, g_bout, g_qscale, g_qshift, g_gain, g_lnbias, g_bup, g_bdown = found
    return (
        output,
        input_grad,
        *ema_grads,
        g_mix,
        g_bmix,
        g_value,
        g_bvalue,
        g_out,
        g_bout,
        g_qscale,
        g_qshift,
        g_gain,
        g_lnbias,
        g_up,
        g_bup,
        g_down,
        g_bdown,
    )


def solution(mesh):
    by_ch = P("ch", None)
    placed = P(None, "ch", "tok")
    return jax.shard_map(
        local,
        mesh=mesh,
        in_specs=(placed, placed, P()) + (by_ch,) * 4 + (P("ch"),) + (P(),) * 14,
        out_specs=(
            (placed, placed)
            + (by_ch,) * 4
            + (P("ch"), by_ch, P(), by_ch, P(), by_ch)
            + (P(),) * 5
            + (by_ch, P(), by_ch, P())
        ),
        check_vma=False,
    )
```

```python
import functools
import jax
import jax.numpy as jnp
from jax import lax
from jax.experimental import pallas as pl
from jax.experimental.pallas import tpu as pltpu
from jax.sharding import PartitionSpec as P

GROUP = 128
SUB = 8
LANES = 128
f32 = jnp.float32


def by_tile(shape, dim):
    block = tuple(LANES if k == dim else size for k, size in enumerate(shape))
    return pl.BlockSpec(block, lambda i: tuple(i if k == dim else 0 for k in range(len(shape))))


def in_smem():
    return pl.BlockSpec(memory_space=pltpu.SMEM)


def roomy(mib=5):
    return pltpu.CompilerParams(vmem_limit_bytes=mib * 1024 * 1024)


def work(flops, moved, exps=0):
    return pl.CostEstimate(flops=1, bytes_accessed=1, transcendentals=0)


def launch(kernel, outs, ins, in_specs, out_specs, after=(), grid=(), scratch=(), mib=5, cost=None):
    count = len(ins)

    def run(*refs):
        kernel(*refs[:count], *refs[count + len(after) :])

    return pl.pallas_call(
        run,
        grid=grid,
        out_shape=tuple(jax.ShapeDtypeStruct(shape, kind) for shape, kind in outs),
        in_specs=list(in_specs) + [pl.BlockSpec(memory_space=pl.ANY)] * len(after),
        out_specs=tuple(out_specs),
        scratch_shapes=list(scratch),
        compiler_params=roomy(mib),
        cost_estimate=cost,
    )(*ins, *after)


def rates(params_ref):
    rate = jax.nn.sigmoid(params_ref[0])
    drop = rate * jax.nn.sigmoid(params_ref[1])
    weight = params_ref[3] * rate * params_ref[2]
    return 1.0 - drop, jnp.log1p(-drop), weight


def spread(ref, j):
    return jnp.broadcast_to(ref[pl.ds(j, 1), :], (SUB, LANES))


def tree_sum(parts):
    while len(parts) > 1:
        parts = [a + b for a, b in zip(parts[::2], parts[1::2])] + parts[len(parts) & ~1 :]
    return parts[0]


def block_rows(g, t):
    return pl.ds(g * GROUP + t, SUB, stride=GROUP)


def state_rows(g, j, expand):
    return pl.ds(g * expand + j, SUB, stride=expand)


def blocks_kernel(spot_ref, first_ref, second_ref, out_ref, sems):
    copies = []
    for b in range(out_ref.shape[0]):
        cols = pl.ds(b * GROUP, GROUP)
        for which, ref in enumerate((first_ref, second_ref)):
            copies.append(pltpu.make_async_copy(ref.at[:, cols], out_ref.at[b, which], sems.at[2 * b + which]))
    for copy in copies:
        copy.start()
    for copy in copies:
        copy.wait()


def by_blocks(spot, first, second):
    columns, length = first.shape
    blocks = length // GROUP
    anywhere = pl.BlockSpec(memory_space=pl.ANY)
    return launch(
        blocks_kernel,
        [((blocks, 2, columns, GROUP), first.dtype)],
        (spot, first, second),
        [in_smem(), anywhere, anywhere],
        [anywhere],
        scratch=[pltpu.SemaphoreType.DMA((2 * blocks,))],
        mib=1,
    )[0]


def ema_ends_kernel(x_ref, params_ref, xs_ref, ends_ref, total_ref, decay_ref):
    length = x_ref.shape[1]
    expand = params_ref.shape[1]
    blocks = length // GROUP
    decay, log_decay, _ = rates(params_ref)
    decay_ref[...] = decay
    for b in range(blocks):
        rows = pl.ds(b * GROUP, GROUP)
        xs_ref[rows, :] = x_ref[:, rows].astype(f32).T
    factors = [spread(decay_ref, j) for j in range(expand)]
    for g in range(0, blocks, SUB):

        def step(t, states):
            now = xs_ref[block_rows(g, t), :]
            return tuple(f * s + now for f, s in zip(factors, states))

        states = (jnp.zeros((SUB, LANES), f32),) * expand
        states = lax.fori_loop(0, GROUP, step, states, unroll=8)
        for j in range(expand):
            ends_ref[state_rows(g, j, expand), :] = states[j]
    jump = jnp.exp(GROUP * log_decay)
    carry = jnp.zeros_like(jump)
    for b in range(blocks):
        carry = jump * carry + ends_ref[pl.ds(b * expand, expand), :]
    total_ref[...] = carry


def ema_ends(x, params, after=()):
    columns, length = x.shape
    expand = params.shape[1]
    shapes = ((length, columns), (length // GROUP * expand, columns), (expand, columns))
    return launch(
        ema_ends_kernel,
        [(shape, f32) for shape in shapes],
        (x, params),
        [by_tile(x.shape, 0), by_tile(params.shape, 2)],
        [by_tile(shape, 1) for shape in shapes],
        after=after,
        grid=(columns // LANES,),
        scratch=[pltpu.VMEM((expand, LANES), f32)],
        mib=5 * max(1, length // 1024),
        cost=work(2 * expand * length * columns, 6 * length * columns),
    )


def ema_mix_kernel(
    spot_ref, xs_ref, ends_ref, params_ref, omega_ref, totals_ref, *refs
):
    mixed_refs, (slope_ref, entry_ref, decay_ref, weight_ref, smooth_ref) = refs[:-5], refs[-5:]
    length = xs_ref.shape[0]
    expand = params_ref.shape[1]
    blocks = length // GROUP
    decay, log_decay, weight = rates(params_ref)
    decay_ref[...] = decay
    weight_ref[...] = weight
    whole = jnp.exp(length * log_decay)
    jump = jnp.exp(GROUP * log_decay)
    carry = jnp.zeros_like(jump)
    for k in range(totals_ref.shape[0]):
        carry = jnp.where(k < spot_ref[2], whole * carry + totals_ref[k], carry)
    for b in range(blocks):
        rows = pl.ds(b * expand, expand)
        entry_ref[rows, :] = carry
        carry = jump * carry + ends_ref[rows, :]
    factors = [spread(decay_ref, j) for j in range(expand)]
    weights = [spread(weight_ref, j) for j in range(expand)]
    for g in range(0, blocks, SUB):

        def step(t, states):
            now = xs_ref[block_rows(g, t), :]
            states = tuple(f * s + now for f, s in zip(factors, states))
            smooth_ref[block_rows(g, t), :] = tree_sum([w * s for w, s in zip(weights, states)])
            return states

        start = tuple(entry_ref[state_rows(g, j, expand), :] for j in range(expand))
        lax.fori_loop(0, GROUP, step, start, unroll=8)
    for k in range(blocks):
        rows = pl.ds(pl.multiple_of((spot_ref[1] ^ k) * GROUP, GROUP), GROUP)
        pre = smooth_ref[rows, :] + omega_ref[...] * xs_ref[rows, :]
        sigma = jax.nn.sigmoid(pre)
        block = (pre * sigma).T.astype(jnp.bfloat16)
        if len(mixed_refs) == 1:
            mixed_refs[0][spot_ref[1] ^ k] = block
        else:
            mixed_refs[k][...] = block
        slope_ref[rows, :] = (sigma * (1.0 + pre * (1.0 - sigma))).astype(slope_ref.dtype)


def ema_mix(spot, xs, ends, params, omega, totals, apart, after=()):
    length, columns = xs.shape
    expand = params.shape[1]
    blocks = length // GROUP
    mixed = [(columns, GROUP)] * blocks if apart else [(blocks, columns, GROUP)]
    *found, slope, entry = launch(
        ema_mix_kernel,
        [(shape, jnp.bfloat16) for shape in mixed] + [(xs.shape, jnp.bfloat16), (ends.shape, f32)],
        (spot, xs, ends, params, omega, totals),
        [
            in_smem(), by_tile(xs.shape, 1), by_tile(ends.shape, 1), by_tile(params.shape, 2),
            by_tile(omega.shape, 1), by_tile(totals.shape, 2),
        ],
        [by_tile(shape, len(shape) - 2) for shape in mixed] + [by_tile(xs.shape, 1), by_tile(ends.shape, 1)],
        after=after,
        grid=(columns // LANES,),
        scratch=[
            pltpu.VMEM((expand, LANES), f32),
            pltpu.VMEM((expand, LANES), f32),
            pltpu.VMEM((length, LANES), f32),
        ],
        mib=5 * max(1, length // 1024),
        cost=work(4 * expand * length * columns, 10 * length * columns, length * columns),
    )
    return found, slope, entry


def ema_back_kernel(dmix_ref, slope_ref, params_ref, pull_ref, heads_ref, total_ref, decay_ref):
    length = slope_ref.shape[0]
    expand = params_ref.shape[1]
    blocks = length // GROUP
    decay, log_decay, _ = rates(params_ref)
    decay_ref[...] = decay
    for b in range(blocks):
        rows = pl.ds(b * GROUP, GROUP)
        pull_ref[rows, :] = dmix_ref[b].astype(f32).T * slope_ref[rows, :].astype(f32)
    factors = [spread(decay_ref, j) for j in range(expand)]
    for g in range(0, blocks, SUB):

        def step(t, states):
            now = pull_ref[block_rows(g, GROUP - 1 - t), :]
            return tuple(f * s + now for f, s in zip(factors, states))

        states = (jnp.zeros((SUB, LANES), f32),) * expand
        states = lax.fori_loop(0, GROUP, step, states, unroll=8)
        for j in range(expand):
            heads_ref[state_rows(g, j, expand), :] = states[j]
    jump = jnp.exp(GROUP * log_decay)
    carry = jnp.zeros_like(jump)
    for b in reversed(range(blocks)):
        carry = jump * carry + heads_ref[pl.ds(b * expand, expand), :]
    total_ref[...] = carry


def ema_back(dmix, slope, params, after=()):
    length, columns = slope.shape
    expand = params.shape[1]
    shapes = ((length, columns), (length // GROUP * expand, columns), (expand, columns))
    return launch(
        ema_back_kernel,
        [(shape, f32) for shape in shapes],
        (dmix, slope, params),
        [by_tile(dmix.shape, 1), by_tile(slope.shape, 1), by_tile(params.shape, 2)],
        [by_tile(shape, 1) for shape in shapes],
        after=after,
        grid=(columns // LANES,),
        scratch=[pltpu.VMEM((expand, LANES), f32)],
        mib=5 * max(1, length // 1024),
        cost=work(2 * expand * length * columns, 8 * length * columns),
    )


def enter_from_later(spot_ref, heads_ref, totals_ref, enter_ref, log_decay, length):
    expand = log_decay.shape[0]
    whole = jnp.exp(length * log_decay)
    jump = jnp.exp(GROUP * log_decay)
    carry = jnp.zeros_like(jump)
    for k in reversed(range(totals_ref.shape[0])):
        carry = jnp.where(k > spot_ref[2], whole * carry + totals_ref[k], carry)
    for b in reversed(range(length // GROUP)):
        rows = pl.ds(b * expand, expand)
        enter_ref[rows, :] = carry
        carry = jump * carry + heads_ref[rows, :]


def ema_finish_kernel(
    spot_ref, pull_ref, heads_ref, params_ref, omega_ref, totals_ref, direct_ref, result_ref,
    grad_ref, output_ref, decay_ref, weight_ref, enter_ref, smooth_ref,
):
    length = pull_ref.shape[0]
    expand = params_ref.shape[1]
    blocks = length // GROUP
    decay, log_decay, weight = rates(params_ref)
    decay_ref[...] = decay
    weight_ref[...] = weight
    enter_from_later(spot_ref, heads_ref, totals_ref, enter_ref, log_decay, length)
    factors = [spread(decay_ref, j) for j in range(expand)]
    weights = [spread(weight_ref, j) for j in range(expand)]
    for g in range(0, blocks, SUB):

        def step(t, states):
            now = pull_ref[block_rows(g, GROUP - 1 - t), :]
            states = tuple(f * s + now for f, s in zip(factors, states))
            back = tree_sum([w * s for w, s in zip(weights, states)])
            smooth_ref[block_rows(g, GROUP - 1 - t), :] = back
            return states

        start = tuple(enter_ref[state_rows(g, j, expand), :] for j in range(expand))
        lax.fori_loop(0, GROUP, step, start, unroll=8)
    for b in range(blocks):
        rows = pl.ds(b * GROUP, GROUP)
        back = smooth_ref[rows, :] + omega_ref[...] * pull_ref[rows, :]
        grad_ref[:, rows] = back.T + direct_ref[b, 0].astype(f32)
        output_ref[:, rows] = result_ref[b, 0]


def ema_finish(spot, pull, heads, params, omega, totals, joint, after=()):
    length, columns = pull.shape

    def part(which):
        return pl.BlockSpec((length // GROUP, 1, LANES, GROUP), lambda i: (0, which, i, 0))

    expand = params.shape[1]
    return launch(
        ema_finish_kernel,
        [((columns, length), f32), ((columns, length), joint.dtype)],
        (spot, pull, heads, params, omega, totals, joint, joint),
        [
            in_smem(), by_tile(pull.shape, 1), by_tile(heads.shape, 1), by_tile(params.shape, 2),
            by_tile(omega.shape, 1), by_tile(totals.shape, 2), part(0), part(1),
        ],
        [by_tile((columns, length), 0)] * 2,
        after=after,
        grid=(columns // LANES,),
        scratch=[
            pltpu.VMEM((expand, LANES), f32),
            pltpu.VMEM((expand, LANES), f32),
            pltpu.VMEM((heads.shape[0], LANES), f32),
            pltpu.VMEM((length, LANES), f32),
        ],
        mib=5 * max(1, length // 1024),
        cost=work(4 * expand * length * columns, 14 * length * columns),
    )


def ema_sums_kernel(spot_ref, xs_ref, pull_ref, entry_ref, heads_ref, totals_ref, params_ref, sums_ref, decay_ref, enter_ref):
    length = xs_ref.shape[0]
    expand = params_ref.shape[1]
    blocks = length // GROUP
    half = expand // 2
    decay, log_decay, _ = rates(params_ref)
    decay_ref[...] = decay
    enter_from_later(spot_ref, heads_ref, totals_ref, enter_ref, log_decay, length)
    for low in range(0, expand, half):
        factors = [spread(decay_ref, low + j) for j in range(half)]
        zero = (jnp.zeros((SUB, LANES), f32),) * half
        plain, turned = zero, zero
        for g in range(0, blocks, SUB):

            def step(t, held):
                states, slants, plain, turned = held
                now, pull = xs_ref[block_rows(g, t), :], pull_ref[block_rows(g, t), :]
                slants = tuple(f * p + s for f, p, s in zip(factors, slants, states))
                states = tuple(f * s + now for f, s in zip(factors, states))
                plain = tuple(a + pull * s for a, s in zip(plain, states))
                turned = tuple(a + pull * p for a, p in zip(turned, slants))
                return states, slants, plain, turned

            start = tuple(entry_ref[state_rows(g, low + j, expand), :] for j in range(half))
            held = (start, zero, plain, turned)
            _, slants, plain, turned = lax.fori_loop(0, GROUP, step, held, unroll=4)
            turned = tuple(
                a + f * p * enter_ref[state_rows(g, low + j, expand), :]
                for j, (a, f, p) in enumerate(zip(turned, factors, slants))
            )
        for j in range(half):
            sums_ref[pl.ds(low + j, 1), :] = jnp.sum(plain[j], axis=0, keepdims=True)
            sums_ref[pl.ds(expand + low + j, 1), :] = jnp.sum(turned[j], axis=0, keepdims=True)
    straight = jnp.zeros((SUB, LANES), f32)
    for b in range(0, length, SUB):
        straight = straight + xs_ref[pl.ds(b, SUB), :] * pull_ref[pl.ds(b, SUB), :]
    sums_ref[pl.ds(2 * expand, SUB), :] = straight


def ema_sums(spot, xs, pull, entry, heads, totals, params, after=()):
    length, columns = xs.shape
    expand = params.shape[1]
    shape = (2 * expand + SUB, columns)
    return launch(
        ema_sums_kernel,
        [(shape, f32)],
        (spot, xs, pull, entry, heads, totals, params),
        [
            in_smem(), by_tile(xs.shape, 1), by_tile(xs.shape, 1), by_tile(entry.shape, 1), by_tile(entry.shape, 1),
            by_tile(totals.shape, 2), by_tile(params.shape, 2),
        ],
        [by_tile(shape, 1)],
        after=after,
        grid=(columns // LANES,),
        scratch=[pltpu.VMEM((expand, LANES), f32), pltpu.VMEM((entry.shape[0], LANES), f32)],
        mib=5 * max(1, length // 1024),
        cost=work(8 * expand * length * columns, 8 * length * columns),
    )[0]


def pad_to_lanes(part, dim):
    extra = -part.shape[dim] % LANES
    if extra == 0:
        return part
    return jnp.pad(part, [(0, extra if k == dim else 0) for k in range(part.ndim)])


def ema_params(alpha, delta, beta, eta, count):
    packed = jnp.swapaxes(jnp.stack([alpha, delta, beta, eta]), 1, 2)
    return pad_to_lanes(jnp.tile(packed, (1, 1, count)), 2)


def ema_param_grads(total, alpha, delta, beta, eta, count):
    channels, expand = alpha.shape
    summed = jnp.sum(total[:, : count * channels].reshape(-1, count, channels), axis=1)
    plain, turned = summed[:expand].T, summed[expand : 2 * expand].T
    omega = jnp.sum(summed[2 * expand :], axis=0)
    rate, damp = jax.nn.sigmoid(alpha), jax.nn.sigmoid(delta)
    g_alpha = eta * beta * rate * (1.0 - rate) * (plain - damp * rate * turned)
    g_delta = -(eta * beta * rate * rate * damp * (1.0 - damp)) * turned
    return g_alpha, g_delta, rate * eta * plain, rate * beta * plain, omega


low = jnp.bfloat16
CHUNK = 256
MIB = (3, 11, 8, 5, 6, 8, 8, 6, 4, 4)
TABLE = 384


def nn(left, right):
    return jnp.dot(left, right, preferred_element_type=f32)


def nt(left, right):
    return lax.dot_general(left, right, (((1,), (1,)), ((), ())), preferred_element_type=f32)


def silu_pair(pre):
    sigma = jax.nn.sigmoid(pre)
    return pre * sigma, sigma * (1.0 + pre * (1.0 - sigma))


def each(width, body, size=CHUNK):
    for at in range(0, width, size):
        body(at)


def wide_block(ref, which, n):
    part = ref[:, which, n]
    return part.reshape(part.shape[0] * part.shape[1], part.shape[2])


def live_lanes(spot_ref, lengths_ref, n, shape):
    return spot_ref[0] + lax.broadcasted_iota(jnp.int32, shape, 1) < lengths_ref[n]


def span_of(ref, n):
    return pl.ds(n * GROUP, GROUP)


def call(kernel, outs, ins, smem=0, hbm=0, scratch=(), moved=1, mib=16, after=()):
    spaces = [pltpu.SMEM] * smem + [pl.ANY] * hbm + [pltpu.VMEM] * (len(ins) - smem - hbm)
    return launch(
        kernel,
        outs,
        ins,
        [pl.BlockSpec(memory_space=space) for space in spaces],
        [pl.BlockSpec(memory_space=pltpu.VMEM) for _ in outs],
        after=after,
        scratch=scratch,
        mib=mib,
        cost=pl.CostEstimate(flops=1, bytes_accessed=moved, transcendentals=0),
    )


def vectors(width, mwidth, vwidth, ff):
    sizes = (
        ("mix", mwidth), ("value", vwidth), ("out", width), ("gain", width),
        ("shift", width), ("up", ff), ("down", width),
    )
    place, at = {}, 0
    for name, size in sizes:
        place[name] = at
        at += size
    return place


def piece(ref, base, at, size):
    return ref[:, pl.ds(base + at, size)]


def value_kernel(base, w_ref, x_ref, vec_ref, rows_ref, values_ref, slope_ref, rows_t_ref):
    for n in range(x_ref.shape[2]):
        rows = pl.ds(n * GROUP, GROUP)
        block = wide_block(x_ref, 0, n)
        rows_t_ref[:, rows] = block
        rows_ref[rows, :] = block.T

    def chunk(at):
        cols = pl.ds(at, CHUNK)
        act, slope = silu_pair(nn(rows_ref[...], w_ref[:, cols]) + piece(vec_ref, base, at, CHUNK))
        values_ref[:, cols] = act.astype(low)
        slope_ref[:, cols] = slope.astype(low)

    each(w_ref.shape[1], chunk)


def value_part(x, w_value, vec, where, after=()):
    width, vwidth = w_value.shape
    count = x.shape[2] * GROUP
    return call(
        functools.partial(value_kernel, where["value"]),
        [((count, width), low), ((count, vwidth), low), ((count, vwidth), low), ((width, count), low)],
        (w_value, x, vec),
        mib=MIB[0],
        after=after,
    )


def forward_kernel(
    pieces, where, spot_ref, lengths_ref, wmix_ref, wout_ref, wup_ref, wdown_ref,
    x_ref, values_ref, vec_ref, qscale_ref, qshift_ref, *refs
):
    forward_rows(spot_ref, refs[:pieces], refs[pieces], refs[-6])
    forward_body(
        where, spot_ref, lengths_ref, wmix_ref, wout_ref, wup_ref, wdown_ref,
        x_ref, values_ref, vec_ref, qscale_ref, qshift_ref, *refs[pieces + 1 :]
    )


def forward_rows(spot_ref, mixed_refs, mixed_t_ref, m_ref):
    for k, ref in enumerate(mixed_refs):
        seqs, channels, _ = ref.shape
        at = pl.multiple_of((spot_ref[1] ^ k) * channels, 16) if len(mixed_refs) > 1 else 0
        for n in range(seqs):
            mixed_t_ref[pl.ds(at, channels), pl.ds(n * GROUP, GROUP)] = ref[n]
    for n in range(m_ref.shape[0] // GROUP):
        rows = pl.ds(n * GROUP, GROUP)
        m_ref[rows, :] = mixed_t_ref[:, rows].T


def forward_body(
    where, spot_ref, lengths_ref, wmix_ref, wout_ref, wup_ref, wdown_ref,
    x_ref, values_ref, vec_ref, qscale_ref, qshift_ref,
    out_ref, query_ref, key_ref, shared_ref, qslope_ref, probs_ref, reset_ref, turned_ref, gated_t_ref,
    hslope_ref, uslope_ref, keep_ref, unit_ref, rstd_ref, normed_t_ref, hidden_t_ref, fslope_ref,
    m_ref, update_ref, gated_ref, blend_ref, normed_ref, ffn_ref,
):
    width, vwidth = wout_ref.shape[1], wout_ref.shape[0]
    zwidth = qscale_ref.shape[1]
    seqs = x_ref.shape[0] // GROUP

    def mix(at, size=CHUNK):
        cols = pl.ds(at, size)
        return nn(m_ref[...], wmix_ref[:, cols]) + piece(vec_ref, where["mix"], at, size)

    shared, qslope = silu_pair(mix(width, zwidth))
    shared_ref[...] = shared
    qslope_ref[...] = qslope
    query_ref[...] = (shared * qscale_ref[pl.ds(0, 1), :] + qshift_ref[pl.ds(0, 1), :]).astype(low)
    key_ref[...] = (shared * qscale_ref[pl.ds(1, 1), :] + qshift_ref[pl.ds(1, 1), :]).astype(low)
    causal = lax.broadcasted_iota(jnp.int32, (GROUP, GROUP), 0) >= lax.broadcasted_iota(
        jnp.int32, (GROUP, GROUP), 1
    )
    for n in range(seqs):
        rows = pl.ds(n * GROUP, GROUP)
        scores = jnp.where(causal, nt(query_ref[rows, :], key_ref[rows, :]) * zwidth**-0.5, -1e30)
        scores = jnp.exp(scores - jnp.max(scores, axis=-1, keepdims=True))
        probs_ref[rows, :] = scores / jnp.sum(scores, axis=-1, keepdims=True)

    def gate(at):
        update_ref[:, pl.ds(at, CHUNK)] = jax.nn.sigmoid(mix(at))

    each(width, gate)

    def attend(at):
        cols = pl.ds(at, CHUNK)
        reset, slope = silu_pair(mix(width + zwidth + at))
        attended = jnp.concatenate(
            [
                nn(probs_ref[pl.ds(n * GROUP, GROUP), :].astype(low), values_ref[pl.ds(n * GROUP, GROUP), cols])
                for n in range(seqs)
            ],
            axis=0,
        )
        reset_ref[:, cols] = reset.astype(low)
        turned_ref[:, cols] = (attended * slope).astype(low)
        gated = (reset * attended).astype(low)
        gated_ref[:, cols] = gated
        gated_t_ref[cols, :] = gated.T

    each(vwidth, attend)

    def hide(at):
        cols = pl.ds(at, CHUNK)
        pre = mix(width + zwidth + vwidth + at)
        pre = pre + nn(gated_ref[...], wout_ref[:, cols]) + piece(vec_ref, where["out"], at, CHUNK)
        hidden, slope = silu_pair(pre)
        update = update_ref[:, cols]
        keep = 1.0 - update
        resid = x_ref[:, cols].astype(f32)
        hslope_ref[:, cols] = (update * slope).astype(low)
        uslope_ref[:, cols] = ((hidden - resid) * update * keep).astype(low)
        keep_ref[:, cols] = keep.astype(low)
        blend_ref[:, cols] = update * hidden + keep * resid

    each(width, hide)
    for n in range(seqs):
        rows = pl.ds(n * GROUP, GROUP)
        blend = blend_ref[rows, :]
        centered = blend - jnp.mean(blend, axis=-1, keepdims=True)
        rstd = lax.rsqrt(jnp.mean(centered * centered, axis=-1, keepdims=True) + 1e-05)
        unit = centered * rstd
        unit_ref[rows, :] = unit.astype(low)
        rstd_ref[rows, :] = jnp.broadcast_to(rstd, (GROUP, LANES))
        normed = unit * piece(vec_ref, where["gain"], 0, width) + piece(vec_ref, where["shift"], 0, width)
        blend_ref[rows, :] = normed
        normed_ref[rows, :] = normed.astype(low)
        normed_t_ref[:, rows] = normed.astype(low).T

    def lift(at):
        cols = pl.ds(at, CHUNK)
        act, slope = silu_pair(nn(normed_ref[...], wup_ref[:, cols]) + piece(vec_ref, where["up"], at, CHUNK))
        fslope_ref[:, cols] = slope.astype(low)
        act = act.astype(low)
        ffn_ref[:, cols] = act
        hidden_t_ref[cols, :] = act.T

    each(wup_ref.shape[1], lift)

    def drop(at):
        cols = pl.ds(at, CHUNK)
        blend_ref[:, cols] = blend_ref[:, cols] + nn(ffn_ref[...], wdown_ref[:, cols]) + piece(vec_ref, where["down"], at, CHUNK)

    each(width, drop)
    for n in range(seqs):
        result = blend_ref[pl.ds(n * GROUP, GROUP), :].astype(low).T
        result = jnp.where(live_lanes(spot_ref, lengths_ref, n, result.shape), result, jnp.zeros_like(result))
        out_ref[:, n] = result.reshape(out_ref.shape[0], out_ref.shape[2], GROUP)


def forward_part(spot, lengths, folded, mixed, x, values, w_mix, w_out, w_up, w_down, vec, where, qk_scale, qk_shift, after=()):
    vwidth, width = w_out.shape
    zwidth = qk_scale.shape[1]
    ff = w_up.shape[1]
    count = x.shape[0]
    narrow, wide = (count, width), (count, vwidth)
    outs = [
        ((width, count), low), (folded, low), ((count, zwidth), low), ((count, zwidth), low), ((count, zwidth), f32),
        ((count, zwidth), f32), ((count, GROUP), f32), (wide, low), (wide, low), ((vwidth, count), low),
        (narrow, low), (narrow, low), (narrow, low), (narrow, low), ((count, LANES), f32),
        ((width, count), low), ((ff, count), low), ((count, ff), low),
    ]
    scratch = [pltpu.VMEM(narrow, low), pltpu.VMEM(narrow, f32), pltpu.VMEM(wide, low)]
    scratch += [pltpu.VMEM(narrow, f32), pltpu.VMEM(narrow, low), pltpu.VMEM((count, ff), low)]
    macs = w_mix.size + w_out.size + w_up.size + w_down.size
    return call(
        functools.partial(forward_kernel, len(mixed), where),
        outs,
        (spot, lengths, w_mix, w_out, w_up, w_down, x, values, vec, qk_scale, qk_shift, *mixed),
        smem=2,
        mib=MIB[1],
        after=after,
        scratch=scratch,
    )


def column_sum(part):
    return jnp.sum(part.astype(f32), axis=0, keepdims=True)


def put(ref, row, value, columns):
    if isinstance(ref, tuple):
        lone = value.shape[0] // len(ref)
        for k, one in enumerate(ref):
            put(one, row, value[k * lone : (k + 1) * lone], columns)
        return
    if len(ref.shape) == 2:
        ref[...] = value
        return
    owners = ref.shape[0]
    lone = value.shape[0] // owners
    for owner in range(owners):
        part = value[owner * lone : (owner + 1) * lone]
        for i, at in enumerate(range(0, value.shape[1], columns)):
            ref[owner, pl.ds(row + i * lone, lone), :] = part[:, at : at + columns]


def split_product(side, keep_ref, send_ref, left, right_ref, half, columns, row=0):
    total = right_ref.shape[1]
    for ref, which in ((keep_ref, side), (send_ref, 1 - side)):
        base = which * (total - half)
        parts = []
        for at in range(0, half, CHUNK):
            cols = pl.ds(pl.multiple_of(base + at, 128), min(CHUNK, half - at))
            parts.append(nn(left, right_ref[:, cols]).astype(low))
        put(ref, row, jnp.concatenate(parts, axis=1), columns)


def split_narrow(side, keep_ref, send_ref, left_ref, right_ref):
    both = [nn(left_ref[pl.ds(at, CHUNK), :], right_ref[...]).astype(low) for at in range(0, left_ref.shape[0], CHUNK)]
    both = jnp.concatenate(both, axis=0)
    half = both.shape[1] // 2
    near, far = both[:, :half], both[:, half:]
    put(keep_ref, 0, jnp.where(side == 0, near, far), half)
    put(send_ref, 0, jnp.where(side == 0, far, near), half)


def pair_outs(tall, wide, owners, lines=0):
    if not owners:
        return [((tall[0], tall[1] // 2), low)] * 2 + [((wide[0], wide[1] // 2), low)] * 2
    rows = (tall[0] * tall[1] + wide[0] * wide[1]) // (tall[1] * owners) + lines
    return [((owners, rows, tall[1] // 2), low)] * 2


def back_ffn_kernel(
    spot_ref, lengths_ref, wdown_ref, grad_ref, hidden_t_ref, fslope_ref, normed_t_ref, *refs
):
    halves, (g_ref, dffn_ref, small_ref) = refs[:-3], refs[-3:]
    width, ff = g_ref.shape[1], wdown_ref.shape[0]
    for n in range(grad_ref.shape[2]):
        part = wide_block(grad_ref, 1, n)
        part = jnp.where(live_lanes(spot_ref, lengths_ref, n, part.shape), part, jnp.zeros_like(part))
        g_ref[pl.ds(n * GROUP, GROUP), :] = part.T
    small_ref[:, pl.ds(0, width)] = column_sum(g_ref[...])
    side = spot_ref[2] & 1
    split_narrow(side, halves[0], halves[1], hidden_t_ref, g_ref)

    def lift(at):
        part = pl.ds(at, CHUNK)
        pulled = (nt(g_ref[...], wdown_ref[part, :]) * fslope_ref[:, part].astype(f32)).astype(low)
        dffn_ref[:, part] = pulled
        small_ref[:, pl.ds(width + at, CHUNK)] = column_sum(pulled)

    each(ff, lift)
    tall = hidden_t_ref.shape[0] // halves[0].shape[0]
    split_product(side, halves[-2], halves[-1], normed_t_ref[...], dffn_ref, ff // 2, halves[-2].shape[-1], tall)
    if len(halves) == 2:
        for ref in halves:
            owners, rows, columns = ref.shape
            ref[:, pl.ds(2 * tall, rows - 2 * tall), :] = jnp.zeros((owners, rows - 2 * tall, columns), low)


def back_ffn(spot, lengths, owners, lines, grad, hidden_t, fslope, normed_t, w_down, after=()):
    ff, width = w_down.shape
    count = fslope.shape[0]
    outs = pair_outs((ff, width), (width, ff), owners, lines)
    outs += [((count, width), low), ((count, ff), low), ((1, width + ff), f32)]
    *halves, g, dffn, small = call(
        back_ffn_kernel,
        outs,
        (spot, lengths, w_down, grad, hidden_t, fslope, normed_t),
        smem=2,
        mib=MIB[2],
        after=after,
    )
    return halves, g, dffn, small


def back_norm_kernel(
    base, wup_ref, g_ref, dffn_ref, unit_ref, rstd_ref, vec_ref, hslope_ref, uslope_ref, kept_ref,
    dh_ref, du_ref, direct_ref, small_ref, dn_ref,
):
    width = wup_ref.shape[0]

    def drop(at):
        part = pl.ds(at, CHUNK)
        pulled = g_ref[:, part].astype(f32) + nt(dffn_ref[...], wup_ref[part, :])
        dn_ref[:, part] = pulled
        small_ref[:, part] = column_sum(pulled * unit_ref[:, part].astype(f32))
        small_ref[:, pl.ds(width + at, CHUNK)] = column_sum(pulled)

    each(width, drop)
    for n in range(g_ref.shape[0] // GROUP):
        rows = pl.ds(n * GROUP, GROUP)
        unit = unit_ref[rows, :].astype(f32)
        pulled = dn_ref[rows, :] * piece(vec_ref, base, 0, width)
        inner = jnp.mean(pulled * unit, axis=-1, keepdims=True)
        blend = pulled - jnp.mean(pulled, axis=-1, keepdims=True) - unit * inner
        blend = blend * rstd_ref[rows, :][:, :1]
        dh_ref[rows, :] = (blend * hslope_ref[rows, :].astype(f32)).astype(low)
        du_ref[rows, :] = (blend * uslope_ref[rows, :].astype(f32)).astype(low)
        direct_ref[rows, :] = (blend * kept_ref[rows, :].astype(f32)).astype(low)


def back_norm(g, dffn, unit, rstd, vec, where, hslope, uslope, kept, w_up, after=()):
    width = w_up.shape[0]
    narrow = g.shape
    return call(
        functools.partial(back_norm_kernel, where["gain"]),
        [(narrow, low)] * 3 + [((1, 2 * width), f32)],
        (w_up, g, dffn, unit, rstd, vec, hslope, uslope, kept),
        mib=MIB[3],
        after=after,
        scratch=[pltpu.VMEM(narrow, f32)],
    )


def back_attend_kernel(
    wout_ref, wmix_ref, wvalue_ref,
    dh_ref, du_ref, direct_ref, reset_ref, turned_ref, values_ref, vslope_ref, probs_ref,
    query_ref, key_ref, shared_ref, qslope_ref, qscale_ref, small_ffn_ref, small_norm_ref, result_ref,
    dmix_ref, dvalue_ref, mixed_ref, joint_ref,
    table_ref,
    datt_ref,
):
    vwidth, width = wout_ref.shape
    zwidth = qscale_ref.shape[1]
    count = dh_ref.shape[0]
    seqs = count // GROUP
    dmix_ref[:, pl.ds(0, width)] = du_ref[...]
    dmix_ref[:, pl.ds(width + zwidth + vwidth, width)] = dh_ref[...]

    def gate(at):
        part = pl.ds(at, CHUNK)
        pulled = nt(dh_ref[...], wout_ref[part, :])
        dmix_ref[:, pl.ds(width + zwidth + at, CHUNK)] = (
            pulled * turned_ref[:, part].astype(f32)
        ).astype(low)
        datt_ref[:, part] = (pulled * reset_ref[:, part].astype(f32)).astype(low)

    each(vwidth, gate)
    scale = zwidth**-0.5
    q_scale, k_scale = qscale_ref[pl.ds(0, 1), :], qscale_ref[pl.ds(1, 1), :]
    zero = jnp.zeros((1, zwidth), f32)
    sums = [zero, zero, zero, zero]
    for n in range(seqs):
        rows = pl.ds(n * GROUP, GROUP)
        probs = probs_ref[rows, :]
        pulled = nt(datt_ref[rows, :], values_ref[rows, :])
        pulled = probs * (pulled - jnp.sum(pulled * probs, axis=-1, keepdims=True))
        pulled = pulled.astype(low)
        d_query = nn(pulled, key_ref[rows, :]) * scale
        d_key = nn(pulled.T, query_ref[rows, :]) * scale
        probs_t = probs.astype(low).T
        shared = shared_ref[rows, :]
        found = (d_query * shared, d_key * shared, d_query, d_key)
        sums = [a + jnp.sum(b, axis=0, keepdims=True) for a, b in zip(sums, found)]
        dmix_ref[rows, pl.ds(width, zwidth)] = (
            (d_query * q_scale + d_key * k_scale) * qslope_ref[rows, :]
        ).astype(low)
        dvalue_ref[rows, :] = (nn(probs_t, datt_ref[rows, :]) * vslope_ref[rows, :].astype(f32)).astype(low)

    def turn(result):
        devices, _, channels, _ = mixed_ref.shape
        return result.astype(low).T.reshape(devices, channels, GROUP)

    for n in range(0, seqs, 2):
        result = nt(dmix_ref[pl.ds(n * GROUP, 2 * GROUP), :], wmix_ref[...])
        mixed_ref[:, n] = turn(result[:GROUP])
        mixed_ref[:, n + 1] = turn(result[GROUP:])
    for n in range(0, seqs, 2):
        rows = pl.ds(n * GROUP, 2 * GROUP)
        result = direct_ref[rows, :].astype(f32) + nt(dvalue_ref[rows, :], wvalue_ref[...])
        joint_ref[:, 0, n] = turn(result[:GROUP])
        joint_ref[:, 0, n + 1] = turn(result[GROUP:])
    joint_ref[:, 1] = result_ref[...]
    ff = small_ffn_ref.shape[1] - width
    found = (
        column_sum(dmix_ref[...]), column_sum(dvalue_ref[...]), column_sum(dh_ref[...]),
        sums[0], sums[1], sums[2], sums[3], small_norm_ref[:, :width], small_norm_ref[:, width:],
        small_ffn_ref[:, width:], small_ffn_ref[:, :width],
    )
    lines = []
    for part in found:
        for at in range(0, part.shape[1], TABLE):
            line = part[:, at : at + TABLE]
            lack = TABLE - line.shape[1]
            lines.append(line if lack == 0 else jnp.concatenate([line, jnp.zeros((1, lack), f32)], axis=1))
    lines.append(jnp.zeros((table_ref.shape[0] - len(lines), TABLE), f32))
    table_ref[...] = jnp.concatenate(lines, axis=0).astype(low)


def back_attend(dh, du, direct, reset, turned, values, vslope, probs, query, key, shared, qslope, qk_scale, small_ffn, small_norm, result, w_out, w_mix, w_value, after=()):
    vwidth, width = w_out.shape
    mwidth = w_mix.shape[1]
    count = dh.shape[0]
    outs = [((count, mwidth), low), ((count, vwidth), low)]
    outs += [(result.shape, low), (result.shape[:1] + (2,) + result.shape[1:], low), ((64, TABLE), low)]
    scratch = [pltpu.VMEM((count, vwidth), low)]
    macs = w_out.size + w_mix.size + w_value.size
    return call(
        back_attend_kernel,
        outs,
        (w_out, w_mix, w_value, dh, du, direct, reset, turned, values, vslope, probs, query, key, shared, qslope, qk_scale, small_ffn, small_norm, result),
        mib=MIB[4],
        after=after,
        scratch=scratch,
    )


def back_mid_kernel(spot_ref, gated_t_ref, dh_ref, x_t_ref, dvalue_ref, table_ref, *halves):
    side = spot_ref[2] & 1
    if len(halves) == 4:
        (kept, sent, wide_kept, wide_sent), tall = halves, 0
    else:
        kept, sent = halves[0], halves[1:]
        wide_kept, wide_sent, tall = kept, sent, gated_t_ref.shape[0] // kept.shape[0]
    split_narrow(side, kept, sent, gated_t_ref, dh_ref)
    split_product(
        side, wide_kept, wide_sent, x_t_ref[...], dvalue_ref, dvalue_ref.shape[1] // 2, wide_kept.shape[-1], tall
    )
    if len(halves) == 4:
        return
    lines = kept.shape[1] - 2 * tall
    high = table_ref.shape[0] // (2 * lines)
    for refs, which in (((kept,), side), (sent, 1 - side)):
        for ref in refs:
            for owner in range(ref.shape[0]):
                at = pl.multiple_of((2 * (owner % high) + which) * lines, 16)
                ref[owner, pl.ds(2 * tall, lines), :] = table_ref[pl.ds(at, lines), :]


def halved(outs):
    (kept, kind), (sent, _) = outs
    return [(kept, kind)] + [((sent[0] // 2,) + sent[1:], kind)] * 2


def back_mid(spot, owners, gated_t, dh, x_t, dvalue, table, lines, after=()):
    count, width = dh.shape
    vwidth = dvalue.shape[1]
    outs = pair_outs((vwidth, width), (width, vwidth), owners, lines)
    found = call(
        back_mid_kernel,
        halved(outs) if owners else outs,
        (spot, gated_t, dh, x_t, dvalue, table),
        smem=1,
        mib=MIB[5],
        after=after,
    )
    if owners:
        return [found[0]], [list(found[1:])]
    return [found[0], found[2]], [[found[1]], [found[3]]]


def back_mix_kernel(spot_ref, mixed_t_ref, dmix_ref, keep_ref, *send_refs):
    half = keep_ref.shape[-1]
    split_product(spot_ref[2] & 1, keep_ref, send_refs, mixed_t_ref[...], dmix_ref, half, half)


def back_mix_weight(spot, owners, mixed_t, dmix, after=()):
    mwidth = dmix.shape[1]
    width, count = mixed_t.shape
    half = -(-mwidth // 256) * 128
    outs = [((width, half), low)] * 2
    kept, *sent = call(
        back_mix_kernel,
        halved(outs) if owners else outs,
        (spot, mixed_t, dmix),
        smem=1,
        mib=MIB[6],
        after=after,
    )
    return [kept], [sent]


def halve_kernel(index, bit, spot_ref, kept_ref, *refs):
    arrived, (sent_ref, stay_ref) = refs[:-2], refs[-2:]
    outer, inner, _, _ = sent_ref.shape
    lone = outer // len(arrived)
    mine = (spot_ref[index] >> bit) & 1
    for ref, which in ((sent_ref, 1 - mine), (stay_ref, mine)):
        for a in range(outer):
            for b in range(inner):
                total = kept_ref[a, which, b].astype(f32) + arrived[a // lone][a % lone, which, b].astype(f32)
                ref[a, b] = total.astype(low)


def halve(spot, kept, arrived, index, bit, at, after=()):
    dims = kept.shape[:-2]
    outer, inner = 1 << at, 1 << (len(dims) - at - 1)
    block = kept.shape[-2:]

    def shaped(part):
        return part.reshape((-1, 2, inner) + block)

    sent, stay = call(
        functools.partial(halve_kernel, index, bit),
        [((outer, inner) + block, low)] * 2,
        (spot, shaped(kept), *map(shaped, arrived)),
        smem=1,
        mib=MIB[7],
        after=after,

    )
    rest = dims[:at] + dims[at + 1 :] + block
    return sent.reshape(rest), stay.reshape(rest)


def finish_pair_kernel(count, lines, spot_ref, *refs):
    shares, outs = refs[:count], refs[count:]
    tall_ref, wide_ref = outs[:2]
    columns = shares[0].shape[1]
    cut = tall_ref.shape[0] * 2 // len(shares)
    lone = wide_ref.shape[0] * 2 // len(shares)
    for k, ref in enumerate(shares):
        at = spot_ref[2] ^ k
        high, side = at >> 1, at & 1
        tall_ref[pl.ds(pl.multiple_of(high * cut, 8), cut), pl.ds(pl.multiple_of(side * columns, 128), columns)] = ref[
            pl.ds(0, cut), :
        ].astype(f32)
        runs = wide_ref.shape[1] // 2 // columns
        for run in range(runs):
            wide_ref[
                pl.ds(pl.multiple_of(high * lone, 8), lone),
                pl.ds(pl.multiple_of((side * runs + run) * columns, 128), columns),
            ] = ref[pl.ds(cut + run * lone, lone), :].astype(f32)
        if lines:
            outs[-1][pl.ds(pl.multiple_of(at * lines, 8), lines), :] = ref[pl.ds(2 * cut, lines), :].astype(f32)
    if lines:
        row = 0
        for ref in outs[2:-1]:
            if len(ref.shape) == 2:
                for k in range(ref.shape[0]):
                    ref[pl.ds(k, 1), :] = outs[-1][pl.ds(row, 1), :][:, : ref.shape[1]]
                    row += 1
                continue
            for at in range(0, ref.shape[0], columns):
                size = min(columns, ref.shape[0] - at)
                ref[pl.ds(at, size)] = outs[-1][row, :size]
                row += 1


def finish_pair(spot, shares, tall, wide, lines=0, vectors=(), after=()):
    outs = [(tall, f32), (wide, f32)] + [(shape, f32) for shape in vectors]
    count = len(shares)
    scratch = [pltpu.VMEM((count * lines, shares[0].shape[1]), f32)] if lines else []
    kernel = functools.partial(finish_pair_kernel, count, lines)
    return call(kernel, outs, (spot, *shares), smem=1, mib=MIB[8], scratch=scratch, after=after)


def finish_mix_kernel(spot_ref, *refs):
    shares, out_ref = refs[:-1], refs[-1]
    half, mwidth = shares[0].shape[1], out_ref.shape[1]
    common = 2 * half - mwidth
    lone = out_ref.shape[0] * 2 // len(shares)
    for k, ref in enumerate(shares):
        at = spot_ref[2] ^ k
        rows = pl.ds(pl.multiple_of((at >> 1) * lone, 8), lone)
        base = pl.multiple_of(common + (at & 1) * (mwidth - half), 128)
        out_ref[rows, pl.ds(base, half - common)] = ref[:, common:].astype(f32)
        if common:

            @pl.when(at & 1 == 0)
            def _():
                out_ref[rows, pl.ds(0, common)] = ref[:, :common].astype(f32)


def finish_mix(spot, shares, shape, after=()):
    return call(finish_mix_kernel, [(shape, f32)], (spot, *shares), smem=1, mib=MIB[9], after=after)[0]


Y_FIRST = (("tok", 1), ("ch", 0))
Y_THEN_Z = (("tok", 1), ("ch", 1), ("ch", 0))
X_FIRST = (("ch", 0), ("tok", 1))


def bits_of(axis):
    return lax.axis_size(axis).bit_length() - 1


def across(part, axis, turn):
    return lax.ppermute(part, axis, [(i, i ^ turn) for i in range(lax.axis_size(axis))])


def exchange(part, axis, bit):
    return across(part, axis, 1 << bit)


def side_of(axis, bit):
    return (lax.axis_index(axis) >> bit) & 1


def by_owner(grad):
    dims = (2,) * (bits_of("ch") + bits_of("tok") - 1)
    return grad.reshape(dims + (-1, grad.shape[-1]))


def fold(part, columns):
    runs = [part[..., at : at + columns] for at in range(0, part.shape[-1], columns)]
    return jnp.concatenate(runs, axis=-2)


def add(left, right):
    return (left.astype(f32) + right.astype(f32)).astype(low)


def plain_halve(kept, arrived, mine, at):
    columns = min(part.shape[-1] for part in kept)

    def pick(which):
        def one(part):
            return lax.dynamic_index_in_dim(part, which, at, keepdims=False)

        return jnp.concatenate([fold(add(one(a), one(b)), columns) for a, b in zip(kept, arrived)], axis=-2)

    return pick(1 - mine), pick(mine)


class Sum:
    def __init__(self, spot, kept, sent, order):
        self.spot = spot
        self.names = [("ch", k) for k in reversed(range(bits_of("ch")))]
        self.names += [("tok", k) for k in reversed(range(1, bits_of("tok")))]
        self.stages = list(order) + [name for name in reversed(self.names) if name not in order]
        self.kept = [by_owner(part) for part in kept]
        arrived = [[exchange(piece, "tok", 0) for piece in part] for part in sent]
        self.arrived = arrived[0] if self.by_kernel() else [by_owner(part) for part, in arrived]

    def by_kernel(self):
        return len(self.kept) == 1 and self.kept[0].shape[-2] % 16 == 0

    def step(self, after=()):
        axis, bit = self.stages.pop(0)
        at = self.names.index((axis, bit))
        self.names.remove((axis, bit))
        if self.by_kernel():
            index = 1 if axis == "ch" else 2
            sent, stay = halve(self.spot, self.kept[0], self.arrived, index, bit, at, after)
        else:
            sent, stay = plain_halve(self.kept, self.arrived, side_of(axis, bit), at)
        self.kept, self.arrived = [stay], [exchange(sent, axis, bit)]
        return stay

    def shares(self):
        found = [add(self.kept[0], self.arrived[0])]
        for bit in reversed(range(1, bits_of("tok"))):
            found += [exchange(part, "tok", bit) for part in found]
        lower = [exchange(part, "tok", 0) for part in found]
        size = bits_of("tok") - 1
        order = [sum(((k >> (size - 1 - i)) & 1) << i for i in range(size)) for k in range(len(found))]
        found = [part for k in order for part in (found[k], lower[k])]
        return found


def in_order(shares, place):
    bit = 1
    while bit < len(shares):
        swapped = (place & bit) != 0
        shares = [jnp.where(swapped, shares[k ^ bit], shares[k]) for k in range(len(shares))]
        bit *= 2
    return jnp.stack(shares)


def plain_pair(place, shares, tall, wide):
    whole = in_order(shares, place).astype(f32)
    high = len(shares) // 2
    cut, lone = tall[0] // high, wide[0] // high
    whole = whole.reshape((high, 2) + whole.shape[1:])
    first = whole[:, :, :cut].transpose(0, 2, 1, 3).reshape(tall)
    second = whole[:, :, cut:].reshape(high, 2, -1, lone, whole.shape[-1])
    return first, second.transpose(0, 3, 1, 2, 4).reshape(wide)


def plain_mix(place, shares, shape):
    whole = in_order(shares, place).astype(f32)
    half = whole.shape[-1]
    whole = whole.reshape((len(shares) // 2, 2) + whole.shape[1:])
    whole = jnp.concatenate([whole[:, 0], whole[:, 1, :, 2 * half - shape[1] :]], axis=-1)
    return whole.reshape(shape)


def sum_tok(part):
    for bit in range(bits_of("tok")):
        part = part + exchange(part, "tok", bit)
    return part


def swap(parts):
    return lax.all_to_all(parts, "ch", split_axis=0, concat_axis=0, tiled=True)


def folded(parts):
    devices, channels, span = parts.shape[0], parts.shape[-2], parts.shape[-1]
    if channels % 16 == 0:
        return parts
    return jnp.moveaxis(parts, 0, -3).reshape((1,) + parts.shape[1:-2] + (devices * channels, span))


def unfolded(parts, devices):
    if parts.shape[0] == devices:
        return parts
    channels, span = parts.shape[-2] // devices, parts.shape[-1]
    return jnp.moveaxis(parts.reshape(parts.shape[1:-2] + (devices, channels, span)), -3, 0)


def local(
    inputs,
    out_grad,
    seq_lengths,
    ema_alpha,
    ema_delta,
    ema_beta,
    ema_eta,
    ema_omega,
    w_mix,
    b_mix,
    w_value,
    b_value,
    w_out,
    b_out,
    qk_scale,
    qk_shift,
    ln_gain,
    ln_bias,
    w_up,
    b_up,
    w_down,
    b_down,
):
    count, channels, local_len = inputs.shape
    width, mwidth = w_mix.shape
    vwidth, ff = w_value.shape[1], w_up.shape[1]
    devices, tok_size = lax.axis_size("ch"), lax.axis_size("tok")
    columns = count * channels
    span = local_len // devices
    tok_index = lax.axis_index("tok").astype(jnp.int32)
    ch_index = lax.axis_index("ch").astype(jnp.int32)
    spot = jnp.stack([tok_index * local_len + ch_index * span, ch_index, tok_index])
    apart = devices <= 8 and channels % 16 == 0

    def by_column(parts):
        whole = unfolded(parts, devices)
        return pad_to_lanes(whole.reshape(whole.shape[:-3] + (columns, span)), whole.ndim - 3)

    where = vectors(width, mwidth, vwidth, ff)
    vec = jnp.concatenate([b_mix, b_value, b_out, ln_gain, ln_bias, b_up, b_down])[None]
    params = ema_params(ema_alpha, ema_delta, ema_beta, ema_eta, count)
    omega = pad_to_lanes(jnp.tile(ema_omega, count)[None], 1)

    flat = inputs.reshape(columns, local_len)
    raw = by_blocks(spot, flat, out_grad.reshape(columns, local_len))
    raw = folded(swap(raw.reshape(devices, 2, count, channels, span)))
    xs, ends, total = ema_ends(pad_to_lanes(flat, 0), params)
    totals = lax.all_gather(total, "tok")
    mixed, slope, entry = ema_mix(spot, xs, ends, params, omega, totals, apart)
    if apart:
        mixed = [part.reshape(count, channels, span) for part in mixed]
        mixed = [part if k == 0 else across(part, "ch", k) for k, part in enumerate(mixed)]
    else:
        mixed = folded(swap(mixed[0][:, :columns].reshape(devices, count, channels, span)))
        mixed = [mixed[0]] if mixed.shape[0] == 1 else [mixed.transpose(1, 0, 2, 3).reshape(count, width, span)]
    x, values, vslope, x_t = value_part(raw, w_value, vec, where, (entry,))
    (
        mixed_t, result, query, key, shared, qslope, probs, reset, turned, gated_t,
        hslope, uslope, keep, unit, rstd, normed_t, hidden_t, fslope,
    ) = forward_part(
        spot, seq_lengths, raw.shape[:1] + raw.shape[2:], mixed, x, values, w_mix, w_out, w_up, w_down, vec,
        where, qk_scale, qk_shift,
    )
    owners = devices * tok_size // 2
    joined = owners if width // owners % 16 == 0 else 0
    lines = 64 // tok_size
    halves, g, dffn, small_ffn = back_ffn(
        spot, seq_lengths, joined, lines, raw, hidden_t, fslope, normed_t, w_down
    )
    ffn = Sum(spot, halves[::2], [[part] for part in halves[1::2]], Y_THEN_Z)
    dh, du, direct, small_norm = back_norm(g, dffn, unit, rstd, vec, where, hslope, uslope, keep, w_up)
    last = ffn.step((small_norm,))
    dmix, dvalue, back_mix, joint, table = back_attend(
        dh, du, direct, reset, turned, values, vslope, probs, query, key, shared, qslope,
        qk_scale, small_ffn, small_norm, result, w_out, w_mix, w_value, (last,),
    )
    kept, sent = back_mix_weight(spot, joined, mixed_t, dmix, (table,))
    mix = Sum(spot, kept, sent, X_FIRST)
    kept, sent = back_mid(spot, joined, gated_t, dh, x_t, dvalue, table, lines, (kept[0],))
    last = kept[0]
    back_mix = swap(unfolded(back_mix, devices))
    if not joined:
        table = table.reshape(tok_size // 2, 2, lines, TABLE)
        for group, which in ((kept, side_of("tok", 0)), (sent, 1 - side_of("tok", 0))):
            part = lax.dynamic_index_in_dim(table, which, 1, keepdims=False)
            part = jnp.broadcast_to(part[None], (devices,) + part.shape).reshape(-1, TABLE)
            group.append(part if group is kept else [part])
    mid = Sum(spot, kept, sent, Y_FIRST)
    last = ffn.step((last,))
    last = mix.step((last,))
    last = mid.step((last,))
    pull, heads, total = ema_back(by_column(back_mix), slope, params, (last,))
    totals = lax.all_gather(total, "tok")
    last = mix.step((totals,))
    joint, _ = lax.optimization_barrier((unfolded(joint, devices), last))
    joint = swap(joint)
    last = mid.step((last,))
    sums = ema_sums(spot, xs, pull, entry, heads, totals, params, (last,))
    last = mix.step((sums,))
    last = mid.step((last,))
    last = ffn.step((last,))
    last = mix.step((last,))
    while len(mid.stages) + len(mix.stages) + len(ffn.stages):
        for group in (mid, ffn, mix):
            last = group.step((last,)) if group.stages else last
    input_grad, output = ema_finish(spot, pull, heads, params, omega, totals, by_column(joint), (last,))
    ema_grads = ema_param_grads(sum_tok(sums), ema_alpha, ema_delta, ema_beta, ema_eta, count)
    mix.arrived[0], output, ema_grads = lax.optimization_barrier((mix.arrived[0], output, ema_grads))
    last = output
    input_grad = input_grad[:columns].reshape(inputs.shape)
    output = output[:columns].reshape(inputs.shape)

    tall, wide = (vwidth // devices, width), (width // devices, vwidth)
    shares = mid.shares()
    half = qk_scale.shape[1]
    across_mix = (width // devices, mwidth)
    if joined:
        vectors_of = [(mwidth,), (vwidth,), (width,), qk_scale.shape, qk_scale.shape, (width,), (width,), (ff,), (width,)]
        g_down, g_up = finish_pair(spot, ffn.shares(), tall, wide, after=(last,))
        g_out, g_value, *found = finish_pair(spot, shares, tall, wide, lines, vectors_of, (last,))
        g_mix = finish_mix(spot, mix.shares(), across_mix, (last,))
    else:
        table = in_order([part[-lines:] for part in shares], tok_index).astype(f32).reshape(-1)
        shares = [part[:-lines] for part in shares]
        g_out, g_value = plain_pair(tok_index, shares, tall, wide)
        g_down, g_up = plain_pair(tok_index, ffn.shares(), tall, wide)
        g_mix = plain_mix(tok_index, mix.shares(), across_mix)
        found, at = [], 0
        for size in (mwidth, vwidth, width, half, half, half, half, width, width, ff, width):
            found.append(table[at : at + size])
            at += -(-size // TABLE) * TABLE
        found = found[:3] + [jnp.stack(found[3:5]), jnp.stack(found[5:7])] + found[7:]
    g_bmix, g_bvalue, g_bout, g_qscale, g_qshift, g_gain, g_lnbias, g_bup, g_bdown = found
    return (
        output,
        input_grad,
        *ema_grads,
        g_mix,
        g_bmix,
        g_value,
        g_bvalue,
        g_out,
        g_bout,
        g_qscale,
        g_qshift,
        g_gain,
        g_lnbias,
        g_up,
        g_bup,
        g_down,
        g_bdown,
    )


def solution(mesh):
    by_ch = P("ch", None)
    placed = P(None, "ch", "tok")
    return jax.shard_map(
        local,
        mesh=mesh,
        in_specs=(placed, placed, P()) + (by_ch,) * 4 + (P("ch"),) + (P(),) * 14,
        out_specs=(
            (placed, placed)
            + (by_ch,) * 4
            + (P("ch"), by_ch, P(), by_ch, P(), by_ch)
            + (P(),) * 5
            + (by_ch, P(), by_ch, P())
        ),
        check_vma=False,
    )
```

```python
import functools
import jax
import jax.numpy as jnp
from jax import lax
from jax.experimental import pallas as pl
from jax.experimental.pallas import tpu as pltpu
from jax.sharding import PartitionSpec as P

GROUP = 128
SUB = 8
LANES = 128
f32 = jnp.float32


def by_tile(shape, dim):
    block = tuple(LANES if k == dim else size for k, size in enumerate(shape))
    return pl.BlockSpec(block, lambda i: tuple(i if k == dim else 0 for k in range(len(shape))))


def in_smem():
    return pl.BlockSpec(memory_space=pltpu.SMEM)


def roomy(mib=5):
    return pltpu.CompilerParams(vmem_limit_bytes=mib * 1024 * 1024)


def work(flops, moved, exps=0):
    return pl.CostEstimate(flops=1, bytes_accessed=1, transcendentals=0)


def launch(kernel, outs, ins, in_specs, out_specs, after=(), grid=(), scratch=(), mib=5, cost=None):
    count = len(ins)

    def run(*refs):
        kernel(*refs[:count], *refs[count + len(after) :])

    return pl.pallas_call(
        run,
        grid=grid,
        out_shape=tuple(jax.ShapeDtypeStruct(shape, kind) for shape, kind in outs),
        in_specs=list(in_specs) + [pl.BlockSpec(memory_space=pl.ANY)] * len(after),
        out_specs=tuple(out_specs),
        scratch_shapes=list(scratch),
        compiler_params=roomy(mib),
        cost_estimate=cost,
    )(*ins, *after)


def rates(params_ref):
    rate = jax.nn.sigmoid(params_ref[0])
    drop = rate * jax.nn.sigmoid(params_ref[1])
    weight = params_ref[3] * rate * params_ref[2]
    return 1.0 - drop, jnp.log1p(-drop), weight


def spread(ref, j):
    return jnp.broadcast_to(ref[pl.ds(j, 1), :], (SUB, LANES))


def tree_sum(parts):
    while len(parts) > 1:
        parts = [a + b for a, b in zip(parts[::2], parts[1::2])] + parts[len(parts) & ~1 :]
    return parts[0]


def block_rows(g, t):
    return pl.ds(g * GROUP + t, SUB, stride=GROUP)


def state_rows(g, j, expand):
    return pl.ds(g * expand + j, SUB, stride=expand)


def blocks_kernel(spot_ref, first_ref, second_ref, out_ref, sems):
    copies = []
    for b in range(out_ref.shape[0]):
        cols = pl.ds(b * GROUP, GROUP)
        for which, ref in enumerate((first_ref, second_ref)):
            copies.append(pltpu.make_async_copy(ref.at[:, cols], out_ref.at[b, which], sems.at[2 * b + which]))
    for copy in copies:
        copy.start()
    for copy in copies:
        copy.wait()


def by_blocks(spot, first, second):
    columns, length = first.shape
    blocks = length // GROUP
    anywhere = pl.BlockSpec(memory_space=pl.ANY)
    return launch(
        blocks_kernel,
        [((blocks, 2, columns, GROUP), first.dtype)],
        (spot, first, second),
        [in_smem(), anywhere, anywhere],
        [anywhere],
        scratch=[pltpu.SemaphoreType.DMA((2 * blocks,))],
        mib=1,
    )[0]


def ema_ends_kernel(x_ref, params_ref, xs_ref, ends_ref, total_ref, decay_ref):
    length = x_ref.shape[1]
    expand = params_ref.shape[1]
    blocks = length // GROUP
    decay, log_decay, _ = rates(params_ref)
    decay_ref[...] = decay
    for b in range(blocks):
        rows = pl.ds(b * GROUP, GROUP)
        xs_ref[rows, :] = x_ref[:, rows].astype(f32).T
    factors = [spread(decay_ref, j) for j in range(expand)]
    for g in range(0, blocks, SUB):

        def step(t, states):
            now = xs_ref[block_rows(g, t), :]
            return tuple(f * s + now for f, s in zip(factors, states))

        states = (jnp.zeros((SUB, LANES), f32),) * expand
        states = lax.fori_loop(0, GROUP, step, states, unroll=8)
        for j in range(expand):
            ends_ref[state_rows(g, j, expand), :] = states[j]
    jump = jnp.exp(GROUP * log_decay)
    carry = jnp.zeros_like(jump)
    for b in range(blocks):
        carry = jump * carry + ends_ref[pl.ds(b * expand, expand), :]
    total_ref[...] = carry


def ema_ends(x, params, after=()):
    columns, length = x.shape
    expand = params.shape[1]
    shapes = ((length, columns), (length // GROUP * expand, columns), (expand, columns))
    return launch(
        ema_ends_kernel,
        [(shape, f32) for shape in shapes],
        (x, params),
        [by_tile(x.shape, 0), by_tile(params.shape, 2)],
        [by_tile(shape, 1) for shape in shapes],
        after=after,
        grid=(columns // LANES,),
        scratch=[pltpu.VMEM((expand, LANES), f32)],
        mib=5 * max(1, length // 1024),
        cost=work(2 * expand * length * columns, 6 * length * columns),
    )


def ema_mix_kernel(
    spot_ref, xs_ref, ends_ref, params_ref, omega_ref, totals_ref, *refs
):
    mixed_refs, (slope_ref, entry_ref, decay_ref, weight_ref, smooth_ref) = refs[:-5], refs[-5:]
    length = xs_ref.shape[0]
    expand = params_ref.shape[1]
    blocks = length // GROUP
    decay, log_decay, weight = rates(params_ref)
    decay_ref[...] = decay
    weight_ref[...] = weight
    whole = jnp.exp(length * log_decay)
    jump = jnp.exp(GROUP * log_decay)
    carry = jnp.zeros_like(jump)
    for k in range(totals_ref.shape[0]):
        carry = jnp.where(k < spot_ref[2], whole * carry + totals_ref[k], carry)
    for b in range(blocks):
        rows = pl.ds(b * expand, expand)
        entry_ref[rows, :] = carry
        carry = jump * carry + ends_ref[rows, :]
    factors = [spread(decay_ref, j) for j in range(expand)]
    weights = [spread(weight_ref, j) for j in range(expand)]
    for g in range(0, blocks, SUB):

        def step(t, states):
            now = xs_ref[block_rows(g, t), :]
            states = tuple(f * s + now for f, s in zip(factors, states))
            smooth_ref[block_rows(g, t), :] = tree_sum([w * s for w, s in zip(weights, states)])
            return states

        start = tuple(entry_ref[state_rows(g, j, expand), :] for j in range(expand))
        lax.fori_loop(0, GROUP, step, start, unroll=8)
    for k in range(blocks):
        rows = pl.ds(pl.multiple_of((spot_ref[1] ^ k) * GROUP, GROUP), GROUP)
        pre = smooth_ref[rows, :] + omega_ref[...] * xs_ref[rows, :]
        sigma = jax.nn.sigmoid(pre)
        block = (pre * sigma).T.astype(jnp.bfloat16)
        if len(mixed_refs) == 1:
            mixed_refs[0][spot_ref[1] ^ k] = block
        else:
            mixed_refs[k][...] = block
        slope_ref[rows, :] = (sigma * (1.0 + pre * (1.0 - sigma))).astype(slope_ref.dtype)


def ema_mix(spot, xs, ends, params, omega, totals, apart, after=()):
    length, columns = xs.shape
    expand = params.shape[1]
    blocks = length // GROUP
    mixed = [(columns, GROUP)] * blocks if apart else [(blocks, columns, GROUP)]
    *found, slope, entry = launch(
        ema_mix_kernel,
        [(shape, jnp.bfloat16) for shape in mixed] + [(xs.shape, jnp.bfloat16), (ends.shape, f32)],
        (spot, xs, ends, params, omega, totals),
        [
            in_smem(), by_tile(xs.shape, 1), by_tile(ends.shape, 1), by_tile(params.shape, 2),
            by_tile(omega.shape, 1), by_tile(totals.shape, 2),
        ],
        [by_tile(shape, len(shape) - 2) for shape in mixed] + [by_tile(xs.shape, 1), by_tile(ends.shape, 1)],
        after=after,
        grid=(columns // LANES,),
        scratch=[
            pltpu.VMEM((expand, LANES), f32),
            pltpu.VMEM((expand, LANES), f32),
            pltpu.VMEM((length, LANES), f32),
        ],
        mib=5 * max(1, length // 1024),
        cost=work(4 * expand * length * columns, 10 * length * columns, length * columns),
    )
    return found, slope, entry


def ema_back_kernel(dmix_ref, slope_ref, params_ref, pull_ref, heads_ref, total_ref, decay_ref):
    length = slope_ref.shape[0]
    expand = params_ref.shape[1]
    blocks = length // GROUP
    decay, log_decay, _ = rates(params_ref)
    decay_ref[...] = decay
    for b in range(blocks):
        rows = pl.ds(b * GROUP, GROUP)
        pull_ref[rows, :] = dmix_ref[b].astype(f32).T * slope_ref[rows, :].astype(f32)
    factors = [spread(decay_ref, j) for j in range(expand)]
    for g in range(0, blocks, SUB):

        def step(t, states):
            now = pull_ref[block_rows(g, GROUP - 1 - t), :]
            return tuple(f * s + now for f, s in zip(factors, states))

        states = (jnp.zeros((SUB, LANES), f32),) * expand
        states = lax.fori_loop(0, GROUP, step, states, unroll=8)
        for j in range(expand):
            heads_ref[state_rows(g, j, expand), :] = states[j]
    jump = jnp.exp(GROUP * log_decay)
    carry = jnp.zeros_like(jump)
    for b in reversed(range(blocks)):
        carry = jump * carry + heads_ref[pl.ds(b * expand, expand), :]
    total_ref[...] = carry


def ema_back(dmix, slope, params, after=()):
    length, columns = slope.shape
    expand = params.shape[1]
    shapes = ((length, columns), (length // GROUP * expand, columns), (expand, columns))
    return launch(
        ema_back_kernel,
        [(shape, f32) for shape in shapes],
        (dmix, slope, params),
        [by_tile(dmix.shape, 1), by_tile(slope.shape, 1), by_tile(params.shape, 2)],
        [by_tile(shape, 1) for shape in shapes],
        after=after,
        grid=(columns // LANES,),
        scratch=[pltpu.VMEM((expand, LANES), f32)],
        mib=5 * max(1, length // 1024),
        cost=work(2 * expand * length * columns, 8 * length * columns),
    )


def enter_from_later(spot_ref, heads_ref, totals_ref, enter_ref, log_decay, length):
    expand = log_decay.shape[0]
    whole = jnp.exp(length * log_decay)
    jump = jnp.exp(GROUP * log_decay)
    carry = jnp.zeros_like(jump)
    for k in reversed(range(totals_ref.shape[0])):
        carry = jnp.where(k > spot_ref[2], whole * carry + totals_ref[k], carry)
    for b in reversed(range(length // GROUP)):
        rows = pl.ds(b * expand, expand)
        enter_ref[rows, :] = carry
        carry = jump * carry + heads_ref[rows, :]


def ema_finish_kernel(
    spot_ref, pull_ref, heads_ref, params_ref, omega_ref, totals_ref, direct_ref, result_ref,
    grad_ref, output_ref, decay_ref, weight_ref, enter_ref, smooth_ref,
):
    length = pull_ref.shape[0]
    expand = params_ref.shape[1]
    blocks = length // GROUP
    decay, log_decay, weight = rates(params_ref)
    decay_ref[...] = decay
    weight_ref[...] = weight
    enter_from_later(spot_ref, heads_ref, totals_ref, enter_ref, log_decay, length)
    factors = [spread(decay_ref, j) for j in range(expand)]
    weights = [spread(weight_ref, j) for j in range(expand)]
    for g in range(0, blocks, SUB):

        def step(t, states):
            now = pull_ref[block_rows(g, GROUP - 1 - t), :]
            states = tuple(f * s + now for f, s in zip(factors, states))
            back = tree_sum([w * s for w, s in zip(weights, states)])
            smooth_ref[block_rows(g, GROUP - 1 - t), :] = back
            return states

        start = tuple(enter_ref[state_rows(g, j, expand), :] for j in range(expand))
        lax.fori_loop(0, GROUP, step, start, unroll=8)
    for b in range(blocks):
        rows = pl.ds(b * GROUP, GROUP)
        back = smooth_ref[rows, :] + omega_ref[...] * pull_ref[rows, :]
        grad_ref[:, rows] = back.T + direct_ref[b, 0].astype(f32)
        output_ref[:, rows] = result_ref[b, 0]


def ema_finish(spot, pull, heads, params, omega, totals, joint, after=()):
    length, columns = pull.shape

    def part(which):
        return pl.BlockSpec((length // GROUP, 1, LANES, GROUP), lambda i: (0, which, i, 0))

    expand = params.shape[1]
    return launch(
        ema_finish_kernel,
        [((columns, length), f32), ((columns, length), joint.dtype)],
        (spot, pull, heads, params, omega, totals, joint, joint),
        [
            in_smem(), by_tile(pull.shape, 1), by_tile(heads.shape, 1), by_tile(params.shape, 2),
            by_tile(omega.shape, 1), by_tile(totals.shape, 2), part(0), part(1),
        ],
        [by_tile((columns, length), 0)] * 2,
        after=after,
        grid=(columns // LANES,),
        scratch=[
            pltpu.VMEM((expand, LANES), f32),
            pltpu.VMEM((expand, LANES), f32),
            pltpu.VMEM((heads.shape[0], LANES), f32),
            pltpu.VMEM((length, LANES), f32),
        ],
        mib=5 * max(1, length // 1024),
        cost=work(4 * expand * length * columns, 14 * length * columns),
    )


def ema_sums_kernel(spot_ref, xs_ref, pull_ref, entry_ref, heads_ref, totals_ref, params_ref, sums_ref, decay_ref, enter_ref):
    length = xs_ref.shape[0]
    expand = params_ref.shape[1]
    blocks = length // GROUP
    half = expand // 2
    decay, log_decay, _ = rates(params_ref)
    decay_ref[...] = decay
    enter_from_later(spot_ref, heads_ref, totals_ref, enter_ref, log_decay, length)
    for low in range(0, expand, half):
        factors = [spread(decay_ref, low + j) for j in range(half)]
        zero = (jnp.zeros((SUB, LANES), f32),) * half
        plain, turned = zero, zero
        for g in range(0, blocks, SUB):

            def step(t, held):
                states, slants, plain, turned = held
                now, pull = xs_ref[block_rows(g, t), :], pull_ref[block_rows(g, t), :]
                slants = tuple(f * p + s for f, p, s in zip(factors, slants, states))
                states = tuple(f * s + now for f, s in zip(factors, states))
                plain = tuple(a + pull * s for a, s in zip(plain, states))
                turned = tuple(a + pull * p for a, p in zip(turned, slants))
                return states, slants, plain, turned

            start = tuple(entry_ref[state_rows(g, low + j, expand), :] for j in range(half))
            held = (start, zero, plain, turned)
            _, slants, plain, turned = lax.fori_loop(0, GROUP, step, held, unroll=8)
            turned = tuple(
                a + f * p * enter_ref[state_rows(g, low + j, expand), :]
                for j, (a, f, p) in enumerate(zip(turned, factors, slants))
            )
        for j in range(half):
            sums_ref[pl.ds(low + j, 1), :] = jnp.sum(plain[j], axis=0, keepdims=True)
            sums_ref[pl.ds(expand + low + j, 1), :] = jnp.sum(turned[j], axis=0, keepdims=True)
    straight = jnp.zeros((SUB, LANES), f32)
    for b in range(0, length, SUB):
        straight = straight + xs_ref[pl.ds(b, SUB), :] * pull_ref[pl.ds(b, SUB), :]
    sums_ref[pl.ds(2 * expand, SUB), :] = straight


def ema_sums(spot, xs, pull, entry, heads, totals, params, after=()):
    length, columns = xs.shape
    expand = params.shape[1]
    shape = (2 * expand + SUB, columns)
    return launch(
        ema_sums_kernel,
        [(shape, f32)],
        (spot, xs, pull, entry, heads, totals, params),
        [
            in_smem(), by_tile(xs.shape, 1), by_tile(xs.shape, 1), by_tile(entry.shape, 1), by_tile(entry.shape, 1),
            by_tile(totals.shape, 2), by_tile(params.shape, 2),
        ],
        [by_tile(shape, 1)],
        after=after,
        grid=(columns // LANES,),
        scratch=[pltpu.VMEM((expand, LANES), f32), pltpu.VMEM((entry.shape[0], LANES), f32)],
        mib=5 * max(1, length // 1024),
        cost=work(8 * expand * length * columns, 8 * length * columns),
    )[0]


def pad_to_lanes(part, dim):
    extra = -part.shape[dim] % LANES
    if extra == 0:
        return part
    return jnp.pad(part, [(0, extra if k == dim else 0) for k in range(part.ndim)])


def ema_params(alpha, delta, beta, eta, count):
    packed = jnp.swapaxes(jnp.stack([alpha, delta, beta, eta]), 1, 2)
    return pad_to_lanes(jnp.tile(packed, (1, 1, count)), 2)


def ema_param_grads(total, alpha, delta, beta, eta, count):
    channels, expand = alpha.shape
    summed = jnp.sum(total[:, : count * channels].reshape(-1, count, channels), axis=1)
    plain, turned = summed[:expand].T, summed[expand : 2 * expand].T
    omega = jnp.sum(summed[2 * expand :], axis=0)
    rate, damp = jax.nn.sigmoid(alpha), jax.nn.sigmoid(delta)
    g_alpha = eta * beta * rate * (1.0 - rate) * (plain - damp * rate * turned)
    g_delta = -(eta * beta * rate * rate * damp * (1.0 - damp)) * turned
    return g_alpha, g_delta, rate * eta * plain, rate * beta * plain, omega


low = jnp.bfloat16
CHUNK = 256
MIB = (3, 11, 8, 5, 6, 8, 8, 6, 4, 4)
TABLE = 384


def nn(left, right):
    return jnp.dot(left, right, preferred_element_type=f32)


def nt(left, right):
    return lax.dot_general(left, right, (((1,), (1,)), ((), ())), preferred_element_type=f32)


def silu_pair(pre):
    sigma = jax.nn.sigmoid(pre)
    return pre * sigma, sigma * (1.0 + pre * (1.0 - sigma))


def each(width, body, size=CHUNK):
    for at in range(0, width, size):
        body(at)


def wide_block(ref, which, n):
    part = ref[:, which, n]
    return part.reshape(part.shape[0] * part.shape[1], part.shape[2])


def live_lanes(spot_ref, lengths_ref, n, shape):
    return spot_ref[0] + lax.broadcasted_iota(jnp.int32, shape, 1) < lengths_ref[n]


def span_of(ref, n):
    return pl.ds(n * GROUP, GROUP)


def call(kernel, outs, ins, smem=0, hbm=0, scratch=(), moved=1, mib=16, after=()):
    spaces = [pltpu.SMEM] * smem + [pl.ANY] * hbm + [pltpu.VMEM] * (len(ins) - smem - hbm)
    return launch(
        kernel,
        outs,
        ins,
        [pl.BlockSpec(memory_space=space) for space in spaces],
        [pl.BlockSpec(memory_space=pltpu.VMEM) for _ in outs],
        after=after,
        scratch=scratch,
        mib=mib,
        cost=pl.CostEstimate(flops=1, bytes_accessed=moved, transcendentals=0),
    )


def vectors(width, mwidth, vwidth, ff):
    sizes = (
        ("mix", mwidth), ("value", vwidth), ("out", width), ("gain", width),
        ("shift", width), ("up", ff), ("down", width),
    )
    place, at = {}, 0
    for name, size in sizes:
        place[name] = at
        at += size
    return place


def piece(ref, base, at, size):
    return ref[:, pl.ds(base + at, size)]


def value_kernel(base, w_ref, x_ref, vec_ref, rows_ref, values_ref, slope_ref, rows_t_ref):
    for n in range(x_ref.shape[2]):
        rows = pl.ds(n * GROUP, GROUP)
        block = wide_block(x_ref, 0, n)
        rows_t_ref[:, rows] = block
        rows_ref[rows, :] = block.T

    def chunk(at):
        cols = pl.ds(at, CHUNK)
        act, slope = silu_pair(nn(rows_ref[...], w_ref[:, cols]) + piece(vec_ref, base, at, CHUNK))
        values_ref[:, cols] = act.astype(low)
        slope_ref[:, cols] = slope.astype(low)

    each(w_ref.shape[1], chunk)


def value_part(x, w_value, vec, where, after=()):
    width, vwidth = w_value.shape
    count = x.shape[2] * GROUP
    return call(
        functools.partial(value_kernel, where["value"]),
        [((count, width), low), ((count, vwidth), low), ((count, vwidth), low), ((width, count), low)],
        (w_value, x, vec),
        mib=MIB[0],
        after=after,
    )


def forward_kernel(
    pieces, where, spot_ref, lengths_ref, wmix_ref, wout_ref, wup_ref, wdown_ref,
    x_ref, values_ref, vec_ref, qscale_ref, qshift_ref, *refs
):
    forward_rows(spot_ref, refs[:pieces], refs[pieces], refs[-6])
    forward_body(
        where, spot_ref, lengths_ref, wmix_ref, wout_ref, wup_ref, wdown_ref,
        x_ref, values_ref, vec_ref, qscale_ref, qshift_ref, *refs[pieces + 1 :]
    )


def forward_rows(spot_ref, mixed_refs, mixed_t_ref, m_ref):
    for k, ref in enumerate(mixed_refs):
        seqs, channels, _ = ref.shape
        at = pl.multiple_of((spot_ref[1] ^ k) * channels, 16) if len(mixed_refs) > 1 else 0
        for n in range(seqs):
            mixed_t_ref[pl.ds(at, channels), pl.ds(n * GROUP, GROUP)] = ref[n]
    for n in range(m_ref.shape[0] // GROUP):
        rows = pl.ds(n * GROUP, GROUP)
        m_ref[rows, :] = mixed_t_ref[:, rows].T


def forward_body(
    where, spot_ref, lengths_ref, wmix_ref, wout_ref, wup_ref, wdown_ref,
    x_ref, values_ref, vec_ref, qscale_ref, qshift_ref,
    out_ref, query_ref, key_ref, shared_ref, qslope_ref, probs_ref, reset_ref, turned_ref, gated_t_ref,
    hslope_ref, uslope_ref, keep_ref, unit_ref, rstd_ref, normed_t_ref, hidden_t_ref, fslope_ref,
    m_ref, update_ref, gated_ref, blend_ref, normed_ref, ffn_ref,
):
    width, vwidth = wout_ref.shape[1], wout_ref.shape[0]
    zwidth = qscale_ref.shape[1]
    seqs = x_ref.shape[0] // GROUP

    def mix(at, size=CHUNK):
        cols = pl.ds(at, size)
        return nn(m_ref[...], wmix_ref[:, cols]) + piece(vec_ref, where["mix"], at, size)

    shared, qslope = silu_pair(mix(width, zwidth))
    shared_ref[...] = shared
    qslope_ref[...] = qslope
    query_ref[...] = (shared * qscale_ref[pl.ds(0, 1), :] + qshift_ref[pl.ds(0, 1), :]).astype(low)
    key_ref[...] = (shared * qscale_ref[pl.ds(1, 1), :] + qshift_ref[pl.ds(1, 1), :]).astype(low)
    causal = lax.broadcasted_iota(jnp.int32, (GROUP, GROUP), 0) >= lax.broadcasted_iota(
        jnp.int32, (GROUP, GROUP), 1
    )
    for n in range(seqs):
        rows = pl.ds(n * GROUP, GROUP)
        scores = jnp.where(causal, nt(query_ref[rows, :], key_ref[rows, :]) * zwidth**-0.5, -1e30)
        scores = jnp.exp(scores - jnp.max(scores, axis=-1, keepdims=True))
        probs_ref[rows, :] = scores / jnp.sum(scores, axis=-1, keepdims=True)

    def gate(at):
        update_ref[:, pl.ds(at, CHUNK)] = jax.nn.sigmoid(mix(at))

    each(width, gate)

    def attend(at):
        cols = pl.ds(at, CHUNK)
        reset, slope = silu_pair(mix(width + zwidth + at))
        attended = jnp.concatenate(
            [
                nn(probs_ref[pl.ds(n * GROUP, GROUP), :].astype(low), values_ref[pl.ds(n * GROUP, GROUP), cols])
                for n in range(seqs)
            ],
            axis=0,
        )
        reset_ref[:, cols] = reset.astype(low)
        turned_ref[:, cols] = (attended * slope).astype(low)
        gated = (reset * attended).astype(low)
        gated_ref[:, cols] = gated
        gated_t_ref[cols, :] = gated.T

    each(vwidth, attend)

    def hide(at):
        cols = pl.ds(at, CHUNK)
        pre = mix(width + zwidth + vwidth + at)
        pre = pre + nn(gated_ref[...], wout_ref[:, cols]) + piece(vec_ref, where["out"], at, CHUNK)
        hidden, slope = silu_pair(pre)
        update = update_ref[:, cols]
        keep = 1.0 - update
        resid = x_ref[:, cols].astype(f32)
        hslope_ref[:, cols] = (update * slope).astype(low)
        uslope_ref[:, cols] = ((hidden - resid) * update * keep).astype(low)
        keep_ref[:, cols] = keep.astype(low)
        blend_ref[:, cols] = update * hidden + keep * resid

    each(width, hide)
    for n in range(seqs):
        rows = pl.ds(n * GROUP, GROUP)
        blend = blend_ref[rows, :]
        centered = blend - jnp.mean(blend, axis=-1, keepdims=True)
        rstd = lax.rsqrt(jnp.mean(centered * centered, axis=-1, keepdims=True) + 1e-05)
        unit = centered * rstd
        unit_ref[rows, :] = unit.astype(low)
        rstd_ref[rows, :] = jnp.broadcast_to(rstd, (GROUP, LANES))
        normed = unit * piece(vec_ref, where["gain"], 0, width) + piece(vec_ref, where["shift"], 0, width)
        blend_ref[rows, :] = normed
        normed_ref[rows, :] = normed.astype(low)
        normed_t_ref[:, rows] = normed.astype(low).T

    def lift(at):
        cols = pl.ds(at, CHUNK)
        act, slope = silu_pair(nn(normed_ref[...], wup_ref[:, cols]) + piece(vec_ref, where["up"], at, CHUNK))
        fslope_ref[:, cols] = slope.astype(low)
        act = act.astype(low)
        ffn_ref[:, cols] = act
        hidden_t_ref[cols, :] = act.T

    each(wup_ref.shape[1], lift)

    def drop(at):
        cols = pl.ds(at, CHUNK)
        blend_ref[:, cols] = blend_ref[:, cols] + nn(ffn_ref[...], wdown_ref[:, cols]) + piece(vec_ref, where["down"], at, CHUNK)

    each(width, drop)
    for n in range(seqs):
        result = blend_ref[pl.ds(n * GROUP, GROUP), :].astype(low).T
        result = jnp.where(live_lanes(spot_ref, lengths_ref, n, result.shape), result, jnp.zeros_like(result))
        out_ref[:, n] = result.reshape(out_ref.shape[0], out_ref.shape[2], GROUP)


def forward_part(spot, lengths, folded, mixed, x, values, w_mix, w_out, w_up, w_down, vec, where, qk_scale, qk_shift, after=()):
    vwidth, width = w_out.shape
    zwidth = qk_scale.shape[1]
    ff = w_up.shape[1]
    count = x.shape[0]
    narrow, wide = (count, width), (count, vwidth)
    outs = [
        ((width, count), low), (folded, low), ((count, zwidth), low), ((count, zwidth), low), ((count, zwidth), f32),
        ((count, zwidth), f32), ((count, GROUP), f32), (wide, low), (wide, low), ((vwidth, count), low),
        (narrow, low), (narrow, low), (narrow, low), (narrow, low), ((count, LANES), f32),
        ((width, count), low), ((ff, count), low), ((count, ff), low),
    ]
    scratch = [pltpu.VMEM(narrow, low), pltpu.VMEM(narrow, f32), pltpu.VMEM(wide, low)]
    scratch += [pltpu.VMEM(narrow, f32), pltpu.VMEM(narrow, low), pltpu.VMEM((count, ff), low)]
    macs = w_mix.size + w_out.size + w_up.size + w_down.size
    return call(
        functools.partial(forward_kernel, len(mixed), where),
        outs,
        (spot, lengths, w_mix, w_out, w_up, w_down, x, values, vec, qk_scale, qk_shift, *mixed),
        smem=2,
        mib=MIB[1],
        after=after,
        scratch=scratch,
    )


def column_sum(part):
    return jnp.sum(part.astype(f32), axis=0, keepdims=True)


def put(ref, row, value, columns):
    if isinstance(ref, tuple):
        lone = value.shape[0] // len(ref)
        for k, one in enumerate(ref):
            put(one, row, value[k * lone : (k + 1) * lone], columns)
        return
    if len(ref.shape) == 2:
        ref[...] = value
        return
    owners = ref.shape[0]
    lone = value.shape[0] // owners
    for owner in range(owners):
        part = value[owner * lone : (owner + 1) * lone]
        for i, at in enumerate(range(0, value.shape[1], columns)):
            ref[owner, pl.ds(row + i * lone, lone), :] = part[:, at : at + columns]


def split_product(side, keep_ref, send_ref, left, right_ref, half, columns, row=0):
    total = right_ref.shape[1]
    for ref, which in ((keep_ref, side), (send_ref, 1 - side)):
        base = which * (total - half)
        parts = []
        for at in range(0, half, CHUNK):
            cols = pl.ds(pl.multiple_of(base + at, 128), min(CHUNK, half - at))
            parts.append(nn(left, right_ref[:, cols]).astype(low))
        put(ref, row, jnp.concatenate(parts, axis=1), columns)


def split_narrow(side, keep_ref, send_ref, left_ref, right_ref):
    both = [nn(left_ref[pl.ds(at, CHUNK), :], right_ref[...]).astype(low) for at in range(0, left_ref.shape[0], CHUNK)]
    both = jnp.concatenate(both, axis=0)
    half = both.shape[1] // 2
    near, far = both[:, :half], both[:, half:]
    put(keep_ref, 0, jnp.where(side == 0, near, far), half)
    put(send_ref, 0, jnp.where(side == 0, far, near), half)


def pair_outs(tall, wide, owners, lines=0):
    if not owners:
        return [((tall[0], tall[1] // 2), low)] * 2 + [((wide[0], wide[1] // 2), low)] * 2
    rows = (tall[0] * tall[1] + wide[0] * wide[1]) // (tall[1] * owners) + lines
    return [((owners, rows, tall[1] // 2), low)] * 2


def back_ffn_kernel(
    spot_ref, lengths_ref, wdown_ref, grad_ref, hidden_t_ref, fslope_ref, normed_t_ref, *refs
):
    halves, (g_ref, dffn_ref, small_ref) = refs[:-3], refs[-3:]
    width, ff = g_ref.shape[1], wdown_ref.shape[0]
    for n in range(grad_ref.shape[2]):
        part = wide_block(grad_ref, 1, n)
        part = jnp.where(live_lanes(spot_ref, lengths_ref, n, part.shape), part, jnp.zeros_like(part))
        g_ref[pl.ds(n * GROUP, GROUP), :] = part.T
    small_ref[:, pl.ds(0, width)] = column_sum(g_ref[...])
    side = spot_ref[2] & 1
    split_narrow(side, halves[0], halves[1], hidden_t_ref, g_ref)

    def lift(at):
        part = pl.ds(at, CHUNK)
        pulled = (nt(g_ref[...], wdown_ref[part, :]) * fslope_ref[:, part].astype(f32)).astype(low)
        dffn_ref[:, part] = pulled
        small_ref[:, pl.ds(width + at, CHUNK)] = column_sum(pulled)

    each(ff, lift)
    tall = hidden_t_ref.shape[0] // halves[0].shape[0]
    split_product(side, halves[-2], halves[-1], normed_t_ref[...], dffn_ref, ff // 2, halves[-2].shape[-1], tall)
    if len(halves) == 2:
        for ref in halves:
            owners, rows, columns = ref.shape
            ref[:, pl.ds(2 * tall, rows - 2 * tall), :] = jnp.zeros((owners, rows - 2 * tall, columns), low)


def back_ffn(spot, lengths, owners, lines, grad, hidden_t, fslope, normed_t, w_down, after=()):
    ff, width = w_down.shape
    count = fslope.shape[0]
    outs = pair_outs((ff, width), (width, ff), owners, lines)
    outs += [((count, width), low), ((count, ff), low), ((1, width + ff), f32)]
    *halves, g, dffn, small = call(
        back_ffn_kernel,
        outs,
        (spot, lengths, w_down, grad, hidden_t, fslope, normed_t),
        smem=2,
        mib=MIB[2],
        after=after,
    )
    return halves, g, dffn, small


def back_norm_kernel(
    base, wup_ref, g_ref, dffn_ref, unit_ref, rstd_ref, vec_ref, hslope_ref, uslope_ref, kept_ref,
    dh_ref, du_ref, direct_ref, small_ref, dn_ref,
):
    width = wup_ref.shape[0]

    def drop(at):
        part = pl.ds(at, CHUNK)
        pulled = g_ref[:, part].astype(f32) + nt(dffn_ref[...], wup_ref[part, :])
        dn_ref[:, part] = pulled
        small_ref[:, part] = column_sum(pulled * unit_ref[:, part].astype(f32))
        small_ref[:, pl.ds(width + at, CHUNK)] = column_sum(pulled)

    each(width, drop)
    for n in range(g_ref.shape[0] // GROUP):
        rows = pl.ds(n * GROUP, GROUP)
        unit = unit_ref[rows, :].astype(f32)
        pulled = dn_ref[rows, :] * piece(vec_ref, base, 0, width)
        inner = jnp.mean(pulled * unit, axis=-1, keepdims=True)
        blend = pulled - jnp.mean(pulled, axis=-1, keepdims=True) - unit * inner
        blend = blend * rstd_ref[rows, :][:, :1]
        dh_ref[rows, :] = (blend * hslope_ref[rows, :].astype(f32)).astype(low)
        du_ref[rows, :] = (blend * uslope_ref[rows, :].astype(f32)).astype(low)
        direct_ref[rows, :] = (blend * kept_ref[rows, :].astype(f32)).astype(low)


def back_norm(g, dffn, unit, rstd, vec, where, hslope, uslope, kept, w_up, after=()):
    width = w_up.shape[0]
    narrow = g.shape
    return call(
        functools.partial(back_norm_kernel, where["gain"]),
        [(narrow, low)] * 3 + [((1, 2 * width), f32)],
        (w_up, g, dffn, unit, rstd, vec, hslope, uslope, kept),
        mib=MIB[3],
        after=after,
        scratch=[pltpu.VMEM(narrow, f32)],
    )


def back_attend_kernel(
    wout_ref, wmix_ref, wvalue_ref,
    dh_ref, du_ref, direct_ref, reset_ref, turned_ref, values_ref, vslope_ref, probs_ref,
    query_ref, key_ref, shared_ref, qslope_ref, qscale_ref, small_ffn_ref, small_norm_ref, result_ref,
    dmix_ref, dvalue_ref, mixed_ref, joint_ref,
    table_ref,
    datt_ref,
):
    vwidth, width = wout_ref.shape
    zwidth = qscale_ref.shape[1]
    count = dh_ref.shape[0]
    seqs = count // GROUP
    dmix_ref[:, pl.ds(0, width)] = du_ref[...]
    dmix_ref[:, pl.ds(width + zwidth + vwidth, width)] = dh_ref[...]

    def gate(at):
        part = pl.ds(at, CHUNK)
        pulled = nt(dh_ref[...], wout_ref[part, :])
        dmix_ref[:, pl.ds(width + zwidth + at, CHUNK)] = (
            pulled * turned_ref[:, part].astype(f32)
        ).astype(low)
        datt_ref[:, part] = (pulled * reset_ref[:, part].astype(f32)).astype(low)

    each(vwidth, gate)
    scale = zwidth**-0.5
    q_scale, k_scale = qscale_ref[pl.ds(0, 1), :], qscale_ref[pl.ds(1, 1), :]
    zero = jnp.zeros((1, zwidth), f32)
    sums = [zero, zero, zero, zero]
    for n in range(seqs):
        rows = pl.ds(n * GROUP, GROUP)
        probs = probs_ref[rows, :]
        pulled = nt(datt_ref[rows, :], values_ref[rows, :])
        pulled = probs * (pulled - jnp.sum(pulled * probs, axis=-1, keepdims=True))
        pulled = pulled.astype(low)
        d_query = nn(pulled, key_ref[rows, :]) * scale
        d_key = nn(pulled.T, query_ref[rows, :]) * scale
        probs_t = probs.astype(low).T
        shared = shared_ref[rows, :]
        found = (d_query * shared, d_key * shared, d_query, d_key)
        sums = [a + jnp.sum(b, axis=0, keepdims=True) for a, b in zip(sums, found)]
        dmix_ref[rows, pl.ds(width, zwidth)] = (
            (d_query * q_scale + d_key * k_scale) * qslope_ref[rows, :]
        ).astype(low)
        dvalue_ref[rows, :] = (nn(probs_t, datt_ref[rows, :]) * vslope_ref[rows, :].astype(f32)).astype(low)

    def turn(result):
        devices, _, channels, _ = mixed_ref.shape
        return result.astype(low).T.reshape(devices, channels, GROUP)

    for n in range(0, seqs, 2):
        result = nt(dmix_ref[pl.ds(n * GROUP, 2 * GROUP), :], wmix_ref[...])
        mixed_ref[:, n] = turn(result[:GROUP])
        mixed_ref[:, n + 1] = turn(result[GROUP:])
    for n in range(0, seqs, 2):
        rows = pl.ds(n * GROUP, 2 * GROUP)
        result = direct_ref[rows, :].astype(f32) + nt(dvalue_ref[rows, :], wvalue_ref[...])
        joint_ref[:, 0, n] = turn(result[:GROUP])
        joint_ref[:, 0, n + 1] = turn(result[GROUP:])
    joint_ref[:, 1] = result_ref[...]
    ff = small_ffn_ref.shape[1] - width
    found = (
        column_sum(dmix_ref[...]), column_sum(dvalue_ref[...]), column_sum(dh_ref[...]),
        sums[0], sums[1], sums[2], sums[3], small_norm_ref[:, :width], small_norm_ref[:, width:],
        small_ffn_ref[:, width:], small_ffn_ref[:, :width],
    )
    lines = []
    for part in found:
        for at in range(0, part.shape[1], TABLE):
            line = part[:, at : at + TABLE]
            lack = TABLE - line.shape[1]
            lines.append(line if lack == 0 else jnp.concatenate([line, jnp.zeros((1, lack), f32)], axis=1))
    lines.append(jnp.zeros((table_ref.shape[0] - len(lines), TABLE), f32))
    table_ref[...] = jnp.concatenate(lines, axis=0).astype(low)


def back_attend(dh, du, direct, reset, turned, values, vslope, probs, query, key, shared, qslope, qk_scale, small_ffn, small_norm, result, w_out, w_mix, w_value, after=()):
    vwidth, width = w_out.shape
    mwidth = w_mix.shape[1]
    count = dh.shape[0]
    outs = [((count, mwidth), low), ((count, vwidth), low)]
    outs += [(result.shape, low), (result.shape[:1] + (2,) + result.shape[1:], low), ((64, TABLE), low)]
    scratch = [pltpu.VMEM((count, vwidth), low)]
    macs = w_out.size + w_mix.size + w_value.size
    return call(
        back_attend_kernel,
        outs,
        (w_out, w_mix, w_value, dh, du, direct, reset, turned, values, vslope, probs, query, key, shared, qslope, qk_scale, small_ffn, small_norm, result),
        mib=MIB[4],
        after=after,
        scratch=scratch,
    )


def back_mid_kernel(spot_ref, gated_t_ref, dh_ref, x_t_ref, dvalue_ref, table_ref, *halves):
    side = spot_ref[2] & 1
    if len(halves) == 4:
        (kept, sent, wide_kept, wide_sent), tall = halves, 0
    else:
        kept, sent = halves[0], halves[1:]
        wide_kept, wide_sent, tall = kept, sent, gated_t_ref.shape[0] // kept.shape[0]
    split_narrow(side, kept, sent, gated_t_ref, dh_ref)
    split_product(
        side, wide_kept, wide_sent, x_t_ref[...], dvalue_ref, dvalue_ref.shape[1] // 2, wide_kept.shape[-1], tall
    )
    if len(halves) == 4:
        return
    lines = kept.shape[1] - 2 * tall
    high = table_ref.shape[0] // (2 * lines)
    for refs, which in (((kept,), side), (sent, 1 - side)):
        for ref in refs:
            for owner in range(ref.shape[0]):
                at = pl.multiple_of((2 * (owner % high) + which) * lines, 16)
                ref[owner, pl.ds(2 * tall, lines), :] = table_ref[pl.ds(at, lines), :]


def halved(outs):
    (kept, kind), (sent, _) = outs
    return [(kept, kind)] + [((sent[0] // 2,) + sent[1:], kind)] * 2


def back_mid(spot, owners, gated_t, dh, x_t, dvalue, table, lines, after=()):
    count, width = dh.shape
    vwidth = dvalue.shape[1]
    outs = pair_outs((vwidth, width), (width, vwidth), owners, lines)
    found = call(
        back_mid_kernel,
        halved(outs) if owners else outs,
        (spot, gated_t, dh, x_t, dvalue, table),
        smem=1,
        mib=MIB[5],
        after=after,
    )
    if owners:
        return [found[0]], [list(found[1:])]
    return [found[0], found[2]], [[found[1]], [found[3]]]


def back_mix_kernel(spot_ref, mixed_t_ref, dmix_ref, keep_ref, *send_refs):
    half = keep_ref.shape[-1]
    split_product(spot_ref[2] & 1, keep_ref, send_refs, mixed_t_ref[...], dmix_ref, half, half)


def back_mix_weight(spot, owners, mixed_t, dmix, after=()):
    mwidth = dmix.shape[1]
    width, count = mixed_t.shape
    half = -(-mwidth // 256) * 128
    outs = [((width, half), low)] * 2
    kept, *sent = call(
        back_mix_kernel,
        halved(outs) if owners else outs,
        (spot, mixed_t, dmix),
        smem=1,
        mib=MIB[6],
        after=after,
    )
    return [kept], [sent]


def halve_kernel(index, bit, spot_ref, kept_ref, *refs):
    arrived, (sent_ref, stay_ref) = refs[:-2], refs[-2:]
    outer, inner, _, _ = sent_ref.shape
    lone = outer // len(arrived)
    mine = (spot_ref[index] >> bit) & 1
    for ref, which in ((sent_ref, 1 - mine), (stay_ref, mine)):
        for a in range(outer):
            for b in range(inner):
                total = kept_ref[a, which, b].astype(f32) + arrived[a // lone][a % lone, which, b].astype(f32)
                ref[a, b] = total.astype(low)


def halve(spot, kept, arrived, index, bit, at, after=()):
    dims = kept.shape[:-2]
    outer, inner = 1 << at, 1 << (len(dims) - at - 1)
    block = kept.shape[-2:]

    def shaped(part):
        return part.reshape((-1, 2, inner) + block)

    sent, stay = call(
        functools.partial(halve_kernel, index, bit),
        [((outer, inner) + block, low)] * 2,
        (spot, shaped(kept), *map(shaped, arrived)),
        smem=1,
        mib=MIB[7],
        after=after,

    )
    rest = dims[:at] + dims[at + 1 :] + block
    return sent.reshape(rest), stay.reshape(rest)


def finish_pair_kernel(count, lines, spot_ref, *refs):
    shares, outs = refs[:count], refs[count:]
    tall_ref, wide_ref = outs[:2]
    columns = shares[0].shape[1]
    cut = tall_ref.shape[0] * 2 // len(shares)
    lone = wide_ref.shape[0] * 2 // len(shares)
    for k, ref in enumerate(shares):
        at = spot_ref[2] ^ k
        high, side = at >> 1, at & 1
        tall_ref[pl.ds(pl.multiple_of(high * cut, 8), cut), pl.ds(pl.multiple_of(side * columns, 128), columns)] = ref[
            pl.ds(0, cut), :
        ].astype(f32)
        runs = wide_ref.shape[1] // 2 // columns
        for run in range(runs):
            wide_ref[
                pl.ds(pl.multiple_of(high * lone, 8), lone),
                pl.ds(pl.multiple_of((side * runs + run) * columns, 128), columns),
            ] = ref[pl.ds(cut + run * lone, lone), :].astype(f32)
        if lines:
            outs[-1][pl.ds(pl.multiple_of(at * lines, 8), lines), :] = ref[pl.ds(2 * cut, lines), :].astype(f32)
    if lines:
        row = 0
        for ref in outs[2:-1]:
            if len(ref.shape) == 2:
                for k in range(ref.shape[0]):
                    ref[pl.ds(k, 1), :] = outs[-1][pl.ds(row, 1), :][:, : ref.shape[1]]
                    row += 1
                continue
            for at in range(0, ref.shape[0], columns):
                size = min(columns, ref.shape[0] - at)
                ref[pl.ds(at, size)] = outs[-1][row, :size]
                row += 1


def finish_pair(spot, shares, tall, wide, lines=0, vectors=(), after=()):
    outs = [(tall, f32), (wide, f32)] + [(shape, f32) for shape in vectors]
    count = len(shares)
    scratch = [pltpu.VMEM((count * lines, shares[0].shape[1]), f32)] if lines else []
    kernel = functools.partial(finish_pair_kernel, count, lines)
    return call(kernel, outs, (spot, *shares), smem=1, mib=MIB[8], scratch=scratch, after=after)


def finish_mix_kernel(spot_ref, *refs):
    shares, out_ref = refs[:-1], refs[-1]
    half, mwidth = shares[0].shape[1], out_ref.shape[1]
    common = 2 * half - mwidth
    lone = out_ref.shape[0] * 2 // len(shares)
    for k, ref in enumerate(shares):
        at = spot_ref[2] ^ k
        rows = pl.ds(pl.multiple_of((at >> 1) * lone, 8), lone)
        base = pl.multiple_of(common + (at & 1) * (mwidth - half), 128)
        out_ref[rows, pl.ds(base, half - common)] = ref[:, common:].astype(f32)
        if common:

            @pl.when(at & 1 == 0)
            def _():
                out_ref[rows, pl.ds(0, common)] = ref[:, :common].astype(f32)


def finish_mix(spot, shares, shape, after=()):
    return call(finish_mix_kernel, [(shape, f32)], (spot, *shares), smem=1, mib=MIB[9], after=after)[0]


Y_FIRST = (("tok", 1), ("ch", 0))
Y_THEN_Z = (("tok", 1), ("ch", 1), ("ch", 0))
X_FIRST = (("ch", 0), ("tok", 1))


def bits_of(axis):
    return lax.axis_size(axis).bit_length() - 1


def across(part, axis, turn):
    return lax.ppermute(part, axis, [(i, i ^ turn) for i in range(lax.axis_size(axis))])


def exchange(part, axis, bit):
    return across(part, axis, 1 << bit)


def side_of(axis, bit):
    return (lax.axis_index(axis) >> bit) & 1


def by_owner(grad):
    dims = (2,) * (bits_of("ch") + bits_of("tok") - 1)
    return grad.reshape(dims + (-1, grad.shape[-1]))


def fold(part, columns):
    runs = [part[..., at : at + columns] for at in range(0, part.shape[-1], columns)]
    return jnp.concatenate(runs, axis=-2)


def add(left, right):
    return (left.astype(f32) + right.astype(f32)).astype(low)


def plain_halve(kept, arrived, mine, at):
    columns = min(part.shape[-1] for part in kept)

    def pick(which):
        def one(part):
            return lax.dynamic_index_in_dim(part, which, at, keepdims=False)

        return jnp.concatenate([fold(add(one(a), one(b)), columns) for a, b in zip(kept, arrived)], axis=-2)

    return pick(1 - mine), pick(mine)


class Sum:
    def __init__(self, spot, kept, sent, order):
        self.spot = spot
        self.names = [("ch", k) for k in reversed(range(bits_of("ch")))]
        self.names += [("tok", k) for k in reversed(range(1, bits_of("tok")))]
        self.stages = list(order) + [name for name in reversed(self.names) if name not in order]
        self.kept = [by_owner(part) for part in kept]
        arrived = [[exchange(piece, "tok", 0) for piece in part] for part in sent]
        self.arrived = arrived[0] if self.by_kernel() else [by_owner(part) for part, in arrived]

    def by_kernel(self):
        return len(self.kept) == 1 and self.kept[0].shape[-2] % 16 == 0

    def step(self, after=()):
        axis, bit = self.stages.pop(0)
        at = self.names.index((axis, bit))
        self.names.remove((axis, bit))
        if self.by_kernel():
            index = 1 if axis == "ch" else 2
            sent, stay = halve(self.spot, self.kept[0], self.arrived, index, bit, at, after)
        else:
            sent, stay = plain_halve(self.kept, self.arrived, side_of(axis, bit), at)
        self.kept, self.arrived = [stay], [exchange(sent, axis, bit)]
        return stay

    def shares(self):
        found = [add(self.kept[0], self.arrived[0])]
        for bit in reversed(range(1, bits_of("tok"))):
            found += [exchange(part, "tok", bit) for part in found]
        lower = [exchange(part, "tok", 0) for part in found]
        size = bits_of("tok") - 1
        order = [sum(((k >> (size - 1 - i)) & 1) << i for i in range(size)) for k in range(len(found))]
        found = [part for k in order for part in (found[k], lower[k])]
        return found


def in_order(shares, place):
    bit = 1
    while bit < len(shares):
        swapped = (place & bit) != 0
        shares = [jnp.where(swapped, shares[k ^ bit], shares[k]) for k in range(len(shares))]
        bit *= 2
    return jnp.stack(shares)


def plain_pair(place, shares, tall, wide):
    whole = in_order(shares, place).astype(f32)
    high = len(shares) // 2
    cut, lone = tall[0] // high, wide[0] // high
    whole = whole.reshape((high, 2) + whole.shape[1:])
    first = whole[:, :, :cut].transpose(0, 2, 1, 3).reshape(tall)
    second = whole[:, :, cut:].reshape(high, 2, -1, lone, whole.shape[-1])
    return first, second.transpose(0, 3, 1, 2, 4).reshape(wide)


def plain_mix(place, shares, shape):
    whole = in_order(shares, place).astype(f32)
    half = whole.shape[-1]
    whole = whole.reshape((len(shares) // 2, 2) + whole.shape[1:])
    whole = jnp.concatenate([whole[:, 0], whole[:, 1, :, 2 * half - shape[1] :]], axis=-1)
    return whole.reshape(shape)


def sum_tok(part):
    for bit in range(bits_of("tok")):
        part = part + exchange(part, "tok", bit)
    return part


def swap(parts):
    return lax.all_to_all(parts, "ch", split_axis=0, concat_axis=0, tiled=True)


def folded(parts):
    devices, channels, span = parts.shape[0], parts.shape[-2], parts.shape[-1]
    if channels % 16 == 0:
        return parts
    return jnp.moveaxis(parts, 0, -3).reshape((1,) + parts.shape[1:-2] + (devices * channels, span))


def unfolded(parts, devices):
    if parts.shape[0] == devices:
        return parts
    channels, span = parts.shape[-2] // devices, parts.shape[-1]
    return jnp.moveaxis(parts.reshape(parts.shape[1:-2] + (devices, channels, span)), -3, 0)


def local(
    inputs,
    out_grad,
    seq_lengths,
    ema_alpha,
    ema_delta,
    ema_beta,
    ema_eta,
    ema_omega,
    w_mix,
    b_mix,
    w_value,
    b_value,
    w_out,
    b_out,
    qk_scale,
    qk_shift,
    ln_gain,
    ln_bias,
    w_up,
    b_up,
    w_down,
    b_down,
):
    count, channels, local_len = inputs.shape
    width, mwidth = w_mix.shape
    vwidth, ff = w_value.shape[1], w_up.shape[1]
    devices, tok_size = lax.axis_size("ch"), lax.axis_size("tok")
    columns = count * channels
    span = local_len // devices
    tok_index = lax.axis_index("tok").astype(jnp.int32)
    ch_index = lax.axis_index("ch").astype(jnp.int32)
    spot = jnp.stack([tok_index * local_len + ch_index * span, ch_index, tok_index])
    apart = devices <= 8 and channels % 16 == 0

    def by_column(parts):
        whole = unfolded(parts, devices)
        return pad_to_lanes(whole.reshape(whole.shape[:-3] + (columns, span)), whole.ndim - 3)

    where = vectors(width, mwidth, vwidth, ff)
    vec = jnp.concatenate([b_mix, b_value, b_out, ln_gain, ln_bias, b_up, b_down])[None]
    params = ema_params(ema_alpha, ema_delta, ema_beta, ema_eta, count)
    omega = pad_to_lanes(jnp.tile(ema_omega, count)[None], 1)

    flat = inputs.reshape(columns, local_len)
    raw = by_blocks(spot, flat, out_grad.reshape(columns, local_len))
    raw = folded(swap(raw.reshape(devices, 2, count, channels, span)))
    xs, ends, total = ema_ends(pad_to_lanes(flat, 0), params)
    totals = lax.all_gather(total, "tok")
    mixed, slope, entry = ema_mix(spot, xs, ends, params, omega, totals, apart)
    if apart:
        mixed = [part.reshape(count, channels, span) for part in mixed]
        mixed = [part if k == 0 else across(part, "ch", k) for k, part in enumerate(mixed)]
    else:
        mixed = folded(swap(mixed[0][:, :columns].reshape(devices, count, channels, span)))
        mixed = [mixed[0]] if mixed.shape[0] == 1 else [mixed.transpose(1, 0, 2, 3).reshape(count, width, span)]
    x, values, vslope, x_t = value_part(raw, w_value, vec, where, (entry,))
    (
        mixed_t, result, query, key, shared, qslope, probs, reset, turned, gated_t,
        hslope, uslope, keep, unit, rstd, normed_t, hidden_t, fslope,
    ) = forward_part(
        spot, seq_lengths, raw.shape[:1] + raw.shape[2:], mixed, x, values, w_mix, w_out, w_up, w_down, vec,
        where, qk_scale, qk_shift,
    )
    owners = devices * tok_size // 2
    joined = owners if width // owners % 16 == 0 else 0
    lines = 64 // tok_size
    halves, g, dffn, small_ffn = back_ffn(
        spot, seq_lengths, joined, lines, raw, hidden_t, fslope, normed_t, w_down
    )
    ffn = Sum(spot, halves[::2], [[part] for part in halves[1::2]], Y_THEN_Z)
    dh, du, direct, small_norm = back_norm(g, dffn, unit, rstd, vec, where, hslope, uslope, keep, w_up)
    last = ffn.step((small_norm,))
    dmix, dvalue, back_mix, joint, table = back_attend(
        dh, du, direct, reset, turned, values, vslope, probs, query, key, shared, qslope,
        qk_scale, small_ffn, small_norm, result, w_out, w_mix, w_value, (last,),
    )
    kept, sent = back_mix_weight(spot, joined, mixed_t, dmix, (table,))
    mix = Sum(spot, kept, sent, X_FIRST)
    kept, sent = back_mid(spot, joined, gated_t, dh, x_t, dvalue, table, lines, (kept[0],))
    last = kept[0]
    back_mix = swap(unfolded(back_mix, devices))
    if not joined:
        table = table.reshape(tok_size // 2, 2, lines, TABLE)
        for group, which in ((kept, side_of("tok", 0)), (sent, 1 - side_of("tok", 0))):
            part = lax.dynamic_index_in_dim(table, which, 1, keepdims=False)
            part = jnp.broadcast_to(part[None], (devices,) + part.shape).reshape(-1, TABLE)
            group.append(part if group is kept else [part])
    mid = Sum(spot, kept, sent, Y_FIRST)
    last = ffn.step((last,))
    last = mix.step((last,))
    last = mid.step((last,))
    joint, back_mix, _ = lax.optimization_barrier((unfolded(joint, devices), back_mix, last))
    joint = swap(joint)
    pull, heads, total = ema_back(by_column(back_mix), slope, params, (last,))
    totals = lax.all_gather(total, "tok")
    sums = ema_sums(spot, xs, pull, entry, heads, totals, params, (last,))
    last = mix.step((sums,))
    last = mid.step((last,))
    last = mix.step((last,))
    last = mid.step((last,))
    last = ffn.step((last,))
    last = mix.step((last,))
    while len(mid.stages) + len(mix.stages) + len(ffn.stages):
        for group in (mid, ffn, mix):
            last = group.step((last,)) if group.stages else last
    input_grad, output = ema_finish(spot, pull, heads, params, omega, totals, by_column(joint), (last,))
    ema_grads = ema_param_grads(sum_tok(sums), ema_alpha, ema_delta, ema_beta, ema_eta, count)
    mix.arrived[0], output, ema_grads = lax.optimization_barrier((mix.arrived[0], output, ema_grads))
    last = output
    input_grad = input_grad[:columns].reshape(inputs.shape)
    output = output[:columns].reshape(inputs.shape)

    tall, wide = (vwidth // devices, width), (width // devices, vwidth)
    shares = mid.shares()
    half = qk_scale.shape[1]
    across_mix = (width // devices, mwidth)
    if joined:
        vectors_of = [(mwidth,), (vwidth,), (width,), qk_scale.shape, qk_scale.shape, (width,), (width,), (ff,), (width,)]
        g_down, g_up = finish_pair(spot, ffn.shares(), tall, wide, after=(last,))
        g_out, g_value, *found = finish_pair(spot, shares, tall, wide, lines, vectors_of, (last,))
        g_mix = finish_mix(spot, mix.shares(), across_mix, (last,))
    else:
        table = in_order([part[-lines:] for part in shares], tok_index).astype(f32).reshape(-1)
        shares = [part[:-lines] for part in shares]
        g_out, g_value = plain_pair(tok_index, shares, tall, wide)
        g_down, g_up = plain_pair(tok_index, ffn.shares(), tall, wide)
        g_mix = plain_mix(tok_index, mix.shares(), across_mix)
        found, at = [], 0
        for size in (mwidth, vwidth, width, half, half, half, half, width, width, ff, width):
            found.append(table[at : at + size])
            at += -(-size // TABLE) * TABLE
        found = found[:3] + [jnp.stack(found[3:5]), jnp.stack(found[5:7])] + found[7:]
    g_bmix, g_bvalue, g_bout, g_qscale, g_qshift, g_gain, g_lnbias, g_bup, g_bdown = found
    return (
        output,
        input_grad,
        *ema_grads,
        g_mix,
        g_bmix,
        g_value,
        g_bvalue,
        g_out,
        g_bout,
        g_qscale,
        g_qshift,
        g_gain,
        g_lnbias,
        g_up,
        g_bup,
        g_down,
        g_bdown,
    )


def solution(mesh):
    by_ch = P("ch", None)
    placed = P(None, "ch", "tok")
    return jax.shard_map(
        local,
        mesh=mesh,
        in_specs=(placed, placed, P()) + (by_ch,) * 4 + (P("ch"),) + (P(),) * 14,
        out_specs=(
            (placed, placed)
            + (by_ch,) * 4
            + (P("ch"), by_ch, P(), by_ch, P(), by_ch)
            + (P(),) * 5
            + (by_ch, P(), by_ch, P())
        ),
        check_vma=False,
    )
```
